32 devices in a mesh: dp: 8 (over z, y), sp: 4 (over x, core).
Axes of the slice: x: 2, y: 2, z: 4, core: 2. Of those that a mesh axis runs over, the one named last changes fastest.
Arguments:
- clip_video: bfloat16 [128, 3, 32, 128], P('dp', None, 'sp'), may hold values from -6 to 6
- section_input: bfloat16 [128, 8, 16, 2048], P('dp', 'sp'), may hold values from -20 to 20
- keep_mask: int32 [128], P('dp'), may hold values from 0 to 1, as said below
- w_rgb: bfloat16 [9, 3, 64], P(None, None, 'dp'), may hold values from -1.25 to 1.25
- w_stem_diff: bfloat16 [9, 6, 64], P(None, None, 'dp'), may hold values from -0.875 to 0.875
- w_first: bfloat16 [2048, 512], P('dp'), may hold values from -0.125 to 0.125
- w_middle: bfloat16 [9, 512, 512], P(None, 'dp'), may hold values from -0.09375 to 0.09375
- w_last: bfloat16 [512, 2048], P('dp'), may hold values from -0.25 to 0.25
- w_reduce: bfloat16 [512, 128], P('dp'), may hold values from -0.25 to 0.25
- w_diff_full: bfloat16 [9, 128, 128], P(None, 'dp'), may hold values from -0.1875 to 0.1875
- w_diff_half: bfloat16 [9, 128, 128], P(None, 'dp'), may hold values from -0.1875 to 0.1875
- w_expand: bfloat16 [128, 512], P('dp'), may hold values from -0.5 to 0.5
- gain_first: bfloat16 [512], P('dp'), may hold values from 0.25 to 1.75
- bias_first: bfloat16 [512], P('dp'), may hold values from -3 to 3
- gain_middle: bfloat16 [512], P('dp'), may hold values from 0.25 to 1.75
- bias_middle: bfloat16 [512], P('dp'), may hold values from -3 to 3
- gain_last: bfloat16 [2048], P('dp'), may hold values from 0.25 to 1.75
- bias_last: bfloat16 [2048], P('dp'), may hold values from -3 to 3
- stem_cot: bfloat16 [128, 64, 32, 128], P('dp', None, 'sp'), may hold values from -6 to 6
- section_cot: bfloat16 [128, 8, 16, 2048], P('dp', 'sp'), may hold values from -6 to 6
Outputs:
- stem_features: bfloat16 [128, 64, 32, 128], P('dp', None, 'sp')
- video_grad: float32 [128, 3, 32, 128], P('dp', None, 'sp')
- section_output: bfloat16 [128, 8, 16, 2048], P('dp', 'sp')
- section_input_grad: bfloat16 [128, 8, 16, 2048], P('dp', 'sp')
- grad_rgb: float32 [9, 3, 64], P(None, None, 'dp')
- grad_stem_diff: float32 [9, 6, 64], P(None, None, 'dp')
- grad_first: float32 [2048, 512], P('dp')
- grad_middle: float32 [9, 512, 512], P(None, 'dp')
- grad_last: float32 [512, 2048], P('dp')
- grad_reduce: float32 [512, 128], P('dp')
- grad_diff_full: float32 [9, 128, 128], P(None, 'dp')
- grad_diff_half: float32 [9, 128, 128], P(None, 'dp')
- grad_expand: float32 [128, 512], P('dp')
- grad_gain_first: float32 [512], P('dp')
- grad_bias_first: float32 [512], P('dp')
- grad_gain_middle: float32 [512], P('dp')
- grad_bias_middle: float32 [512], P('dp')
- grad_gain_last: float32 [2048], P('dp')
- grad_bias_last: float32 [2048], P('dp')
The draws below stay inside these ranges and needn't reach their ends.
Inputs may be any that keep to these rules, and one draw needn't show every extreme that they name: In each clip of 8 consecutive frames starting at a multiple of 8, keep_mask is 0 at the first frame and at exactly one other frame, where the second video starts, and 1 elsewhere.
All inputs are finite; a program needn't handle non-finite values.
Results may differ from the reference program's by a relative error of at most 0.018.
Values may be sent and summed in bfloat16 or wider, within the bound.
A program may use at most 256 MiB of HBM per device.

```python
import jax
import jax.numpy as jnp
from jax import lax

C5 = 2048
MID = 512
TDM_C = 128
STEM_C = 64
STEM_DIFF = 6
SEG = 8
CLIP_MB = 1
W5 = 16
WS = 128
FRAMES = 128
H5 = 8
HS = 32


def draw_keep_mask(key, part):
    clips_all = FRAMES // SEG
    split_at = jax.random.randint(key, (clips_all,), 1, SEG)
    position = jnp.arange(FRAMES, dtype=jnp.int32) % SEG
    split_each = jnp.repeat(split_at, SEG)
    return ((position != 0) & (position != split_each)).astype(jnp.int32)


def draw_section_input(key, part):
    key_a = jax.random.fold_in(key, 11)
    key_b = jax.random.fold_in(key, 12)
    row_index = jnp.arange(H5, dtype=jnp.float32)
    row_scale = jnp.exp(jnp.log(3.0) * row_index / max(H5 - 1, 1))[None, :, None, None]
    base_draw = jax.random.normal(key_a, (FRAMES, H5, W5, C5), jnp.float32)
    offset = 0.5 * jax.random.normal(key_b, (C5,), jnp.float32)
    values = base_draw * row_scale + offset
    return jnp.clip(values, -20.0, 20.0).astype(jnp.bfloat16)


def raised(drawn, own_key, source, target, parts, factor):
    owner, partner = [(jnp.arange(drawn.shape[dim]) // (drawn.shape[dim] // parts)).reshape([-1 if axis == dim else 1 for axis in range(drawn.ndim)]) for dim in (source, target)]
    chosen = jax.random.permutation(own_key, parts)[partner]
    strong = (owner == chosen) | (owner == (partner + parts // 2) % parts)
    return jnp.where(strong, factor * drawn, drawn)


def shard_levels(stream_key, dims, split, smallest, high):
    def one(axis_at, shards_of):
        steps = jax.random.uniform(jax.random.fold_in(jax.random.fold_in(stream_key, 6), axis_at), (shards_of,), jnp.float32, smallest / len(split), high / len(split))
        return jnp.repeat(jnp.exp(steps), dims[axis_at] // shards_of).reshape((-1,) + (1,) * (len(dims) - axis_at - 1))

    loudness = one(*split[0])
    for cut in split[1:]:
        loudness = loudness * one(*cut)
    return loudness


def normal_values(own_key, shape, spread, bound, split=(), kind=jnp.bfloat16):
    loudness = shard_levels(own_key, shape, split, -0.22, 0.18) if split else 1.0
    array = jax.random.normal(own_key, shape, jnp.float32) * spread * loudness
    return jnp.minimum(jnp.maximum(array, -bound), bound).astype(kind)


def noise_with(stream_key, shape, width, reach, pieces, heavy, kind=jnp.bfloat16):
    values = width * jax.random.normal(stream_key, shape, jnp.float32)
    if pieces:
        values = values * shard_levels(stream_key, shape, pieces, -0.22, 0.18)
    return jnp.clip(raised(values, jax.random.fold_in(stream_key, 3), *heavy), -reach, reach).astype(kind)


def setup_inputs(seed: int = 0) -> dict:
    key_list = jax.random.split(jax.random.key(seed), 21)
    return {
        "clip_video": normal_values(key_list[0], (FRAMES, 3, HS, WS), 1.0, 6.0, ((0, 8), (2, 4))),
        "section_input": draw_section_input(jax.random.fold_in(key_list[20], 71), 0),
        "keep_mask": draw_keep_mask(jax.random.fold_in(key_list[20], 71), 0),
        "w_rgb": normal_values(key_list[3], (9, 3, STEM_C), 27 ** -0.5, 1.25, ((2, 8),)),
        "w_stem_diff": normal_values(key_list[4], (9, STEM_DIFF, STEM_C), (9 * STEM_DIFF) ** -0.5, 0.875, ((2, 8),)),
        "w_first": normal_values(key_list[5], (C5, MID), C5 ** -0.5, 0.125, ((0, 8),)),
        "w_middle": normal_values(key_list[6], (9, MID, MID), (9 * MID) ** -0.5, 0.09375, ((1, 8),)),
        "w_last": normal_values(key_list[7], (MID, C5), MID ** -0.5, 0.25, ((0, 8),)),
        "w_reduce": normal_values(key_list[8], (MID, TDM_C), MID ** -0.5, 0.25, ((0, 8),)),
        "w_diff_full": normal_values(key_list[9], (9, TDM_C, TDM_C), (9 * TDM_C) ** -0.5, 0.1875, ((1, 8),)),
        "w_diff_half": normal_values(key_list[10], (9, TDM_C, TDM_C), (9 * TDM_C) ** -0.5, 0.1875, ((1, 8),)),
        "w_expand": normal_values(key_list[11], (TDM_C, MID), TDM_C ** -0.5, 0.5, ((0, 8),)),
        "gain_first": jnp.clip(1.0 + 0.15 * jax.random.normal(key_list[12], (MID,), jnp.float32), 0.25, 1.75).astype(jnp.bfloat16),
        "bias_first": normal_values(key_list[13], (MID,), 0.3, 3.0, ((0, 8),)),
        "gain_middle": jnp.clip(1.0 + 0.15 * jax.random.normal(key_list[14], (MID,), jnp.float32), 0.25, 1.75).astype(jnp.bfloat16),
        "bias_middle": normal_values(key_list[15], (MID,), 0.3, 3.0, ((0, 8),)),
        "gain_last": jnp.clip(1.0 + 0.15 * jax.random.normal(key_list[16], (C5,), jnp.float32), 0.25, 1.75).astype(jnp.bfloat16),
        "bias_last": normal_values(key_list[17], (C5,), 0.3, 3.0, ((0, 8),)),
        "stem_cot": noise_with(key_list[18], (FRAMES, STEM_C, HS, WS), 1.0, 6.0, ((0, 8), (2, 4)), (0, 1, 8, 2.0)),
        "section_cot": noise_with(key_list[19], (FRAMES, H5, W5, C5), 1.0, 6.0, ((0, 8), (1, 4)), (0, 3, 8, 2.0)),
    }


EPS = 1e-05

@jax.custom_vjp
def low(v):
    return lax.optimization_barrier(v.astype(jnp.bfloat16)).astype(jnp.float32)

@jax.custom_vjp
def low_back(v):
    return v

def low_keep(v):
    return (low(v), None)

def low_pass(kept, grad):
    return (grad,)

def back_keep(v):
    return (v, None)

def back_low(kept, grad):
    return (low(grad),)
low.defvjp(low_keep, low_pass)
low_back.defvjp(back_keep, back_low)

def conv_last(values, kernel):
    shaped = kernel.reshape(3, 3, kernel.shape[1], kernel.shape[2])
    return lax.conv_general_dilated(values, shaped, (1, 1), ((1, 1), (1, 1)), dimension_numbers=('NHWC', 'HWIO', 'NHWC'), precision=lax.Precision.HIGHEST)

def conv_first(values, kernel):
    shaped = kernel.reshape(3, 3, kernel.shape[1], kernel.shape[2])
    return lax.conv_general_dilated(values, shaped, (1, 1), ((1, 1), (1, 1)), dimension_numbers=('NCHW', 'HWIO', 'NCHW'), precision=lax.Precision.HIGHEST)

def pair_mean(values):
    return values.reshape(values.shape[0], values.shape[1] // 2, 2, values.shape[2] // 2, 2, values.shape[3]).mean(axis=(2, 4))

def pair_grow(values):
    return jnp.repeat(jnp.repeat(values, 2, axis=1), 2, axis=2)

def batch_norm(values, gain, bias):
    mean_value = lax.optimization_barrier(jnp.mean(values, axis=(0, 1, 2)))
    variance = lax.optimization_barrier(jnp.mean(values * values, axis=(0, 1, 2))) - mean_value * mean_value
    return gain * ((values - mean_value) * lax.rsqrt(variance + EPS)) + bias

def project(values, kernel):
    return jnp.einsum('fhwc,cd->fhwd', values, kernel, precision=lax.Precision.HIGHEST)

def section_group(features, keep_group, params):
    first_k, middle_k, last_k, reduce_k, dfull_k, dhalf_k, expand_k, gain_one, bias_one, gain_two, bias_two, gain_three, bias_three = params
    first_pre = low_back(project(features, first_k))
    first_act = jax.nn.silu(batch_norm(first_pre, gain_one, bias_one))
    reduced = low_back(project(low(first_act), reduce_k))
    keep_col = keep_group.astype(features.dtype)[:, None, None, None]
    change = low(keep_col * (reduced - jnp.roll(reduced, 1, axis=0)))
    full_out = conv_last(change, dfull_k)
    pooled = low(pair_mean(change))
    half_out = low_back(conv_last(pooled, dhalf_k))
    combined = low_back(full_out + pair_grow(half_out))
    gate_value = jax.nn.sigmoid(low_back(project(low(combined), expand_k)))
    gated = first_act * (1.0 + gate_value)
    middle_pre = low_back(conv_last(low(gated), middle_k))
    second_act = jax.nn.silu(batch_norm(middle_pre, gain_two, bias_two))
    last_pre = low_back(project(low(second_act), last_k))
    return features + batch_norm(last_pre, gain_three, bias_three)

def stem_forward(frames, keep_mask, rgb_k, diff_k):
    keep_col = keep_mask.astype(frames.dtype)[:, None, None, None]
    next_col = jnp.roll(keep_col, -1, axis=0)
    before = keep_col * (frames - jnp.roll(frames, 1, axis=0))
    after = next_col * (jnp.roll(frames, -1, axis=0) - frames)
    diff_stack = low(jnp.concatenate([before, after], axis=1))
    return conv_first(frames, rgb_k) + conv_first(diff_stack, diff_k)

def section_forward(features, keep_mask, params):
    group_frames = SEG * CLIP_MB
    group_count = features.shape[0] // group_frames
    feat_groups = features.reshape((group_count, group_frames) + features.shape[1:])
    keep_groups = keep_mask.reshape(group_count, group_frames)
    checked = jax.checkpoint(section_group)

    def one_group(grouped):
        return checked(grouped[0], grouped[1], params)
    result = lax.map(one_group, (feat_groups, keep_groups))
    return result.reshape(features.shape)

def reference(clip_video, section_input, keep_mask, w_rgb, w_stem_diff, w_first, w_middle, w_last, w_reduce, w_diff_full, w_diff_half, w_expand, gain_first, bias_first, gain_middle, bias_middle, gain_last, bias_last, stem_cot, section_cot):
    params = tuple((item.astype(jnp.float32) for item in (w_rgb, w_stem_diff, w_first, w_middle, w_last, w_reduce, w_diff_full, w_diff_half, w_expand, gain_first, bias_first, gain_middle, bias_middle, gain_last, bias_last)))
    frames = clip_video.astype(jnp.float32)
    features = section_input.astype(jnp.float32)

    def forward(frames_in, features_in, weights):
        return (stem_forward(frames_in, keep_mask, weights[0], weights[1]), section_forward(features_in, keep_mask, weights[2:]))
    outputs, pullback = jax.vjp(forward, frames, features, params)
    video_grad, feature_grad, grads = pullback((stem_cot.astype(jnp.float32), section_cot.astype(jnp.float32)))
    return (outputs[0].astype(jnp.bfloat16), video_grad, outputs[1].astype(jnp.bfloat16), feature_grad.astype(jnp.bfloat16), grads[0], grads[1], grads[2], grads[3], grads[4], grads[5], grads[6], grads[7], grads[8], grads[9], grads[10], grads[11], grads[12], grads[13], grads[14])
```

```python
import functools

import jax
import jax.numpy as jnp
import numpy as np
from jax import lax
from jax.experimental import pallas as pl
from jax.experimental.pallas import tpu as pltpu
from jax.sharding import PartitionSpec as P

H5, HS, MID, TDM_C, C5, STEM_C = 8, 32, 512, 128, 2048, 64
VMEM_BYTES = 63 * 2**20

MICRO = 2


EPS = 1e-05


def with_halo(block, sides, width):
    for axis, dim in sides:
        count = lax.axis_size(axis)
        forward = [(i, i + 1) for i in range(count - 1)]
        backward = [(target, source) for source, target in forward]
        low = lax.ppermute(
            lax.slice_in_dim(block, block.shape[dim] - width, None, axis=dim), axis, forward
        )
        high = lax.ppermute(lax.slice_in_dim(block, 0, width, axis=dim), axis, backward)
        block = jnp.concatenate([low, block, high], axis=dim)
    return block


def silu_slope(values):
    sig_value = jax.nn.sigmoid(values)
    return sig_value * (1.0 + values * (1.0 - sig_value))


def tap_window(padded, row_off, col_off, row_count, col_count, row_axis):
    part_rows = lax.slice_in_dim(padded, row_off, row_off + row_count, axis=row_axis)
    return lax.slice_in_dim(part_rows, col_off, col_off + col_count, axis=row_axis + 1)


def pad_columns(haloed, row_axis):
    widths = [(0, 0)] * haloed.ndim
    widths[row_axis + 1] = (1, 1)
    return jnp.pad(haloed, widths)


def tap_conv(haloed, kernel, channels_last):
    row_axis = 1 if channels_last else 2
    row_count = haloed.shape[row_axis] - 2
    col_count = haloed.shape[row_axis + 1]
    padded = pad_columns(haloed, row_axis)
    einsum_form = "fhwc,cd->fhwd" if channels_last else "fchw,cd->fdhw"
    result = None
    for tap_index in range(9):
        window = tap_window(padded, tap_index // 3, tap_index % 3, row_count, col_count, row_axis)
        tap_term = jnp.einsum(
            einsum_form, window, kernel[tap_index], preferred_element_type=jnp.float32
        )
        result = tap_term if result is None else result + tap_term
    return result


def tap_conv_back(grad_halo, kernel, channels_last):
    row_axis = 1 if channels_last else 2
    row_count = grad_halo.shape[row_axis] - 2
    col_count = grad_halo.shape[row_axis + 1]
    padded = pad_columns(grad_halo, row_axis)
    einsum_form = "fhwd,cd->fhwc" if channels_last else "fdhw,cd->fchw"
    result = None
    for tap_index in range(9):
        window = tap_window(
            padded, 2 - tap_index // 3, 2 - tap_index % 3, row_count, col_count, row_axis
        )
        tap_term = jnp.einsum(
            einsum_form, window, kernel[tap_index], preferred_element_type=jnp.float32
        )
        result = tap_term if result is None else result + tap_term
    return result


def tap_kernel_grad(haloed, out_grad, channels_last):
    row_axis = 1 if channels_last else 2
    row_count = out_grad.shape[row_axis]
    col_count = out_grad.shape[row_axis + 1]
    padded = pad_columns(haloed, row_axis)
    einsum_form = "fhwc,fhwd->cd" if channels_last else "fchw,fdhw->cd"
    tap_list = []
    for tap_index in range(9):
        window = tap_window(padded, tap_index // 3, tap_index % 3, row_count, col_count, row_axis)
        tap_list.append(
            jnp.einsum(einsum_form, window, out_grad, preferred_element_type=jnp.float32)
        )
    return jnp.stack(tap_list, axis=0)


def pair_mean(values):
    return values.reshape(
        values.shape[0], values.shape[1] // 2, 2, values.shape[2] // 2, 2, values.shape[3]
    ).mean(axis=(2, 4))


def pair_total(values):
    return values.reshape(
        values.shape[0], values.shape[1] // 2, 2, values.shape[2] // 2, 2, values.shape[3]
    ).sum(axis=(2, 4))


def pair_grow(values):
    return jnp.repeat(jnp.repeat(values, 2, axis=1), 2, axis=2)


def norm_forward(pre_norm, gain, bias, pixel_count):
    local_sums = (jnp.sum(pre_norm, axis=(0, 1, 2)), jnp.sum(pre_norm * pre_norm, axis=(0, 1, 2)))
    total_sum, total_square = lax.psum((local_sums[0], local_sums[1]), "sp")
    mean_value = total_sum / pixel_count
    variance = total_square / pixel_count - mean_value * mean_value
    inverse = lax.rsqrt(variance + EPS)
    normed = (pre_norm - mean_value) * inverse
    return (normed, inverse, gain * normed + bias)


def norm_backward(out_grad, normed, inverse, gain, pixel_count):
    local_bias = jnp.sum(out_grad, axis=(0, 1, 2))
    local_gain = jnp.sum(out_grad * normed, axis=(0, 1, 2))
    total_bias, total_gain = lax.psum((local_bias, local_gain), "sp")
    pre_grad = (
        gain * inverse * (out_grad - total_bias / pixel_count - normed * total_gain / pixel_count)
    )
    return (pre_grad, local_gain, local_bias)


def reduce_grads(grads):
    summed = (
        lax.psum_scatter(grads[0], "dp", scatter_dimension=2, tiled=True),
        lax.psum_scatter(grads[1], "dp", scatter_dimension=2, tiled=True),
        lax.psum_scatter(grads[2], "dp", scatter_dimension=0, tiled=True),
        lax.psum_scatter(grads[3], "dp", scatter_dimension=1, tiled=True),
        lax.psum_scatter(grads[4], "dp", scatter_dimension=0, tiled=True),
        lax.psum_scatter(grads[5], "dp", scatter_dimension=0, tiled=True),
        lax.psum_scatter(grads[6], "dp", scatter_dimension=1, tiled=True),
        lax.psum_scatter(grads[7], "dp", scatter_dimension=1, tiled=True),
        lax.psum_scatter(grads[8], "dp", scatter_dimension=0, tiled=True),
        lax.psum_scatter(grads[9], "dp", scatter_dimension=0, tiled=True),
        lax.psum_scatter(grads[10], "dp", scatter_dimension=0, tiled=True),
        lax.psum_scatter(grads[11], "dp", scatter_dimension=0, tiled=True),
        lax.psum_scatter(grads[12], "dp", scatter_dimension=0, tiled=True),
        lax.psum_scatter(grads[13], "dp", scatter_dimension=0, tiled=True),
        lax.psum_scatter(grads[14], "dp", scatter_dimension=0, tiled=True),
    )
    return (
        lax.psum(summed[0].astype(jnp.bfloat16), "sp").astype(jnp.float32),
        lax.psum(summed[1].astype(jnp.bfloat16), "sp").astype(jnp.float32),
        lax.psum(summed[2].astype(jnp.bfloat16), "sp").astype(jnp.float32),
        lax.psum(summed[3].astype(jnp.bfloat16), "sp").astype(jnp.float32),
        lax.psum(summed[4].astype(jnp.bfloat16), "sp").astype(jnp.float32),
        lax.psum(summed[5].astype(jnp.bfloat16), "sp").astype(jnp.float32),
        lax.psum(summed[6].astype(jnp.bfloat16), "sp").astype(jnp.float32),
        lax.psum(summed[7].astype(jnp.bfloat16), "sp").astype(jnp.float32),
        lax.psum(summed[8].astype(jnp.bfloat16), "sp").astype(jnp.float32),
        lax.psum(summed[9].astype(jnp.bfloat16), "sp").astype(jnp.float32),
        lax.psum(summed[10].astype(jnp.bfloat16), "sp").astype(jnp.float32),
        lax.psum(summed[11].astype(jnp.bfloat16), "sp").astype(jnp.float32),
        lax.psum(summed[12].astype(jnp.bfloat16), "sp").astype(jnp.float32),
        lax.psum(summed[13].astype(jnp.bfloat16), "sp").astype(jnp.float32),
        lax.psum(summed[14].astype(jnp.bfloat16), "sp").astype(jnp.float32),
    )


def run_micro(
    video_part, feat_part, keep_part, stem_grad_in, section_grad_in, weights, pixel_count
):
    (
        rgb_k,
        stemd_k,
        first_k,
        middle_k,
        last_k,
        reduce_k,
        dfull_k,
        dhalf_k,
        expand_k,
        gain_one,
        bias_one,
        gain_two,
        bias_two,
        gain_three,
        bias_three,
    ) = weights
    keep_float = keep_part.astype(jnp.float32)
    keep_col = keep_float[:, None, None, None]
    next_col = jnp.roll(keep_float, -1)[:, None, None, None]
    frames_halo = with_halo(video_part, (("sp", 2),), 1)
    frames_wide = frames_halo.astype(jnp.float32)
    before = keep_col * (frames_wide - jnp.roll(frames_wide, 1, axis=0))
    after = next_col * (jnp.roll(frames_wide, -1, axis=0) - frames_wide)
    diff_stack = jnp.concatenate([before, after], axis=1).astype(jnp.bfloat16)
    stem_out = (tap_conv(frames_halo, rgb_k, False) + tap_conv(diff_stack, stemd_k, False)).astype(
        jnp.bfloat16
    )
    cot_halo = with_halo(stem_grad_in, (("sp", 2),), 1)
    direct_grad = tap_conv_back(cot_halo, rgb_k, False)
    diff_grad = tap_conv_back(cot_halo, stemd_k, False)
    before_grad = keep_col * diff_grad[:, :3]
    after_grad = next_col * diff_grad[:, 3:]
    video_grad = (
        direct_grad
        + before_grad
        - jnp.roll(before_grad, -1, axis=0)
        + jnp.roll(after_grad, 1, axis=0)
        - after_grad
    )
    rgb_grad = tap_kernel_grad(frames_halo, stem_grad_in, False)
    stemd_grad = tap_kernel_grad(diff_stack, stem_grad_in, False)
    row_count = feat_part.shape[1]
    col_count = feat_part.shape[2]
    first_pre = jnp.einsum("fhwc,cd->fhwd", feat_part, first_k, preferred_element_type=jnp.float32)
    normed_one, inverse_one, norm_one = norm_forward(
        first_pre, gain_one.astype(jnp.float32), bias_one.astype(jnp.float32), pixel_count
    )
    first_act = jax.nn.silu(norm_one)
    first_low = first_act.astype(jnp.bfloat16)
    reduced = jnp.einsum("fhwc,cd->fhwd", first_low, reduce_k, preferred_element_type=jnp.float32)
    change_low = (keep_col * (reduced - jnp.roll(reduced, 1, axis=0))).astype(jnp.bfloat16)
    change_halo = with_halo(change_low, (("sp", 1),), 2)
    near_rows = change_halo[:, 1 : row_count + 3]
    full_out = tap_conv(near_rows, dfull_k, True)
    pooled = pair_mean(change_halo.astype(jnp.float32)).astype(jnp.bfloat16)
    half_out = tap_conv(pooled, dhalf_k, True)
    combined_low = (full_out + pair_grow(half_out)).astype(jnp.bfloat16)
    gate_value = jax.nn.sigmoid(
        jnp.einsum("fhwc,cd->fhwd", combined_low, expand_k, preferred_element_type=jnp.float32)
    )
    gated_low = (first_act * (1.0 + gate_value)).astype(jnp.bfloat16)
    gated_halo = with_halo(gated_low, (("sp", 1),), 1)
    middle_pre = tap_conv(gated_halo, middle_k, True)
    normed_two, inverse_two, norm_two = norm_forward(
        middle_pre, gain_two.astype(jnp.float32), bias_two.astype(jnp.float32), pixel_count
    )
    second_low = jax.nn.silu(norm_two).astype(jnp.bfloat16)
    last_pre = jnp.einsum("fhwc,cd->fhwd", second_low, last_k, preferred_element_type=jnp.float32)
    normed_three, inverse_three, norm_three = norm_forward(
        last_pre, gain_three.astype(jnp.float32), bias_three.astype(jnp.float32), pixel_count
    )
    section_out = (feat_part.astype(jnp.float32) + norm_three).astype(jnp.bfloat16)
    out_grad = section_grad_in.astype(jnp.float32)
    last_grad, gain_three_grad, bias_three_grad = norm_backward(
        out_grad, normed_three, inverse_three, gain_three.astype(jnp.float32), pixel_count
    )
    last_grad_low = last_grad.astype(jnp.bfloat16)
    last_k_grad = jnp.einsum(
        "fhwc,fhwd->cd", second_low, last_grad_low, preferred_element_type=jnp.float32
    )
    second_grad = jnp.einsum(
        "fhwd,cd->fhwc", last_grad_low, last_k, preferred_element_type=jnp.float32
    ) * silu_slope(norm_two)
    middle_grad, gain_two_grad, bias_two_grad = norm_backward(
        second_grad, normed_two, inverse_two, gain_two.astype(jnp.float32), pixel_count
    )
    middle_low = middle_grad.astype(jnp.bfloat16)
    middle_halo = with_halo(middle_low, (("sp", 1),), 1)
    gated_grad = tap_conv_back(middle_halo, middle_k, True)
    middle_k_grad = tap_kernel_grad(gated_halo, middle_low, True)
    gate_grad = (gated_grad * first_act * gate_value * (1.0 - gate_value)).astype(jnp.bfloat16)
    expand_grad = jnp.einsum(
        "fhwc,fhwd->cd", combined_low, gate_grad, preferred_element_type=jnp.float32
    )
    combined_grad = jnp.einsum(
        "fhwd,cd->fhwc", gate_grad, expand_k, preferred_element_type=jnp.float32
    ).astype(jnp.bfloat16)
    half_grad = pair_total(combined_grad.astype(jnp.float32)).astype(jnp.bfloat16)
    stacked = jnp.concatenate([combined_grad, jnp.repeat(half_grad, 2, axis=1)], axis=2)
    stacked_halo = with_halo(stacked, (("sp", 1),), 2)
    full_grad_halo = stacked_halo[:, 1 : row_count + 3, :col_count]
    half_grad_halo = stacked_halo[:, 0::2, col_count:]
    change_grad = tap_conv_back(full_grad_halo, dfull_k, True) + 0.25 * pair_grow(
        tap_conv_back(half_grad_halo, dhalf_k, True)
    )
    dfull_grad = tap_kernel_grad(near_rows, combined_grad, True)
    dhalf_grad = tap_kernel_grad(pooled, half_grad, True)
    weighted = keep_col * change_grad
    reduced_grad = (weighted - jnp.roll(weighted, -1, axis=0)).astype(jnp.bfloat16)
    reduce_grad = jnp.einsum(
        "fhwc,fhwd->cd", first_low, reduced_grad, preferred_element_type=jnp.float32
    )
    first_sum = gated_grad * (1.0 + gate_value) + jnp.einsum(
        "fhwd,cd->fhwc", reduced_grad, reduce_k, preferred_element_type=jnp.float32
    )
    first_grad, gain_one_grad, bias_one_grad = norm_backward(
        first_sum * silu_slope(norm_one),
        normed_one,
        inverse_one,
        gain_one.astype(jnp.float32),
        pixel_count,
    )
    first_grad_low = first_grad.astype(jnp.bfloat16)
    first_k_grad = jnp.einsum(
        "fhwc,fhwd->cd", feat_part, first_grad_low, preferred_element_type=jnp.float32
    )
    input_grad = (
        out_grad
        + jnp.einsum("fhwd,cd->fhwc", first_grad_low, first_k, preferred_element_type=jnp.float32)
    ).astype(jnp.bfloat16)
    grads = (
        rgb_grad,
        stemd_grad,
        first_k_grad,
        middle_k_grad,
        last_k_grad,
        reduce_grad,
        dfull_grad,
        dhalf_grad,
        expand_grad,
        gain_one_grad,
        bias_one_grad,
        gain_two_grad,
        bias_two_grad,
        gain_three_grad,
        bias_three_grad,
    )
    return ((stem_out, video_grad, section_out, input_grad), grads)


def add_trees(first_tree, second_tree):
    if first_tree is None:
        return second_tree
    return jax.tree.map(
        lambda left_part, right_part: left_part + right_part, first_tree, second_tree
    )


def on_device(
    clip_video,
    section_input,
    keep_mask,
    w_rgb,
    w_stem_diff,
    w_first,
    w_middle,
    w_last,
    w_reduce,
    w_diff_full,
    w_diff_half,
    w_expand,
    gain_first,
    bias_first,
    gain_middle,
    bias_middle,
    gain_last,
    bias_last,
    stem_cot,
    section_cot,
):
    micro_frames = clip_video.shape[0] // MICRO
    pixel_count = (
        micro_frames * section_input.shape[1] * lax.axis_size("sp") * section_input.shape[2]
    )
    results = []
    grad_totals = None
    for micro_index in range(MICRO):
        weights = (
            lax.all_gather(w_rgb, "dp", axis=2, tiled=True),
            lax.all_gather(w_stem_diff, "dp", axis=2, tiled=True),
            lax.all_gather(w_first, "dp", axis=0, tiled=True),
            lax.all_gather(w_middle, "dp", axis=1, tiled=True),
            lax.all_gather(w_last, "dp", axis=0, tiled=True),
            lax.all_gather(w_reduce, "dp", axis=0, tiled=True),
            lax.all_gather(w_diff_full, "dp", axis=1, tiled=True),
            lax.all_gather(w_diff_half, "dp", axis=1, tiled=True),
            lax.all_gather(w_expand, "dp", axis=0, tiled=True),
            lax.all_gather(gain_first, "dp", axis=0, tiled=True),
            lax.all_gather(bias_first, "dp", axis=0, tiled=True),
            lax.all_gather(gain_middle, "dp", axis=0, tiled=True),
            lax.all_gather(bias_middle, "dp", axis=0, tiled=True),
            lax.all_gather(gain_last, "dp", axis=0, tiled=True),
            lax.all_gather(bias_last, "dp", axis=0, tiled=True),
        )
        low_end = micro_index * micro_frames
        high_end = low_end + micro_frames
        outputs, grads = run_micro(
            clip_video[low_end:high_end],
            section_input[low_end:high_end],
            keep_mask[low_end:high_end],
            stem_cot[low_end:high_end],
            section_cot[low_end:high_end],
            weights,
            pixel_count,
        )
        results.append(outputs)
        grad_totals = add_trees(grad_totals, reduce_grads(grads))
    stem_features = jnp.concatenate([item[0] for item in results], axis=0)
    video_grad = jnp.concatenate([item[1] for item in results], axis=0)
    section_output = jnp.concatenate([item[2] for item in results], axis=0)
    section_input_grad = jnp.concatenate([item[3] for item in results], axis=0)
    return (
        stem_features,
        video_grad,
        section_output,
        section_input_grad,
        grad_totals[0],
        grad_totals[1],
        grad_totals[2],
        grad_totals[3],
        grad_totals[4],
        grad_totals[5],
        grad_totals[6],
        grad_totals[7],
        grad_totals[8],
        grad_totals[9],
        grad_totals[10],
        grad_totals[11],
        grad_totals[12],
        grad_totals[13],
        grad_totals[14],
    )


F32 = jnp.float32
BF16 = jnp.bfloat16
MESH_ID = pl.DeviceIdType.MESH
GROUP = 8
LANES = 128
STEP = 32
PART = 2


def dot_nn(left, right):
    return lax.dot_general(left, right, (((1,), (0,)), ((), ())), preferred_element_type=F32)


def dot_nt(left, right):
    return lax.dot_general(left, right, (((1,), (1,)), ((), ())), preferred_element_type=F32)


def dot_tn(left, right):
    return lax.dot_general(left, right, (((0,), (0,)), ((), ())), preferred_element_type=F32)


def shift_down(values, count):
    size = values.shape[0]
    column = lax.broadcasted_iota(jnp.int32, values.shape, 0) & 15
    return jnp.where(column < count, 0.0, pltpu.roll(values, count, 0))


def shift_up(values, count):
    size = values.shape[0]
    column = lax.broadcasted_iota(jnp.int32, values.shape, 0) & 15
    return jnp.where(column >= 16 - count, 0.0, pltpu.roll(values, size - count, 0))


def pair_sum(values):
    size = values.shape[0]
    parity = lax.broadcasted_iota(jnp.int32, values.shape, 0) & 1
    return values + jnp.where(parity == 0, pltpu.roll(values, size - 1, 0), pltpu.roll(values, 1, 0))


def band_table(rows):
    table = np.zeros((rows, 96, 3 * LANES), np.float32)
    for i in range(rows):
        for a in range(3):
            for b in range(3):
                for ch in range(9):
                    base = (b * 3 + ch // 3) * 32
                    row = i + a - 1
                    if row < 0:
                        n = base + 24 + (ch % 3) * 2
                    elif row >= rows:
                        n = base + 24 + (ch % 3) * 2 + 1
                    else:
                        n = base + (ch % 3) * 8 + row
                    table[i, (3 * a + b) * 9 + ch, n] = 1.0
    return table


def silu_parts(values):
    sig = jax.nn.sigmoid(values)
    return values * sig, sig * (1.0 + values * (1.0 - sig))


def whole_kernel(
    sizes, keep, uin, small, band, x_hbm, ct_hbm, sc_hbm, wf_in, wm_in, wl_in, wr_in, wd0_in, wd1_in, we_in,
    so_hbm, vg_out, out_hbm, ig_hbm, of_out, om_out, ol_out, or_out, od_out, oe_out, osm_out,
    ssem, rsem, lsem, wf, wm, wl, wr, wd, we, x3, ct3, sc, so, ust, uprev, unext, sm, tf, tff, tb, dg,
    vgh, vgr, stg, stgr, stat_s, stat_r, st3_s, st3_r, z1, fab, gt, rd, chb, chr_, cs, ps, comb,
    gb, gr, gs, z2, sab, z3, lgb, cgx, cgr, cgs, hgs, fgb, ost,
    g_first, g_mid, g_last, g_diff, g_re, rcf, rxf, ryf, rzf, rcm, rxm, rym, rzm, rcl, rxl, ryl, rzl,
    rcd, ryd, rzd, fdx, rxd, fdo, rcr, ryr, rzr, frx, rxr, fbf, fbm, fbl, sms, smr,
):
    D, S, NF = sizes
    DZ, SX = D // 2, S // 2
    NG = NF // GROUP
    NW = NF * 16
    GW = GROUP * 16
    dp, sp = lax.axis_index("dp"), lax.axis_index("sp")
    z, y = dp // 2, dp % 2
    x, c = sp // 2, sp % 2
    oy, oc = 1 - y, 1 - c
    q_own = c * SX + x

    def at_zy(zz, yy):
        return (zz * 2 + yy, sp)

    y_peer = at_zy(z, oy)
    c_peer = (dp, x * 2 + oc)

    def z_to(k):
        return lax.rem(z + k, DZ)

    def z_from(k):
        return lax.rem(z + DZ - k, DZ)

    def x_to(k):
        return lax.rem(x + k, SX)

    def x_from(k):
        return lax.rem(x + SX - k, SX)

    def x_peer(k):
        return (dp, x_to(k) * 2 + c)

    sp_peers = [(dp, lax.rem(sp + k, S)) for k in range(1, S)]
    dp_peers = [(lax.rem(dp + k, D), sp) for k in range(1, D)]
    has_prev, has_next = sp > 0, sp < S - 1
    prev_dev, next_dev = (dp, sp - 1), (dp, sp + 1)

    counters = {"r": 0, "l": 0}
    sends = []

    def remote(src, dst, dev):
        i = counters["r"]
        counters["r"] += 1
        copy = pltpu.make_async_remote_copy(
            src_ref=src, dst_ref=dst, send_sem=ssem.at[i], recv_sem=rsem.at[i],
            device_id=dev, device_id_type=MESH_ID,
        )
        copy.start()
        sends.append(copy)
        return copy

    def local(src, dst):
        i = counters["l"]
        counters["l"] += 1
        copy = pltpu.make_async_copy(src, dst, lsem.at[i])
        copy.start()
        return copy

    @pl.when(sp == 0)
    def _():
        uprev[...] = jnp.zeros_like(uprev)
        vgr[0] = jnp.zeros(vgr.shape[1:], F32)
        chr_[0] = jnp.zeros(chr_.shape[1:], BF16)
        gr[0] = jnp.zeros(gr.shape[1:], BF16)
        cgr[0] = jnp.zeros(cgr.shape[1:], BF16)

    @pl.when(sp == S - 1)
    def _():
        unext[...] = jnp.zeros_like(unext)
        vgr[1] = jnp.zeros(vgr.shape[1:], F32)
        chr_[1] = jnp.zeros(chr_.shape[1:], BF16)
        gr[1] = jnp.zeros(gr.shape[1:], BF16)
        cgr[1] = jnp.zeros(cgr.shape[1:], BF16)

    barrier = pltpu.get_barrier_semaphore()
    for peer in sp_peers + dp_peers:
        pl.semaphore_signal(barrier, inc=1, device_id=peer, device_id_type=MESH_ID)
    own_small = local(small, sm.at[dp])
    own = [
        local(wf_in, wf.at[z, y]), local(wd0_in, wd.at[0, :, z, y]), local(wd1_in, wd.at[1, :, z, y]),
        local(wr_in, wr.at[z, y]), local(we_in, we.at[z, y]), local(wm_in, wm.at[:, z, y]),
        local(wl_in, wl.at[z, y]),
    ]

    def load_cot(part):
        lo = part * PART
        return local(sc_hbm.at[pl.ds(lo, PART)], sc.at[pl.ds(lo % (2 * PART), PART)])

    load_sc = [load_cot(0), load_cot(1)]
    load_x = [local(x_hbm.at[:, r], x3.at[pl.ds(r * NF, NF)]) for r in range(2)]
    load_ct = [local(ct_hbm.at[:, r], ct3.at[pl.ds(r * NF, NF)]) for r in range(2)]
    pl.semaphore_wait(barrier, S - 1 + D - 1)

    halo_waits = []

    def halo(to_prev, to_next, from_prev, from_next, land_prev, land_next):
        i = counters["r"]
        counters["r"] += 2

        def up():
            return pltpu.make_async_remote_copy(
                src_ref=to_prev, dst_ref=land_next, send_sem=ssem.at[i], recv_sem=rsem.at[i],
                device_id=prev_dev, device_id_type=MESH_ID)

        def down():
            return pltpu.make_async_remote_copy(
                src_ref=to_next, dst_ref=land_prev, send_sem=ssem.at[i + 1], recv_sem=rsem.at[i + 1],
                device_id=next_dev, device_id_type=MESH_ID)

        @pl.when(has_prev)
        def _():
            up().start()

        @pl.when(has_next)
        def _():
            down().start()

        def wait():
            @pl.when(has_prev)
            def _():
                down().wait_recv()

            @pl.when(has_next)
            def _():
                up().wait_recv()

        def finish():
            @pl.when(has_prev)
            def _():
                up().wait_send()

            @pl.when(has_next)
            def _():
                down().wait_send()

        halo_waits.append(finish)
        return wait, finish

    small_copies = [remote(small, sm.at[dp], peer) for peer in dp_peers]
    edge = uin.at[:, pl.ds(24, 8)]
    wait_edges, _ = halo(edge, edge, None, None, uprev, unext)

    def gather(mode, src, dst):
        piece = q_own if mode == "A" else c
        zs = [remote(src(piece), dst(z, y, piece), at_zy(z_to(k), y)) for k in range(1, DZ)]
        ys = [remote(src(piece), dst(z, y, piece), y_peer)]
        yield
        xs, cores = [], []

        def fan(zz, yy):
            part = dst(zz, yy, piece)
            if mode == "A":
                for k in range(1, SX):
                    xs.append((zz, yy, k, remote(part, part, x_peer(k))))
            if mode != "D":
                cores.append(remote(part, part, c_peer))

        for k in range(1, DZ):
            zs[k - 1].wait_recv()
            part = dst(z_from(k), y, piece)
            ys.append(remote(part, part, y_peer))
            fan(z_from(k), y)
        yield
        for k in range(DZ):
            ys[k].wait_recv()
            fan(z_from(k), oy)
        yield
        for zz, yy, k, copy in xs:
            copy.wait_recv()
            part = dst(zz, yy, c * SX + x_from(k))
            cores.append(remote(part, part, c_peer))
        yield
        for copy in cores:
            copy.wait_recv()

    def lane_block(index, width):
        return pl.ds(pl.multiple_of(index * width, width), width)

    fr, fw = wf_in.shape[0], wf_in.shape[1] // S
    mw = wm_in.shape[2] // S
    lr, lw = wl_in.shape[0], wl_in.shape[1] // S

    def first_part(lo, n):
        return gather("A", lambda q: wf_in.at[pl.ds(lo, n), lane_block(q, fw)],
                      lambda zz, yy, q: wf.at[zz, yy, pl.ds(lo, n), lane_block(q, fw)])

    def mid_part(lo, n):
        return gather("A", lambda q: wm_in.at[pl.ds(lo, n), :, lane_block(q, mw)],
                      lambda zz, yy, q: wm.at[pl.ds(lo, n), zz, yy, :, lane_block(q, mw)])

    def last_part(lo, n):
        return gather("A", lambda q: wl_in.at[pl.ds(lo, n), lane_block(q, lw)],
                      lambda zz, yy, q: wl.at[zz, yy, pl.ds(lo, n), lane_block(q, lw)])

    for copy in own:
        copy.wait()
    chunks = [
        first_part(0, fr // 2),
        first_part(fr // 2, fr // 2),
        gather("D", lambda q: wr_in, lambda zz, yy, q: wr.at[zz, yy]),
        gather("B", lambda q: wd.at[q, :, z, y], lambda zz, yy, q: wd.at[q, :, zz, yy]),
        gather("D", lambda q: we_in, lambda zz, yy, q: we.at[zz, yy]),
        mid_part(0, 3), mid_part(3, 3), mid_part(6, 3),
        last_part(0, lr // 2), last_part(lr // 2, lr // 2),
    ]
    slot_of = [0, 1, 2, 2, 2, 3, 4, 5, 6, 7]
    slot = [0]

    def pump():
        for start, chunk in zip(slot_of, chunks):
            if start <= slot[0]:
                next(chunk, None)
        slot[0] += 1

    pump()

    own_small.wait()
    for copy in small_copies:
        copy.wait_recv()
    wt = sm[:, 0:8, :].reshape(D * 8, LANES)[:, 0:96].astype(BF16)
    for i in range(8):
        rows = dot_nn(wt, band[i])
        for n in range(3):
            tff[n, pl.ds(i, D * 8, stride=8), :] = rows[:, n * LANES : (n + 1) * LANES]
    for n in range(3):
        columns = min(288 - n * LANES, LANES)
        tf[:, n * LANES : n * LANES + columns] = tff[n, :, 0:columns].astype(BF16)
        tb[n * LANES : n * LANES + columns, :] = tff[n].T[0:columns].astype(BF16)

    per = D * LANES // 512

    def mid_vec(j):
        parts = []
        for m in range(D // per):
            row = sm[m * per, 8 + j : 9 + j, :]
            for n in range(1, per):
                row = row + sm[m * per + n, 8 + j : 9 + j, :]
            parts.append(row)
        return jnp.concatenate(parts, axis=1)

    rows_last = 2048 // D // LANES

    def last_vec(j):
        return jnp.concatenate(
            [sm[d, 8 + j + n : 9 + j + n, :] for d in range(D) for n in range(rows_last)], axis=1)

    gain_1, bias_1, gain_2, bias_2 = [mid_vec(j) for j in range(4)]
    gain_3, bias_3 = last_vec(4), last_vec(4 + rows_last)

    wait_edges()
    side = lax.broadcasted_iota(jnp.int32, (8, LANES), 0) & 1
    ust[...] = uin[...]
    for f in range(NF):
        ust[f, 24:32, :] = jnp.where(
            side == 0, pltpu.roll(uprev[f], 7, 0), pltpu.roll(unext[f], 1, 0))
    zt = tff
    zt[...] = jnp.zeros_like(zt)

    def stem_frame(f, carry):
        before_at, after_at = lax.rem(f + NF - 1, NF), lax.rem(f + 1, NF)
        k_here, k_next = keep[f].astype(F32), keep[after_at].astype(F32)
        frame = ust[f]
        stacked = jnp.concatenate(
            [frame, k_here * (frame - ust[before_at]), k_next * (ust[after_at] - frame)], axis=0)
        stacked = stacked.astype(BF16).astype(F32)
        lane = lax.broadcasted_iota(jnp.int32, stacked.shape, 1)
        left = jnp.where(lane == 0, 0.0, pltpu.roll(stacked, 1, 1))
        right = jnp.where(lane == LANES - 1, 0.0, pltpu.roll(stacked, LANES - 1, 1))
        taps = jnp.concatenate([left, stacked, right], axis=0).astype(BF16)
        place = lax.rem(f, 2 * PART)
        cot = sc[place]
        so[place] = dot_nn(tf[...], taps).astype(BF16)
        back = dot_nn(tb[...], cot)
        dg[f] = (
            jnp.where(lane == LANES - 1, 0.0, pltpu.roll(back[0:96], LANES - 1, 1))
            + back[96:192]
            + jnp.where(lane == 0, 0.0, pltpu.roll(back[192:288], 1, 1)))
        cross = dot_nt(cot, taps)
        for n in range(3):
            columns = min(288 - n * LANES, LANES)
            zt[n, :, 0:columns] += cross[:, n * LANES : n * LANES + columns]
        return carry

    store_so = []
    for part in range(NF // PART):
        lo = part * PART
        load_sc[part].wait()
        if part >= 2:
            store_so[part - 2].wait()
        lax.fori_loop(lo, lo + PART, stem_frame, 0)
        store_so.append(local(so.at[pl.ds(lo % (2 * PART), PART)], so_hbm.at[pl.ds(lo, PART)]))
        if part + 2 < NF // PART:
            load_sc.append(load_cot(part + 2))
        pump()
    for copy in store_so[-2:]:
        copy.wait()

    def video_frame(f, carry):
        before_at, after_at = lax.rem(f + NF - 1, NF), lax.rem(f + 1, NF)
        k_here, k_next = keep[f].astype(F32), keep[after_at].astype(F32)
        total = (
            dg[f, 0:32] + k_here * dg[f, 32:64] - k_next * dg[after_at, 32:64]
            + k_here * dg[before_at, 64:96] - k_next * dg[f, 64:96])
        vg_out[f] = total[0:24]
        vgh[f] = total[24:32]
        return carry

    lax.fori_loop(0, NF, video_frame, 0)
    wait_video, _ = halo(vgh, vgh, None, None, vgr.at[0], vgr.at[1])

    stem_grad = jnp.zeros((D * 8, 96), F32)
    for i in range(8):
        for n in range(3):
            part = zt[n, pl.ds(i, D * 8, stride=8), :]
            high = part.astype(BF16)
            low = (part - high.astype(F32)).astype(BF16)
            table = band[i, :, n * LANES : (n + 1) * LANES]
            stem_grad = stem_grad + dot_nt(high, table) + dot_nt(low, table)
    stg[...] = jnp.concatenate([stem_grad, jnp.zeros((D * 8, LANES - 96), F32)], axis=1)
    stem_copies = [remote(stg, stgr.at[k], peer) for k, peer in enumerate(sp_peers)]
    pump()
    pump()

    def rows_loop(group, fn, init):
        def body(i, carry):
            start = (i // (GW // STEP)) * NW + group * GW + (i % (GW // STEP)) * STEP
            return fn(pl.multiple_of(start, STEP), carry)
        return lax.fori_loop(0, 2 * (GW // STEP), body, init)

    def fold(values):
        return values.reshape(STEP // 8, 8, values.shape[1]).sum(axis=0)

    def sp_send(i, parts):
        width = parts[0].shape[1]
        fill = [jnp.zeros((8 - len(parts), width), F32)] if len(parts) < 8 else []
        stat_s[i] = jnp.concatenate(parts + fill, axis=0)
        return [remote(stat_s.at[i], stat_r.at[i, k], peer) for k, peer in enumerate(sp_peers)]

    def sp_total(i, copies):
        total = stat_s[i]
        for k, copy in enumerate(copies):
            copy.wait_recv()
            total = total + stat_r[i, k]
        return total

    pixels = jnp.float32(GROUP * 2 * S * 16)
    inv_pixels = 1.0 / (GROUP * 2 * S * 16)

    def two_sums(ref):
        parts = []
        for group in range(NG):
            def add(start, carry):
                value = ref[pl.ds(start, STEP), :]
                return carry[0] + fold(value), carry[1] + fold(value * value)
            zero = jnp.zeros((8, ref.shape[1]), F32)
            one, two = rows_loop(group, add, (zero, zero))
            parts += [jnp.sum(one, axis=0, keepdims=True), jnp.sum(two, axis=0, keepdims=True)]
        return parts

    def moments(total, row):
        mean = total[row : row + 1] * inv_pixels
        variance = total[row + 1 : row + 2] * inv_pixels - mean * mean
        return mean, lax.rsqrt(variance + EPS)

    for copy in load_x:
        copy.wait()
    xs = x3[...].reshape(2 * NW, x3.shape[2])
    for n in range(2):
        z1[:, n * 256 : (n + 1) * 256] = dot_nn(xs, wf[:, :, :, n * 256 : (n + 1) * 256].reshape(x3.shape[2], 256))
    copies = sp_send(0, two_sums(z1))
    pump()
    total = sp_total(0, copies)
    inv_1 = []
    for group in range(NG):
        mean, inv = moments(total, 2 * group)
        inv_1.append(inv)

        def apply_1(start, carry):
            normed = (z1[pl.ds(start, STEP), :] - mean) * inv
            act = jax.nn.silu(gain_1 * normed + bias_1)
            z1[pl.ds(start, STEP), :] = normed
            z3[pl.ds(start, STEP), 0:512] = act
            fab[pl.ds(start, STEP), :] = act.astype(BF16)
            return carry
        rows_loop(group, apply_1, 0)

    rd[...] = dot_nn(fab[...], wr[...].reshape(512, LANES))
    for r in range(2):
        for f in range(NF):
            here = r * NW + f * 16
            past = r * NW + ((f - 1) % NF) * 16
            diff = keep[f].astype(F32) * (rd[here : here + 16, :] - rd[past : past + 16, :])
            chb[r, f * 16 : f * 16 + 16, :] = diff.astype(BF16)
    wait_change, free_change = halo(chb, chb, None, None, chr_.at[0], chr_.at[1])

    def put_shifts(ref, at, values, count, flip):
        width = values.shape[1]
        down, up = shift_down(values, count), shift_up(values, count)
        low, high = (up, down) if flip else (down, up)
        ref[at, :, 0:width] = low.astype(BF16)
        ref[at, :, width : 2 * width] = values.astype(BF16)
        ref[at, :, 2 * width : 3 * width] = high.astype(BF16)

    change = [chb[r].astype(F32) for r in range(2)]
    for r in range(2):
        put_shifts(cs, 1 + r, change[r], 1, False)

    def pool(upper, lower):
        return (pair_sum(upper + lower) * 0.25).astype(BF16).astype(F32)

    put_shifts(ps, 1, pool(change[0], change[1]), 2, False)
    pump()
    wait_change()
    above = [chr_[0, r].astype(F32) for r in range(2)]
    below = [chr_[1, r].astype(F32) for r in range(2)]
    put_shifts(cs, 0, above[1], 1, False)
    put_shifts(cs, 3, below[0], 1, False)
    put_shifts(ps, 0, pool(above[0], above[1]), 2, False)
    put_shifts(ps, 2, pool(below[0], below[1]), 2, False)
    full = jnp.zeros((2 * NW, LANES), F32)
    half = jnp.zeros((NW, LANES), F32)
    for a in range(3):
        full = full + dot_nn(cs[a : a + 2].reshape(2 * NW, 384), wd[0, 3 * a : 3 * a + 3].reshape(384, LANES))
        half = half + dot_nn(ps[a], wd[1, 3 * a : 3 * a + 3].reshape(384, LANES))
    comb[...] = (full + jnp.concatenate([half, half], axis=0)).astype(BF16)
    gt[...] = dot_nn(comb[...], we[...].reshape(LANES, 512))

    def apply_gate(i, carry):
        start = pl.multiple_of(i * STEP, STEP)
        gate = jax.nn.sigmoid(gt[pl.ds(start, STEP), :])
        gt[pl.ds(start, STEP), :] = gate
        gated = (z3[pl.ds(start, STEP), 0:512] * (1.0 + gate)).astype(BF16)
        gb[pl.ds(start, STEP), :] = gated
        return carry

    lax.fori_loop(0, 2 * NW // STEP, apply_gate, 0)
    wait_gated, free_gated = halo(gb.at[pl.ds(0, NW)], gb.at[pl.ds(NW, NW)], None, None, gr.at[0], gr.at[1])

    def spread(dst, at, src_fn, flip):
        def body(i, carry):
            start = pl.multiple_of(i * STEP, STEP)
            values = src_fn(start).astype(F32)
            down, up = shift_down(values, 1), shift_up(values, 1)
            low, high = (up, down) if flip else (down, up)
            dst[at, pl.ds(start, STEP), 0:512] = low.astype(BF16)
            dst[at, pl.ds(start, STEP), 512:1024] = values.astype(BF16)
            dst[at, pl.ds(start, STEP), 1024:1536] = high.astype(BF16)
            return carry
        lax.fori_loop(0, NW // STEP, body, 0)

    for r in range(2):
        spread(gs, 1 + r, lambda start, r=r: gb[pl.ds(r * NW + start, STEP), :], False)
    pump()
    pump()
    pump()
    pump()

    def taps_of(a):
        return wm[3 * a : 3 * a + 3].reshape(1536, 512)

    z2[...] = dot_nn(gs[1:3].reshape(2 * NW, 1536), taps_of(1))
    z2[0:NW, :] += dot_nn(gs[2], taps_of(2))
    z2[NW : 2 * NW, :] += dot_nn(gs[1], taps_of(0))
    wait_gated()
    spread(gs, 0, lambda start: gr[0, pl.ds(start, STEP), :], False)
    spread(gs, 3, lambda start: gr[1, pl.ds(start, STEP), :], False)
    z2[0:NW, :] += dot_nn(gs[0], taps_of(0))
    z2[NW : 2 * NW, :] += dot_nn(gs[3], taps_of(2))
    copies = sp_send(1, two_sums(z2))
    for copy in load_ct:
        copy.wait()
    total = sp_total(1, copies)
    inv_2 = []
    for group in range(NG):
        mean, inv = moments(total, 2 * group)
        inv_2.append(inv)

        def apply_2(start, carry):
            normed = (z2[pl.ds(start, STEP), :] - mean) * inv
            z2[pl.ds(start, STEP), :] = normed
            sab[pl.ds(start, STEP), :] = jax.nn.silu(gain_2 * normed + bias_2).astype(BF16)
            return carry
        rows_loop(group, apply_2, 0)

    def ct_rows(start, lo, width):
        return ct3[pl.ds(start // 16, STEP // 16), :, lo : lo + width].reshape(STEP, width).astype(F32)

    def x_rows(start, lo, width):
        return x3[pl.ds(start // 16, STEP // 16), :, lo : lo + width].reshape(STEP, width).astype(F32)

    last_copies = []
    for n in range(4):
        lo = n * 512
        z3[:, lo : lo + 512] = dot_nn(sab[...], wl[:, :, :, lo : lo + 512].reshape(512, 512))
        parts = []
        for group in range(NG):
            def add_3(start, carry):
                value = z3[pl.ds(start, STEP), lo : lo + 512]
                cot = ct_rows(start, lo, 512)
                return (carry[0] + fold(value), carry[1] + fold(value * value),
                        carry[2] + fold(cot), carry[3] + fold(cot * value))
            zero = jnp.zeros((8, 512), F32)
            sums = rows_loop(group, add_3, (zero, zero, zero, zero))
            parts += [jnp.sum(item, axis=0, keepdims=True) for item in sums]
        st3_s[n] = jnp.concatenate(parts, axis=0)
        last_copies.append(
            [remote(st3_s.at[n], st3_r.at[n, k], peer) for k, peer in enumerate(sp_peers)])
    gain_3_grad, bias_3_grad = [], []
    stores = []

    def free_part():
        if len(stores) >= 2:
            for copy in stores[-2]:
                copy.wait()

    def store_part(n, target):
        stores.append([local(ost.at[n % 2, pl.ds(r * NF, NF)], target.at[:, r, :, pl.ds(n * 512, 512)]) for r in range(2)])

    for n in range(4):
        lo = n * 512
        free_part()
        total = st3_s[n]
        for k, copy in enumerate(last_copies[n]):
            copy.wait_recv()
            total = total + st3_r[n, k]
        gain, bias = gain_3[:, lo : lo + 512], bias_3[:, lo : lo + 512]
        gain_sum = bias_sum = jnp.zeros((1, 512), F32)
        for group in range(NG):
            row = 4 * group
            mean, inv = moments(total, row)
            cot_sum = total[row + 2 : row + 3]
            cot_normed = inv * (total[row + 3 : row + 4] - mean * cot_sum)
            gain_sum, bias_sum = gain_sum + cot_normed, bias_sum + cot_sum
            cot_mean, slope_mean = cot_sum * inv_pixels, cot_normed * inv_pixels
            scale = gain * inv

            def apply_3(start, carry):
                normed = (z3[pl.ds(start, STEP), lo : lo + 512] - mean) * inv
                cot = ct_rows(start, lo, 512)
                out = x_rows(start, lo, 512) + gain * normed + bias
                ost[n % 2, pl.ds(start // 16, STEP // 16)] = out.astype(BF16).reshape(STEP // 16, 16, 512)
                lgb[pl.ds(start, STEP), lo : lo + 512] = (
                    scale * (cot - cot_mean - normed * slope_mean)).astype(BF16)
                return carry
            rows_loop(group, apply_3, 0)
        store_part(n, out_hbm)
        gain_3_grad.append(gain_sum)
        bias_3_grad.append(bias_sum)

    def each(count, fn):
        def body(i, carry):
            fn(i)
            return carry
        lax.fori_loop(0, count, body, 0)

    def reduce_wide(grad, rc, rx, ry, rz, fb, taps, put):
        mine = q_own

        def lead(ref, head, t, tail):
            return ref.at[head + ((t,) if taps else ()) + tail]

        rows_n = taps if taps else 1
        got = remote(grad.at[pl.ds(oc * SX, SX)], rc, c_peer)
        yield
        got.wait_recv()
        for xx in range(SX):
            def add_c(i):
                t, zz = i // DZ, i % DZ
                for yy in range(2):
                    dst = lead(grad, (c * SX + xx,), t, (zz, yy))
                    src = lead(rc, (xx,), t, (zz, yy))
                    dst[...] = (dst[...].astype(F32) + src[...].astype(F32)).astype(BF16)
            each(rows_n * DZ, add_c)
        got = [remote(grad.at[c * SX + x_to(k)], rx.at[k - 1], x_peer(k)) for k in range(1, SX)]
        yield
        for copy in got:
            copy.wait_recv()

        def add_x(i):
            t, zz = i // DZ, i % DZ
            for yy in range(2):
                dst = lead(grad, (mine,), t, (zz, yy))
                value = dst[...].astype(F32)
                for k in range(1, SX):
                    value = value + lead(rx, (k - 1,), t, (zz, yy))[...].astype(F32)
                dst[...] = value.astype(BF16)
        each(rows_n * DZ, add_x)
        every = (slice(None),)
        got = remote(grad.at[(mine,) + (every if taps else ()) + (slice(None), oy)], ry, y_peer)
        yield
        got.wait_recv()

        def add_y(i):
            t, zz = i // DZ, i % DZ
            dst = lead(grad, (mine,), t, (zz, y))
            src = lead(ry, (), t, (zz,))
            dst[...] = (dst[...].astype(F32) + src[...].astype(F32)).astype(BF16)
        each(rows_n * DZ, add_y)
        got = [remote(grad.at[(mine,) + (every if taps else ()) + (z_to(k), y)], rz.at[k - 1], at_zy(z_to(k), y))
               for k in range(1, DZ)]
        yield
        for copy in got:
            copy.wait_recv()

        def add_z(t):
            value = lead(grad, (mine,), t, (z, y))[...].astype(F32)
            for k in range(1, DZ):
                value = value + lead(rz, (k - 1,), t, ())[...].astype(F32)
            lead(fb, (mine,), t, ())[...] = value.astype(BF16)
        each(rows_n, add_z)
        got = [remote(fb.at[mine], fb.at[mine], peer) for peer in sp_peers]
        yield
        for copy in got:
            copy.wait_recv()
        for qq in range(S):
            put(qq, fb[qq].astype(F32))

    def reduce_diff():
        got = remote(g_diff.at[oc], rcd, c_peer)
        yield
        got.wait_recv()

        def add_c(i):
            t, zz = i // DZ, i % DZ
            for yy in range(2):
                value = g_diff[c, t, zz, yy].astype(F32) + rcd[t, zz, yy].astype(F32)
                g_diff[c, t, zz, yy] = value.astype(BF16)
        each(9 * DZ, add_c)
        got = remote(g_diff.at[c, :, :, oy], ryd, y_peer)
        yield
        got.wait_recv()

        def add_y(i):
            t, zz = i // DZ, i % DZ
            value = g_diff[c, t, zz, y].astype(F32) + ryd[t, zz].astype(F32)
            g_diff[c, t, zz, y] = value.astype(BF16)
        each(9 * DZ, add_y)
        got = [remote(g_diff.at[c, :, z_to(k), y], rzd.at[k - 1], at_zy(z_to(k), y)) for k in range(1, DZ)]
        yield
        for copy in got:
            copy.wait_recv()

        def add_z(t):
            value = g_diff[c, t, z, y].astype(F32)
            for k in range(1, DZ):
                value = value + rzd[k - 1, t].astype(F32)
            fdx[t] = value
        each(9, add_z)
        got = [remote(fdx, rxd.at[k - 1], x_peer(k)) for k in range(1, SX)]
        yield
        for copy in got:
            copy.wait_recv()

        def add_x(t):
            value = fdx[t]
            for k in range(1, SX):
                value = value + rxd[k - 1, t]
            fdo[c, t] = value
        each(9, add_x)
        got = remote(fdo.at[c], fdo.at[c], c_peer)
        yield
        got.wait_recv()
        od_out[...] = fdo[...]

    def reduce_rest():
        got = remote(g_re, rcr, c_peer)
        yield
        got.wait_recv()
        shared = (g_re.shape[2], LANES)

        def add_c(zz):
            for yy in range(2):
                value = g_re[zz, yy].astype(F32) + rcr[zz, yy].astype(F32)
                rcr[zz, yy] = value.astype(BF16)
        each(DZ, add_c)
        got = remote(rcr.at[:, oy], ryr, y_peer)
        yield
        got.wait_recv()

        def add_y(zz):
            value = rcr[zz, y].astype(F32) + ryr[zz].astype(F32)
            rcr[zz, y] = value.astype(BF16)
        each(DZ, add_y)
        got = [remote(rcr.at[z_to(k), y], rzr.at[k - 1], at_zy(z_to(k), y)) for k in range(1, DZ)]
        yield
        for copy in got:
            copy.wait_recv()
        value = rcr[z, y].astype(F32)
        for k in range(1, DZ):
            value = value + rzr[k - 1].astype(F32)
        frx[...] = value
        got = [remote(frx, rxr.at[k - 1], x_peer(k)) for k in range(1, SX)]
        yield
        for copy in got:
            copy.wait_recv()
        value = frx[...]
        for k in range(1, SX):
            value = value + rxr[k - 1]
        n_red, n_exp = or_out.shape[0], oe_out.shape[0]
        or_out[...] = value[0:n_red]
        for b in range(4):
            oe_out[:, b * LANES : (b + 1) * LANES] = value[n_red + b * n_exp : n_red + (b + 1) * n_exp]

    def put_first(qq, value):
        of_out[:, qq * fw : (qq + 1) * fw] = value

    def put_mid(qq, value):
        om_out[:, :, qq * mw : (qq + 1) * mw] = value

    def put_last(qq, value):
        ol_out[:, qq * lw : (qq + 1) * lw] = value

    red_last = reduce_wide(g_last, rcl, rxl, ryl, rzl, fbl, 0, put_last)
    red_mid = reduce_wide(g_mid, rcm, rxm, rym, rzm, fbm, 9, put_mid)
    red_first = reduce_wide(g_first, rcf, rxf, ryf, rzf, fbf, 0, put_first)
    red_diff, red_rest = reduce_diff(), reduce_rest()

    def push(*chains):
        for chain in chains:
            next(chain, None)

    for finish in (free_gated, free_change):
        finish()
        halo_waits.remove(finish)
    mgb, mgr = gb, gr
    sg2, gg = z3.at[:, 0:512], z3.at[:, 512:1024]
    sg2[...] = dot_nt(lgb[...], wl[...].reshape(512, 2048))
    parts = []
    for group in range(NG):
        def slope_2(start, carry):
            normed = z2[pl.ds(start, STEP), :]
            _, slope = silu_parts(gain_2 * normed + bias_2)
            value = sg2[pl.ds(start, STEP), :] * slope
            sg2[pl.ds(start, STEP), :] = value
            return carry[0] + fold(value), carry[1] + fold(value * normed)
        zero = jnp.zeros((8, 512), F32)
        sums = rows_loop(group, slope_2, (zero, zero))
        parts += [jnp.sum(item, axis=0, keepdims=True) for item in sums]
    copies = sp_send(2, parts)
    for n in range(4):
        g_last[n] = dot_tn(sab[...], lgb[:, n * 512 : (n + 1) * 512]).astype(BF16).reshape(DZ, 2, lr, 512)
    push(red_last)
    total = sp_total(2, copies)
    gain_2_grad = bias_2_grad = jnp.zeros((1, 512), F32)
    for group in range(NG):
        row = 2 * group
        bias_sum, gain_sum = total[row : row + 1], total[row + 1 : row + 2]
        gain_2_grad, bias_2_grad = gain_2_grad + gain_sum, bias_2_grad + bias_sum
        scale = gain_2 * inv_2[group]

        def apply_2b(start, carry):
            value = sg2[pl.ds(start, STEP), :] - bias_sum * inv_pixels
            value = scale * (value - z2[pl.ds(start, STEP), :] * (gain_sum * inv_pixels))
            mgb[pl.ds(start, STEP), :] = value.astype(BF16)
            return carry
        rows_loop(group, apply_2b, 0)
    wait_mid, _ = halo(mgb.at[pl.ds(0, NW)], mgb.at[pl.ds(NW, NW)], None, None, mgr.at[0], mgr.at[1])
    push(red_last)
    for a in range(3):
        for b in range(3):
            grad = dot_tn(gs[a : a + 2, :, b * 512 : (b + 1) * 512].reshape(2 * NW, 512), mgb[...]).astype(BF16)
            for qq in range(S):
                g_mid[qq, 3 * a + b] = grad[:, qq * mw : (qq + 1) * mw].reshape(DZ, 2, wm_in.shape[1], mw)
    push(red_mid)
    mgs = gs
    for r in range(2):
        spread(mgs, 1 + r, lambda start, r=r: mgb[pl.ds(r * NW + start, STEP), :], True)

    def back_taps(lhs, a):
        total = dot_nt(lhs[:, 0:512], wm[3 * a].reshape(512, 512))
        for b in range(1, 3):
            total = total + dot_nt(lhs[:, b * 512 : (b + 1) * 512], wm[3 * a + b].reshape(512, 512))
        return total

    gg[...] = back_taps(mgs[1:3].reshape(2 * NW, 1536), 1)
    gg[0:NW, :] += back_taps(mgs[2], 0)
    gg[NW : 2 * NW, :] += back_taps(mgs[1], 2)
    wait_mid()
    spread(mgs, 0, lambda start: mgr[0, pl.ds(start, STEP), :], True)
    spread(mgs, 3, lambda start: mgr[1, pl.ds(start, STEP), :], True)
    gg[0:NW, :] += back_taps(mgs[0], 2)
    gg[NW : 2 * NW, :] += back_taps(mgs[3], 0)

    def gate_back(i, carry):
        start = pl.multiple_of(i * STEP, STEP)
        gate = gt[pl.ds(start, STEP), :]
        act = jax.nn.silu(gain_1 * z1[pl.ds(start, STEP), :] + bias_1)
        value = gg[pl.ds(start, STEP), :] * act * gate * (1.0 - gate)
        fgb[pl.ds(start, STEP), :] = value.astype(BF16)
        return carry

    lax.fori_loop(0, 2 * NW // STEP, gate_back, 0)
    cg = dot_nt(fgb[...], we[...].reshape(LANES, 512)).astype(BF16)
    cg_rows = [cg[r * NW : (r + 1) * NW].astype(F32) for r in range(2)]
    hg = pair_sum(cg_rows[0] + cg_rows[1]).astype(BF16)
    for r in range(2):
        cgx[r, 0] = cg_rows[r].astype(BF16)
        cgx[r, 1] = hg
    wait_cg, _ = halo(cgx.at[0], cgx.at[1], None, None, cgr.at[0], cgr.at[1])
    push(red_last)
    n_exp = we_in.shape[0]
    grad = dot_tn(comb[...], fgb[...]).astype(BF16)
    n_red = wr_in.shape[0]
    for b in range(4):
        g_re[:, :, n_red + b * n_exp : n_red + (b + 1) * n_exp, :] = grad[
            :, b * LANES : (b + 1) * LANES].reshape(DZ, 2, n_exp, LANES)
    for r in range(2):
        put_shifts(cgs, 1 + r, cg_rows[r], 1, True)
    put_shifts(hgs, 1, hg.astype(F32), 2, True)
    for a in range(3):
        grad = dot_tn(cs[a : a + 2].reshape(2 * NW, 384), cg).astype(BF16)
        g_diff[0, 3 * a : 3 * a + 3] = grad.reshape(3, DZ, 2, wd0_in.shape[1], LANES)
        grad = (0.5 * dot_tn(ps[a], hg)).astype(BF16)
        g_diff[1, 3 * a : 3 * a + 3] = grad.reshape(3, DZ, 2, wd0_in.shape[1], LANES)
    push(red_diff)
    wait_cg()
    put_shifts(cgs, 0, cgr[0, 0].astype(F32), 1, True)
    put_shifts(cgs, 3, cgr[1, 0].astype(F32), 1, True)
    put_shifts(hgs, 0, cgr[0, 1].astype(F32), 2, True)
    put_shifts(hgs, 2, cgr[1, 1].astype(F32), 2, True)
    full = jnp.zeros((2 * NW, LANES), F32)
    half = jnp.zeros((NW, LANES), F32)
    for a in range(3):
        for b in range(3):
            lanes = slice(b * LANES, (b + 1) * LANES)
            full = full + dot_nt(
                cgs[2 - a : 4 - a, :, lanes].reshape(2 * NW, LANES), wd[0, 3 * a + b].reshape(LANES, LANES))
            half = half + dot_nt(hgs[2 - a, :, lanes], wd[1, 3 * a + b].reshape(LANES, LANES))
    rd[...] = full + 0.25 * jnp.concatenate([half, half], axis=0)
    for r in range(2):
        for f in range(NF):
            here = r * NW + f * 16
            after = r * NW + ((f + 1) % NF) * 16
            diff = (keep[f].astype(F32) * rd[here : here + 16, :]
                    - keep[(f + 1) % NF].astype(F32) * rd[after : after + 16, :])
            chb[r, f * 16 : f * 16 + 16, :] = diff.astype(BF16)
    rgb = chb[...].reshape(2 * NW, LANES)
    sg2[...] = dot_nt(rgb, wr[...].reshape(512, LANES))

    parts = []
    for group in range(NG):
        def slope_1(start, carry):
            normed = z1[pl.ds(start, STEP), :]
            _, slope = silu_parts(gain_1 * normed + bias_1)
            value = gg[pl.ds(start, STEP), :] * (1.0 + gt[pl.ds(start, STEP), :]) + sg2[pl.ds(start, STEP), :]
            value = value * slope
            sg2[pl.ds(start, STEP), :] = value
            return carry[0] + fold(value), carry[1] + fold(value * normed)
        zero = jnp.zeros((8, 512), F32)
        sums = rows_loop(group, slope_1, (zero, zero))
        parts += [jnp.sum(item, axis=0, keepdims=True) for item in sums]
    copies = sp_send(3, parts)
    g_re[:, :, 0:n_red, :] = dot_tn(fab[...], rgb).astype(BF16).reshape(DZ, 2, n_red, LANES)
    push(red_rest, red_mid, red_last, red_diff)
    total = sp_total(3, copies)
    gain_1_grad = bias_1_grad = jnp.zeros((1, 512), F32)
    for group in range(NG):
        row = 2 * group
        bias_sum, gain_sum = total[row : row + 1], total[row + 1 : row + 2]
        gain_1_grad, bias_1_grad = gain_1_grad + gain_sum, bias_1_grad + bias_sum
        scale = gain_1 * inv_1[group]

        def apply_1b(start, carry):
            value = sg2[pl.ds(start, STEP), :] - bias_sum * inv_pixels
            value = scale * (value - z1[pl.ds(start, STEP), :] * (gain_sum * inv_pixels))
            fgb[pl.ds(start, STEP), :] = value.astype(BF16)
            return carry
        rows_loop(group, apply_1b, 0)

    for k, copy in enumerate(stem_copies):
        copy.wait_recv()
    stem_total = stg[...]
    for k in range(S - 1):
        stem_total = stem_total + stgr[k]
    gain_3_all = jnp.concatenate(gain_3_grad, axis=1)
    bias_3_all = jnp.concatenate(bias_3_grad, axis=1)
    for d in range(D):
        mid_at, last_at = (d // per) * LANES, d * rows_last * LANES
        rows = [v[:, mid_at : mid_at + LANES] for v in (gain_1_grad, bias_1_grad, gain_2_grad, bias_2_grad)]
        for v in (gain_3_all, bias_3_all):
            rows += [v[:, last_at + n * LANES : last_at + (n + 1) * LANES] for n in range(rows_last)]
        sms[d, 0:8, :] = stem_total[d * 8 : d * 8 + 8]
        sms[d, 8:16, :] = jnp.concatenate(rows, axis=0)
    small_back = [
        remote(sms.at[lax.rem(dp + k, D)], smr.at[k - 1], dp_peers[k - 1]) for k in range(1, D)]

    for n in range(4):
        grad = dot_tn(x3[:, :, n * 512 : (n + 1) * 512].reshape(2 * NW, 512), fgb[...]).astype(BF16)
        per_chunk = 512 // (2 * fr)
        for qq in range(S):
            g_first[qq, n * per_chunk : (n + 1) * per_chunk] = grad[:, qq * fw : (qq + 1) * fw].reshape(
                per_chunk, 2, fr, fw)
    push(red_first, red_rest, red_mid, red_last, red_diff)
    weights_first = wf[...].reshape(2048, 512)
    for n in range(4):
        lo = n * 512
        free_part()
        z3[:, lo : lo + 512] = dot_nt(fgb[...], weights_first[lo : lo + 512])

        def apply_in(i, carry):
            start = pl.multiple_of(i * STEP, STEP)
            value = z3[pl.ds(start, STEP), lo : lo + 512] + ct_rows(start, lo, 512)
            ost[n % 2, pl.ds(start // 16, STEP // 16)] = value.astype(BF16).reshape(STEP // 16, 16, 512)
            return carry
        lax.fori_loop(0, 2 * NW // STEP, apply_in, 0)
        store_part(n, ig_hbm)
    for _ in range(6):
        push(red_first, red_rest, red_mid, red_last, red_diff)

    assert counters["r"] <= ssem.shape[0] and counters["l"] <= lsem.shape[0], counters
    wait_video()
    row8 = lax.broadcasted_iota(jnp.int32, (8, LANES), 0)

    def video_edges(f, carry):
        for ch in range(3):
            rows = slice(ch * 8, ch * 8 + 8)
            from_prev = vgr[0, f, ch * 2 + 1 : ch * 2 + 2, :]
            from_next = vgr[1, f, ch * 2 : ch * 2 + 1, :]
            vg_out[f, rows] += jnp.where(row8 == 0, from_prev, jnp.where(row8 == 7, from_next, 0.0))
        return carry

    lax.fori_loop(0, NF, video_edges, 0)
    value = sms[dp]
    for k, copy in enumerate(small_back):
        copy.wait_recv()
        value = value + smr[k]
    osm_out[...] = value
    for copy in sends:
        copy.wait_send()
    for finish in halo_waits:
        finish()
    for part in stores[-2:]:
        for copy in part:
            copy.wait()


def on_device_kernel(
    clip_video, section_input, keep_mask, w_rgb, w_stem_diff, w_first, w_middle, w_last, w_reduce,
    w_diff_full, w_diff_half, w_expand, gain_first, bias_first, gain_middle, bias_middle, gain_last,
    bias_last, stem_cot, section_cot,
):
    D, S = lax.axis_size("dp"), lax.axis_size("sp")
    DZ, SX = D // 2, S // 2
    NF = clip_video.shape[0]
    NW = NF * 16
    dp = lax.axis_index("dp")
    frames = clip_video.astype(F32)
    edges = jnp.stack([frames[:, :, 0], frames[:, :, 7]], axis=2).reshape(NF, 6, LANES)
    uin = jnp.concatenate([frames.reshape(NF, 24, LANES), edges, jnp.zeros((NF, 2, LANES), F32)], axis=1)
    per = D * LANES // 512
    width = 512 // D
    lane = jnp.arange(LANES)
    stem_w = jnp.concatenate([w_rgb, w_stem_diff], axis=1).astype(F32).transpose(2, 0, 1).reshape(8, 81)
    stem_w = jnp.pad(stem_w, ((0, 0), (0, LANES - 81)))
    mids = jnp.stack([gain_first, bias_first, gain_middle, bias_middle]).astype(F32)
    mids = jnp.where(lane // width == dp % per, jnp.tile(mids, (1, per)), 0.0)
    lasts = jnp.concatenate([gain_last, bias_last]).astype(F32).reshape(-1, LANES)
    small = jnp.concatenate([stem_w, mids, lasts], axis=0)
    band = jnp.asarray(band_table(8), BF16)
    fr, fw = w_first.shape[0], 512 // S
    mr, lr, rr = w_middle.shape[1], w_last.shape[0], w_reduce.shape[0]
    dr, er = w_diff_full.shape[1], w_expand.shape[0]
    lw = 2048 // S
    shape = jax.ShapeDtypeStruct
    vm = pltpu.VMEM
    any_spec = pl.BlockSpec(memory_space=pl.ANY)
    vmem_spec = pl.BlockSpec(memory_space=pltpu.VMEM)
    n_rem, n_loc = 420, 64
    re_rows = rr + 4 * er
    scratch = [
        pltpu.SemaphoreType.DMA((n_rem,)), pltpu.SemaphoreType.DMA((n_rem,)), pltpu.SemaphoreType.DMA((n_loc,)),
        vm((DZ, 2, fr, 512), BF16), vm((9, DZ, 2, mr, 512), BF16), vm((DZ, 2, lr, 2048), BF16),
        vm((DZ, 2, rr, LANES), BF16), vm((2, 9, DZ, 2, dr, LANES), BF16), vm((DZ, 2, er, 512), BF16),
        vm((2 * NF, 16, 2048), BF16), vm((2 * NF, 16, 2048), BF16),
        vm((2 * PART, 512, LANES), BF16), vm((2 * PART, 512, LANES), BF16),
        vm((NF, 32, LANES), F32), vm((NF, 8, LANES), F32), vm((NF, 8, LANES), F32),
        vm((D, 16, LANES), F32), vm((512, 288), BF16), vm((3, 512, LANES), F32), vm((288, 512), BF16),
        vm((NF, 96, LANES), F32),
        vm((NF, 8, LANES), F32), vm((2, NF, 8, LANES), F32), vm((D * 8, LANES), F32), vm((S - 1, D * 8, LANES), F32),
        vm((4, 8, 512), F32), vm((4, S - 1, 8, 512), F32), vm((4, 8, 512), F32), vm((4, S - 1, 8, 512), F32),
        vm((2 * NW, 512), F32), vm((2 * NW, 512), BF16), vm((2 * NW, 512), F32),
        vm((2 * NW, LANES), F32), vm((2, NW, LANES), BF16), vm((2, 2, NW, LANES), BF16),
        vm((4, NW, 384), BF16), vm((3, NW, 384), BF16), vm((2 * NW, LANES), BF16),
        vm((2 * NW, 512), BF16), vm((2, NW, 512), BF16), vm((4, NW, 1536), BF16),
        vm((2 * NW, 512), F32), vm((2 * NW, 512), BF16), vm((2 * NW, 2048), F32), vm((2 * NW, 2048), BF16),
        vm((2, 2, NW, LANES), BF16), vm((2, 2, NW, LANES), BF16),
        vm((4, NW, 384), BF16), vm((3, NW, 384), BF16), vm((2 * NW, 512), BF16), vm((2, 2 * NF, 16, 512), BF16),
        vm((S, DZ, 2, fr, fw), BF16), vm((S, 9, DZ, 2, mr, fw), BF16), vm((S, DZ, 2, lr, lw), BF16),
        vm((2, 9, DZ, 2, dr, LANES), BF16), vm((DZ, 2, re_rows, LANES), BF16),
        vm((SX, DZ, 2, fr, fw), BF16), vm((SX - 1, DZ, 2, fr, fw), BF16), vm((DZ, fr, fw), BF16),
        vm((DZ - 1, fr, fw), BF16),
        vm((SX, 9, DZ, 2, mr, fw), BF16), vm((SX - 1, 9, DZ, 2, mr, fw), BF16), vm((9, DZ, mr, fw), BF16),
        vm((DZ - 1, 9, mr, fw), BF16),
        vm((SX, DZ, 2, lr, lw), BF16), vm((SX - 1, DZ, 2, lr, lw), BF16), vm((DZ, lr, lw), BF16),
        vm((DZ - 1, lr, lw), BF16),
        vm((9, DZ, 2, dr, LANES), BF16), vm((9, DZ, dr, LANES), BF16), vm((DZ - 1, 9, dr, LANES), BF16),
        vm((9, dr, LANES), F32), vm((SX - 1, 9, dr, LANES), F32), vm((2, 9, dr, LANES), F32),
        vm((DZ, 2, re_rows, LANES), BF16), vm((DZ, re_rows, LANES), BF16), vm((DZ - 1, re_rows, LANES), BF16),
        vm((re_rows, LANES), F32), vm((SX - 1, re_rows, LANES), F32),
        vm((S, fr, fw), BF16), vm((S, 9, mr, fw), BF16), vm((S, lr, lw), BF16),
        vm((D, 16, LANES), F32), vm((D - 1, 16, LANES), F32),
    ]
    outs = pl.pallas_call(
        functools.partial(whole_kernel, (D, S, NF)),
        out_shape=(
            shape((NF, 512, LANES), BF16), shape((NF, 24, LANES), F32),
            shape(section_input.shape, BF16), shape(section_input.shape, BF16),
            shape((fr, 512), F32), shape((9, mr, 512), F32), shape((lr, 2048), F32), shape((rr, LANES), F32),
            shape((2, 9, dr, LANES), F32), shape((er, 512), F32), shape((16, LANES), F32),
        ),
        in_specs=[pl.BlockSpec(memory_space=pltpu.SMEM)] + [vmem_spec] * 3 + [any_spec] * 10,
        out_specs=(any_spec, vmem_spec, any_spec, any_spec) + (vmem_spec,) * 7,
        scratch_shapes=scratch,
        compiler_params=pltpu.CompilerParams(
            collective_id=0, has_side_effects=True, vmem_limit_bytes=VMEM_BYTES),
        name="tdn_blocks",
    )(
        keep_mask, uin, small, band, section_input, section_cot, stem_cot.reshape(NF, 512, LANES),
        w_first, w_middle, w_last, w_reduce, w_diff_full, w_diff_half, w_expand,
    )
    so, vg, section_output, input_grad, g_first, g_mid, g_last, g_red, g_diff, g_exp, g_small = outs
    stem = g_small[0:8, 0:81].reshape(8, 9, 9).transpose(1, 2, 0)
    mids = lax.dynamic_slice_in_dim(g_small[8:12], (dp % per) * width, width, axis=1)
    rows_last = 2048 // D // LANES
    lasts = g_small[12 : 12 + 2 * rows_last].reshape(2, rows_last * LANES)
    return (
        so.reshape(stem_cot.shape), vg.reshape(clip_video.shape), section_output, input_grad,
        stem[:, 0:3], stem[:, 3:9], g_first, g_mid, g_last, g_red, g_diff[0], g_diff[1], g_exp,
        mids[0], mids[1], mids[2], mids[3], lasts[0], lasts[1],
    )


def fits_kernel(mesh):
    dp_count, sp_count = mesh.shape["dp"], mesh.shape["sp"]
    return (
        dp_count % 2 == 0 and sp_count % 2 == 0 and H5 == 2 * sp_count and HS == 8 * sp_count
        and TDM_C % (16 * dp_count) == 0 and STEM_C == 8 * dp_count and MID // sp_count % LANES == 0
        and C5 // dp_count % LANES == 0
    )


def solution(mesh):
    placed = (
        P("dp", None, "sp", None),
        P("dp", "sp", None, None),
        P("dp"),
        P(None, None, "dp"),
        P(None, None, "dp"),
        P("dp", None),
        P(None, "dp", None),
        P("dp", None),
        P("dp", None),
        P(None, "dp", None),
        P(None, "dp", None),
        P("dp", None),
        P("dp"),
        P("dp"),
        P("dp"),
        P("dp"),
        P("dp"),
        P("dp"),
        P("dp", None, "sp", None),
        P("dp", "sp", None, None),
    )
    return jax.shard_map(
        on_device_kernel if fits_kernel(mesh) else on_device,
        mesh=mesh,
        in_specs=placed,
        out_specs=(
            P("dp", None, "sp", None),
            P("dp", None, "sp", None),
            P("dp", "sp", None, None),
            P("dp", "sp", None, None),
            P(None, None, "dp"),
            P(None, None, "dp"),
            P("dp", None),
            P(None, "dp", None),
            P("dp", None),
            P("dp", None),
            P(None, "dp", None),
            P(None, "dp", None),
            P("dp", None),
            P("dp"),
            P("dp"),
            P("dp"),
            P("dp"),
            P("dp"),
            P("dp"),
        ),
        check_vma=False,
    )
```

```python
import functools

import jax
import jax.numpy as jnp
import numpy as np
from jax import lax
from jax.experimental import pallas as pl
from jax.experimental.pallas import tpu as pltpu
from jax.sharding import PartitionSpec as P

H5, HS, MID, TDM_C, C5, STEM_C = 8, 32, 512, 128, 2048, 64
VMEM_BYTES = 63 * 2**20

MICRO = 2


EPS = 1e-05


def with_halo(block, sides, width):
    for axis, dim in sides:
        count = lax.axis_size(axis)
        forward = [(i, i + 1) for i in range(count - 1)]
        backward = [(target, source) for source, target in forward]
        low = lax.ppermute(
            lax.slice_in_dim(block, block.shape[dim] - width, None, axis=dim), axis, forward
        )
        high = lax.ppermute(lax.slice_in_dim(block, 0, width, axis=dim), axis, backward)
        block = jnp.concatenate([low, block, high], axis=dim)
    return block


def silu_slope(values):
    sig_value = jax.nn.sigmoid(values)
    return sig_value * (1.0 + values * (1.0 - sig_value))


def tap_window(padded, row_off, col_off, row_count, col_count, row_axis):
    part_rows = lax.slice_in_dim(padded, row_off, row_off + row_count, axis=row_axis)
    return lax.slice_in_dim(part_rows, col_off, col_off + col_count, axis=row_axis + 1)


def pad_columns(haloed, row_axis):
    widths = [(0, 0)] * haloed.ndim
    widths[row_axis + 1] = (1, 1)
    return jnp.pad(haloed, widths)


def tap_conv(haloed, kernel, channels_last):
    row_axis = 1 if channels_last else 2
    row_count = haloed.shape[row_axis] - 2
    col_count = haloed.shape[row_axis + 1]
    padded = pad_columns(haloed, row_axis)
    einsum_form = "fhwc,cd->fhwd" if channels_last else "fchw,cd->fdhw"
    result = None
    for tap_index in range(9):
        window = tap_window(padded, tap_index // 3, tap_index % 3, row_count, col_count, row_axis)
        tap_term = jnp.einsum(
            einsum_form, window, kernel[tap_index], preferred_element_type=jnp.float32
        )
        result = tap_term if result is None else result + tap_term
    return result


def tap_conv_back(grad_halo, kernel, channels_last):
    row_axis = 1 if channels_last else 2
    row_count = grad_halo.shape[row_axis] - 2
    col_count = grad_halo.shape[row_axis + 1]
    padded = pad_columns(grad_halo, row_axis)
    einsum_form = "fhwd,cd->fhwc" if channels_last else "fdhw,cd->fchw"
    result = None
    for tap_index in range(9):
        window = tap_window(
            padded, 2 - tap_index // 3, 2 - tap_index % 3, row_count, col_count, row_axis
        )
        tap_term = jnp.einsum(
            einsum_form, window, kernel[tap_index], preferred_element_type=jnp.float32
        )
        result = tap_term if result is None else result + tap_term
    return result


def tap_kernel_grad(haloed, out_grad, channels_last):
    row_axis = 1 if channels_last else 2
    row_count = out_grad.shape[row_axis]
    col_count = out_grad.shape[row_axis + 1]
    padded = pad_columns(haloed, row_axis)
    einsum_form = "fhwc,fhwd->cd" if channels_last else "fchw,fdhw->cd"
    tap_list = []
    for tap_index in range(9):
        window = tap_window(padded, tap_index // 3, tap_index % 3, row_count, col_count, row_axis)
        tap_list.append(
            jnp.einsum(einsum_form, window, out_grad, preferred_element_type=jnp.float32)
        )
    return jnp.stack(tap_list, axis=0)


def pair_mean(values):
    return values.reshape(
        values.shape[0], values.shape[1] // 2, 2, values.shape[2] // 2, 2, values.shape[3]
    ).mean(axis=(2, 4))


def pair_total(values):
    return values.reshape(
        values.shape[0], values.shape[1] // 2, 2, values.shape[2] // 2, 2, values.shape[3]
    ).sum(axis=(2, 4))


def pair_grow(values):
    return jnp.repeat(jnp.repeat(values, 2, axis=1), 2, axis=2)


def norm_forward(pre_norm, gain, bias, pixel_count):
    local_sums = (jnp.sum(pre_norm, axis=(0, 1, 2)), jnp.sum(pre_norm * pre_norm, axis=(0, 1, 2)))
    total_sum, total_square = lax.psum((local_sums[0], local_sums[1]), "sp")
    mean_value = total_sum / pixel_count
    variance = total_square / pixel_count - mean_value * mean_value
    inverse = lax.rsqrt(variance + EPS)
    normed = (pre_norm - mean_value) * inverse
    return (normed, inverse, gain * normed + bias)


def norm_backward(out_grad, normed, inverse, gain, pixel_count):
    local_bias = jnp.sum(out_grad, axis=(0, 1, 2))
    local_gain = jnp.sum(out_grad * normed, axis=(0, 1, 2))
    total_bias, total_gain = lax.psum((local_bias, local_gain), "sp")
    pre_grad = (
        gain * inverse * (out_grad - total_bias / pixel_count - normed * total_gain / pixel_count)
    )
    return (pre_grad, local_gain, local_bias)


def reduce_grads(grads):
    summed = (
        lax.psum_scatter(grads[0], "dp", scatter_dimension=2, tiled=True),
        lax.psum_scatter(grads[1], "dp", scatter_dimension=2, tiled=True),
        lax.psum_scatter(grads[2], "dp", scatter_dimension=0, tiled=True),
        lax.psum_scatter(grads[3], "dp", scatter_dimension=1, tiled=True),
        lax.psum_scatter(grads[4], "dp", scatter_dimension=0, tiled=True),
        lax.psum_scatter(grads[5], "dp", scatter_dimension=0, tiled=True),
        lax.psum_scatter(grads[6], "dp", scatter_dimension=1, tiled=True),
        lax.psum_scatter(grads[7], "dp", scatter_dimension=1, tiled=True),
        lax.psum_scatter(grads[8], "dp", scatter_dimension=0, tiled=True),
        lax.psum_scatter(grads[9], "dp", scatter_dimension=0, tiled=True),
        lax.psum_scatter(grads[10], "dp", scatter_dimension=0, tiled=True),
        lax.psum_scatter(grads[11], "dp", scatter_dimension=0, tiled=True),
        lax.psum_scatter(grads[12], "dp", scatter_dimension=0, tiled=True),
        lax.psum_scatter(grads[13], "dp", scatter_dimension=0, tiled=True),
        lax.psum_scatter(grads[14], "dp", scatter_dimension=0, tiled=True),
    )
    return (
        lax.psum(summed[0].astype(jnp.bfloat16), "sp").astype(jnp.float32),
        lax.psum(summed[1].astype(jnp.bfloat16), "sp").astype(jnp.float32),
        lax.psum(summed[2].astype(jnp.bfloat16), "sp").astype(jnp.float32),
        lax.psum(summed[3].astype(jnp.bfloat16), "sp").astype(jnp.float32),
        lax.psum(summed[4].astype(jnp.bfloat16), "sp").astype(jnp.float32),
        lax.psum(summed[5].astype(jnp.bfloat16), "sp").astype(jnp.float32),
        lax.psum(summed[6].astype(jnp.bfloat16), "sp").astype(jnp.float32),
        lax.psum(summed[7].astype(jnp.bfloat16), "sp").astype(jnp.float32),
        lax.psum(summed[8].astype(jnp.bfloat16), "sp").astype(jnp.float32),
        lax.psum(summed[9].astype(jnp.bfloat16), "sp").astype(jnp.float32),
        lax.psum(summed[10].astype(jnp.bfloat16), "sp").astype(jnp.float32),
        lax.psum(summed[11].astype(jnp.bfloat16), "sp").astype(jnp.float32),
        lax.psum(summed[12].astype(jnp.bfloat16), "sp").astype(jnp.float32),
        lax.psum(summed[13].astype(jnp.bfloat16), "sp").astype(jnp.float32),
        lax.psum(summed[14].astype(jnp.bfloat16), "sp").astype(jnp.float32),
    )


def run_micro(
    video_part, feat_part, keep_part, stem_grad_in, section_grad_in, weights, pixel_count
):
    (
        rgb_k,
        stemd_k,
        first_k,
        middle_k,
        last_k,
        reduce_k,
        dfull_k,
        dhalf_k,
        expand_k,
        gain_one,
        bias_one,
        gain_two,
        bias_two,
        gain_three,
        bias_three,
    ) = weights
    keep_float = keep_part.astype(jnp.float32)
    keep_col = keep_float[:, None, None, None]
    next_col = jnp.roll(keep_float, -1)[:, None, None, None]
    frames_halo = with_halo(video_part, (("sp", 2),), 1)
    frames_wide = frames_halo.astype(jnp.float32)
    before = keep_col * (frames_wide - jnp.roll(frames_wide, 1, axis=0))
    after = next_col * (jnp.roll(frames_wide, -1, axis=0) - frames_wide)
    diff_stack = jnp.concatenate([before, after], axis=1).astype(jnp.bfloat16)
    stem_out = (tap_conv(frames_halo, rgb_k, False) + tap_conv(diff_stack, stemd_k, False)).astype(
        jnp.bfloat16
    )
    cot_halo = with_halo(stem_grad_in, (("sp", 2),), 1)
    direct_grad = tap_conv_back(cot_halo, rgb_k, False)
    diff_grad = tap_conv_back(cot_halo, stemd_k, False)
    before_grad = keep_col * diff_grad[:, :3]
    after_grad = next_col * diff_grad[:, 3:]
    video_grad = (
        direct_grad
        + before_grad
        - jnp.roll(before_grad, -1, axis=0)
        + jnp.roll(after_grad, 1, axis=0)
        - after_grad
    )
    rgb_grad = tap_kernel_grad(frames_halo, stem_grad_in, False)
    stemd_grad = tap_kernel_grad(diff_stack, stem_grad_in, False)
    row_count = feat_part.shape[1]
    col_count = feat_part.shape[2]
    first_pre = jnp.einsum("fhwc,cd->fhwd", feat_part, first_k, preferred_element_type=jnp.float32)
    normed_one, inverse_one, norm_one = norm_forward(
        first_pre, gain_one.astype(jnp.float32), bias_one.astype(jnp.float32), pixel_count
    )
    first_act = jax.nn.silu(norm_one)
    first_low = first_act.astype(jnp.bfloat16)
    reduced = jnp.einsum("fhwc,cd->fhwd", first_low, reduce_k, preferred_element_type=jnp.float32)
    change_low = (keep_col * (reduced - jnp.roll(reduced, 1, axis=0))).astype(jnp.bfloat16)
    change_halo = with_halo(change_low, (("sp", 1),), 2)
    near_rows = change_halo[:, 1 : row_count + 3]
    full_out = tap_conv(near_rows, dfull_k, True)
    pooled = pair_mean(change_halo.astype(jnp.float32)).astype(jnp.bfloat16)
    half_out = tap_conv(pooled, dhalf_k, True)
    combined_low = (full_out + pair_grow(half_out)).astype(jnp.bfloat16)
    gate_value = jax.nn.sigmoid(
        jnp.einsum("fhwc,cd->fhwd", combined_low, expand_k, preferred_element_type=jnp.float32)
    )
    gated_low = (first_act * (1.0 + gate_value)).astype(jnp.bfloat16)
    gated_halo = with_halo(gated_low, (("sp", 1),), 1)
    middle_pre = tap_conv(gated_halo, middle_k, True)
    normed_two, inverse_two, norm_two = norm_forward(
        middle_pre, gain_two.astype(jnp.float32), bias_two.astype(jnp.float32), pixel_count
    )
    second_low = jax.nn.silu(norm_two).astype(jnp.bfloat16)
    last_pre = jnp.einsum("fhwc,cd->fhwd", second_low, last_k, preferred_element_type=jnp.float32)
    normed_three, inverse_three, norm_three = norm_forward(
        last_pre, gain_three.astype(jnp.float32), bias_three.astype(jnp.float32), pixel_count
    )
    section_out = (feat_part.astype(jnp.float32) + norm_three).astype(jnp.bfloat16)
    out_grad = section_grad_in.astype(jnp.float32)
    last_grad, gain_three_grad, bias_three_grad = norm_backward(
        out_grad, normed_three, inverse_three, gain_three.astype(jnp.float32), pixel_count
    )
    last_grad_low = last_grad.astype(jnp.bfloat16)
    last_k_grad = jnp.einsum(
        "fhwc,fhwd->cd", second_low, last_grad_low, preferred_element_type=jnp.float32
    )
    second_grad = jnp.einsum(
        "fhwd,cd->fhwc", last_grad_low, last_k, preferred_element_type=jnp.float32
    ) * silu_slope(norm_two)
    middle_grad, gain_two_grad, bias_two_grad = norm_backward(
        second_grad, normed_two, inverse_two, gain_two.astype(jnp.float32), pixel_count
    )
    middle_low = middle_grad.astype(jnp.bfloat16)
    middle_halo = with_halo(middle_low, (("sp", 1),), 1)
    gated_grad = tap_conv_back(middle_halo, middle_k, True)
    middle_k_grad = tap_kernel_grad(gated_halo, middle_low, True)
    gate_grad = (gated_grad * first_act * gate_value * (1.0 - gate_value)).astype(jnp.bfloat16)
    expand_grad = jnp.einsum(
        "fhwc,fhwd->cd", combined_low, gate_grad, preferred_element_type=jnp.float32
    )
    combined_grad = jnp.einsum(
        "fhwd,cd->fhwc", gate_grad, expand_k, preferred_element_type=jnp.float32
    ).astype(jnp.bfloat16)
    half_grad = pair_total(combined_grad.astype(jnp.float32)).astype(jnp.bfloat16)
    stacked = jnp.concatenate([combined_grad, jnp.repeat(half_grad, 2, axis=1)], axis=2)
    stacked_halo = with_halo(stacked, (("sp", 1),), 2)
    full_grad_halo = stacked_halo[:, 1 : row_count + 3, :col_count]
    half_grad_halo = stacked_halo[:, 0::2, col_count:]
    change_grad = tap_conv_back(full_grad_halo, dfull_k, True) + 0.25 * pair_grow(
        tap_conv_back(half_grad_halo, dhalf_k, True)
    )
    dfull_grad = tap_kernel_grad(near_rows, combined_grad, True)
    dhalf_grad = tap_kernel_grad(pooled, half_grad, True)
    weighted = keep_col * change_grad
    reduced_grad = (weighted - jnp.roll(weighted, -1, axis=0)).astype(jnp.bfloat16)
    reduce_grad = jnp.einsum(
        "fhwc,fhwd->cd", first_low, reduced_grad, preferred_element_type=jnp.float32
    )
    first_sum = gated_grad * (1.0 + gate_value) + jnp.einsum(
        "fhwd,cd->fhwc", reduced_grad, reduce_k, preferred_element_type=jnp.float32
    )
    first_grad, gain_one_grad, bias_one_grad = norm_backward(
        first_sum * silu_slope(norm_one),
        normed_one,
        inverse_one,
        gain_one.astype(jnp.float32),
        pixel_count,
    )
    first_grad_low = first_grad.astype(jnp.bfloat16)
    first_k_grad = jnp.einsum(
        "fhwc,fhwd->cd", feat_part, first_grad_low, preferred_element_type=jnp.float32
    )
    input_grad = (
        out_grad
        + jnp.einsum("fhwd,cd->fhwc", first_grad_low, first_k, preferred_element_type=jnp.float32)
    ).astype(jnp.bfloat16)
    grads = (
        rgb_grad,
        stemd_grad,
        first_k_grad,
        middle_k_grad,
        last_k_grad,
        reduce_grad,
        dfull_grad,
        dhalf_grad,
        expand_grad,
        gain_one_grad,
        bias_one_grad,
        gain_two_grad,
        bias_two_grad,
        gain_three_grad,
        bias_three_grad,
    )
    return ((stem_out, video_grad, section_out, input_grad), grads)


def add_trees(first_tree, second_tree):
    if first_tree is None:
        return second_tree
    return jax.tree.map(
        lambda left_part, right_part: left_part + right_part, first_tree, second_tree
    )


def on_device(
    clip_video,
    section_input,
    keep_mask,
    w_rgb,
    w_stem_diff,
    w_first,
    w_middle,
    w_last,
    w_reduce,
    w_diff_full,
    w_diff_half,
    w_expand,
    gain_first,
    bias_first,
    gain_middle,
    bias_middle,
    gain_last,
    bias_last,
    stem_cot,
    section_cot,
):
    micro_frames = clip_video.shape[0] // MICRO
    pixel_count = (
        micro_frames * section_input.shape[1] * lax.axis_size("sp") * section_input.shape[2]
    )
    results = []
    grad_totals = None
    for micro_index in range(MICRO):
        weights = (
            lax.all_gather(w_rgb, "dp", axis=2, tiled=True),
            lax.all_gather(w_stem_diff, "dp", axis=2, tiled=True),
            lax.all_gather(w_first, "dp", axis=0, tiled=True),
            lax.all_gather(w_middle, "dp", axis=1, tiled=True),
            lax.all_gather(w_last, "dp", axis=0, tiled=True),
            lax.all_gather(w_reduce, "dp", axis=0, tiled=True),
            lax.all_gather(w_diff_full, "dp", axis=1, tiled=True),
            lax.all_gather(w_diff_half, "dp", axis=1, tiled=True),
            lax.all_gather(w_expand, "dp", axis=0, tiled=True),
            lax.all_gather(gain_first, "dp", axis=0, tiled=True),
            lax.all_gather(bias_first, "dp", axis=0, tiled=True),
            lax.all_gather(gain_middle, "dp", axis=0, tiled=True),
            lax.all_gather(bias_middle, "dp", axis=0, tiled=True),
            lax.all_gather(gain_last, "dp", axis=0, tiled=True),
            lax.all_gather(bias_last, "dp", axis=0, tiled=True),
        )
        low_end = micro_index * micro_frames
        high_end = low_end + micro_frames
        outputs, grads = run_micro(
            clip_video[low_end:high_end],
            section_input[low_end:high_end],
            keep_mask[low_end:high_end],
            stem_cot[low_end:high_end],
            section_cot[low_end:high_end],
            weights,
            pixel_count,
        )
        results.append(outputs)
        grad_totals = add_trees(grad_totals, reduce_grads(grads))
    stem_features = jnp.concatenate([item[0] for item in results], axis=0)
    video_grad = jnp.concatenate([item[1] for item in results], axis=0)
    section_output = jnp.concatenate([item[2] for item in results], axis=0)
    section_input_grad = jnp.concatenate([item[3] for item in results], axis=0)
    return (
        stem_features,
        video_grad,
        section_output,
        section_input_grad,
        grad_totals[0],
        grad_totals[1],
        grad_totals[2],
        grad_totals[3],
        grad_totals[4],
        grad_totals[5],
        grad_totals[6],
        grad_totals[7],
        grad_totals[8],
        grad_totals[9],
        grad_totals[10],
        grad_totals[11],
        grad_totals[12],
        grad_totals[13],
        grad_totals[14],
    )


F32 = jnp.float32
BF16 = jnp.bfloat16
MESH_ID = pl.DeviceIdType.MESH
GROUP = 8
LANES = 128
STEP = 32
PART = 2


def dot_nn(left, right):
    return lax.dot_general(left, right, (((1,), (0,)), ((), ())), preferred_element_type=F32)


def dot_nt(left, right):
    return lax.dot_general(left, right, (((1,), (1,)), ((), ())), preferred_element_type=F32)


def dot_tn(left, right):
    return lax.dot_general(left, right, (((0,), (0,)), ((), ())), preferred_element_type=F32)


def shift_down(values, count):
    size = values.shape[0]
    column = lax.broadcasted_iota(jnp.int32, values.shape, 0) & 15
    return jnp.where(column < count, 0.0, pltpu.roll(values, count, 0))


def shift_up(values, count):
    size = values.shape[0]
    column = lax.broadcasted_iota(jnp.int32, values.shape, 0) & 15
    return jnp.where(column >= 16 - count, 0.0, pltpu.roll(values, size - count, 0))


def pair_sum(values):
    size = values.shape[0]
    parity = lax.broadcasted_iota(jnp.int32, values.shape, 0) & 1
    return values + jnp.where(parity == 0, pltpu.roll(values, size - 1, 0), pltpu.roll(values, 1, 0))


def band_table(rows):
    table = np.zeros((rows, 96, 3 * LANES), np.float32)
    for i in range(rows):
        for a in range(3):
            for b in range(3):
                for ch in range(9):
                    base = (b * 3 + ch // 3) * 32
                    row = i + a - 1
                    if row < 0:
                        n = base + 24 + (ch % 3) * 2
                    elif row >= rows:
                        n = base + 24 + (ch % 3) * 2 + 1
                    else:
                        n = base + (ch % 3) * 8 + row
                    table[i, (3 * a + b) * 9 + ch, n] = 1.0
    return table


def silu_parts(values):
    sig = jax.nn.sigmoid(values)
    return values * sig, sig * (1.0 + values * (1.0 - sig))


def whole_kernel(
    sizes, keep, uin, small, band, x_hbm, ct_hbm, sc_hbm, wf_in, wm_in, wl_in, wr_in, wd0_in, wd1_in, we_in,
    so_hbm, vg_out, out_hbm, ig_hbm, fbf_hbm, fbm_hbm, fbl_hbm, or_out, od_out, oe_out, osm_out,
    ssem, rsem, lsem, wf, wm, wl, wr, wd, we, x3, ct3, sc, so, ust, uprev, unext, sm, tf, tff, tb, dg,
    vgh, vgr, stg, stgr, stat_s, stat_r, st3_s, st3_r, z1, fab, gt, rd, chb, chr_, cs, ps, comb,
    gb, gr, gs, z2, sab, z3, lgb, cgx, cgr, cgs, hgs, fgb, ost,
    g_first, g_mid, g_last, g_diff, g_re, rcd, ryd, rzd, fdx, rxd, fdo, rcr, ryr, rzr, frx, rxr, fbf, fbm, fbl, sms, smr, *bufs,
):
    D, S, NF = sizes
    DZ, SX = D // 2, S // 2
    NG = NF // GROUP
    NW = NF * 16
    GW = GROUP * 16
    dp, sp = lax.axis_index("dp"), lax.axis_index("sp")
    z, y = dp // 2, dp % 2
    x, c = sp // 2, sp % 2
    oy, oc = 1 - y, 1 - c
    q_own = c * SX + x

    def at_zy(zz, yy):
        return (zz * 2 + yy, sp)

    y_peer = at_zy(z, oy)
    c_peer = (dp, x * 2 + oc)

    def z_to(k):
        return lax.rem(z + k, DZ)

    def z_from(k):
        return lax.rem(z + DZ - k, DZ)

    def x_to(k):
        return lax.rem(x + k, SX)

    def x_from(k):
        return lax.rem(x + SX - k, SX)

    def x_peer(k):
        return (dp, x_to(k) * 2 + c)

    sp_peers = [(dp, lax.rem(sp + k, S)) for k in range(1, S)]
    dp_peers = [(lax.rem(dp + k, D), sp) for k in range(1, D)]
    has_prev, has_next = sp > 0, sp < S - 1
    prev_dev, next_dev = (dp, sp - 1), (dp, sp + 1)

    counters = {"r": 0, "l": 0}
    sends = []

    def bundle(whole):
        i = counters["r"]
        counters["r"] += 1

        def start(src, dst, dev):
            pltpu.make_async_remote_copy(
                src_ref=src, dst_ref=dst, send_sem=ssem.at[i], recv_sem=rsem.at[i],
                device_id=dev, device_id_type=MESH_ID,
            ).start()

        def wait():
            pltpu.make_async_copy(whole, whole, rsem.at[i]).wait()

        def finish():
            pltpu.make_async_copy(whole, whole, ssem.at[i]).wait()

        sends.append(finish)
        return start, wait

    def remote(src, dst, dev):
        start, wait = bundle(dst)
        start(src, dst, dev)
        return wait

    def to_peers(src, dst_of, peers, whole):
        start, wait = bundle(whole)
        for k, peer in enumerate(peers):
            start(src, dst_of(k), peer)
        return wait

    def local(src, dst):
        i = counters["l"]
        counters["l"] += 1
        copy = pltpu.make_async_copy(src, dst, lsem.at[i])
        copy.start()
        return copy

    @pl.when(sp == 0)
    def _():
        uprev[...] = jnp.zeros_like(uprev)
        vgr[0] = jnp.zeros(vgr.shape[1:], F32)
        chr_[0] = jnp.zeros(chr_.shape[1:], BF16)
        gr[0] = jnp.zeros(gr.shape[1:], BF16)
        cgr[0] = jnp.zeros(cgr.shape[1:], BF16)

    @pl.when(sp == S - 1)
    def _():
        unext[...] = jnp.zeros_like(unext)
        vgr[1] = jnp.zeros(vgr.shape[1:], F32)
        chr_[1] = jnp.zeros(chr_.shape[1:], BF16)
        gr[1] = jnp.zeros(gr.shape[1:], BF16)
        cgr[1] = jnp.zeros(cgr.shape[1:], BF16)

    barrier = pltpu.get_barrier_semaphore()
    for peer in sp_peers + dp_peers:
        pl.semaphore_signal(barrier, inc=1, device_id=peer, device_id_type=MESH_ID)
    own_small = local(small, sm.at[dp])
    own = [
        local(wf_in, wf.at[dp]), local(wd0_in, wd.at[0, :, dp]), local(wd1_in, wd.at[1, :, dp]),
        local(wr_in, wr.at[dp]), local(we_in, we.at[dp]), local(wm_in, wm.at[:, dp]), local(wl_in, wl.at[dp]),
    ]

    def load_cot(part):
        lo = part * PART
        return local(sc_hbm.at[pl.ds(lo, PART)], sc.at[pl.ds(lo % (2 * PART), PART)])

    load_sc = [load_cot(0), load_cot(1)]
    load_x = [local(x_hbm.at[:, r], x3.at[pl.ds(r * NF, NF)]) for r in range(2)]
    load_ct = [local(ct_hbm.at[:, r], ct3.at[pl.ds(r * NF, NF)]) for r in range(2)]
    pl.semaphore_wait(barrier, S - 1 + D - 1)

    halo_waits = []

    def halo(to_prev, to_next, from_prev, from_next, land_prev, land_next):
        i = counters["r"]
        counters["r"] += 2

        def up():
            return pltpu.make_async_remote_copy(
                src_ref=to_prev, dst_ref=land_next, send_sem=ssem.at[i], recv_sem=rsem.at[i],
                device_id=prev_dev, device_id_type=MESH_ID)

        def down():
            return pltpu.make_async_remote_copy(
                src_ref=to_next, dst_ref=land_prev, send_sem=ssem.at[i + 1], recv_sem=rsem.at[i + 1],
                device_id=next_dev, device_id_type=MESH_ID)

        @pl.when(has_prev)
        def _():
            up().start()

        @pl.when(has_next)
        def _():
            down().start()

        def wait():
            @pl.when(has_prev)
            def _():
                down().wait_recv()

            @pl.when(has_next)
            def _():
                up().wait_recv()

        def finish():
            @pl.when(has_prev)
            def _():
                up().wait_send()

            @pl.when(has_next)
            def _():
                down().wait_send()

        halo_waits.append(finish)
        return wait, finish

    wait_small = to_peers(small, lambda k: sm.at[dp], dp_peers, sm.at[pl.ds(0, D - 1)])
    edge = uin.at[:, pl.ds(24, 8)]
    wait_edges, _ = halo(edge, edge, None, None, uprev, unext)

    def gather(mode, src, dst):
        wide = {"A": 1, "B": SX, "D": S}[mode]
        first_q = {"A": q_own, "B": c * SX, "D": 0}[mode]
        only = pl.ds(dp, 1)
        z_start, z_wait = bundle(dst(pl.ds(0, DZ - 1), first_q, wide))
        y_start, y_wait = bundle(dst(pl.ds(0, DZ), first_q, wide))
        if mode == "A":
            x_start, x_wait = bundle(dst(pl.ds(0, (D - 1) * (SX - 1)), first_q, 1))
        if mode != "D":
            c_start, c_wait = bundle(dst(pl.ds(0, D - 1), c * SX, SX))
        for k in range(1, DZ):
            z_start(src(first_q, wide), dst(only, first_q, wide), at_zy(z_to(k), y))
        y_start(src(first_q, wide), dst(only, first_q, wide), y_peer)
        yield

        def fan(d):
            part = dst(d, first_q, wide)
            if mode == "A":
                for k in range(1, SX):
                    x_start(part, part, x_peer(k))
            if mode != "D":
                c_start(part, part, c_peer)

        z_wait()
        for k in range(1, DZ):
            d = pl.ds(z_from(k) * 2 + y, 1)
            y_start(dst(d, first_q, wide), dst(d, first_q, wide), y_peer)
            fan(d)
        yield
        y_wait()
        for k in range(DZ):
            fan(pl.ds(z_from(k) * 2 + oy, 1))
        yield
        if mode == "A":
            x_wait()
            for k in range(1, SX):
                for n in range(1, D):
                    part = dst(pl.ds(lax.rem(dp + n, D), 1), c * SX + x_from(k), 1)
                    c_start(part, part, c_peer)
            yield
        if mode != "D":
            c_wait()

    def lane_block(index, width, count):
        return pl.ds(pl.multiple_of(index * width, width), width * count)

    fr, fw = wf_in.shape[0], wf_in.shape[1] // S
    mw = wm_in.shape[2] // S
    lr, lw = wl_in.shape[0], wl_in.shape[1] // S

    def first_part(mode, lo, n):
        rows = pl.ds(lo, n)
        return gather(mode, lambda q, w: wf.at[pl.ds(dp, 1), rows, lane_block(q, fw, w)],
                      lambda d, q, w: wf.at[d, rows, lane_block(q, fw, w)])

    def mid_part(mode, lo, n):
        rows = pl.ds(lo, n)
        return gather(mode, lambda q, w: wm.at[rows, pl.ds(dp, 1), :, lane_block(q, mw, w)],
                      lambda d, q, w: wm.at[rows, d, :, lane_block(q, mw, w)])

    def last_part(mode, lo, n):
        rows = pl.ds(lo, n)
        return gather(mode, lambda q, w: wl.at[pl.ds(dp, 1), rows, lane_block(q, lw, w)],
                      lambda d, q, w: wl.at[d, rows, lane_block(q, lw, w)])

    for copy in own:
        copy.wait()
    part_b = fr * 3 // 8
    part_a = (fr - part_b) // 2
    chunks = [
        (0, first_part("A", 0, part_a)),
        (0, first_part("B", 2 * part_a, part_b)),
        (0, first_part("A", part_a, part_a)),
        (1, gather("D", lambda q, w: wr.at[pl.ds(dp, 1)], lambda d, q, w: wr.at[d])),
        (1, gather("B", lambda q, w: wd.at[c, :, pl.ds(dp, 1)], lambda d, q, w: wd.at[c, :, d])),
        (1, gather("D", lambda q, w: we.at[pl.ds(dp, 1)], lambda d, q, w: we.at[d])),
        (1, mid_part("A", 0, 3)), (2, mid_part("B", 6, 3)), (2, mid_part("A", 3, 3)),
        (3, last_part("A", 0, lr // 2)), (3, last_part("B", lr // 2, lr // 4)),
        (4, last_part("A", lr * 3 // 4, lr // 4)),
    ]
    slot = [0]

    def pump(count=1):
        for _ in range(count):
            for start, chunk in chunks:
                if start <= slot[0]:
                    next(chunk, None)
            slot[0] += 1

    pump()

    own_small.wait()
    wait_small()
    wt = sm[:, 0:8, :].reshape(D * 8, LANES)[:, 0:96].astype(BF16)
    for i in range(8):
        rows = dot_nn(wt, band[i])
        for n in range(3):
            tff[n, pl.ds(i, D * 8, stride=8), :] = rows[:, n * LANES : (n + 1) * LANES]
    for n in range(3):
        columns = min(288 - n * LANES, LANES)
        tf[:, n * LANES : n * LANES + columns] = tff[n, :, 0:columns].astype(BF16)
        tb[n * LANES : n * LANES + columns, :] = tff[n].T[0:columns].astype(BF16)

    per = D * LANES // 512

    def mid_vec(j):
        parts = []
        for m in range(D // per):
            row = sm[m * per, 8 + j : 9 + j, :]
            for n in range(1, per):
                row = row + sm[m * per + n, 8 + j : 9 + j, :]
            parts.append(row)
        return jnp.concatenate(parts, axis=1)

    rows_last = 2048 // D // LANES

    def last_vec(j):
        return jnp.concatenate(
            [sm[d, 8 + j + n : 9 + j + n, :] for d in range(D) for n in range(rows_last)], axis=1)

    gain_1, bias_1, gain_2, bias_2 = [mid_vec(j) for j in range(4)]
    gain_3, bias_3 = last_vec(4), last_vec(4 + rows_last)

    wait_edges()
    side = lax.broadcasted_iota(jnp.int32, (8, LANES), 0) & 1
    ust[...] = uin[...]
    for f in range(NF):
        ust[f, 24:32, :] = jnp.where(
            side == 0, pltpu.roll(uprev[f], 7, 0), pltpu.roll(unext[f], 1, 0))
    zt = tff
    zt[...] = jnp.zeros_like(zt)

    def stem_frame(f, carry):
        before_at, after_at = lax.rem(f + NF - 1, NF), lax.rem(f + 1, NF)
        k_here, k_next = keep[f].astype(F32), keep[after_at].astype(F32)
        frame = ust[f]
        stacked = jnp.concatenate(
            [frame, k_here * (frame - ust[before_at]), k_next * (ust[after_at] - frame)], axis=0)
        stacked = stacked.astype(BF16).astype(F32)
        lane = lax.broadcasted_iota(jnp.int32, stacked.shape, 1)
        left = jnp.where(lane == 0, 0.0, pltpu.roll(stacked, 1, 1))
        right = jnp.where(lane == LANES - 1, 0.0, pltpu.roll(stacked, LANES - 1, 1))
        taps = jnp.concatenate([left, stacked, right], axis=0).astype(BF16)
        place = lax.rem(f, 2 * PART)
        cot = sc[place]
        so[place] = dot_nn(tf[...], taps).astype(BF16)
        back = dot_nn(tb[...], cot)
        dg[f] = (
            jnp.where(lane == LANES - 1, 0.0, pltpu.roll(back[0:96], LANES - 1, 1))
            + back[96:192]
            + jnp.where(lane == 0, 0.0, pltpu.roll(back[192:288], 1, 1)))
        cross = dot_nt(cot, taps)
        for n in range(3):
            columns = min(288 - n * LANES, LANES)
            zt[n, :, 0:columns] += cross[:, n * LANES : n * LANES + columns]
        return carry

    store_so = []
    for part in range(NF // PART):
        lo = part * PART
        load_sc[part].wait()
        if part >= 2:
            store_so[part - 2].wait()
        lax.fori_loop(lo, lo + PART, stem_frame, 0)
        store_so.append(local(so.at[pl.ds(lo % (2 * PART), PART)], so_hbm.at[pl.ds(lo, PART)]))
        if part + 2 < NF // PART:
            load_sc.append(load_cot(part + 2))
        if part % 2:
            pump()
    for copy in store_so[-2:]:
        copy.wait()

    def video_frame(f, carry):
        before_at, after_at = lax.rem(f + NF - 1, NF), lax.rem(f + 1, NF)
        k_here, k_next = keep[f].astype(F32), keep[after_at].astype(F32)
        total = (
            dg[f, 0:32] + k_here * dg[f, 32:64] - k_next * dg[after_at, 32:64]
            + k_here * dg[before_at, 64:96] - k_next * dg[f, 64:96])
        vg_out[f] = total[0:24]
        vgh[f] = total[24:32]
        return carry

    lax.fori_loop(0, NF, video_frame, 0)
    wait_video, _ = halo(vgh, vgh, None, None, vgr.at[0], vgr.at[1])

    stem_grad = jnp.zeros((D * 8, 96), F32)
    for i in range(8):
        for n in range(3):
            part = zt[n, pl.ds(i, D * 8, stride=8), :]
            high = part.astype(BF16)
            low = (part - high.astype(F32)).astype(BF16)
            table = band[i, :, n * LANES : (n + 1) * LANES]
            stem_grad = stem_grad + dot_nt(high, table) + dot_nt(low, table)
    stg[...] = jnp.concatenate([stem_grad, jnp.zeros((D * 8, LANES - 96), F32)], axis=1)
    wait_stem = to_peers(stg, lambda k: stgr.at[k], sp_peers, stgr)

    def rows_loop(group, fn, init):
        def body(i, carry):
            start = (i // (GW // STEP)) * NW + group * GW + (i % (GW // STEP)) * STEP
            return fn(pl.multiple_of(start, STEP), carry)
        return lax.fori_loop(0, 2 * (GW // STEP), body, init)

    def fold(values):
        return values.reshape(STEP // 8, 8, values.shape[1]).sum(axis=0)

    def sp_send(i, parts):
        width = parts[0].shape[1]
        fill = [jnp.zeros((8 - len(parts), width), F32)] if len(parts) < 8 else []
        stat_s[i] = jnp.concatenate(parts + fill, axis=0)
        return to_peers(stat_s.at[i], lambda k: stat_r.at[i, k], sp_peers, stat_r.at[i])

    def sp_total(i, wait):
        wait()
        total = stat_s[i]
        for k in range(S - 1):
            total = total + stat_r[i, k]
        return total

    pixels = jnp.float32(GROUP * 2 * S * 16)
    inv_pixels = 1.0 / (GROUP * 2 * S * 16)

    def two_sums(ref):
        parts = []
        for group in range(NG):
            def add(start, carry):
                value = ref[pl.ds(start, STEP), :]
                return carry[0] + fold(value), carry[1] + fold(value * value)
            zero = jnp.zeros((8, ref.shape[1]), F32)
            one, two = rows_loop(group, add, (zero, zero))
            parts += [jnp.sum(one, axis=0, keepdims=True), jnp.sum(two, axis=0, keepdims=True)]
        return parts

    def moments(total, row):
        mean = total[row : row + 1] * inv_pixels
        variance = total[row + 1 : row + 2] * inv_pixels - mean * mean
        return mean, lax.rsqrt(variance + EPS)

    for copy in load_x:
        copy.wait()
    xs = x3[...].reshape(2 * NW, x3.shape[2])
    for n in range(2):
        z1[:, n * 256 : (n + 1) * 256] = dot_nn(xs, wf[:, :, n * 256 : (n + 1) * 256].reshape(x3.shape[2], 256))
    copies = sp_send(0, two_sums(z1))
    pump()
    total = sp_total(0, copies)
    inv_1 = []
    for group in range(NG):
        mean, inv = moments(total, 2 * group)
        inv_1.append(inv)

        def apply_1(start, carry):
            normed = (z1[pl.ds(start, STEP), :] - mean) * inv
            act = jax.nn.silu(gain_1 * normed + bias_1)
            z1[pl.ds(start, STEP), :] = normed
            z3[pl.ds(start, STEP), 0:512] = act
            fab[pl.ds(start, STEP), :] = act.astype(BF16)
            return carry
        rows_loop(group, apply_1, 0)

    rd[...] = dot_nn(fab[...], wr[...].reshape(512, LANES))
    for r in range(2):
        for f in range(NF):
            here = r * NW + f * 16
            past = r * NW + ((f - 1) % NF) * 16
            diff = keep[f].astype(F32) * (rd[here : here + 16, :] - rd[past : past + 16, :])
            chb[r, f * 16 : f * 16 + 16, :] = diff.astype(BF16)
    wait_change, free_change = halo(chb, chb, None, None, chr_.at[0], chr_.at[1])

    def put_shifts(ref, at, values, count, flip):
        width = values.shape[1]
        down, up = shift_down(values, count), shift_up(values, count)
        low, high = (up, down) if flip else (down, up)
        ref[at, :, 0:width] = low.astype(BF16)
        ref[at, :, width : 2 * width] = values.astype(BF16)
        ref[at, :, 2 * width : 3 * width] = high.astype(BF16)

    change = [chb[r].astype(F32) for r in range(2)]
    for r in range(2):
        put_shifts(cs, 1 + r, change[r], 1, False)

    def pool(upper, lower):
        return (pair_sum(upper + lower) * 0.25).astype(BF16).astype(F32)

    put_shifts(ps, 1, pool(change[0], change[1]), 2, False)
    pump()
    wait_change()
    above = [chr_[0, r].astype(F32) for r in range(2)]
    below = [chr_[1, r].astype(F32) for r in range(2)]
    put_shifts(cs, 0, above[1], 1, False)
    put_shifts(cs, 3, below[0], 1, False)
    put_shifts(ps, 0, pool(above[0], above[1]), 2, False)
    put_shifts(ps, 2, pool(below[0], below[1]), 2, False)
    full = jnp.zeros((2 * NW, LANES), F32)
    half = jnp.zeros((NW, LANES), F32)
    for a in range(3):
        full = full + dot_nn(cs[a : a + 2].reshape(2 * NW, 384), wd[0, 3 * a : 3 * a + 3].reshape(384, LANES))
        half = half + dot_nn(ps[a], wd[1, 3 * a : 3 * a + 3].reshape(384, LANES))
    comb[...] = (full + jnp.concatenate([half, half], axis=0)).astype(BF16)
    gt[...] = dot_nn(comb[...], we[...].reshape(LANES, 512))

    def apply_gate(i, carry):
        start = pl.multiple_of(i * STEP, STEP)
        gate = jax.nn.sigmoid(gt[pl.ds(start, STEP), :])
        gt[pl.ds(start, STEP), :] = gate
        gated = (z3[pl.ds(start, STEP), 0:512] * (1.0 + gate)).astype(BF16)
        gb[pl.ds(start, STEP), :] = gated
        return carry

    lax.fori_loop(0, 2 * NW // STEP, apply_gate, 0)
    wait_gated, free_gated = halo(gb.at[pl.ds(0, NW)], gb.at[pl.ds(NW, NW)], None, None, gr.at[0], gr.at[1])

    def spread(dst, at, src_fn, flip):
        def body(i, carry):
            start = pl.multiple_of(i * STEP, STEP)
            values = src_fn(start).astype(F32)
            down, up = shift_down(values, 1), shift_up(values, 1)
            low, high = (up, down) if flip else (down, up)
            dst[at, pl.ds(start, STEP), 0:512] = low.astype(BF16)
            dst[at, pl.ds(start, STEP), 512:1024] = values.astype(BF16)
            dst[at, pl.ds(start, STEP), 1024:1536] = high.astype(BF16)
            return carry
        lax.fori_loop(0, NW // STEP, body, 0)

    for r in range(2):
        spread(gs, 1 + r, lambda start, r=r: gb[pl.ds(r * NW + start, STEP), :], False)

    def taps_of(a):
        return wm[3 * a : 3 * a + 3].reshape(1536, 512)

    z2[...] = dot_nn(gs[1:3].reshape(2 * NW, 1536), taps_of(1))
    z2[0:NW, :] += dot_nn(gs[2], taps_of(2))
    z2[NW : 2 * NW, :] += dot_nn(gs[1], taps_of(0))
    wait_gated()
    spread(gs, 0, lambda start: gr[0, pl.ds(start, STEP), :], False)
    spread(gs, 3, lambda start: gr[1, pl.ds(start, STEP), :], False)
    z2[0:NW, :] += dot_nn(gs[0], taps_of(0))
    z2[NW : 2 * NW, :] += dot_nn(gs[3], taps_of(2))
    copies = sp_send(1, two_sums(z2))
    pump(2)
    for copy in load_ct:
        copy.wait()
    total = sp_total(1, copies)
    inv_2 = []
    for group in range(NG):
        mean, inv = moments(total, 2 * group)
        inv_2.append(inv)

        def apply_2(start, carry):
            normed = (z2[pl.ds(start, STEP), :] - mean) * inv
            z2[pl.ds(start, STEP), :] = normed
            sab[pl.ds(start, STEP), :] = jax.nn.silu(gain_2 * normed + bias_2).astype(BF16)
            return carry
        rows_loop(group, apply_2, 0)

    def ct_rows(start, lo, width):
        return ct3[pl.ds(start // 16, STEP // 16), :, lo : lo + width].reshape(STEP, width).astype(F32)

    def x_rows(start, lo, width):
        return x3[pl.ds(start // 16, STEP // 16), :, lo : lo + width].reshape(STEP, width).astype(F32)

    last_copies = []
    for n in range(4):
        lo = n * 512
        z3[:, lo : lo + 512] = dot_nn(sab[...], wl[:, :, lo : lo + 512].reshape(512, 512))
        parts = []
        for group in range(NG):
            def add_3(start, carry):
                value = z3[pl.ds(start, STEP), lo : lo + 512]
                cot = ct_rows(start, lo, 512)
                return (carry[0] + fold(value), carry[1] + fold(value * value),
                        carry[2] + fold(cot), carry[3] + fold(cot * value))
            zero = jnp.zeros((8, 512), F32)
            sums = rows_loop(group, add_3, (zero, zero, zero, zero))
            parts += [jnp.sum(item, axis=0, keepdims=True) for item in sums]
        st3_s[n] = jnp.concatenate(parts, axis=0)
        last_copies.append(to_peers(st3_s.at[n], lambda k, n=n: st3_r.at[n, k], sp_peers, st3_r.at[n]))
    gain_3_grad, bias_3_grad = [], []
    stores = []

    def free_part():
        if len(stores) >= 2:
            for copy in stores[-2]:
                copy.wait()

    def store_part(n, target):
        stores.append([local(ost.at[n % 2, pl.ds(r * NF, NF)], target.at[:, r, :, pl.ds(n * 512, 512)]) for r in range(2)])

    for n in range(4):
        lo = n * 512
        free_part()
        last_copies[n]()
        total = st3_s[n]
        for k in range(S - 1):
            total = total + st3_r[n, k]
        gain, bias = gain_3[:, lo : lo + 512], bias_3[:, lo : lo + 512]
        gain_sum = bias_sum = jnp.zeros((1, 512), F32)
        for group in range(NG):
            row = 4 * group
            mean, inv = moments(total, row)
            cot_sum = total[row + 2 : row + 3]
            cot_normed = inv * (total[row + 3 : row + 4] - mean * cot_sum)
            gain_sum, bias_sum = gain_sum + cot_normed, bias_sum + cot_sum
            cot_mean, slope_mean = cot_sum * inv_pixels, cot_normed * inv_pixels
            scale = gain * inv

            def apply_3(start, carry):
                normed = (z3[pl.ds(start, STEP), lo : lo + 512] - mean) * inv
                cot = ct_rows(start, lo, 512)
                out = x_rows(start, lo, 512) + gain * normed + bias
                ost[n % 2, pl.ds(start // 16, STEP // 16)] = out.astype(BF16).reshape(STEP // 16, 16, 512)
                lgb[pl.ds(start, STEP), lo : lo + 512] = (
                    scale * (cot - cot_mean - normed * slope_mean)).astype(BF16)
                return carry
            rows_loop(group, apply_3, 0)
        store_part(n, out_hbm)
        gain_3_grad.append(gain_sum)
        bias_3_grad.append(bias_sum)

    def each(count, fn):
        def body(i, carry):
            fn(i)
            return carry
        lax.fori_loop(0, count, body, 0)

    def wide_first(grad, lo, n, order, rc, rx, ry, rz, fb):
        rows = pl.ds(lo, n)
        half = pl.ds(c * SX, SX)
        mine = q_own

        def add(dst, *others):
            value = dst[...].astype(F32)
            for other in others:
                value = value + other[...].astype(F32)
            dst[...] = value.astype(BF16)

        wait = remote(grad.at[pl.ds(oc * SX, SX), :, :, rows], rc, c_peer)
        yield
        wait()

        def add_c(i):
            for xx in range(SX):
                for yy in range(2):
                    add(grad.at[c * SX + xx, i, yy, rows], rc.at[xx, i, yy])
        each(DZ, add_c)
        if order == "xyz":
            start, wait = bundle(rx)
            for k in range(1, SX):
                start(grad.at[c * SX + x_to(k), :, :, rows], rx.at[k - 1], x_peer(k))
            yield
            wait()

            def add_x(i):
                for yy in range(2):
                    add(grad.at[mine, i, yy, rows], *[rx.at[k, i, yy] for k in range(SX - 1)])
            each(DZ, add_x)
            wait = remote(grad.at[mine, :, oy, rows], ry, y_peer)
            yield
            wait()
            each(DZ, lambda i: add(grad.at[mine, i, y, rows], ry.at[i]))
            start, wait = bundle(rz)
            for k in range(1, DZ):
                start(grad.at[mine, z_to(k), y, rows], rz.at[k - 1], at_zy(z_to(k), y))
            yield
            wait()
            parts = [rz.at[k] for k in range(DZ - 1)]
        else:
            wait = remote(grad.at[half, :, oy, rows], ry, y_peer)
            yield
            wait()

            def add_y(i):
                for xx in range(SX):
                    add(grad.at[c * SX + xx, i, y, rows], ry.at[xx, i])
            each(DZ, add_y)
            start, wait = bundle(rz)
            for k in range(1, DZ):
                start(grad.at[half, z_to(k), y, rows], rz.at[k - 1], at_zy(z_to(k), y))
            yield
            wait()
            for xx in range(SX):
                add(grad.at[c * SX + xx, z, y, rows], *[rz.at[k, xx] for k in range(DZ - 1)])
            start, wait = bundle(rx)
            for k in range(1, SX):
                start(grad.at[c * SX + x_to(k), z, y, rows], rx.at[k - 1], x_peer(k))
            yield
            wait()
            parts = [rx.at[k] for k in range(SX - 1)]
        value = grad[mine, z, y, rows].astype(F32)
        for part in parts:
            value = value + part[...].astype(F32)
        fb[mine, rows] = value.astype(BF16)
        done = fb.at[mine, rows]
        wait = to_peers(done, lambda k: done, sp_peers, fb.at[pl.ds(0, S - 1), rows])
        yield
        wait()

    def wide_mid(grad, lo, n, order, rc, rx, ry, rz, fb):
        taps = pl.ds(lo, n)
        half = pl.ds(c * SX, SX)
        mine = q_own

        def add(dst, *others):
            value = dst[...].astype(F32)
            for other in others:
                value = value + other[...].astype(F32)
            dst[...] = value.astype(BF16)

        wait = remote(grad.at[pl.ds(oc * SX, SX), taps], rc, c_peer)
        yield
        wait()

        def add_c(i):
            t, zz = i // DZ, i % DZ
            for xx in range(SX):
                add(grad.at[c * SX + xx, lo + t, zz], rc.at[xx, t, zz])
        each(n * DZ, add_c)
        if order == "xyz":
            start, wait = bundle(rx)
            for k in range(1, SX):
                start(grad.at[c * SX + x_to(k), taps], rx.at[k - 1], x_peer(k))
            yield
            wait()

            def add_x(i):
                t, zz = i // DZ, i % DZ
                add(grad.at[mine, lo + t, zz], *[rx.at[k, t, zz] for k in range(SX - 1)])
            each(n * DZ, add_x)
            wait = remote(grad.at[mine, taps, :, oy], ry, y_peer)
            yield
            wait()

            def add_y(i):
                t, zz = i // DZ, i % DZ
                add(grad.at[mine, lo + t, zz, y], ry.at[t, zz])
            each(n * DZ, add_y)
            start, wait = bundle(rz)
            for k in range(1, DZ):
                start(grad.at[mine, taps, z_to(k), y], rz.at[k - 1], at_zy(z_to(k), y))
            yield
            wait()
            parts = [rz.at[k] for k in range(DZ - 1)]
        else:
            wait = remote(grad.at[half, taps, :, oy], ry, y_peer)
            yield
            wait()

            def add_y(i):
                t, zz = i // DZ, i % DZ
                for xx in range(SX):
                    add(grad.at[c * SX + xx, lo + t, zz, y], ry.at[xx, t, zz])
            each(n * DZ, add_y)
            start, wait = bundle(rz)
            for k in range(1, DZ):
                start(grad.at[half, taps, z_to(k), y], rz.at[k - 1], at_zy(z_to(k), y))
            yield
            wait()
            for xx in range(SX):
                each(n, lambda t, xx=xx: add(
                    grad.at[c * SX + xx, lo + t, z, y], *[rz.at[k, xx, t] for k in range(DZ - 1)]))
            start, wait = bundle(rx)
            for k in range(1, SX):
                start(grad.at[c * SX + x_to(k), taps, z, y], rx.at[k - 1], x_peer(k))
            yield
            wait()
            parts = [rx.at[k] for k in range(SX - 1)]

        def finish(t):
            value = grad[mine, lo + t, z, y].astype(F32)
            for part in parts:
                value = value + part[t].astype(F32)
            fb[mine, lo + t] = value.astype(BF16)
        each(n, finish)
        done = fb.at[mine, taps]
        wait = to_peers(done, lambda k: done, sp_peers, fb.at[pl.ds(0, S - 1), taps])
        yield
        wait()

    def reduce_diff():
        wait = remote(g_diff.at[oc], rcd, c_peer)
        yield
        wait()

        def add_c(i):
            t, zz = i // DZ, i % DZ
            for yy in range(2):
                value = g_diff[c, t, zz, yy].astype(F32) + rcd[t, zz, yy].astype(F32)
                g_diff[c, t, zz, yy] = value.astype(BF16)
        each(9 * DZ, add_c)
        wait = remote(g_diff.at[c, :, :, oy], ryd, y_peer)
        yield
        wait()

        def add_y(i):
            t, zz = i // DZ, i % DZ
            value = g_diff[c, t, zz, y].astype(F32) + ryd[t, zz].astype(F32)
            g_diff[c, t, zz, y] = value.astype(BF16)
        each(9 * DZ, add_y)
        start, wait = bundle(rzd)
        for k in range(1, DZ):
            start(g_diff.at[c, :, z_to(k), y], rzd.at[k - 1], at_zy(z_to(k), y))
        yield
        wait()

        def add_z(t):
            value = g_diff[c, t, z, y].astype(F32)
            for k in range(1, DZ):
                value = value + rzd[k - 1, t].astype(F32)
            fdx[t] = value
        each(9, add_z)
        start, wait = bundle(rxd)
        for k in range(1, SX):
            start(fdx, rxd.at[k - 1], x_peer(k))
        yield
        wait()

        def add_x(t):
            value = fdx[t]
            for k in range(1, SX):
                value = value + rxd[k - 1, t]
            fdo[c, t] = value
        each(9, add_x)
        wait = remote(fdo.at[c], fdo.at[c], c_peer)
        yield
        wait()
        od_out[...] = fdo[...]

    def reduce_rest():
        wait = remote(g_re, rcr, c_peer)
        yield
        wait()

        def add_c(zz):
            for yy in range(2):
                value = g_re[zz, yy].astype(F32) + rcr[zz, yy].astype(F32)
                rcr[zz, yy] = value.astype(BF16)
        each(DZ, add_c)
        wait = remote(rcr.at[:, oy], ryr, y_peer)
        yield
        wait()

        def add_y(zz):
            value = rcr[zz, y].astype(F32) + ryr[zz].astype(F32)
            rcr[zz, y] = value.astype(BF16)
        each(DZ, add_y)
        start, wait = bundle(rzr)
        for k in range(1, DZ):
            start(rcr.at[z_to(k), y], rzr.at[k - 1], at_zy(z_to(k), y))
        yield
        wait()
        value = rcr[z, y].astype(F32)
        for k in range(1, DZ):
            value = value + rzr[k - 1].astype(F32)
        frx[...] = value
        start, wait = bundle(rxr)
        for k in range(1, SX):
            start(frx, rxr.at[k - 1], x_peer(k))
        yield
        wait()
        value = frx[...]
        for k in range(1, SX):
            value = value + rxr[k - 1]
        n_red, n_exp = or_out.shape[0], oe_out.shape[0]
        or_out[...] = value[0:n_red]
        for b in range(4):
            oe_out[:, b * LANES : (b + 1) * LANES] = value[n_red + b * n_exp : n_red + (b + 1) * n_exp]

    first_x, mid_x, last_x = fr * 5 // 8, 6, lr // 2
    red_first_x = wide_first(g_first, 0, first_x, "xyz", *bufs[0:4], fbf)
    red_first_y = wide_first(g_first, first_x, fr - first_x, "yzx", *bufs[4:8], fbf)
    red_mid_x = wide_mid(g_mid, 0, mid_x, "xyz", *bufs[8:12], fbm)
    red_mid_y = wide_mid(g_mid, mid_x, 9 - mid_x, "yzx", *bufs[12:16], fbm)
    red_last_x = wide_first(g_last, 0, last_x, "xyz", *bufs[16:20], fbl)
    red_last_y = wide_first(g_last, last_x, lr - last_x, "yzx", *bufs[20:24], fbl)
    red_diff, red_rest = reduce_diff(), reduce_rest()

    def push(*chains):
        for chain in chains:
            next(chain, None)

    for finish in (free_gated, free_change):
        finish()
        halo_waits.remove(finish)
    mgb, mgr = gb, gr
    sg2, gg = z3.at[:, 0:512], z3.at[:, 512:1024]
    sg2[...] = dot_nt(lgb[...], wl[...].reshape(512, 2048))
    parts = []
    for group in range(NG):
        def slope_2(start, carry):
            normed = z2[pl.ds(start, STEP), :]
            _, slope = silu_parts(gain_2 * normed + bias_2)
            value = sg2[pl.ds(start, STEP), :] * slope
            sg2[pl.ds(start, STEP), :] = value
            return carry[0] + fold(value), carry[1] + fold(value * normed)
        zero = jnp.zeros((8, 512), F32)
        sums = rows_loop(group, slope_2, (zero, zero))
        parts += [jnp.sum(item, axis=0, keepdims=True) for item in sums]
    copies = sp_send(2, parts)
    for n in range(4):
        g_last[n] = dot_tn(sab[...], lgb[:, n * 512 : (n + 1) * 512]).astype(BF16).reshape(DZ, 2, lr, 512)
    push(red_last_x, red_last_y)
    total = sp_total(2, copies)
    gain_2_grad = bias_2_grad = jnp.zeros((1, 512), F32)
    for group in range(NG):
        row = 2 * group
        bias_sum, gain_sum = total[row : row + 1], total[row + 1 : row + 2]
        gain_2_grad, bias_2_grad = gain_2_grad + gain_sum, bias_2_grad + bias_sum
        scale = gain_2 * inv_2[group]

        def apply_2b(start, carry):
            value = sg2[pl.ds(start, STEP), :] - bias_sum * inv_pixels
            value = scale * (value - z2[pl.ds(start, STEP), :] * (gain_sum * inv_pixels))
            mgb[pl.ds(start, STEP), :] = value.astype(BF16)
            return carry
        rows_loop(group, apply_2b, 0)
    wait_mid, _ = halo(mgb.at[pl.ds(0, NW)], mgb.at[pl.ds(NW, NW)], None, None, mgr.at[0], mgr.at[1])
    push(red_last_x, red_last_y)
    for a in range(3):
        for b in range(3):
            grad = dot_tn(gs[a : a + 2, :, b * 512 : (b + 1) * 512].reshape(2 * NW, 512), mgb[...]).astype(BF16)
            for qq in range(S):
                g_mid[qq, 3 * a + b] = grad[:, qq * mw : (qq + 1) * mw].reshape(DZ, 2, wm_in.shape[1], mw)
    push(red_mid_x, red_mid_y)
    mgs = gs
    for r in range(2):
        spread(mgs, 1 + r, lambda start, r=r: mgb[pl.ds(r * NW + start, STEP), :], True)

    def back_taps(lhs, a):
        total = dot_nt(lhs[:, 0:512], wm[3 * a].reshape(512, 512))
        for b in range(1, 3):
            total = total + dot_nt(lhs[:, b * 512 : (b + 1) * 512], wm[3 * a + b].reshape(512, 512))
        return total

    gg[...] = back_taps(mgs[1:3].reshape(2 * NW, 1536), 1)
    gg[0:NW, :] += back_taps(mgs[2], 0)
    gg[NW : 2 * NW, :] += back_taps(mgs[1], 2)
    wait_mid()
    spread(mgs, 0, lambda start: mgr[0, pl.ds(start, STEP), :], True)
    spread(mgs, 3, lambda start: mgr[1, pl.ds(start, STEP), :], True)
    gg[0:NW, :] += back_taps(mgs[0], 2)
    gg[NW : 2 * NW, :] += back_taps(mgs[3], 0)

    def gate_back(i, carry):
        start = pl.multiple_of(i * STEP, STEP)
        gate = gt[pl.ds(start, STEP), :]
        act = jax.nn.silu(gain_1 * z1[pl.ds(start, STEP), :] + bias_1)
        value = gg[pl.ds(start, STEP), :] * act * gate * (1.0 - gate)
        fgb[pl.ds(start, STEP), :] = value.astype(BF16)
        return carry

    lax.fori_loop(0, 2 * NW // STEP, gate_back, 0)
    cg = dot_nt(fgb[...], we[...].reshape(LANES, 512)).astype(BF16)
    cg_rows = [cg[r * NW : (r + 1) * NW].astype(F32) for r in range(2)]
    hg = pair_sum(cg_rows[0] + cg_rows[1]).astype(BF16)
    for r in range(2):
        cgx[r, 0] = cg_rows[r].astype(BF16)
        cgx[r, 1] = hg
    wait_cg, _ = halo(cgx.at[0], cgx.at[1], None, None, cgr.at[0], cgr.at[1])
    push(red_mid_x, red_mid_y)
    n_exp = we_in.shape[0]
    grad = dot_tn(comb[...], fgb[...]).astype(BF16)
    n_red = wr_in.shape[0]
    for b in range(4):
        g_re[:, :, n_red + b * n_exp : n_red + (b + 1) * n_exp, :] = grad[
            :, b * LANES : (b + 1) * LANES].reshape(DZ, 2, n_exp, LANES)
    for r in range(2):
        put_shifts(cgs, 1 + r, cg_rows[r], 1, True)
    put_shifts(hgs, 1, hg.astype(F32), 2, True)
    for a in range(3):
        grad = dot_tn(cs[a : a + 2].reshape(2 * NW, 384), cg).astype(BF16)
        g_diff[0, 3 * a : 3 * a + 3] = grad.reshape(3, DZ, 2, wd0_in.shape[1], LANES)
        grad = (0.5 * dot_tn(ps[a], hg)).astype(BF16)
        g_diff[1, 3 * a : 3 * a + 3] = grad.reshape(3, DZ, 2, wd0_in.shape[1], LANES)
    push(red_diff, red_last_y, red_last_x)
    wait_cg()
    put_shifts(cgs, 0, cgr[0, 0].astype(F32), 1, True)
    put_shifts(cgs, 3, cgr[1, 0].astype(F32), 1, True)
    put_shifts(hgs, 0, cgr[0, 1].astype(F32), 2, True)
    put_shifts(hgs, 2, cgr[1, 1].astype(F32), 2, True)
    full = jnp.zeros((2 * NW, LANES), F32)
    half = jnp.zeros((NW, LANES), F32)
    for a in range(3):
        for b in range(3):
            lanes = slice(b * LANES, (b + 1) * LANES)
            full = full + dot_nt(
                cgs[2 - a : 4 - a, :, lanes].reshape(2 * NW, LANES), wd[0, 3 * a + b].reshape(LANES, LANES))
            half = half + dot_nt(hgs[2 - a, :, lanes], wd[1, 3 * a + b].reshape(LANES, LANES))
    rd[...] = full + 0.25 * jnp.concatenate([half, half], axis=0)
    for r in range(2):
        for f in range(NF):
            here = r * NW + f * 16
            after = r * NW + ((f + 1) % NF) * 16
            diff = (keep[f].astype(F32) * rd[here : here + 16, :]
                    - keep[(f + 1) % NF].astype(F32) * rd[after : after + 16, :])
            chb[r, f * 16 : f * 16 + 16, :] = diff.astype(BF16)
    rgb = chb[...].reshape(2 * NW, LANES)
    sg2[...] = dot_nt(rgb, wr[...].reshape(512, LANES))

    parts = []
    for group in range(NG):
        def slope_1(start, carry):
            normed = z1[pl.ds(start, STEP), :]
            _, slope = silu_parts(gain_1 * normed + bias_1)
            value = gg[pl.ds(start, STEP), :] * (1.0 + gt[pl.ds(start, STEP), :]) + sg2[pl.ds(start, STEP), :]
            value = value * slope
            sg2[pl.ds(start, STEP), :] = value
            return carry[0] + fold(value), carry[1] + fold(value * normed)
        zero = jnp.zeros((8, 512), F32)
        sums = rows_loop(group, slope_1, (zero, zero))
        parts += [jnp.sum(item, axis=0, keepdims=True) for item in sums]
    copies = sp_send(3, parts)
    g_re[:, :, 0:n_red, :] = dot_tn(fab[...], rgb).astype(BF16).reshape(DZ, 2, n_red, LANES)
    push(red_rest, red_diff, red_last_x, red_last_y)
    total = sp_total(3, copies)
    gain_1_grad = bias_1_grad = jnp.zeros((1, 512), F32)
    for group in range(NG):
        row = 2 * group
        bias_sum, gain_sum = total[row : row + 1], total[row + 1 : row + 2]
        gain_1_grad, bias_1_grad = gain_1_grad + gain_sum, bias_1_grad + bias_sum
        scale = gain_1 * inv_1[group]

        def apply_1b(start, carry):
            value = sg2[pl.ds(start, STEP), :] - bias_sum * inv_pixels
            value = scale * (value - z1[pl.ds(start, STEP), :] * (gain_sum * inv_pixels))
            fgb[pl.ds(start, STEP), :] = value.astype(BF16)
            return carry
        rows_loop(group, apply_1b, 0)

    wait_stem()
    stem_total = stg[...]
    for k in range(S - 1):
        stem_total = stem_total + stgr[k]
    gain_3_all = jnp.concatenate(gain_3_grad, axis=1)
    bias_3_all = jnp.concatenate(bias_3_grad, axis=1)
    for d in range(D):
        mid_at, last_at = (d // per) * LANES, d * rows_last * LANES
        rows = [v[:, mid_at : mid_at + LANES] for v in (gain_1_grad, bias_1_grad, gain_2_grad, bias_2_grad)]
        for v in (gain_3_all, bias_3_all):
            rows += [v[:, last_at + n * LANES : last_at + (n + 1) * LANES] for n in range(rows_last)]
        sms[d, 0:8, :] = stem_total[d * 8 : d * 8 + 8]
        sms[d, 8:16, :] = jnp.concatenate(rows, axis=0)
    small_start, wait_small_back = bundle(smr)
    for k in range(1, D):
        small_start(sms.at[lax.rem(dp + k, D)], smr.at[k - 1], dp_peers[k - 1])

    for n in range(4):
        grad = dot_tn(x3[:, :, n * 512 : (n + 1) * 512].reshape(2 * NW, 512), fgb[...]).astype(BF16)
        per_chunk = 512 // (2 * fr)
        for qq in range(S):
            g_first[qq, n * per_chunk : (n + 1) * per_chunk] = grad[:, qq * fw : (qq + 1) * fw].reshape(
                per_chunk, 2, fr, fw)
    push(red_first_x, red_first_y, red_rest, red_diff)
    push(red_first_x, red_first_y)
    weights_first = wf[...].reshape(2048, 512)
    for n in range(4):
        lo = n * 512
        free_part()
        z3[:, lo : lo + 512] = dot_nt(fgb[...], weights_first[lo : lo + 512])

        def apply_in(i, carry):
            start = pl.multiple_of(i * STEP, STEP)
            value = z3[pl.ds(start, STEP), lo : lo + 512] + ct_rows(start, lo, 512)
            ost[n % 2, pl.ds(start // 16, STEP // 16)] = value.astype(BF16).reshape(STEP // 16, 16, 512)
            return carry
        lax.fori_loop(0, 2 * NW // STEP, apply_in, 0)
        store_part(n, ig_hbm)
        if n == 1:
            push(red_mid_y, red_mid_x)
    push(red_rest, red_diff, red_last_x, red_last_y)
    push(red_mid_y, red_mid_x)
    push(red_first_y, red_first_x)
    push(red_rest, red_diff)
    push(red_mid_y, red_mid_x)
    push(red_first_y, red_first_x)
    push(red_rest, red_diff)
    for _ in range(3):
        push(red_mid_y, red_mid_x, red_last_x, red_last_y, red_rest, red_diff)
        push(red_first_y, red_first_x)
    grad_stores = [local(fbf, fbf_hbm), local(fbm, fbm_hbm), local(fbl, fbl_hbm)]

    assert counters["r"] <= ssem.shape[0] and counters["l"] <= lsem.shape[0], counters
    wait_video()
    row8 = lax.broadcasted_iota(jnp.int32, (8, LANES), 0)

    def video_edges(f, carry):
        for ch in range(3):
            rows = slice(ch * 8, ch * 8 + 8)
            from_prev = vgr[0, f, ch * 2 + 1 : ch * 2 + 2, :]
            from_next = vgr[1, f, ch * 2 : ch * 2 + 1, :]
            vg_out[f, rows] += jnp.where(row8 == 0, from_prev, jnp.where(row8 == 7, from_next, 0.0))
        return carry

    lax.fori_loop(0, NF, video_edges, 0)
    value = sms[dp]
    wait_small_back()
    for k in range(D - 1):
        value = value + smr[k]
    osm_out[...] = value
    for finish in sends + halo_waits:
        finish()
    for copy in grad_stores:
        copy.wait()
    for part in stores[-2:]:
        for copy in part:
            copy.wait()


def final_kernel(
    sizes, so, vg, out, ig, fbf, fbm, fbl, gr, gd, ge, gsm,
    so_o, vg_o, out_o, ig_o, rgb_o, stemd_o, first_o, mid_o, last_o, red_o, dfull_o, dhalf_o, exp_o,
    g1_o, b1_o, g2_o, b2_o, g3_o, b3_o, sems, turned,
):
    D, S = sizes
    copies = [
        pltpu.make_async_copy(src, dst, sems.at[i])
        for i, (src, dst) in enumerate(((so, so_o), (out, out_o), (ig, ig_o), (vg, vg_o)))]
    for copy in copies:
        copy.start()
    fw, lw = fbf.shape[2], fbl.shape[2]
    for q in range(S):
        first_o[:, q * fw : (q + 1) * fw] = fbf[q].astype(F32)
        last_o[:, q * lw : (q + 1) * lw] = fbl[q].astype(F32)
        for t in range(9):
            mid_o[t, :, q * fw : (q + 1) * fw] = fbm[q, t].astype(F32)
    red_o[...] = gr[...]
    dfull_o[...] = gd[0]
    dhalf_o[...] = gd[1]
    exp_o[...] = ge[...]
    turned[:, 0:8] = gsm[0:8, :].T
    for t in range(9):
        rgb_o[t] = turned[t * 9 : t * 9 + 3, 0:8]
        stemd_o[t] = turned[t * 9 + 3 : t * 9 + 9, 0:8]
    width = g1_o.shape[0]
    per = LANES // width
    here = lax.rem(lax.axis_index("dp"), per)
    for j, ref in enumerate((g1_o, b1_o, g2_o, b2_o)):
        row = gsm[8 + j]
        value = row[0:width]
        for n in range(1, per):
            value = jnp.where(here == n, row[n * width : (n + 1) * width], value)
        ref[...] = value
    count = g3_o.shape[0] // LANES
    for j, ref in enumerate((g3_o, b3_o)):
        for n in range(count):
            ref[n * LANES : (n + 1) * LANES] = gsm[12 + j * count + n]
    for copy in copies:
        copy.wait()


def on_device_kernel(
    clip_video, section_input, keep_mask, w_rgb, w_stem_diff, w_first, w_middle, w_last, w_reduce,
    w_diff_full, w_diff_half, w_expand, gain_first, bias_first, gain_middle, bias_middle, gain_last,
    bias_last, stem_cot, section_cot,
):
    D, S = lax.axis_size("dp"), lax.axis_size("sp")
    DZ, SX = D // 2, S // 2
    NF = clip_video.shape[0]
    NW = NF * 16
    dp = lax.axis_index("dp")
    frames = clip_video.astype(F32)
    edges = jnp.stack([frames[:, :, 0], frames[:, :, 7]], axis=2).reshape(NF, 6, LANES)
    uin = jnp.concatenate([frames.reshape(NF, 24, LANES), edges, jnp.zeros((NF, 2, LANES), F32)], axis=1)
    per = D * LANES // 512
    width = 512 // D
    lane = jnp.arange(LANES)
    stem_w = jnp.concatenate([w_rgb, w_stem_diff], axis=1).astype(F32).transpose(2, 0, 1).reshape(8, 81)
    stem_w = jnp.pad(stem_w, ((0, 0), (0, LANES - 81)))
    mids = jnp.stack([gain_first, bias_first, gain_middle, bias_middle]).astype(F32)
    mids = jnp.where(lane // width == dp % per, jnp.tile(mids, (1, per)), 0.0)
    lasts = jnp.concatenate([gain_last, bias_last]).astype(F32).reshape(-1, LANES)
    small = jnp.concatenate([stem_w, mids, lasts], axis=0)
    band = jnp.asarray(band_table(8), BF16)
    fr, fw = w_first.shape[0], 512 // S
    mr, lr, rr = w_middle.shape[1], w_last.shape[0], w_reduce.shape[0]
    dr, er = w_diff_full.shape[1], w_expand.shape[0]
    lw = 2048 // S
    shape = jax.ShapeDtypeStruct
    vm = pltpu.VMEM
    any_spec = pl.BlockSpec(memory_space=pl.ANY)
    vmem_spec = pl.BlockSpec(memory_space=pltpu.VMEM)
    n_rem, n_loc = 128, 50
    re_rows = rr + 4 * er
    scratch = [
        pltpu.SemaphoreType.DMA((n_rem,)), pltpu.SemaphoreType.DMA((n_rem,)), pltpu.SemaphoreType.DMA((n_loc,)),
        vm((D, fr, 512), BF16), vm((9, D, mr, 512), BF16), vm((D, lr, 2048), BF16),
        vm((D, rr, LANES), BF16), vm((2, 9, D, dr, LANES), BF16), vm((D, er, 512), BF16),
        vm((2 * NF, 16, 2048), BF16), vm((2 * NF, 16, 2048), BF16),
        vm((2 * PART, 512, LANES), BF16), vm((2 * PART, 512, LANES), BF16),
        vm((NF, 32, LANES), F32), vm((NF, 8, LANES), F32), vm((NF, 8, LANES), F32),
        vm((D, 16, LANES), F32), vm((512, 288), BF16), vm((3, 512, LANES), F32), vm((288, 512), BF16),
        vm((NF, 96, LANES), F32),
        vm((NF, 8, LANES), F32), vm((2, NF, 8, LANES), F32), vm((D * 8, LANES), F32), vm((S - 1, D * 8, LANES), F32),
        vm((4, 8, 512), F32), vm((4, S - 1, 8, 512), F32), vm((4, 8, 512), F32), vm((4, S - 1, 8, 512), F32),
        vm((2 * NW, 512), F32), vm((2 * NW, 512), BF16), vm((2 * NW, 512), F32),
        vm((2 * NW, LANES), F32), vm((2, NW, LANES), BF16), vm((2, 2, NW, LANES), BF16),
        vm((4, NW, 384), BF16), vm((3, NW, 384), BF16), vm((2 * NW, LANES), BF16),
        vm((2 * NW, 512), BF16), vm((2, NW, 512), BF16), vm((4, NW, 1536), BF16),
        vm((2 * NW, 512), F32), vm((2 * NW, 512), BF16), vm((2 * NW, 2048), F32), vm((2 * NW, 2048), BF16),
        vm((2, 2, NW, LANES), BF16), vm((2, 2, NW, LANES), BF16),
        vm((4, NW, 384), BF16), vm((3, NW, 384), BF16), vm((2 * NW, 512), BF16), vm((2, 2 * NF, 16, 512), BF16),
        vm((S, DZ, 2, fr, fw), BF16), vm((S, 9, DZ, 2, mr, fw), BF16), vm((S, DZ, 2, lr, lw), BF16),
        vm((2, 9, DZ, 2, dr, LANES), BF16), vm((DZ, 2, re_rows, LANES), BF16),
        vm((9, DZ, 2, dr, LANES), BF16), vm((9, DZ, dr, LANES), BF16), vm((DZ - 1, 9, dr, LANES), BF16),
        vm((9, dr, LANES), F32), vm((SX - 1, 9, dr, LANES), F32), vm((2, 9, dr, LANES), F32),
        vm((DZ, 2, re_rows, LANES), BF16), vm((DZ, re_rows, LANES), BF16), vm((DZ - 1, re_rows, LANES), BF16),
        vm((re_rows, LANES), F32), vm((SX - 1, re_rows, LANES), F32),
        vm((S, fr, fw), BF16), vm((S, 9, mr, fw), BF16), vm((S, lr, lw), BF16),
        vm((D, 16, LANES), F32), vm((D - 1, 16, LANES), F32),
    ]

    def landing(rows, shape_of):
        for order, n in (("xyz", rows[0]), ("yzx", rows[1])):
            extra = (SX,) if order == "yzx" else ()
            scratch.append(vm((SX,) + shape_of(n, (DZ, 2)), BF16))
            scratch.append(vm((SX - 1,) + shape_of(n, (DZ, 2) if order == "xyz" else ()), BF16))
            scratch.append(vm(extra + shape_of(n, (DZ,)), BF16))
            scratch.append(vm((DZ - 1,) + extra + shape_of(n, ()), BF16))

    landing((fr * 5 // 8, fr - fr * 5 // 8), lambda n, lead: lead + (n, fw))
    landing((6, 3), lambda n, lead: (n,) + lead + (mr, fw))
    landing((lr // 2, lr - lr // 2), lambda n, lead: lead + (n, lw))
    outs = pl.pallas_call(
        functools.partial(whole_kernel, (D, S, NF)),
        out_shape=(
            shape((NF, 512, LANES), BF16), shape((NF, 24, LANES), F32),
            shape(section_input.shape, BF16), shape(section_input.shape, BF16),
            shape((S, fr, fw), BF16), shape((S, 9, mr, fw), BF16), shape((S, lr, lw), BF16), shape((rr, LANES), F32),
            shape((2, 9, dr, LANES), F32), shape((er, 512), F32), shape((16, LANES), F32),
        ),
        in_specs=[pl.BlockSpec(memory_space=pltpu.SMEM)] + [vmem_spec] * 3 + [any_spec] * 10,
        out_specs=(any_spec, vmem_spec) + (any_spec,) * 5 + (vmem_spec,) * 4,
        scratch_shapes=scratch,
        compiler_params=pltpu.CompilerParams(
            collective_id=0, has_side_effects=True, vmem_limit_bytes=VMEM_BYTES),
        name="tdn_blocks",
    )(
        keep_mask, uin, small, band, section_input, section_cot, stem_cot.reshape(NF, 512, LANES),
        w_first, w_middle, w_last, w_reduce, w_diff_full, w_diff_half, w_expand,
    )
    results = (
        shape(stem_cot.shape, BF16), shape(clip_video.shape, F32), shape(section_input.shape, BF16),
        shape(section_input.shape, BF16), shape(w_rgb.shape, F32), shape(w_stem_diff.shape, F32),
        shape(w_first.shape, F32), shape(w_middle.shape, F32), shape(w_last.shape, F32), shape(w_reduce.shape, F32),
        shape(w_diff_full.shape, F32), shape(w_diff_half.shape, F32), shape(w_expand.shape, F32),
    ) + (shape((width,), F32),) * 4 + (shape((2048 // D,), F32),) * 2
    so, vg, section_output, input_grad, *grads = outs
    return pl.pallas_call(
        functools.partial(final_kernel, (D, S)),
        out_shape=results,
        in_specs=[any_spec] * 4 + [vmem_spec] * 7,
        out_specs=(any_spec,) * 4 + (vmem_spec,) * 15,
        scratch_shapes=[pltpu.SemaphoreType.DMA((4,)), vm((LANES, LANES), F32)],
        compiler_params=pltpu.CompilerParams(vmem_limit_bytes=24 * 2**20),
        name="final_outputs",
    )(so.reshape(stem_cot.shape), vg.reshape(clip_video.shape), section_output, input_grad, *grads)


def fits_kernel(mesh):
    dp_count, sp_count = mesh.shape["dp"], mesh.shape["sp"]
    return (
        dp_count % 2 == 0 and sp_count % 2 == 0 and H5 == 2 * sp_count and HS == 8 * sp_count
        and TDM_C % (16 * dp_count) == 0 and STEM_C == 8 * dp_count and MID // sp_count % LANES == 0
        and C5 // dp_count % LANES == 0 and (dp_count - 1) * (sp_count // 2 - 1) <= dp_count
    )


def solution(mesh):
    placed = (
        P("dp", None, "sp", None),
        P("dp", "sp", None, None),
        P("dp"),
        P(None, None, "dp"),
        P(None, None, "dp"),
        P("dp", None),
        P(None, "dp", None),
        P("dp", None),
        P("dp", None),
        P(None, "dp", None),
        P(None, "dp", None),
        P("dp", None),
        P("dp"),
        P("dp"),
        P("dp"),
        P("dp"),
        P("dp"),
        P("dp"),
        P("dp", None, "sp", None),
        P("dp", "sp", None, None),
    )
    return jax.shard_map(
        on_device_kernel if fits_kernel(mesh) else on_device,
        mesh=mesh,
        in_specs=placed,
        out_specs=(
            P("dp", None, "sp", None),
            P("dp", None, "sp", None),
            P("dp", "sp", None, None),
            P("dp", "sp", None, None),
            P(None, None, "dp"),
            P(None, None, "dp"),
            P("dp", None),
            P(None, "dp", None),
            P("dp", None),
            P("dp", None),
            P(None, "dp", None),
            P(None, "dp", None),
            P("dp", None),
            P("dp"),
            P("dp"),
            P("dp"),
            P("dp"),
            P("dp"),
            P("dp"),
        ),
        check_vma=False,
    )
```

```python
import functools

import jax
import jax.numpy as jnp
import numpy as np
from jax import lax
from jax.experimental import pallas as pl
from jax.experimental.pallas import tpu as pltpu
from jax.sharding import PartitionSpec as P

H5, HS, MID, TDM_C, C5, STEM_C = 8, 32, 512, 128, 2048, 64
VMEM_BYTES = 63 * 2**20

MICRO = 2


EPS = 1e-05


def with_halo(block, sides, width):
    for axis, dim in sides:
        count = lax.axis_size(axis)
        forward = [(i, i + 1) for i in range(count - 1)]
        backward = [(target, source) for source, target in forward]
        low = lax.ppermute(
            lax.slice_in_dim(block, block.shape[dim] - width, None, axis=dim), axis, forward
        )
        high = lax.ppermute(lax.slice_in_dim(block, 0, width, axis=dim), axis, backward)
        block = jnp.concatenate([low, block, high], axis=dim)
    return block


def silu_slope(values):
    sig_value = jax.nn.sigmoid(values)
    return sig_value * (1.0 + values * (1.0 - sig_value))


def tap_window(padded, row_off, col_off, row_count, col_count, row_axis):
    part_rows = lax.slice_in_dim(padded, row_off, row_off + row_count, axis=row_axis)
    return lax.slice_in_dim(part_rows, col_off, col_off + col_count, axis=row_axis + 1)


def pad_columns(haloed, row_axis):
    widths = [(0, 0)] * haloed.ndim
    widths[row_axis + 1] = (1, 1)
    return jnp.pad(haloed, widths)


def tap_conv(haloed, kernel, channels_last):
    row_axis = 1 if channels_last else 2
    row_count = haloed.shape[row_axis] - 2
    col_count = haloed.shape[row_axis + 1]
    padded = pad_columns(haloed, row_axis)
    einsum_form = "fhwc,cd->fhwd" if channels_last else "fchw,cd->fdhw"
    result = None
    for tap_index in range(9):
        window = tap_window(padded, tap_index // 3, tap_index % 3, row_count, col_count, row_axis)
        tap_term = jnp.einsum(
            einsum_form, window, kernel[tap_index], preferred_element_type=jnp.float32
        )
        result = tap_term if result is None else result + tap_term
    return result


def tap_conv_back(grad_halo, kernel, channels_last):
    row_axis = 1 if channels_last else 2
    row_count = grad_halo.shape[row_axis] - 2
    col_count = grad_halo.shape[row_axis + 1]
    padded = pad_columns(grad_halo, row_axis)
    einsum_form = "fhwd,cd->fhwc" if channels_last else "fdhw,cd->fchw"
    result = None
    for tap_index in range(9):
        window = tap_window(
            padded, 2 - tap_index // 3, 2 - tap_index % 3, row_count, col_count, row_axis
        )
        tap_term = jnp.einsum(
            einsum_form, window, kernel[tap_index], preferred_element_type=jnp.float32
        )
        result = tap_term if result is None else result + tap_term
    return result


def tap_kernel_grad(haloed, out_grad, channels_last):
    row_axis = 1 if channels_last else 2
    row_count = out_grad.shape[row_axis]
    col_count = out_grad.shape[row_axis + 1]
    padded = pad_columns(haloed, row_axis)
    einsum_form = "fhwc,fhwd->cd" if channels_last else "fchw,fdhw->cd"
    tap_list = []
    for tap_index in range(9):
        window = tap_window(padded, tap_index // 3, tap_index % 3, row_count, col_count, row_axis)
        tap_list.append(
            jnp.einsum(einsum_form, window, out_grad, preferred_element_type=jnp.float32)
        )
    return jnp.stack(tap_list, axis=0)


def pair_mean(values):
    return values.reshape(
        values.shape[0], values.shape[1] // 2, 2, values.shape[2] // 2, 2, values.shape[3]
    ).mean(axis=(2, 4))


def pair_total(values):
    return values.reshape(
        values.shape[0], values.shape[1] // 2, 2, values.shape[2] // 2, 2, values.shape[3]
    ).sum(axis=(2, 4))


def pair_grow(values):
    return jnp.repeat(jnp.repeat(values, 2, axis=1), 2, axis=2)


def norm_forward(pre_norm, gain, bias, pixel_count):
    local_sums = (jnp.sum(pre_norm, axis=(0, 1, 2)), jnp.sum(pre_norm * pre_norm, axis=(0, 1, 2)))
    total_sum, total_square = lax.psum((local_sums[0], local_sums[1]), "sp")
    mean_value = total_sum / pixel_count
    variance = total_square / pixel_count - mean_value * mean_value
    inverse = lax.rsqrt(variance + EPS)
    normed = (pre_norm - mean_value) * inverse
    return (normed, inverse, gain * normed + bias)


def norm_backward(out_grad, normed, inverse, gain, pixel_count):
    local_bias = jnp.sum(out_grad, axis=(0, 1, 2))
    local_gain = jnp.sum(out_grad * normed, axis=(0, 1, 2))
    total_bias, total_gain = lax.psum((local_bias, local_gain), "sp")
    pre_grad = (
        gain * inverse * (out_grad - total_bias / pixel_count - normed * total_gain / pixel_count)
    )
    return (pre_grad, local_gain, local_bias)


def reduce_grads(grads):
    summed = (
        lax.psum_scatter(grads[0], "dp", scatter_dimension=2, tiled=True),
        lax.psum_scatter(grads[1], "dp", scatter_dimension=2, tiled=True),
        lax.psum_scatter(grads[2], "dp", scatter_dimension=0, tiled=True),
        lax.psum_scatter(grads[3], "dp", scatter_dimension=1, tiled=True),
        lax.psum_scatter(grads[4], "dp", scatter_dimension=0, tiled=True),
        lax.psum_scatter(grads[5], "dp", scatter_dimension=0, tiled=True),
        lax.psum_scatter(grads[6], "dp", scatter_dimension=1, tiled=True),
        lax.psum_scatter(grads[7], "dp", scatter_dimension=1, tiled=True),
        lax.psum_scatter(grads[8], "dp", scatter_dimension=0, tiled=True),
        lax.psum_scatter(grads[9], "dp", scatter_dimension=0, tiled=True),
        lax.psum_scatter(grads[10], "dp", scatter_dimension=0, tiled=True),
        lax.psum_scatter(grads[11], "dp", scatter_dimension=0, tiled=True),
        lax.psum_scatter(grads[12], "dp", scatter_dimension=0, tiled=True),
        lax.psum_scatter(grads[13], "dp", scatter_dimension=0, tiled=True),
        lax.psum_scatter(grads[14], "dp", scatter_dimension=0, tiled=True),
    )
    return (
        lax.psum(summed[0].astype(jnp.bfloat16), "sp").astype(jnp.float32),
        lax.psum(summed[1].astype(jnp.bfloat16), "sp").astype(jnp.float32),
        lax.psum(summed[2].astype(jnp.bfloat16), "sp").astype(jnp.float32),
        lax.psum(summed[3].astype(jnp.bfloat16), "sp").astype(jnp.float32),
        lax.psum(summed[4].astype(jnp.bfloat16), "sp").astype(jnp.float32),
        lax.psum(summed[5].astype(jnp.bfloat16), "sp").astype(jnp.float32),
        lax.psum(summed[6].astype(jnp.bfloat16), "sp").astype(jnp.float32),
        lax.psum(summed[7].astype(jnp.bfloat16), "sp").astype(jnp.float32),
        lax.psum(summed[8].astype(jnp.bfloat16), "sp").astype(jnp.float32),
        lax.psum(summed[9].astype(jnp.bfloat16), "sp").astype(jnp.float32),
        lax.psum(summed[10].astype(jnp.bfloat16), "sp").astype(jnp.float32),
        lax.psum(summed[11].astype(jnp.bfloat16), "sp").astype(jnp.float32),
        lax.psum(summed[12].astype(jnp.bfloat16), "sp").astype(jnp.float32),
        lax.psum(summed[13].astype(jnp.bfloat16), "sp").astype(jnp.float32),
        lax.psum(summed[14].astype(jnp.bfloat16), "sp").astype(jnp.float32),
    )


def run_micro(
    video_part, feat_part, keep_part, stem_grad_in, section_grad_in, weights, pixel_count
):
    (
        rgb_k,
        stemd_k,
        first_k,
        middle_k,
        last_k,
        reduce_k,
        dfull_k,
        dhalf_k,
        expand_k,
        gain_one,
        bias_one,
        gain_two,
        bias_two,
        gain_three,
        bias_three,
    ) = weights
    keep_float = keep_part.astype(jnp.float32)
    keep_col = keep_float[:, None, None, None]
    next_col = jnp.roll(keep_float, -1)[:, None, None, None]
    frames_halo = with_halo(video_part, (("sp", 2),), 1)
    frames_wide = frames_halo.astype(jnp.float32)
    before = keep_col * (frames_wide - jnp.roll(frames_wide, 1, axis=0))
    after = next_col * (jnp.roll(frames_wide, -1, axis=0) - frames_wide)
    diff_stack = jnp.concatenate([before, after], axis=1).astype(jnp.bfloat16)
    stem_out = (tap_conv(frames_halo, rgb_k, False) + tap_conv(diff_stack, stemd_k, False)).astype(
        jnp.bfloat16
    )
    cot_halo = with_halo(stem_grad_in, (("sp", 2),), 1)
    direct_grad = tap_conv_back(cot_halo, rgb_k, False)
    diff_grad = tap_conv_back(cot_halo, stemd_k, False)
    before_grad = keep_col * diff_grad[:, :3]
    after_grad = next_col * diff_grad[:, 3:]
    video_grad = (
        direct_grad
        + before_grad
        - jnp.roll(before_grad, -1, axis=0)
        + jnp.roll(after_grad, 1, axis=0)
        - after_grad
    )
    rgb_grad = tap_kernel_grad(frames_halo, stem_grad_in, False)
    stemd_grad = tap_kernel_grad(diff_stack, stem_grad_in, False)
    row_count = feat_part.shape[1]
    col_count = feat_part.shape[2]
    first_pre = jnp.einsum("fhwc,cd->fhwd", feat_part, first_k, preferred_element_type=jnp.float32)
    normed_one, inverse_one, norm_one = norm_forward(
        first_pre, gain_one.astype(jnp.float32), bias_one.astype(jnp.float32), pixel_count
    )
    first_act = jax.nn.silu(norm_one)
    first_low = first_act.astype(jnp.bfloat16)
    reduced = jnp.einsum("fhwc,cd->fhwd", first_low, reduce_k, preferred_element_type=jnp.float32)
    change_low = (keep_col * (reduced - jnp.roll(reduced, 1, axis=0))).astype(jnp.bfloat16)
    change_halo = with_halo(change_low, (("sp", 1),), 2)
    near_rows = change_halo[:, 1 : row_count + 3]
    full_out = tap_conv(near_rows, dfull_k, True)
    pooled = pair_mean(change_halo.astype(jnp.float32)).astype(jnp.bfloat16)
    half_out = tap_conv(pooled, dhalf_k, True)
    combined_low = (full_out + pair_grow(half_out)).astype(jnp.bfloat16)
    gate_value = jax.nn.sigmoid(
        jnp.einsum("fhwc,cd->fhwd", combined_low, expand_k, preferred_element_type=jnp.float32)
    )
    gated_low = (first_act * (1.0 + gate_value)).astype(jnp.bfloat16)
    gated_halo = with_halo(gated_low, (("sp", 1),), 1)
    middle_pre = tap_conv(gated_halo, middle_k, True)
    normed_two, inverse_two, norm_two = norm_forward(
        middle_pre, gain_two.astype(jnp.float32), bias_two.astype(jnp.float32), pixel_count
    )
    second_low = jax.nn.silu(norm_two).astype(jnp.bfloat16)
    last_pre = jnp.einsum("fhwc,cd->fhwd", second_low, last_k, preferred_element_type=jnp.float32)
    normed_three, inverse_three, norm_three = norm_forward(
        last_pre, gain_three.astype(jnp.float32), bias_three.astype(jnp.float32), pixel_count
    )
    section_out = (feat_part.astype(jnp.float32) + norm_three).astype(jnp.bfloat16)
    out_grad = section_grad_in.astype(jnp.float32)
    last_grad, gain_three_grad, bias_three_grad = norm_backward(
        out_grad, normed_three, inverse_three, gain_three.astype(jnp.float32), pixel_count
    )
    last_grad_low = last_grad.astype(jnp.bfloat16)
    last_k_grad = jnp.einsum(
        "fhwc,fhwd->cd", second_low, last_grad_low, preferred_element_type=jnp.float32
    )
    second_grad = jnp.einsum(
        "fhwd,cd->fhwc", last_grad_low, last_k, preferred_element_type=jnp.float32
    ) * silu_slope(norm_two)
    middle_grad, gain_two_grad, bias_two_grad = norm_backward(
        second_grad, normed_two, inverse_two, gain_two.astype(jnp.float32), pixel_count
    )
    middle_low = middle_grad.astype(jnp.bfloat16)
    middle_halo = with_halo(middle_low, (("sp", 1),), 1)
    gated_grad = tap_conv_back(middle_halo, middle_k, True)
    middle_k_grad = tap_kernel_grad(gated_halo, middle_low, True)
    gate_grad = (gated_grad * first_act * gate_value * (1.0 - gate_value)).astype(jnp.bfloat16)
    expand_grad = jnp.einsum(
        "fhwc,fhwd->cd", combined_low, gate_grad, preferred_element_type=jnp.float32
    )
    combined_grad = jnp.einsum(
        "fhwd,cd->fhwc", gate_grad, expand_k, preferred_element_type=jnp.float32
    ).astype(jnp.bfloat16)
    half_grad = pair_total(combined_grad.astype(jnp.float32)).astype(jnp.bfloat16)
    stacked = jnp.concatenate([combined_grad, jnp.repeat(half_grad, 2, axis=1)], axis=2)
    stacked_halo = with_halo(stacked, (("sp", 1),), 2)
    full_grad_halo = stacked_halo[:, 1 : row_count + 3, :col_count]
    half_grad_halo = stacked_halo[:, 0::2, col_count:]
    change_grad = tap_conv_back(full_grad_halo, dfull_k, True) + 0.25 * pair_grow(
        tap_conv_back(half_grad_halo, dhalf_k, True)
    )
    dfull_grad = tap_kernel_grad(near_rows, combined_grad, True)
    dhalf_grad = tap_kernel_grad(pooled, half_grad, True)
    weighted = keep_col * change_grad
    reduced_grad = (weighted - jnp.roll(weighted, -1, axis=0)).astype(jnp.bfloat16)
    reduce_grad = jnp.einsum(
        "fhwc,fhwd->cd", first_low, reduced_grad, preferred_element_type=jnp.float32
    )
    first_sum = gated_grad * (1.0 + gate_value) + jnp.einsum(
        "fhwd,cd->fhwc", reduced_grad, reduce_k, preferred_element_type=jnp.float32
    )
    first_grad, gain_one_grad, bias_one_grad = norm_backward(
        first_sum * silu_slope(norm_one),
        normed_one,
        inverse_one,
        gain_one.astype(jnp.float32),
        pixel_count,
    )
    first_grad_low = first_grad.astype(jnp.bfloat16)
    first_k_grad = jnp.einsum(
        "fhwc,fhwd->cd", feat_part, first_grad_low, preferred_element_type=jnp.float32
    )
    input_grad = (
        out_grad
        + jnp.einsum("fhwd,cd->fhwc", first_grad_low, first_k, preferred_element_type=jnp.float32)
    ).astype(jnp.bfloat16)
    grads = (
        rgb_grad,
        stemd_grad,
        first_k_grad,
        middle_k_grad,
        last_k_grad,
        reduce_grad,
        dfull_grad,
        dhalf_grad,
        expand_grad,
        gain_one_grad,
        bias_one_grad,
        gain_two_grad,
        bias_two_grad,
        gain_three_grad,
        bias_three_grad,
    )
    return ((stem_out, video_grad, section_out, input_grad), grads)


def add_trees(first_tree, second_tree):
    if first_tree is None:
        return second_tree
    return jax.tree.map(
        lambda left_part, right_part: left_part + right_part, first_tree, second_tree
    )


def on_device(
    clip_video,
    section_input,
    keep_mask,
    w_rgb,
    w_stem_diff,
    w_first,
    w_middle,
    w_last,
    w_reduce,
    w_diff_full,
    w_diff_half,
    w_expand,
    gain_first,
    bias_first,
    gain_middle,
    bias_middle,
    gain_last,
    bias_last,
    stem_cot,
    section_cot,
):
    micro_frames = clip_video.shape[0] // MICRO
    pixel_count = (
        micro_frames * section_input.shape[1] * lax.axis_size("sp") * section_input.shape[2]
    )
    results = []
    grad_totals = None
    for micro_index in range(MICRO):
        weights = (
            lax.all_gather(w_rgb, "dp", axis=2, tiled=True),
            lax.all_gather(w_stem_diff, "dp", axis=2, tiled=True),
            lax.all_gather(w_first, "dp", axis=0, tiled=True),
            lax.all_gather(w_middle, "dp", axis=1, tiled=True),
            lax.all_gather(w_last, "dp", axis=0, tiled=True),
            lax.all_gather(w_reduce, "dp", axis=0, tiled=True),
            lax.all_gather(w_diff_full, "dp", axis=1, tiled=True),
            lax.all_gather(w_diff_half, "dp", axis=1, tiled=True),
            lax.all_gather(w_expand, "dp", axis=0, tiled=True),
            lax.all_gather(gain_first, "dp", axis=0, tiled=True),
            lax.all_gather(bias_first, "dp", axis=0, tiled=True),
            lax.all_gather(gain_middle, "dp", axis=0, tiled=True),
            lax.all_gather(bias_middle, "dp", axis=0, tiled=True),
            lax.all_gather(gain_last, "dp", axis=0, tiled=True),
            lax.all_gather(bias_last, "dp", axis=0, tiled=True),
        )
        low_end = micro_index * micro_frames
        high_end = low_end + micro_frames
        outputs, grads = run_micro(
            clip_video[low_end:high_end],
            section_input[low_end:high_end],
            keep_mask[low_end:high_end],
            stem_cot[low_end:high_end],
            section_cot[low_end:high_end],
            weights,
            pixel_count,
        )
        results.append(outputs)
        grad_totals = add_trees(grad_totals, reduce_grads(grads))
    stem_features = jnp.concatenate([item[0] for item in results], axis=0)
    video_grad = jnp.concatenate([item[1] for item in results], axis=0)
    section_output = jnp.concatenate([item[2] for item in results], axis=0)
    section_input_grad = jnp.concatenate([item[3] for item in results], axis=0)
    return (
        stem_features,
        video_grad,
        section_output,
        section_input_grad,
        grad_totals[0],
        grad_totals[1],
        grad_totals[2],
        grad_totals[3],
        grad_totals[4],
        grad_totals[5],
        grad_totals[6],
        grad_totals[7],
        grad_totals[8],
        grad_totals[9],
        grad_totals[10],
        grad_totals[11],
        grad_totals[12],
        grad_totals[13],
        grad_totals[14],
    )


F32 = jnp.float32
BF16 = jnp.bfloat16
MESH_ID = pl.DeviceIdType.MESH
GROUP = 8
LANES = 128
STEP = 32
PART = 2


def dot_nn(left, right):
    return lax.dot_general(left, right, (((1,), (0,)), ((), ())), preferred_element_type=F32)


def dot_nt(left, right):
    return lax.dot_general(left, right, (((1,), (1,)), ((), ())), preferred_element_type=F32)


def dot_tn(left, right):
    return lax.dot_general(left, right, (((0,), (0,)), ((), ())), preferred_element_type=F32)


def shift_down(values, count):
    size = values.shape[0]
    column = lax.broadcasted_iota(jnp.int32, values.shape, 0) & 15
    return jnp.where(column < count, 0.0, pltpu.roll(values, count, 0))


def shift_up(values, count):
    size = values.shape[0]
    column = lax.broadcasted_iota(jnp.int32, values.shape, 0) & 15
    return jnp.where(column >= 16 - count, 0.0, pltpu.roll(values, size - count, 0))


def pair_sum(values):
    size = values.shape[0]
    parity = lax.broadcasted_iota(jnp.int32, values.shape, 0) & 1
    return values + jnp.where(parity == 0, pltpu.roll(values, size - 1, 0), pltpu.roll(values, 1, 0))


def band_table(rows):
    table = np.zeros((rows, 96, 3 * LANES), np.float32)
    for i in range(rows):
        for a in range(3):
            for b in range(3):
                for ch in range(9):
                    base = (b * 3 + ch // 3) * 32
                    row = i + a - 1
                    if row < 0:
                        n = base + 24 + (ch % 3) * 2
                    elif row >= rows:
                        n = base + 24 + (ch % 3) * 2 + 1
                    else:
                        n = base + (ch % 3) * 8 + row
                    table[i, ch * 9 + 3 * a + b, n] = 1.0
    return table


def portions(first_rows, taps, last_rows):
    cut = first_rows * 5 // 16
    return (
        (("xyz", 0, cut), ("xyz", cut, cut), ("yzx", 2 * cut, first_rows - 2 * cut)),
        (("xyz", 0, 3), ("xyz", 3, 3), ("yzx", 6, taps - 6)),
        (("xyz", 0, last_rows // 2), ("yzx", last_rows // 2, last_rows // 2)),
    )


def silu_parts(values):
    sig = jax.nn.sigmoid(values)
    return values * sig, sig * (1.0 + values * (1.0 - sig))


def whole_kernel(
    sizes, keep, clip, rgb, stemd, g1, b1, g2, b2, g3, b3, band, x_hbm, ct_hbm, sc_hbm, wf_in, wm_in, wl_in, wr_in, wd0_in, wd1_in, we_in,
    so_hbm, vg_out, out_hbm, ig_hbm, fbf_hbm, fbm_hbm, fbl_hbm, or_out, od_out, oe_out, osm_out,
    ssem, rsem, lsem, wf, wm, wl, wr, wd, we, x3, ct3, sc, so, ust, uprev, unext, small, sm, tf, tff, tb, dg,
    vgh, vgr, stg, stgr, stat_s, stat_r, st3_s, st3_r, z1, fab, gt, rd, chb, chr_, cs, ps, comb,
    gb, gr, gs, z2, sab, z3, lgb, cgx, cgr, cgs, hgs, fgb, ost,
    g_first, g_mid, g_last, g_diff, g_re, rcd, ryd, rzd, fdx, rxd, fdo, rcr, ryr, rzr, frx, rxr, fbf, fbm, fbl, sms, smr, *bufs,
):
    D, S, NF = sizes
    DZ, SX = D // 2, S // 2
    NG = NF // GROUP
    NW = NF * 16
    GW = GROUP * 16
    dp, sp = lax.axis_index("dp"), lax.axis_index("sp")
    z, y = dp // 2, dp % 2
    x, c = sp // 2, sp % 2
    oy, oc = 1 - y, 1 - c
    q_own = c * SX + x

    def at_zy(zz, yy):
        return (zz * 2 + yy, sp)

    y_peer = at_zy(z, oy)
    c_peer = (dp, x * 2 + oc)

    z_bits = [1 << n for n in range(DZ.bit_length() - 1)]

    def z_pair(bit):
        return z + bit - 2 * bit * ((z // bit) % 2)

    def z_class(zz, bit):
        return [zz % (2 * bit) + 2 * bit * j for j in range(DZ // (2 * bit))]

    def x_to(k):
        return lax.rem(x + k, SX)

    def x_from(k):
        return lax.rem(x + SX - k, SX)

    def x_peer(k):
        return (dp, x_to(k) * 2 + c)

    sp_peers = [(dp, lax.rem(sp + k, S)) for k in range(1, S)]
    dp_peers = [(lax.rem(dp + k, D), sp) for k in range(1, D)]
    has_prev, has_next = sp > 0, sp < S - 1
    prev_dev, next_dev = (dp, sp - 1), (dp, sp + 1)

    counters = {"r": 0, "l": 0}
    sends = []

    def bundle(whole):
        i = counters["r"]
        counters["r"] += 1

        def start(src, dst, dev):
            pltpu.make_async_remote_copy(
                src_ref=src, dst_ref=dst, send_sem=ssem.at[i], recv_sem=rsem.at[i],
                device_id=dev, device_id_type=MESH_ID,
            ).start()

        def wait():
            pltpu.make_async_copy(whole, whole, rsem.at[i]).wait()

        def finish():
            pltpu.make_async_copy(whole, whole, ssem.at[i]).wait()

        sends.append(finish)
        return start, wait

    def remote(src, dst, dev):
        start, wait = bundle(dst)
        start(src, dst, dev)
        return wait

    def to_peers(src, dst_of, peers, whole):
        start, wait = bundle(whole)
        for k, peer in enumerate(peers):
            start(src, dst_of(k), peer)
        return wait

    def local(src, dst):
        i = counters["l"]
        counters["l"] += 1
        copy = pltpu.make_async_copy(src, dst, lsem.at[i])
        copy.start()
        return copy

    @pl.when(sp == 0)
    def _():
        uprev[...] = jnp.zeros_like(uprev)
        vgr[0] = jnp.zeros(vgr.shape[1:], F32)
        chr_[0] = jnp.zeros(chr_.shape[1:], BF16)
        gr[0] = jnp.zeros(gr.shape[1:], BF16)
        cgr[0] = jnp.zeros(cgr.shape[1:], BF16)

    @pl.when(sp == S - 1)
    def _():
        unext[...] = jnp.zeros_like(unext)
        vgr[1] = jnp.zeros(vgr.shape[1:], F32)
        chr_[1] = jnp.zeros(chr_.shape[1:], BF16)
        gr[1] = jnp.zeros(gr.shape[1:], BF16)
        cgr[1] = jnp.zeros(cgr.shape[1:], BF16)

    barrier = pltpu.get_barrier_semaphore()
    for peer in sp_peers + dp_peers:
        pl.semaphore_signal(barrier, inc=1, device_id=peer, device_id_type=MESH_ID)
    per = D * LANES // 512
    rows_last = 2048 // D // LANES
    small[...] = jnp.zeros_like(small)
    for ch in range(9):
        small[0:8, ch * 9 : ch * 9 + 9] = (rgb[ch] if ch < 3 else stemd[ch - 3]).astype(F32)
    place = lax.broadcasted_iota(jnp.int32, (1, LANES), 1) // (LANES // per)
    for j, ref in enumerate((g1, b1, g2, b2)):
        row = jnp.concatenate([ref[...].astype(F32)] * per, axis=1)
        small[8 + j : 9 + j, :] = jnp.where(place == lax.rem(dp, per), row, 0.0)
    for j, ref in enumerate((g3, b3)):
        small[12 + j * rows_last : 12 + (j + 1) * rows_last, :] = ref[...].astype(F32)
    own_small = local(small, sm.at[dp])
    own = [
        local(wf_in, wf.at[dp]), local(wd0_in, wd.at[0, :, dp]), local(wd1_in, wd.at[1, :, dp]),
        local(wr_in, wr.at[dp]), local(we_in, we.at[dp]), local(wm_in, wm.at[:, dp]), local(wl_in, wl.at[dp]),
    ]

    def load_cot(part):
        lo = part * PART
        return local(sc_hbm.at[pl.ds(lo, PART)], sc.at[pl.ds(lo % (2 * PART), PART)])

    load_sc = [load_cot(0), load_cot(1)]
    load_x = [local(x_hbm.at[:, r], x3.at[pl.ds(r * NF, NF)]) for r in range(2)]
    load_ct = [local(ct_hbm.at[:, r], ct3.at[pl.ds(r * NF, NF)]) for r in range(2)]
    pl.semaphore_wait(barrier, S - 1 + D - 1)

    halo_waits = []

    def halo(to_prev, to_next, from_prev, from_next, land_prev, land_next):
        i = counters["r"]
        counters["r"] += 2

        def up():
            return pltpu.make_async_remote_copy(
                src_ref=to_prev, dst_ref=land_next, send_sem=ssem.at[i], recv_sem=rsem.at[i],
                device_id=prev_dev, device_id_type=MESH_ID)

        def down():
            return pltpu.make_async_remote_copy(
                src_ref=to_next, dst_ref=land_prev, send_sem=ssem.at[i + 1], recv_sem=rsem.at[i + 1],
                device_id=next_dev, device_id_type=MESH_ID)

        @pl.when(has_prev)
        def _():
            up().start()

        @pl.when(has_next)
        def _():
            down().start()

        def wait():
            @pl.when(has_prev)
            def _():
                down().wait_recv()

            @pl.when(has_next)
            def _():
                up().wait_recv()

        def finish():
            @pl.when(has_prev)
            def _():
                up().wait_send()

            @pl.when(has_next)
            def _():
                down().wait_send()

        halo_waits.append(finish)
        return wait, finish

    wait_small = to_peers(small, lambda k: sm.at[dp], dp_peers, sm.at[pl.ds(0, D - 1)])
    wait_edges, _ = halo(clip, clip, None, None, uprev, unext)

    def gather(mode, dst):
        wide = {"A": 1, "B": SX, "D": S}[mode]
        first_q = {"A": q_own, "B": c * SX, "D": 0}[mode]
        only = pl.ds(dp, 1)
        z_links = {bit: bundle(dst(pl.ds(0, DZ // (2 * bit)), first_q, wide)) for bit in z_bits}
        y_start, y_wait = bundle(dst(pl.ds(0, DZ), first_q, wide))
        if mode == "A":
            x_start, x_wait = bundle(dst(pl.ds(0, (D - 1) * (SX - 1)), first_q, 1))
        if mode != "D":
            c_start, c_wait = bundle(dst(pl.ds(0, D - 1), c * SX, SX))
        mine = dst(pl.ds(dp, 1), first_q, wide)
        for bit in reversed(z_bits):
            z_links[bit][0](mine, mine, at_zy(z_pair(bit), y))
        y_start(mine, mine, y_peer)
        yield

        def fan(part):
            if mode == "A":
                for k in range(1, SX):
                    x_start(part, part, x_peer(k))
            if mode != "D":
                c_start(part, part, c_peer)

        for bit in reversed(z_bits):
            z_links[bit][1]()
            for zz in z_class(z_pair(bit), bit):
                part = dst(pl.ds(zz * 2 + y, 1), first_q, wide)
                for lower in z_bits:
                    if lower < bit:
                        z_links[lower][0](part, part, at_zy(z_pair(lower), y))
                y_start(part, part, y_peer)
                fan(part)
            yield
        y_wait()
        for zz in range(DZ):
            fan(dst(pl.ds(zz * 2 + oy, 1), first_q, wide))
        yield
        if mode == "A":
            x_wait()
            for k in range(1, SX):
                for n in range(1, D):
                    part = dst(pl.ds(lax.rem(dp + n, D), 1), c * SX + x_from(k), 1)
                    c_start(part, part, c_peer)
            yield
        if mode != "D":
            c_wait()

    def lane_block(index, width, count):
        return pl.ds(pl.multiple_of(index * width, width), width * count)

    fr, fw = wf_in.shape[0], wf_in.shape[1] // S
    mw = wm_in.shape[2] // S
    lr, lw = wl_in.shape[0], wl_in.shape[1] // S

    def first_part(mode, lo, n):
        rows = pl.ds(lo, n)
        return gather(mode, lambda d, q, w: wf.at[d, rows, lane_block(q, fw, w)])

    def mid_part(mode, lo, n):
        rows = pl.ds(lo, n)
        return gather(mode, lambda d, q, w: wm.at[rows, d, :, lane_block(q, mw, w)])

    def last_part(mode, lo, n):
        rows = pl.ds(lo, n)
        return gather(mode, lambda d, q, w: wl.at[d, rows, lane_block(q, lw, w)])

    for copy in own:
        copy.wait()
    part_b = fr * 3 // 8
    part_a = (fr - part_b) // 2
    chunks = [
        (0, first_part("A", 0, part_a)),
        (0, first_part("B", 2 * part_a, part_b)),
        (0, first_part("A", part_a, part_a)),
        (1, gather("D", lambda d, q, w: wr.at[d])),
        (1, gather("B", lambda d, q, w: wd.at[c, :, d])),
        (1, gather("D", lambda d, q, w: we.at[d])),
        (1, mid_part("A", 0, 3)), (2, mid_part("B", 6, 3)), (2, mid_part("A", 3, 3)),
        (3, last_part("A", 0, lr // 2)), (3, last_part("B", lr // 2, lr // 4)),
        (4, last_part("A", lr * 3 // 4, lr // 4)),
    ]
    slot = [0]
    arrived = set()

    def pump(count=1):
        for _ in range(count):
            for n, (start, chunk) in enumerate(chunks):
                if start <= slot[0] and n not in arrived:
                    try:
                        next(chunk)
                    except StopIteration:
                        arrived.add(n)
            slot[0] += 1

    def need(low, high):
        while not arrived.issuperset(range(low, high)):
            pump()

    pump()

    own_small.wait()
    wait_small()
    wt = sm[:, 0:8, :].reshape(D * 8, LANES)[:, 0:96].astype(BF16)
    for i in range(8):
        rows = dot_nn(wt, band[i])
        for n in range(3):
            tff[n, pl.ds(i, D * 8, stride=8), :] = rows[:, n * LANES : (n + 1) * LANES]
    for n in range(3):
        columns = min(288 - n * LANES, LANES)
        tf[:, n * LANES : n * LANES + columns] = tff[n, :, 0:columns].astype(BF16)
        tb[n * LANES : n * LANES + columns, :] = tff[n].T[0:columns].astype(BF16)

    def mid_vec(j):
        parts = []
        for m in range(D // per):
            row = sm[m * per, 8 + j : 9 + j, :]
            for n in range(1, per):
                row = row + sm[m * per + n, 8 + j : 9 + j, :]
            parts.append(row)
        return jnp.concatenate(parts, axis=1)

    def last_vec(j):
        return jnp.concatenate(
            [sm[d, 8 + j + n : 9 + j + n, :] for d in range(D) for n in range(rows_last)], axis=1)

    gain_1, bias_1, gain_2, bias_2 = [mid_vec(j) for j in range(4)]
    gain_3, bias_3 = last_vec(4), last_vec(4 + rows_last)

    wait_edges()
    row8 = lax.broadcasted_iota(jnp.int32, (8, LANES), 0)

    def load_frame(f, carry):
        ust[f, 0:24, :] = clip[f].astype(F32)
        above, below = uprev[f].astype(F32), unext[f].astype(F32)
        halo_rows = jnp.zeros((8, LANES), F32)
        for ch in range(3):
            halo_rows = jnp.where(row8 == 2 * ch, above[ch * 8 + 7 : ch * 8 + 8], halo_rows)
            halo_rows = jnp.where(row8 == 2 * ch + 1, below[ch * 8 : ch * 8 + 1], halo_rows)
        ust[f, 24:32, :] = halo_rows
        return carry

    lax.fori_loop(0, NF, load_frame, 0)
    zt = tff
    zt[...] = jnp.zeros_like(zt)

    def stem_frame(f, carry):
        before_at, after_at = lax.rem(f + NF - 1, NF), lax.rem(f + 1, NF)
        k_here, k_next = keep[f].astype(F32), keep[after_at].astype(F32)
        frame = ust[f]
        stacked = jnp.concatenate(
            [frame, k_here * (frame - ust[before_at]), k_next * (ust[after_at] - frame)], axis=0)
        stacked = stacked.astype(BF16).astype(F32)
        lane = lax.broadcasted_iota(jnp.int32, stacked.shape, 1)
        left = jnp.where(lane == 0, 0.0, pltpu.roll(stacked, 1, 1))
        right = jnp.where(lane == LANES - 1, 0.0, pltpu.roll(stacked, LANES - 1, 1))
        taps = jnp.concatenate([left, stacked, right], axis=0).astype(BF16)
        place = lax.rem(f, 2 * PART)
        cot = sc[place]
        so[place] = dot_nn(tf[...], taps).astype(BF16)
        back = dot_nn(tb[...], cot)
        dg[f] = (
            jnp.where(lane == LANES - 1, 0.0, pltpu.roll(back[0:96], LANES - 1, 1))
            + back[96:192]
            + jnp.where(lane == 0, 0.0, pltpu.roll(back[192:288], 1, 1)))
        cross = dot_nt(cot, taps)
        for n in range(3):
            columns = min(288 - n * LANES, LANES)
            zt[n, :, 0:columns] += cross[:, n * LANES : n * LANES + columns]
        return carry

    store_so = []
    for part in range(NF // PART):
        lo = part * PART
        load_sc[part].wait()
        if part >= 2:
            store_so[part - 2].wait()
        lax.fori_loop(lo, lo + PART, stem_frame, 0)
        store_so.append(local(so.at[pl.ds(lo % (2 * PART), PART)], so_hbm.at[pl.ds(lo, PART)]))
        if part + 2 < NF // PART:
            load_sc.append(load_cot(part + 2))
        if part % 2:
            pump()
    for copy in store_so[-2:]:
        copy.wait()

    def video_frame(f, carry):
        before_at, after_at = lax.rem(f + NF - 1, NF), lax.rem(f + 1, NF)
        k_here, k_next = keep[f].astype(F32), keep[after_at].astype(F32)
        total = (
            dg[f, 0:32] + k_here * dg[f, 32:64] - k_next * dg[after_at, 32:64]
            + k_here * dg[before_at, 64:96] - k_next * dg[f, 64:96])
        vg_out[f] = total[0:24]
        vgh[f] = total[24:32]
        return carry

    lax.fori_loop(0, NF, video_frame, 0)
    wait_video, _ = halo(vgh, vgh, None, None, vgr.at[0], vgr.at[1])

    stem_grad = jnp.zeros((D * 8, 96), F32)
    for i in range(8):
        for n in range(3):
            part = zt[n, pl.ds(i, D * 8, stride=8), :]
            high = part.astype(BF16)
            low = (part - high.astype(F32)).astype(BF16)
            table = band[i, :, n * LANES : (n + 1) * LANES]
            stem_grad = stem_grad + dot_nt(high, table) + dot_nt(low, table)
    stg[...] = jnp.concatenate([stem_grad, jnp.zeros((D * 8, LANES - 96), F32)], axis=1)
    wait_stem = to_peers(stg, lambda k: stgr.at[k], sp_peers, stgr)

    def rows_loop(group, fn, init):
        def body(i, carry):
            start = (i // (GW // STEP)) * NW + group * GW + (i % (GW // STEP)) * STEP
            return fn(pl.multiple_of(start, STEP), carry)
        return lax.fori_loop(0, 2 * (GW // STEP), body, init)

    def fold(values):
        return values.reshape(STEP // 8, 8, values.shape[1]).sum(axis=0)

    def sp_send(i, parts):
        width = parts[0].shape[1]
        fill = [jnp.zeros((8 - len(parts), width), F32)] if len(parts) < 8 else []
        stat_s[i] = jnp.concatenate(parts + fill, axis=0)
        return to_peers(stat_s.at[i], lambda k: stat_r.at[i, k], sp_peers, stat_r.at[i])

    def sp_total(i, wait):
        wait()
        total = stat_s[i]
        for k in range(S - 1):
            total = total + stat_r[i, k]
        return total

    pixels = jnp.float32(GROUP * 2 * S * 16)
    inv_pixels = 1.0 / (GROUP * 2 * S * 16)

    def two_sums(ref):
        parts = []
        for group in range(NG):
            def add(start, carry):
                value = ref[pl.ds(start, STEP), :]
                return carry[0] + fold(value), carry[1] + fold(value * value)
            zero = jnp.zeros((8, ref.shape[1]), F32)
            one, two = rows_loop(group, add, (zero, zero))
            parts += [jnp.sum(one, axis=0, keepdims=True), jnp.sum(two, axis=0, keepdims=True)]
        return parts

    def moments(total, row):
        mean = total[row : row + 1] * inv_pixels
        variance = total[row + 1 : row + 2] * inv_pixels - mean * mean
        return mean, lax.rsqrt(variance + EPS)

    for copy in load_x:
        copy.wait()
    need(0, 3)
    xs = x3[...].reshape(2 * NW, x3.shape[2])
    for n in range(2):
        z1[:, n * 256 : (n + 1) * 256] = dot_nn(xs, wf[:, :, n * 256 : (n + 1) * 256].reshape(x3.shape[2], 256))
    copies = sp_send(0, two_sums(z1))
    need(3, 6)
    total = sp_total(0, copies)
    inv_1 = []
    for group in range(NG):
        mean, inv = moments(total, 2 * group)
        inv_1.append(inv)

        def apply_1(start, carry):
            normed = (z1[pl.ds(start, STEP), :] - mean) * inv
            act = jax.nn.silu(gain_1 * normed + bias_1)
            z1[pl.ds(start, STEP), :] = normed
            z3[pl.ds(start, STEP), 0:512] = act
            fab[pl.ds(start, STEP), :] = act.astype(BF16)
            return carry
        rows_loop(group, apply_1, 0)

    rd[...] = dot_nn(fab[...], wr[...].reshape(512, LANES))
    for r in range(2):
        for f in range(NF):
            here = r * NW + f * 16
            past = r * NW + ((f - 1) % NF) * 16
            diff = keep[f].astype(F32) * (rd[here : here + 16, :] - rd[past : past + 16, :])
            chb[r, f * 16 : f * 16 + 16, :] = diff.astype(BF16)
    wait_change, free_change = halo(chb, chb, None, None, chr_.at[0], chr_.at[1])

    def put_shifts(ref, at, values, count, flip):
        width = values.shape[1]
        down, up = shift_down(values, count), shift_up(values, count)
        low, high = (up, down) if flip else (down, up)
        ref[at, :, 0:width] = low.astype(BF16)
        ref[at, :, width : 2 * width] = values.astype(BF16)
        ref[at, :, 2 * width : 3 * width] = high.astype(BF16)

    change = [chb[r].astype(F32) for r in range(2)]
    for r in range(2):
        put_shifts(cs, 1 + r, change[r], 1, False)

    def pool(upper, lower):
        return (pair_sum(upper + lower) * 0.25).astype(BF16).astype(F32)

    put_shifts(ps, 1, pool(change[0], change[1]), 2, False)
    pump()
    wait_change()
    above = [chr_[0, r].astype(F32) for r in range(2)]
    below = [chr_[1, r].astype(F32) for r in range(2)]
    put_shifts(cs, 0, above[1], 1, False)
    put_shifts(cs, 3, below[0], 1, False)
    put_shifts(ps, 0, pool(above[0], above[1]), 2, False)
    put_shifts(ps, 2, pool(below[0], below[1]), 2, False)
    full = jnp.zeros((2 * NW, LANES), F32)
    half = jnp.zeros((NW, LANES), F32)
    for a in range(3):
        full = full + dot_nn(cs[a : a + 2].reshape(2 * NW, 384), wd[0, 3 * a : 3 * a + 3].reshape(384, LANES))
        half = half + dot_nn(ps[a], wd[1, 3 * a : 3 * a + 3].reshape(384, LANES))
    comb[...] = (full + jnp.concatenate([half, half], axis=0)).astype(BF16)
    gt[...] = dot_nn(comb[...], we[...].reshape(LANES, 512))

    def apply_gate(i, carry):
        start = pl.multiple_of(i * STEP, STEP)
        gate = jax.nn.sigmoid(gt[pl.ds(start, STEP), :])
        gt[pl.ds(start, STEP), :] = gate
        gated = (z3[pl.ds(start, STEP), 0:512] * (1.0 + gate)).astype(BF16)
        gb[pl.ds(start, STEP), :] = gated
        return carry

    lax.fori_loop(0, 2 * NW // STEP, apply_gate, 0)
    wait_gated, free_gated = halo(gb.at[pl.ds(0, NW)], gb.at[pl.ds(NW, NW)], None, None, gr.at[0], gr.at[1])

    def spread(dst, at, src_fn, flip):
        def body(i, carry):
            start = pl.multiple_of(i * STEP, STEP)
            values = src_fn(start).astype(F32)
            down, up = shift_down(values, 1), shift_up(values, 1)
            low, high = (up, down) if flip else (down, up)
            dst[at, pl.ds(start, STEP), 0:512] = low.astype(BF16)
            dst[at, pl.ds(start, STEP), 512:1024] = values.astype(BF16)
            dst[at, pl.ds(start, STEP), 1024:1536] = high.astype(BF16)
            return carry
        lax.fori_loop(0, NW // STEP, body, 0)

    for r in range(2):
        spread(gs, 1 + r, lambda start, r=r: gb[pl.ds(r * NW + start, STEP), :], False)

    def taps_of(a):
        return wm[3 * a : 3 * a + 3].reshape(1536, 512)

    need(6, 9)
    z2[...] = dot_nn(gs[1:3].reshape(2 * NW, 1536), taps_of(1))
    z2[0:NW, :] += dot_nn(gs[2], taps_of(2))
    z2[NW : 2 * NW, :] += dot_nn(gs[1], taps_of(0))
    wait_gated()
    spread(gs, 0, lambda start: gr[0, pl.ds(start, STEP), :], False)
    spread(gs, 3, lambda start: gr[1, pl.ds(start, STEP), :], False)
    z2[0:NW, :] += dot_nn(gs[0], taps_of(0))
    z2[NW : 2 * NW, :] += dot_nn(gs[3], taps_of(2))
    copies = sp_send(1, two_sums(z2))
    need(9, 12)
    for copy in load_ct:
        copy.wait()
    total = sp_total(1, copies)
    inv_2 = []
    for group in range(NG):
        mean, inv = moments(total, 2 * group)
        inv_2.append(inv)

        def apply_2(start, carry):
            normed = (z2[pl.ds(start, STEP), :] - mean) * inv
            z2[pl.ds(start, STEP), :] = normed
            sab[pl.ds(start, STEP), :] = jax.nn.silu(gain_2 * normed + bias_2).astype(BF16)
            return carry
        rows_loop(group, apply_2, 0)

    def ct_rows(start, lo, width):
        return ct3[pl.ds(start // 16, STEP // 16), :, lo : lo + width].reshape(STEP, width).astype(F32)

    def x_rows(start, lo, width):
        return x3[pl.ds(start // 16, STEP // 16), :, lo : lo + width].reshape(STEP, width).astype(F32)

    last_copies = []
    for n in range(4):
        lo = n * 512
        z3[:, lo : lo + 512] = dot_nn(sab[...], wl[:, :, lo : lo + 512].reshape(512, 512))
        parts = []
        for group in range(NG):
            def add_3(start, carry):
                value = z3[pl.ds(start, STEP), lo : lo + 512]
                cot = ct_rows(start, lo, 512)
                return (carry[0] + fold(value), carry[1] + fold(value * value),
                        carry[2] + fold(cot), carry[3] + fold(cot * value))
            zero = jnp.zeros((8, 512), F32)
            sums = rows_loop(group, add_3, (zero, zero, zero, zero))
            parts += [jnp.sum(item, axis=0, keepdims=True) for item in sums]
        st3_s[n] = jnp.concatenate(parts, axis=0)
        last_copies.append(to_peers(st3_s.at[n], lambda k, n=n: st3_r.at[n, k], sp_peers, st3_r.at[n]))
    gain_3_grad, bias_3_grad = [], []
    stores = []

    def free_part():
        if len(stores) >= 2:
            for copy in stores[-2]:
                copy.wait()

    def store_part(n, target):
        stores.append([local(ost.at[n % 2, pl.ds(r * NF, NF)], target.at[:, r, :, pl.ds(n * 512, 512)]) for r in range(2)])

    for n in range(4):
        lo = n * 512
        free_part()
        last_copies[n]()
        total = st3_s[n]
        for k in range(S - 1):
            total = total + st3_r[n, k]
        gain, bias = gain_3[:, lo : lo + 512], bias_3[:, lo : lo + 512]
        gain_sum = bias_sum = jnp.zeros((1, 512), F32)
        for group in range(NG):
            row = 4 * group
            mean, inv = moments(total, row)
            cot_sum = total[row + 2 : row + 3]
            cot_normed = inv * (total[row + 3 : row + 4] - mean * cot_sum)
            gain_sum, bias_sum = gain_sum + cot_normed, bias_sum + cot_sum
            cot_mean, slope_mean = cot_sum * inv_pixels, cot_normed * inv_pixels
            scale = gain * inv

            def apply_3(start, carry):
                normed = (z3[pl.ds(start, STEP), lo : lo + 512] - mean) * inv
                cot = ct_rows(start, lo, 512)
                out = x_rows(start, lo, 512) + gain * normed + bias
                ost[n % 2, pl.ds(start // 16, STEP // 16)] = out.astype(BF16).reshape(STEP // 16, 16, 512)
                lgb[pl.ds(start, STEP), lo : lo + 512] = (
                    scale * (cot - cot_mean - normed * slope_mean)).astype(BF16)
                return carry
            rows_loop(group, apply_3, 0)
        store_part(n, out_hbm)
        gain_3_grad.append(gain_sum)
        bias_3_grad.append(bias_sum)

    def each(count, fn):
        def body(i, carry):
            fn(i)
            return carry
        lax.fori_loop(0, count, body, 0)

    def z_steps(part, rz, add):
        at = 0
        for bit in z_bits:
            keep_z, give_z = z_class(z, bit), z_class(z_pair(bit), bit)
            start, wait = bundle(rz.at[pl.ds(at, len(keep_z))])
            for j, zz in enumerate(give_z):
                start(part(zz), rz.at[at + j], at_zy(z_pair(bit), y))
            yield
            wait()
            for j, zz in enumerate(keep_z):
                add(part(zz), rz.at[at + j])
            at += len(keep_z)

    def wide_first(grad, lo, n, order, rc, rx, ry, rz, fb):
        rows = pl.ds(lo, n)
        half = pl.ds(c * SX, SX)
        mine = q_own

        def add(dst, *others):
            value = dst[...].astype(F32)
            for other in others:
                value = value + other[...].astype(F32)
            dst[...] = value.astype(BF16)

        wait = remote(grad.at[pl.ds(oc * SX, SX), :, :, rows], rc, c_peer)
        yield
        wait()

        def add_c(i):
            for xx in range(SX):
                for yy in range(2):
                    add(grad.at[c * SX + xx, i, yy, rows], rc.at[xx, i, yy])
        each(DZ, add_c)
        if order == "xyz":
            start, wait = bundle(rx)
            for k in range(1, SX):
                start(grad.at[c * SX + x_to(k), :, :, rows], rx.at[k - 1], x_peer(k))
            yield
            wait()

            def add_x(i):
                for yy in range(2):
                    add(grad.at[mine, i, yy, rows], *[rx.at[k, i, yy] for k in range(SX - 1)])
            each(DZ, add_x)
            wait = remote(grad.at[mine, :, oy, rows], ry, y_peer)
            yield
            wait()
            each(DZ, lambda i: add(grad.at[mine, i, y, rows], ry.at[i]))
            yield from z_steps(lambda zz: grad.at[mine, zz, y, rows], rz, add)
            parts = []
        else:
            wait = remote(grad.at[half, :, oy, rows], ry, y_peer)
            yield
            wait()

            def add_y(i):
                for xx in range(SX):
                    add(grad.at[c * SX + xx, i, y, rows], ry.at[xx, i])
            each(DZ, add_y)
            def add_half(dst, src):
                for xx in range(SX):
                    add(dst.at[xx], src.at[xx])
            yield from z_steps(lambda zz: grad.at[half, zz, y, rows], rz, add_half)
            start, wait = bundle(rx)
            for k in range(1, SX):
                start(grad.at[c * SX + x_to(k), z, y, rows], rx.at[k - 1], x_peer(k))
            yield
            wait()
            parts = [rx.at[k] for k in range(SX - 1)]
        value = grad[mine, z, y, rows].astype(F32)
        for part in parts:
            value = value + part[...].astype(F32)
        fb[mine, rows] = value.astype(BF16)
        done = fb.at[mine, rows]
        wait = to_peers(done, lambda k: done, sp_peers, fb.at[pl.ds(0, S - 1), rows])
        yield
        wait()

    def wide_mid(grad, lo, n, order, rc, rx, ry, rz, fb):
        taps = pl.ds(lo, n)
        half = pl.ds(c * SX, SX)
        mine = q_own

        def add(dst, *others):
            value = dst[...].astype(F32)
            for other in others:
                value = value + other[...].astype(F32)
            dst[...] = value.astype(BF16)

        wait = remote(grad.at[pl.ds(oc * SX, SX), taps], rc, c_peer)
        yield
        wait()

        def add_c(i):
            t, zz = i // DZ, i % DZ
            for xx in range(SX):
                add(grad.at[c * SX + xx, lo + t, zz], rc.at[xx, t, zz])
        each(n * DZ, add_c)
        if order == "xyz":
            start, wait = bundle(rx)
            for k in range(1, SX):
                start(grad.at[c * SX + x_to(k), taps], rx.at[k - 1], x_peer(k))
            yield
            wait()

            def add_x(i):
                t, zz = i // DZ, i % DZ
                add(grad.at[mine, lo + t, zz], *[rx.at[k, t, zz] for k in range(SX - 1)])
            each(n * DZ, add_x)
            wait = remote(grad.at[mine, taps, :, oy], ry, y_peer)
            yield
            wait()

            def add_y(i):
                t, zz = i // DZ, i % DZ
                add(grad.at[mine, lo + t, zz, y], ry.at[t, zz])
            each(n * DZ, add_y)
            def add_taps(dst, src):
                each(n, lambda t: add(dst.at[t], src.at[t]))
            yield from z_steps(lambda zz: grad.at[mine, taps, zz, y], rz, add_taps)
            parts = []
        else:
            wait = remote(grad.at[half, taps, :, oy], ry, y_peer)
            yield
            wait()

            def add_y(i):
                t, zz = i // DZ, i % DZ
                for xx in range(SX):
                    add(grad.at[c * SX + xx, lo + t, zz, y], ry.at[xx, t, zz])
            each(n * DZ, add_y)
            def add_half(dst, src):
                for xx in range(SX):
                    each(n, lambda t, xx=xx: add(dst.at[xx, t], src.at[xx, t]))
            yield from z_steps(lambda zz: grad.at[half, taps, zz, y], rz, add_half)
            start, wait = bundle(rx)
            for k in range(1, SX):
                start(grad.at[c * SX + x_to(k), taps, z, y], rx.at[k - 1], x_peer(k))
            yield
            wait()
            parts = [rx.at[k] for k in range(SX - 1)]

        def finish(t):
            value = grad[mine, lo + t, z, y].astype(F32)
            for part in parts:
                value = value + part[t].astype(F32)
            fb[mine, lo + t] = value.astype(BF16)
        each(n, finish)
        done = fb.at[mine, taps]
        wait = to_peers(done, lambda k: done, sp_peers, fb.at[pl.ds(0, S - 1), taps])
        yield
        wait()

    def reduce_diff():
        wait = remote(g_diff.at[oc], rcd, c_peer)
        yield
        wait()

        def add_c(i):
            t, zz = i // DZ, i % DZ
            for yy in range(2):
                value = g_diff[c, t, zz, yy].astype(F32) + rcd[t, zz, yy].astype(F32)
                g_diff[c, t, zz, yy] = value.astype(BF16)
        each(9 * DZ, add_c)
        wait = remote(g_diff.at[c, :, :, oy], ryd, y_peer)
        yield
        wait()

        def add_y(i):
            t, zz = i // DZ, i % DZ
            value = g_diff[c, t, zz, y].astype(F32) + ryd[t, zz].astype(F32)
            g_diff[c, t, zz, y] = value.astype(BF16)
        each(9 * DZ, add_y)
        def add_taps(dst, src):
            def one(t):
                dst[t] = (dst[t].astype(F32) + src[t].astype(F32)).astype(BF16)
            each(9, one)
        yield from z_steps(lambda zz: g_diff.at[c, :, zz, y], rzd, add_taps)

        def widen(t):
            fdx[t] = g_diff[c, t, z, y].astype(F32)
        each(9, widen)
        start, wait = bundle(rxd)
        for k in range(1, SX):
            start(fdx, rxd.at[k - 1], x_peer(k))
        yield
        wait()

        def add_x(t):
            value = fdx[t]
            for k in range(1, SX):
                value = value + rxd[k - 1, t]
            fdo[c, t] = value
        each(9, add_x)
        wait = remote(fdo.at[c], fdo.at[c], c_peer)
        yield
        wait()
        od_out[...] = fdo[...]

    def reduce_rest():
        wait = remote(g_re, rcr, c_peer)
        yield
        wait()

        def add_c(zz):
            for yy in range(2):
                value = g_re[zz, yy].astype(F32) + rcr[zz, yy].astype(F32)
                rcr[zz, yy] = value.astype(BF16)
        each(DZ, add_c)
        wait = remote(rcr.at[:, oy], ryr, y_peer)
        yield
        wait()

        def add_y(zz):
            value = rcr[zz, y].astype(F32) + ryr[zz].astype(F32)
            rcr[zz, y] = value.astype(BF16)
        each(DZ, add_y)
        def add_z(dst, src):
            dst[...] = (dst[...].astype(F32) + src[...].astype(F32)).astype(BF16)
        yield from z_steps(lambda zz: rcr.at[zz, y], rzr, add_z)
        frx[...] = rcr[z, y].astype(F32)
        start, wait = bundle(rxr)
        for k in range(1, SX):
            start(frx, rxr.at[k - 1], x_peer(k))
        yield
        wait()
        value = frx[...]
        for k in range(1, SX):
            value = value + rxr[k - 1]
        n_red, n_exp = or_out.shape[0], oe_out.shape[0]
        or_out[...] = value[0:n_red]
        for b in range(4):
            oe_out[:, b * LANES : (b + 1) * LANES] = value[n_red + b * n_exp : n_red + (b + 1) * n_exp]

    bufs = [bufs[n : n + 4] for n in range(0, len(bufs), 4)]
    spans_f, spans_m, spans_l = portions(fr, 9, lr)
    red_first = [wide_first(g_first, lo, n, order, *bufs.pop(0), fbf) for order, lo, n in spans_f]
    red_mid = [wide_mid(g_mid, lo, n, order, *bufs.pop(0), fbm) for order, lo, n in spans_m]
    red_last = [wide_first(g_last, lo, n, order, *bufs.pop(0), fbl) for order, lo, n in spans_l]
    fx0, fx1, fy = red_first
    mx0, mx1, my = red_mid
    lx, ly = red_last
    red_diff, red_rest = reduce_diff(), reduce_rest()

    def push(*chains):
        for chain in chains:
            next(chain, None)

    for finish in (free_gated, free_change):
        finish()
        halo_waits.remove(finish)
    mgb, mgr = gb, gr
    sg2, gg = z3.at[:, 0:512], z3.at[:, 512:1024]
    sg2[...] = dot_nt(lgb[...], wl[...].reshape(512, 2048))
    parts = []
    for group in range(NG):
        def slope_2(start, carry):
            normed = z2[pl.ds(start, STEP), :]
            _, slope = silu_parts(gain_2 * normed + bias_2)
            value = sg2[pl.ds(start, STEP), :] * slope
            sg2[pl.ds(start, STEP), :] = value
            return carry[0] + fold(value), carry[1] + fold(value * normed)
        zero = jnp.zeros((8, 512), F32)
        sums = rows_loop(group, slope_2, (zero, zero))
        parts += [jnp.sum(item, axis=0, keepdims=True) for item in sums]
    copies = sp_send(2, parts)
    for n in range(4):
        g_last[n] = dot_tn(sab[...], lgb[:, n * 512 : (n + 1) * 512]).astype(BF16).reshape(DZ, 2, lr, 512)
    push(lx, ly)
    total = sp_total(2, copies)
    gain_2_grad = bias_2_grad = jnp.zeros((1, 512), F32)
    for group in range(NG):
        row = 2 * group
        bias_sum, gain_sum = total[row : row + 1], total[row + 1 : row + 2]
        gain_2_grad, bias_2_grad = gain_2_grad + gain_sum, bias_2_grad + bias_sum
        scale = gain_2 * inv_2[group]

        def apply_2b(start, carry):
            value = sg2[pl.ds(start, STEP), :] - bias_sum * inv_pixels
            value = scale * (value - z2[pl.ds(start, STEP), :] * (gain_sum * inv_pixels))
            mgb[pl.ds(start, STEP), :] = value.astype(BF16)
            return carry
        rows_loop(group, apply_2b, 0)
    wait_mid, _ = halo(mgb.at[pl.ds(0, NW)], mgb.at[pl.ds(NW, NW)], None, None, mgr.at[0], mgr.at[1])
    push(lx, ly)
    for a in range(3):
        for b in range(3):
            grad = dot_tn(gs[a : a + 2, :, b * 512 : (b + 1) * 512].reshape(2 * NW, 512), mgb[...]).astype(BF16)
            for qq in range(S):
                g_mid[qq, 3 * a + b] = grad[:, qq * mw : (qq + 1) * mw].reshape(DZ, 2, wm_in.shape[1], mw)
        push(red_mid[a])
    mgs = gs
    for r in range(2):
        spread(mgs, 1 + r, lambda start, r=r: mgb[pl.ds(r * NW + start, STEP), :], True)

    def back_taps(lhs, a):
        total = dot_nt(lhs[:, 0:512], wm[3 * a].reshape(512, 512))
        for b in range(1, 3):
            total = total + dot_nt(lhs[:, b * 512 : (b + 1) * 512], wm[3 * a + b].reshape(512, 512))
        return total

    gg[...] = back_taps(mgs[1:3].reshape(2 * NW, 1536), 1)
    gg[0:NW, :] += back_taps(mgs[2], 0)
    gg[NW : 2 * NW, :] += back_taps(mgs[1], 2)
    push(mx0, my, ly)
    wait_mid()
    spread(mgs, 0, lambda start: mgr[0, pl.ds(start, STEP), :], True)
    spread(mgs, 3, lambda start: mgr[1, pl.ds(start, STEP), :], True)
    gg[0:NW, :] += back_taps(mgs[0], 2)
    gg[NW : 2 * NW, :] += back_taps(mgs[3], 0)

    def gate_back(i, carry):
        start = pl.multiple_of(i * STEP, STEP)
        gate = gt[pl.ds(start, STEP), :]
        act = jax.nn.silu(gain_1 * z1[pl.ds(start, STEP), :] + bias_1)
        value = gg[pl.ds(start, STEP), :] * act * gate * (1.0 - gate)
        fgb[pl.ds(start, STEP), :] = value.astype(BF16)
        return carry

    lax.fori_loop(0, 2 * NW // STEP, gate_back, 0)
    cg = dot_nt(fgb[...], we[...].reshape(LANES, 512)).astype(BF16)
    cg_rows = [cg[r * NW : (r + 1) * NW].astype(F32) for r in range(2)]
    hg = pair_sum(cg_rows[0] + cg_rows[1]).astype(BF16)
    for r in range(2):
        cgx[r, 0] = cg_rows[r].astype(BF16)
        cgx[r, 1] = hg
    wait_cg, _ = halo(cgx.at[0], cgx.at[1], None, None, cgr.at[0], cgr.at[1])
    push(mx1, lx, ly)
    n_exp = we_in.shape[0]
    grad = dot_tn(comb[...], fgb[...]).astype(BF16)
    n_red = wr_in.shape[0]
    for b in range(4):
        g_re[:, :, n_red + b * n_exp : n_red + (b + 1) * n_exp, :] = grad[
            :, b * LANES : (b + 1) * LANES].reshape(DZ, 2, n_exp, LANES)
    for r in range(2):
        put_shifts(cgs, 1 + r, cg_rows[r], 1, True)
    put_shifts(hgs, 1, hg.astype(F32), 2, True)
    for a in range(3):
        grad = dot_tn(cs[a : a + 2].reshape(2 * NW, 384), cg).astype(BF16)
        g_diff[0, 3 * a : 3 * a + 3] = grad.reshape(3, DZ, 2, wd0_in.shape[1], LANES)
        grad = (0.5 * dot_tn(ps[a], hg)).astype(BF16)
        g_diff[1, 3 * a : 3 * a + 3] = grad.reshape(3, DZ, 2, wd0_in.shape[1], LANES)
    push(red_diff, my)
    wait_cg()
    put_shifts(cgs, 0, cgr[0, 0].astype(F32), 1, True)
    put_shifts(cgs, 3, cgr[1, 0].astype(F32), 1, True)
    put_shifts(hgs, 0, cgr[0, 1].astype(F32), 2, True)
    put_shifts(hgs, 2, cgr[1, 1].astype(F32), 2, True)
    full = jnp.zeros((2 * NW, LANES), F32)
    half = jnp.zeros((NW, LANES), F32)
    for a in range(3):
        for b in range(3):
            lanes = slice(b * LANES, (b + 1) * LANES)
            full = full + dot_nt(
                cgs[2 - a : 4 - a, :, lanes].reshape(2 * NW, LANES), wd[0, 3 * a + b].reshape(LANES, LANES))
            half = half + dot_nt(hgs[2 - a, :, lanes], wd[1, 3 * a + b].reshape(LANES, LANES))
    rd[...] = full + 0.25 * jnp.concatenate([half, half], axis=0)
    for r in range(2):
        for f in range(NF):
            here = r * NW + f * 16
            after = r * NW + ((f + 1) % NF) * 16
            diff = (keep[f].astype(F32) * rd[here : here + 16, :]
                    - keep[(f + 1) % NF].astype(F32) * rd[after : after + 16, :])
            chb[r, f * 16 : f * 16 + 16, :] = diff.astype(BF16)
    rgb = chb[...].reshape(2 * NW, LANES)
    sg2[...] = dot_nt(rgb, wr[...].reshape(512, LANES))

    parts = []
    for group in range(NG):
        def slope_1(start, carry):
            normed = z1[pl.ds(start, STEP), :]
            _, slope = silu_parts(gain_1 * normed + bias_1)
            value = gg[pl.ds(start, STEP), :] * (1.0 + gt[pl.ds(start, STEP), :]) + sg2[pl.ds(start, STEP), :]
            value = value * slope
            sg2[pl.ds(start, STEP), :] = value
            return carry[0] + fold(value), carry[1] + fold(value * normed)
        zero = jnp.zeros((8, 512), F32)
        sums = rows_loop(group, slope_1, (zero, zero))
        parts += [jnp.sum(item, axis=0, keepdims=True) for item in sums]
    copies = sp_send(3, parts)
    g_re[:, :, 0:n_red, :] = dot_tn(fab[...], rgb).astype(BF16).reshape(DZ, 2, n_red, LANES)
    push(red_rest, lx, ly, red_diff)
    total = sp_total(3, copies)
    gain_1_grad = bias_1_grad = jnp.zeros((1, 512), F32)
    for group in range(NG):
        row = 2 * group
        bias_sum, gain_sum = total[row : row + 1], total[row + 1 : row + 2]
        gain_1_grad, bias_1_grad = gain_1_grad + gain_sum, bias_1_grad + bias_sum
        scale = gain_1 * inv_1[group]

        def apply_1b(start, carry):
            value = sg2[pl.ds(start, STEP), :] - bias_sum * inv_pixels
            value = scale * (value - z1[pl.ds(start, STEP), :] * (gain_sum * inv_pixels))
            fgb[pl.ds(start, STEP), :] = value.astype(BF16)
            return carry
        rows_loop(group, apply_1b, 0)

    wait_stem()
    stem_total = stg[...]
    for k in range(S - 1):
        stem_total = stem_total + stgr[k]
    gain_3_all = jnp.concatenate(gain_3_grad, axis=1)
    bias_3_all = jnp.concatenate(bias_3_grad, axis=1)
    for d in range(D):
        mid_at, last_at = (d // per) * LANES, d * rows_last * LANES
        rows = [v[:, mid_at : mid_at + LANES] for v in (gain_1_grad, bias_1_grad, gain_2_grad, bias_2_grad)]
        for v in (gain_3_all, bias_3_all):
            rows += [v[:, last_at + n * LANES : last_at + (n + 1) * LANES] for n in range(rows_last)]
        sms[d, 0:8, :] = stem_total[d * 8 : d * 8 + 8]
        sms[d, 8:16, :] = jnp.concatenate(rows, axis=0)
    small_start, wait_small_back = bundle(smr)
    for k in range(1, D):
        small_start(sms.at[lax.rem(dp + k, D)], smr.at[k - 1], dp_peers[k - 1])

    for n in range(4):
        grad = dot_tn(x3[:, :, n * 512 : (n + 1) * 512].reshape(2 * NW, 512), fgb[...]).astype(BF16)
        per_chunk = 512 // (2 * fr)
        for qq in range(S):
            g_first[qq, n * per_chunk : (n + 1) * per_chunk] = grad[:, qq * fw : (qq + 1) * fw].reshape(
                per_chunk, 2, fr, fw)
    push(fx0, fx1, fy)
    push(red_rest, red_diff, lx, ly, mx0, my)
    push(fx0, fy, fx1)
    after_part = ((mx0, my, lx), (mx1, ly, red_rest, red_diff), (mx0, my, fy), (lx, ly))
    weights_first = wf[...].reshape(2048, 512)
    for n in range(4):
        lo = n * 512
        free_part()
        z3[:, lo : lo + 512] = dot_nt(fgb[...], weights_first[lo : lo + 512])

        def apply_in(i, carry):
            start = pl.multiple_of(i * STEP, STEP)
            value = z3[pl.ds(start, STEP), lo : lo + 512] + ct_rows(start, lo, 512)
            ost[n % 2, pl.ds(start // 16, STEP // 16)] = value.astype(BF16).reshape(STEP // 16, 16, 512)
            return carry
        lax.fori_loop(0, 2 * NW // STEP, apply_in, 0)
        store_part(n, ig_hbm)
        push(*after_part[n])
    for _ in range(7):
        push(mx0, my, mx1, fx0, fy, fx1, red_rest, red_diff, lx, ly)
    grad_stores = [local(fbf, fbf_hbm), local(fbm, fbm_hbm), local(fbl, fbl_hbm)]

    assert counters["r"] <= ssem.shape[0] and counters["l"] <= lsem.shape[0], counters
    wait_video()

    def video_edges(f, carry):
        for ch in range(3):
            rows = slice(ch * 8, ch * 8 + 8)
            from_prev = vgr[0, f, ch * 2 + 1 : ch * 2 + 2, :]
            from_next = vgr[1, f, ch * 2 : ch * 2 + 1, :]
            vg_out[f, rows] += jnp.where(row8 == 0, from_prev, jnp.where(row8 == 7, from_next, 0.0))
        return carry

    lax.fori_loop(0, NF, video_edges, 0)
    value = sms[dp]
    wait_small_back()
    for k in range(D - 1):
        value = value + smr[k]
    osm_out[...] = value
    for finish in sends + halo_waits:
        finish()
    for copy in grad_stores:
        copy.wait()
    for part in stores[-2:]:
        for copy in part:
            copy.wait()


def final_kernel(
    sizes, so, vg, out, ig, fbf, fbm, fbl, gr, gd, ge, gsm,
    so_o, vg_o, out_o, ig_o, rgb_o, stemd_o, first_o, mid_o, last_o, red_o, dfull_o, dhalf_o, exp_o,
    g1_o, b1_o, g2_o, b2_o, g3_o, b3_o, sems, so_v, out_v, ig_v, vg_v,
):
    D, S = sizes
    loads, copies = [], []
    for src, through, dst in ((so, so_v, so_o), (out, out_v, out_o), (ig, ig_v, ig_o), (vg, vg_v, vg_o)):
        half = src.shape[0] // 2
        for rows in (pl.ds(0, half), pl.ds(half, half)):
            n = len(loads)
            loads.append(pltpu.make_async_copy(src.at[rows], through.at[rows], sems.at[0, n]))
            copies.append(pltpu.make_async_copy(through.at[rows], dst.at[rows], sems.at[1, n]))
    for copy in loads:
        copy.start()
    for load, copy in zip(loads, copies):
        load.wait()
        copy.start()
    fw, lw = fbf.shape[2], fbl.shape[2]
    for q in range(S):
        first_o[:, q * fw : (q + 1) * fw] = fbf[q].astype(F32)
        last_o[:, q * lw : (q + 1) * lw] = fbl[q].astype(F32)
        for t in range(9):
            mid_o[t, :, q * fw : (q + 1) * fw] = fbm[q, t].astype(F32)
    red_o[...] = gr[...]
    dfull_o[...] = gd[0]
    dhalf_o[...] = gd[1]
    exp_o[...] = ge[...]
    for ch in range(9):
        value = gsm[0:8, ch * 9 : ch * 9 + 9]
        if ch < 3:
            rgb_o[ch] = value
        else:
            stemd_o[ch - 3] = value
    width = g1_o.shape[0]
    per = LANES // width
    here = lax.rem(lax.axis_index("dp"), per)
    for j, ref in enumerate((g1_o, b1_o, g2_o, b2_o)):
        row = gsm[8 + j]
        value = row[0:width]
        for n in range(1, per):
            value = jnp.where(here == n, row[n * width : (n + 1) * width], value)
        ref[...] = value
    count = g3_o.shape[0] // LANES
    for j, ref in enumerate((g3_o, b3_o)):
        for n in range(count):
            ref[n * LANES : (n + 1) * LANES] = gsm[12 + j * count + n]
    for copy in copies:
        copy.wait()


def on_device_kernel(
    clip_video, section_input, keep_mask, w_rgb, w_stem_diff, w_first, w_middle, w_last, w_reduce,
    w_diff_full, w_diff_half, w_expand, gain_first, bias_first, gain_middle, bias_middle, gain_last,
    bias_last, stem_cot, section_cot,
):
    D, S = lax.axis_size("dp"), lax.axis_size("sp")
    DZ, SX = D // 2, S // 2
    NF = clip_video.shape[0]
    NW = NF * 16
    width = 512 // D
    band = jnp.asarray(band_table(8), BF16)
    fr, fw = w_first.shape[0], 512 // S
    mr, lr, rr = w_middle.shape[1], w_last.shape[0], w_reduce.shape[0]
    dr, er = w_diff_full.shape[1], w_expand.shape[0]
    lw = 2048 // S
    shape = jax.ShapeDtypeStruct
    vm = pltpu.VMEM
    any_spec = pl.BlockSpec(memory_space=pl.ANY)
    vmem_spec = pl.BlockSpec(memory_space=pltpu.VMEM)
    n_rem, n_loc = 136, 48
    re_rows = rr + 4 * er
    scratch = [
        pltpu.SemaphoreType.DMA((n_rem,)), pltpu.SemaphoreType.DMA((n_rem,)), pltpu.SemaphoreType.DMA((n_loc,)),
        vm((D, fr, 512), BF16), vm((9, D, mr, 512), BF16), vm((D, lr, 2048), BF16),
        vm((D, rr, LANES), BF16), vm((2, 9, D, dr, LANES), BF16), vm((D, er, 512), BF16),
        vm((2 * NF, 16, 2048), BF16), vm((2 * NF, 16, 2048), BF16),
        vm((2 * PART, 512, LANES), BF16), vm((2 * PART, 512, LANES), BF16),
        vm((NF, 32, LANES), F32), vm((NF, 24, LANES), BF16), vm((NF, 24, LANES), BF16),
        vm((16, LANES), F32), vm((D, 16, LANES), F32), vm((512, 288), BF16), vm((3, 512, LANES), F32), vm((288, 512), BF16),
        vm((NF, 96, LANES), F32),
        vm((NF, 8, LANES), F32), vm((2, NF, 8, LANES), F32), vm((D * 8, LANES), F32), vm((S - 1, D * 8, LANES), F32),
        vm((4, 8, 512), F32), vm((4, S - 1, 8, 512), F32), vm((4, 8, 512), F32), vm((4, S - 1, 8, 512), F32),
        vm((2 * NW, 512), F32), vm((2 * NW, 512), BF16), vm((2 * NW, 512), F32),
        vm((2 * NW, LANES), F32), vm((2, NW, LANES), BF16), vm((2, 2, NW, LANES), BF16),
        vm((4, NW, 384), BF16), vm((3, NW, 384), BF16), vm((2 * NW, LANES), BF16),
        vm((2 * NW, 512), BF16), vm((2, NW, 512), BF16), vm((4, NW, 1536), BF16),
        vm((2 * NW, 512), F32), vm((2 * NW, 512), BF16), vm((2 * NW, 2048), F32), vm((2 * NW, 2048), BF16),
        vm((2, 2, NW, LANES), BF16), vm((2, 2, NW, LANES), BF16),
        vm((4, NW, 384), BF16), vm((3, NW, 384), BF16), vm((2 * NW, 512), BF16), vm((2, 2 * NF, 16, 512), BF16),
        vm((S, DZ, 2, fr, fw), BF16), vm((S, 9, DZ, 2, mr, fw), BF16), vm((S, DZ, 2, lr, lw), BF16),
        vm((2, 9, DZ, 2, dr, LANES), BF16), vm((DZ, 2, re_rows, LANES), BF16),
        vm((9, DZ, 2, dr, LANES), BF16), vm((9, DZ, dr, LANES), BF16), vm((DZ - 1, 9, dr, LANES), BF16),
        vm((9, dr, LANES), F32), vm((SX - 1, 9, dr, LANES), F32), vm((2, 9, dr, LANES), F32),
        vm((DZ, 2, re_rows, LANES), BF16), vm((DZ, re_rows, LANES), BF16), vm((DZ - 1, re_rows, LANES), BF16),
        vm((re_rows, LANES), F32), vm((SX - 1, re_rows, LANES), F32),
        vm((S, fr, fw), BF16), vm((S, 9, mr, fw), BF16), vm((S, lr, lw), BF16),
        vm((D, 16, LANES), F32), vm((D - 1, 16, LANES), F32),
    ]

    def landing(spans, shape_of):
        for order, _, n in spans:
            extra = (SX,) if order == "yzx" else ()
            scratch.append(vm((SX,) + shape_of(n, (DZ, 2)), BF16))
            scratch.append(vm((SX - 1,) + shape_of(n, (DZ, 2) if order == "xyz" else ()), BF16))
            scratch.append(vm(extra + shape_of(n, (DZ,)), BF16))
            scratch.append(vm((DZ - 1,) + extra + shape_of(n, ()), BF16))

    spans_f, spans_m, spans_l = portions(fr, 9, lr)
    landing(spans_f, lambda n, lead: lead + (n, fw))
    landing(spans_m, lambda n, lead: (n,) + lead + (mr, fw))
    landing(spans_l, lambda n, lead: lead + (n, lw))
    outs = pl.pallas_call(
        functools.partial(whole_kernel, (D, S, NF)),
        out_shape=(
            shape((NF, 512, LANES), BF16), shape((NF, 24, LANES), F32),
            shape(section_input.shape, BF16), shape(section_input.shape, BF16),
            shape((S, fr, fw), BF16), shape((S, 9, mr, fw), BF16), shape((S, lr, lw), BF16), shape((rr, LANES), F32),
            shape((2, 9, dr, LANES), F32), shape((er, 512), F32), shape((16, LANES), F32),
        ),
        in_specs=[pl.BlockSpec(memory_space=pltpu.SMEM)] + [vmem_spec] * 10 + [any_spec] * 10,
        out_specs=(any_spec, vmem_spec) + (any_spec,) * 5 + (vmem_spec,) * 4,
        scratch_shapes=scratch,
        compiler_params=pltpu.CompilerParams(
            collective_id=0, has_side_effects=True, vmem_limit_bytes=VMEM_BYTES),
        name="tdn_blocks",
    )(
        keep_mask, clip_video.reshape(NF, 24, LANES), w_rgb.transpose(1, 2, 0), w_stem_diff.transpose(1, 2, 0),
        gain_first.reshape(1, -1), bias_first.reshape(1, -1), gain_middle.reshape(1, -1), bias_middle.reshape(1, -1),
        gain_last.reshape(-1, LANES), bias_last.reshape(-1, LANES), band, section_input, section_cot, stem_cot.reshape(NF, 512, LANES),
        w_first, w_middle, w_last, w_reduce, w_diff_full, w_diff_half, w_expand,
    )
    results = (
        shape(stem_cot.shape, BF16), shape(clip_video.shape, F32), shape(section_input.shape, BF16),
        shape(section_input.shape, BF16), shape((3, 8, 9), F32), shape((6, 8, 9), F32),
        shape(w_first.shape, F32), shape(w_middle.shape, F32), shape(w_last.shape, F32), shape(w_reduce.shape, F32),
        shape(w_diff_full.shape, F32), shape(w_diff_half.shape, F32), shape(w_expand.shape, F32),
    ) + (shape((width,), F32),) * 4 + (shape((2048 // D,), F32),) * 2
    so, vg, section_output, input_grad, *grads = outs
    finals = pl.pallas_call(
        functools.partial(final_kernel, (D, S)),
        out_shape=results,
        in_specs=[any_spec] * 4 + [vmem_spec] * 7,
        out_specs=(any_spec,) * 4 + (vmem_spec,) * 15,
        scratch_shapes=[
            pltpu.SemaphoreType.DMA((2, 8)), vm(stem_cot.shape, BF16), vm(section_input.shape, BF16),
            vm(section_input.shape, BF16), vm(clip_video.shape, F32)],
        compiler_params=pltpu.CompilerParams(vmem_limit_bytes=VMEM_BYTES),
        name="final_outputs",
    )(so.reshape(stem_cot.shape), vg.reshape(clip_video.shape), section_output, input_grad, *grads)
    return finals[0:4] + (finals[4].transpose(2, 0, 1), finals[5].transpose(2, 0, 1)) + finals[6:]


def fits_kernel(mesh):
    dp_count, sp_count = mesh.shape["dp"], mesh.shape["sp"]
    return (
        dp_count % 2 == 0 and dp_count & (dp_count - 1) == 0 and sp_count % 2 == 0 and H5 == 2 * sp_count and HS == 8 * sp_count
        and TDM_C % (16 * dp_count) == 0 and STEM_C == 8 * dp_count and MID // sp_count % LANES == 0
        and C5 // dp_count % LANES == 0 and (dp_count - 1) * (sp_count // 2 - 1) <= dp_count
    )


def solution(mesh):
    placed = (
        P("dp", None, "sp", None),
        P("dp", "sp", None, None),
        P("dp"),
        P(None, None, "dp"),
        P(None, None, "dp"),
        P("dp", None),
        P(None, "dp", None),
        P("dp", None),
        P("dp", None),
        P(None, "dp", None),
        P(None, "dp", None),
        P("dp", None),
        P("dp"),
        P("dp"),
        P("dp"),
        P("dp"),
        P("dp"),
        P("dp"),
        P("dp", None, "sp", None),
        P("dp", "sp", None, None),
    )
    return jax.shard_map(
        on_device_kernel if fits_kernel(mesh) else on_device,
        mesh=mesh,
        in_specs=placed,
        out_specs=(
            P("dp", None, "sp", None),
            P("dp", None, "sp", None),
            P("dp", "sp", None, None),
            P("dp", "sp", None, None),
            P(None, None, "dp"),
            P(None, None, "dp"),
            P("dp", None),
            P(None, "dp", None),
            P("dp", None),
            P("dp", None),
            P(None, "dp", None),
            P(None, "dp", None),
            P("dp", None),
            P("dp"),
            P("dp"),
            P("dp"),
            P("dp"),
            P("dp"),
            P("dp"),
        ),
        check_vma=False,
    )
```

```python
import functools

import jax
import jax.numpy as jnp
import numpy as np
from jax import lax
from jax.experimental import pallas as pl
from jax.experimental.pallas import tpu as pltpu
from jax.sharding import PartitionSpec as P

H5, HS, MID, TDM_C, C5, STEM_C = 8, 32, 512, 128, 2048, 64
VMEM_BYTES = 63 * 2**20

MICRO = 2


EPS = 1e-05


def with_halo(block, sides, width):
    for axis, dim in sides:
        count = lax.axis_size(axis)
        forward = [(i, i + 1) for i in range(count - 1)]
        backward = [(target, source) for source, target in forward]
        low = lax.ppermute(
            lax.slice_in_dim(block, block.shape[dim] - width, None, axis=dim), axis, forward
        )
        high = lax.ppermute(lax.slice_in_dim(block, 0, width, axis=dim), axis, backward)
        block = jnp.concatenate([low, block, high], axis=dim)
    return block


def silu_slope(values):
    sig_value = jax.nn.sigmoid(values)
    return sig_value * (1.0 + values * (1.0 - sig_value))


def tap_window(padded, row_off, col_off, row_count, col_count, row_axis):
    part_rows = lax.slice_in_dim(padded, row_off, row_off + row_count, axis=row_axis)
    return lax.slice_in_dim(part_rows, col_off, col_off + col_count, axis=row_axis + 1)


def pad_columns(haloed, row_axis):
    widths = [(0, 0)] * haloed.ndim
    widths[row_axis + 1] = (1, 1)
    return jnp.pad(haloed, widths)


def tap_conv(haloed, kernel, channels_last):
    row_axis = 1 if channels_last else 2
    row_count = haloed.shape[row_axis] - 2
    col_count = haloed.shape[row_axis + 1]
    padded = pad_columns(haloed, row_axis)
    einsum_form = "fhwc,cd->fhwd" if channels_last else "fchw,cd->fdhw"
    result = None
    for tap_index in range(9):
        window = tap_window(padded, tap_index // 3, tap_index % 3, row_count, col_count, row_axis)
        tap_term = jnp.einsum(
            einsum_form, window, kernel[tap_index], preferred_element_type=jnp.float32
        )
        result = tap_term if result is None else result + tap_term
    return result


def tap_conv_back(grad_halo, kernel, channels_last):
    row_axis = 1 if channels_last else 2
    row_count = grad_halo.shape[row_axis] - 2
    col_count = grad_halo.shape[row_axis + 1]
    padded = pad_columns(grad_halo, row_axis)
    einsum_form = "fhwd,cd->fhwc" if channels_last else "fdhw,cd->fchw"
    result = None
    for tap_index in range(9):
        window = tap_window(
            padded, 2 - tap_index // 3, 2 - tap_index % 3, row_count, col_count, row_axis
        )
        tap_term = jnp.einsum(
            einsum_form, window, kernel[tap_index], preferred_element_type=jnp.float32
        )
        result = tap_term if result is None else result + tap_term
    return result


def tap_kernel_grad(haloed, out_grad, channels_last):
    row_axis = 1 if channels_last else 2
    row_count = out_grad.shape[row_axis]
    col_count = out_grad.shape[row_axis + 1]
    padded = pad_columns(haloed, row_axis)
    einsum_form = "fhwc,fhwd->cd" if channels_last else "fchw,fdhw->cd"
    tap_list = []
    for tap_index in range(9):
        window = tap_window(padded, tap_index // 3, tap_index % 3, row_count, col_count, row_axis)
        tap_list.append(
            jnp.einsum(einsum_form, window, out_grad, preferred_element_type=jnp.float32)
        )
    return jnp.stack(tap_list, axis=0)


def pair_mean(values):
    return values.reshape(
        values.shape[0], values.shape[1] // 2, 2, values.shape[2] // 2, 2, values.shape[3]
    ).mean(axis=(2, 4))


def pair_total(values):
    return values.reshape(
        values.shape[0], values.shape[1] // 2, 2, values.shape[2] // 2, 2, values.shape[3]
    ).sum(axis=(2, 4))


def pair_grow(values):
    return jnp.repeat(jnp.repeat(values, 2, axis=1), 2, axis=2)


def norm_forward(pre_norm, gain, bias, pixel_count):
    local_sums = (jnp.sum(pre_norm, axis=(0, 1, 2)), jnp.sum(pre_norm * pre_norm, axis=(0, 1, 2)))
    total_sum, total_square = lax.psum((local_sums[0], local_sums[1]), "sp")
    mean_value = total_sum / pixel_count
    variance = total_square / pixel_count - mean_value * mean_value
    inverse = lax.rsqrt(variance + EPS)
    normed = (pre_norm - mean_value) * inverse
    return (normed, inverse, gain * normed + bias)


def norm_backward(out_grad, normed, inverse, gain, pixel_count):
    local_bias = jnp.sum(out_grad, axis=(0, 1, 2))
    local_gain = jnp.sum(out_grad * normed, axis=(0, 1, 2))
    total_bias, total_gain = lax.psum((local_bias, local_gain), "sp")
    pre_grad = (
        gain * inverse * (out_grad - total_bias / pixel_count - normed * total_gain / pixel_count)
    )
    return (pre_grad, local_gain, local_bias)


def reduce_grads(grads):
    summed = (
        lax.psum_scatter(grads[0], "dp", scatter_dimension=2, tiled=True),
        lax.psum_scatter(grads[1], "dp", scatter_dimension=2, tiled=True),
        lax.psum_scatter(grads[2], "dp", scatter_dimension=0, tiled=True),
        lax.psum_scatter(grads[3], "dp", scatter_dimension=1, tiled=True),
        lax.psum_scatter(grads[4], "dp", scatter_dimension=0, tiled=True),
        lax.psum_scatter(grads[5], "dp", scatter_dimension=0, tiled=True),
        lax.psum_scatter(grads[6], "dp", scatter_dimension=1, tiled=True),
        lax.psum_scatter(grads[7], "dp", scatter_dimension=1, tiled=True),
        lax.psum_scatter(grads[8], "dp", scatter_dimension=0, tiled=True),
        lax.psum_scatter(grads[9], "dp", scatter_dimension=0, tiled=True),
        lax.psum_scatter(grads[10], "dp", scatter_dimension=0, tiled=True),
        lax.psum_scatter(grads[11], "dp", scatter_dimension=0, tiled=True),
        lax.psum_scatter(grads[12], "dp", scatter_dimension=0, tiled=True),
        lax.psum_scatter(grads[13], "dp", scatter_dimension=0, tiled=True),
        lax.psum_scatter(grads[14], "dp", scatter_dimension=0, tiled=True),
    )
    return (
        lax.psum(summed[0].astype(jnp.bfloat16), "sp").astype(jnp.float32),
        lax.psum(summed[1].astype(jnp.bfloat16), "sp").astype(jnp.float32),
        lax.psum(summed[2].astype(jnp.bfloat16), "sp").astype(jnp.float32),
        lax.psum(summed[3].astype(jnp.bfloat16), "sp").astype(jnp.float32),
        lax.psum(summed[4].astype(jnp.bfloat16), "sp").astype(jnp.float32),
        lax.psum(summed[5].astype(jnp.bfloat16), "sp").astype(jnp.float32),
        lax.psum(summed[6].astype(jnp.bfloat16), "sp").astype(jnp.float32),
        lax.psum(summed[7].astype(jnp.bfloat16), "sp").astype(jnp.float32),
        lax.psum(summed[8].astype(jnp.bfloat16), "sp").astype(jnp.float32),
        lax.psum(summed[9].astype(jnp.bfloat16), "sp").astype(jnp.float32),
        lax.psum(summed[10].astype(jnp.bfloat16), "sp").astype(jnp.float32),
        lax.psum(summed[11].astype(jnp.bfloat16), "sp").astype(jnp.float32),
        lax.psum(summed[12].astype(jnp.bfloat16), "sp").astype(jnp.float32),
        lax.psum(summed[13].astype(jnp.bfloat16), "sp").astype(jnp.float32),
        lax.psum(summed[14].astype(jnp.bfloat16), "sp").astype(jnp.float32),
    )


def run_micro(
    video_part, feat_part, keep_part, stem_grad_in, section_grad_in, weights, pixel_count
):
    (
        rgb_k,
        stemd_k,
        first_k,
        middle_k,
        last_k,
        reduce_k,
        dfull_k,
        dhalf_k,
        expand_k,
        gain_one,
        bias_one,
        gain_two,
        bias_two,
        gain_three,
        bias_three,
    ) = weights
    keep_float = keep_part.astype(jnp.float32)
    keep_col = keep_float[:, None, None, None]
    next_col = jnp.roll(keep_float, -1)[:, None, None, None]
    frames_halo = with_halo(video_part, (("sp", 2),), 1)
    frames_wide = frames_halo.astype(jnp.float32)
    before = keep_col * (frames_wide - jnp.roll(frames_wide, 1, axis=0))
    after = next_col * (jnp.roll(frames_wide, -1, axis=0) - frames_wide)
    diff_stack = jnp.concatenate([before, after], axis=1).astype(jnp.bfloat16)
    stem_out = (tap_conv(frames_halo, rgb_k, False) + tap_conv(diff_stack, stemd_k, False)).astype(
        jnp.bfloat16
    )
    cot_halo = with_halo(stem_grad_in, (("sp", 2),), 1)
    direct_grad = tap_conv_back(cot_halo, rgb_k, False)
    diff_grad = tap_conv_back(cot_halo, stemd_k, False)
    before_grad = keep_col * diff_grad[:, :3]
    after_grad = next_col * diff_grad[:, 3:]
    video_grad = (
        direct_grad
        + before_grad
        - jnp.roll(before_grad, -1, axis=0)
        + jnp.roll(after_grad, 1, axis=0)
        - after_grad
    )
    rgb_grad = tap_kernel_grad(frames_halo, stem_grad_in, False)
    stemd_grad = tap_kernel_grad(diff_stack, stem_grad_in, False)
    row_count = feat_part.shape[1]
    col_count = feat_part.shape[2]
    first_pre = jnp.einsum("fhwc,cd->fhwd", feat_part, first_k, preferred_element_type=jnp.float32)
    normed_one, inverse_one, norm_one = norm_forward(
        first_pre, gain_one.astype(jnp.float32), bias_one.astype(jnp.float32), pixel_count
    )
    first_act = jax.nn.silu(norm_one)
    first_low = first_act.astype(jnp.bfloat16)
    reduced = jnp.einsum("fhwc,cd->fhwd", first_low, reduce_k, preferred_element_type=jnp.float32)
    change_low = (keep_col * (reduced - jnp.roll(reduced, 1, axis=0))).astype(jnp.bfloat16)
    change_halo = with_halo(change_low, (("sp", 1),), 2)
    near_rows = change_halo[:, 1 : row_count + 3]
    full_out = tap_conv(near_rows, dfull_k, True)
    pooled = pair_mean(change_halo.astype(jnp.float32)).astype(jnp.bfloat16)
    half_out = tap_conv(pooled, dhalf_k, True)
    combined_low = (full_out + pair_grow(half_out)).astype(jnp.bfloat16)
    gate_value = jax.nn.sigmoid(
        jnp.einsum("fhwc,cd->fhwd", combined_low, expand_k, preferred_element_type=jnp.float32)
    )
    gated_low = (first_act * (1.0 + gate_value)).astype(jnp.bfloat16)
    gated_halo = with_halo(gated_low, (("sp", 1),), 1)
    middle_pre = tap_conv(gated_halo, middle_k, True)
    normed_two, inverse_two, norm_two = norm_forward(
        middle_pre, gain_two.astype(jnp.float32), bias_two.astype(jnp.float32), pixel_count
    )
    second_low = jax.nn.silu(norm_two).astype(jnp.bfloat16)
    last_pre = jnp.einsum("fhwc,cd->fhwd", second_low, last_k, preferred_element_type=jnp.float32)
    normed_three, inverse_three, norm_three = norm_forward(
        last_pre, gain_three.astype(jnp.float32), bias_three.astype(jnp.float32), pixel_count
    )
    section_out = (feat_part.astype(jnp.float32) + norm_three).astype(jnp.bfloat16)
    out_grad = section_grad_in.astype(jnp.float32)
    last_grad, gain_three_grad, bias_three_grad = norm_backward(
        out_grad, normed_three, inverse_three, gain_three.astype(jnp.float32), pixel_count
    )
    last_grad_low = last_grad.astype(jnp.bfloat16)
    last_k_grad = jnp.einsum(
        "fhwc,fhwd->cd", second_low, last_grad_low, preferred_element_type=jnp.float32
    )
    second_grad = jnp.einsum(
        "fhwd,cd->fhwc", last_grad_low, last_k, preferred_element_type=jnp.float32
    ) * silu_slope(norm_two)
    middle_grad, gain_two_grad, bias_two_grad = norm_backward(
        second_grad, normed_two, inverse_two, gain_two.astype(jnp.float32), pixel_count
    )
    middle_low = middle_grad.astype(jnp.bfloat16)
    middle_halo = with_halo(middle_low, (("sp", 1),), 1)
    gated_grad = tap_conv_back(middle_halo, middle_k, True)
    middle_k_grad = tap_kernel_grad(gated_halo, middle_low, True)
    gate_grad = (gated_grad * first_act * gate_value * (1.0 - gate_value)).astype(jnp.bfloat16)
    expand_grad = jnp.einsum(
        "fhwc,fhwd->cd", combined_low, gate_grad, preferred_element_type=jnp.float32
    )
    combined_grad = jnp.einsum(
        "fhwd,cd->fhwc", gate_grad, expand_k, preferred_element_type=jnp.float32
    ).astype(jnp.bfloat16)
    half_grad = pair_total(combined_grad.astype(jnp.float32)).astype(jnp.bfloat16)
    stacked = jnp.concatenate([combined_grad, jnp.repeat(half_grad, 2, axis=1)], axis=2)
    stacked_halo = with_halo(stacked, (("sp", 1),), 2)
    full_grad_halo = stacked_halo[:, 1 : row_count + 3, :col_count]
    half_grad_halo = stacked_halo[:, 0::2, col_count:]
    change_grad = tap_conv_back(full_grad_halo, dfull_k, True) + 0.25 * pair_grow(
        tap_conv_back(half_grad_halo, dhalf_k, True)
    )
    dfull_grad = tap_kernel_grad(near_rows, combined_grad, True)
    dhalf_grad = tap_kernel_grad(pooled, half_grad, True)
    weighted = keep_col * change_grad
    reduced_grad = (weighted - jnp.roll(weighted, -1, axis=0)).astype(jnp.bfloat16)
    reduce_grad = jnp.einsum(
        "fhwc,fhwd->cd", first_low, reduced_grad, preferred_element_type=jnp.float32
    )
    first_sum = gated_grad * (1.0 + gate_value) + jnp.einsum(
        "fhwd,cd->fhwc", reduced_grad, reduce_k, preferred_element_type=jnp.float32
    )
    first_grad, gain_one_grad, bias_one_grad = norm_backward(
        first_sum * silu_slope(norm_one),
        normed_one,
        inverse_one,
        gain_one.astype(jnp.float32),
        pixel_count,
    )
    first_grad_low = first_grad.astype(jnp.bfloat16)
    first_k_grad = jnp.einsum(
        "fhwc,fhwd->cd", feat_part, first_grad_low, preferred_element_type=jnp.float32
    )
    input_grad = (
        out_grad
        + jnp.einsum("fhwd,cd->fhwc", first_grad_low, first_k, preferred_element_type=jnp.float32)
    ).astype(jnp.bfloat16)
    grads = (
        rgb_grad,
        stemd_grad,
        first_k_grad,
        middle_k_grad,
        last_k_grad,
        reduce_grad,
        dfull_grad,
        dhalf_grad,
        expand_grad,
        gain_one_grad,
        bias_one_grad,
        gain_two_grad,
        bias_two_grad,
        gain_three_grad,
        bias_three_grad,
    )
    return ((stem_out, video_grad, section_out, input_grad), grads)


def add_trees(first_tree, second_tree):
    if first_tree is None:
        return second_tree
    return jax.tree.map(
        lambda left_part, right_part: left_part + right_part, first_tree, second_tree
    )


def on_device(
    clip_video,
    section_input,
    keep_mask,
    w_rgb,
    w_stem_diff,
    w_first,
    w_middle,
    w_last,
    w_reduce,
    w_diff_full,
    w_diff_half,
    w_expand,
    gain_first,
    bias_first,
    gain_middle,
    bias_middle,
    gain_last,
    bias_last,
    stem_cot,
    section_cot,
):
    micro_frames = clip_video.shape[0] // MICRO
    pixel_count = (
        micro_frames * section_input.shape[1] * lax.axis_size("sp") * section_input.shape[2]
    )
    results = []
    grad_totals = None
    for micro_index in range(MICRO):
        weights = (
            lax.all_gather(w_rgb, "dp", axis=2, tiled=True),
            lax.all_gather(w_stem_diff, "dp", axis=2, tiled=True),
            lax.all_gather(w_first, "dp", axis=0, tiled=True),
            lax.all_gather(w_middle, "dp", axis=1, tiled=True),
            lax.all_gather(w_last, "dp", axis=0, tiled=True),
            lax.all_gather(w_reduce, "dp", axis=0, tiled=True),
            lax.all_gather(w_diff_full, "dp", axis=1, tiled=True),
            lax.all_gather(w_diff_half, "dp", axis=1, tiled=True),
            lax.all_gather(w_expand, "dp", axis=0, tiled=True),
            lax.all_gather(gain_first, "dp", axis=0, tiled=True),
            lax.all_gather(bias_first, "dp", axis=0, tiled=True),
            lax.all_gather(gain_middle, "dp", axis=0, tiled=True),
            lax.all_gather(bias_middle, "dp", axis=0, tiled=True),
            lax.all_gather(gain_last, "dp", axis=0, tiled=True),
            lax.all_gather(bias_last, "dp", axis=0, tiled=True),
        )
        low_end = micro_index * micro_frames
        high_end = low_end + micro_frames
        outputs, grads = run_micro(
            clip_video[low_end:high_end],
            section_input[low_end:high_end],
            keep_mask[low_end:high_end],
            stem_cot[low_end:high_end],
            section_cot[low_end:high_end],
            weights,
            pixel_count,
        )
        results.append(outputs)
        grad_totals = add_trees(grad_totals, reduce_grads(grads))
    stem_features = jnp.concatenate([item[0] for item in results], axis=0)
    video_grad = jnp.concatenate([item[1] for item in results], axis=0)
    section_output = jnp.concatenate([item[2] for item in results], axis=0)
    section_input_grad = jnp.concatenate([item[3] for item in results], axis=0)
    return (
        stem_features,
        video_grad,
        section_output,
        section_input_grad,
        grad_totals[0],
        grad_totals[1],
        grad_totals[2],
        grad_totals[3],
        grad_totals[4],
        grad_totals[5],
        grad_totals[6],
        grad_totals[7],
        grad_totals[8],
        grad_totals[9],
        grad_totals[10],
        grad_totals[11],
        grad_totals[12],
        grad_totals[13],
        grad_totals[14],
    )


F32 = jnp.float32
BF16 = jnp.bfloat16
MESH_ID = pl.DeviceIdType.MESH
GROUP = 8
LANES = 128
STEP = 32
PART = 2


def dot_nn(left, right):
    return lax.dot_general(left, right, (((1,), (0,)), ((), ())), preferred_element_type=F32)


def dot_nt(left, right):
    return lax.dot_general(left, right, (((1,), (1,)), ((), ())), preferred_element_type=F32)


def dot_tn(left, right):
    return lax.dot_general(left, right, (((0,), (0,)), ((), ())), preferred_element_type=F32)


def shift_down(values, count):
    size = values.shape[0]
    column = lax.broadcasted_iota(jnp.int32, values.shape, 0) & 15
    return jnp.where(column < count, 0.0, pltpu.roll(values, count, 0))


def shift_up(values, count):
    size = values.shape[0]
    column = lax.broadcasted_iota(jnp.int32, values.shape, 0) & 15
    return jnp.where(column >= 16 - count, 0.0, pltpu.roll(values, size - count, 0))


def pair_sum(values):
    size = values.shape[0]
    parity = lax.broadcasted_iota(jnp.int32, values.shape, 0) & 1
    return values + jnp.where(parity == 0, pltpu.roll(values, size - 1, 0), pltpu.roll(values, 1, 0))


def band_table(rows):
    table = np.zeros((rows, 96, 3 * LANES), np.float32)
    for i in range(rows):
        for a in range(3):
            for b in range(3):
                for ch in range(9):
                    base = (b * 3 + ch // 3) * 32
                    row = i + a - 1
                    if row < 0:
                        n = base + 24 + (ch % 3) * 2
                    elif row >= rows:
                        n = base + 24 + (ch % 3) * 2 + 1
                    else:
                        n = base + (ch % 3) * 8 + row
                    table[i, ch * 9 + 3 * a + b, n] = 1.0
    return table


def portions(first_rows, taps, last_rows):
    cut = first_rows // 2
    return (
        (("xyz", 0, cut), ("yzx", cut, first_rows - cut)),
        (("xyz", 0, 2), ("yzx", 2, 4), ("xyz", 6, taps - 6)),
        (("xyz", 0, last_rows // 2), ("yzx", last_rows // 2, last_rows // 2)),
    )


ORDER = {
    "dwl": ("l0", "l1"),
    "bn2": ("l1",),
    "mid": ("l0",),
    "own": ("m1",),
    "gate": ("m0", "l1"),
    "diff": ("d", "l0", "l1"),
    "bn1": ("r", "d", "l1", "l0",),
    "fg": ("m2", "m0",),
    "dwf": ("f0", "f1", "m1", "r", "d", "l0",),
    "add": ("f0", "f1"),
    "in0": ("m1", "m0", "l0",),
    "in1": ("l1", "r", "d"),
    "in2": ("m2",),
    "in3": ("m1", "m0", "l0", "r", "d"),
    "t0": ("f0", "f1", "m2", "l1", "m1"),
    "t1": ("f0", "f1", "m2", "m0", "m1", "r", "d", "l0", "l1"),
    "t2": ("f0", "f1", "m2", "m0", "m1", "r", "d", "l0", "l1"),
    "t4": ("f0", "f1", "m2", "m1", "m0", "r", "d", "l0", "l1",),
    "t5": ("f0", "f1", "m2", "m1", "m0", "r", "d", "l0", "l1",),
    "t3": ("f0", "f1", "m2", "m0", "m1", "r", "d", "l0", "l1"),
}


def silu_parts(values):
    sig = jax.nn.sigmoid(values)
    return values * sig, sig * (1.0 + values * (1.0 - sig))


def whole_kernel(
    sizes, keep, clip, rgb, stemd, g1, b1, g2, b2, g3, b3, band, x_hbm, ct_hbm, sc_hbm, wf_in, wm_in, wl_in, wr_in, wd0_in, wd1_in, we_in,
    so_hbm, vg_out, out_hbm, ig_hbm, fbf_hbm, fbm_hbm, fbl_hbm, or_out, od_out, oe_out, osm_out,
    ssem, rsem, lsem, wf, wm, wl, wr, wd, we, x3, ct3, sc, so, ust, uprev, unext, small, sm, tf, tff, tb, dg,
    vgh, vgr, stg, stgr, stat_s, stat_r, st3_s, st3_r, z1, fab, gt, rd, chb, chr_, cs, ps, comb,
    gb, gr, gs, z2, sab, z3, lgb, cgx, cgr, cgs, hgs, fgb, ost,
    g_first, g_mid, g_last, g_diff, g_re, rcd, ryd, rzd, fdx, rxd, fdo, rcr, ryr, rzr, frx, rxr, fbf, fbm, fbl, sms, smr, *bufs,
):
    D, S, NF = sizes
    DZ, SX = D // 2, S // 2
    NG = NF // GROUP
    NW = NF * 16
    GW = GROUP * 16
    dp, sp = lax.axis_index("dp"), lax.axis_index("sp")
    z, y = dp // 2, dp % 2
    x, c = sp // 2, sp % 2
    oy, oc = 1 - y, 1 - c
    q_own = c * SX + x

    def at_zy(zz, yy):
        return (zz * 2 + yy, sp)

    y_peer = at_zy(z, oy)
    c_peer = (dp, x * 2 + oc)

    z_bits = [1 << n for n in range(DZ.bit_length() - 1)]

    def z_pair(bit):
        return z + bit - 2 * bit * ((z // bit) % 2)

    def z_class(zz, bit):
        return [zz % (2 * bit) + 2 * bit * j for j in range(DZ // (2 * bit))]

    def x_to(k):
        return lax.rem(x + k, SX)

    def x_from(k):
        return lax.rem(x + SX - k, SX)

    def x_peer(k):
        return (dp, x_to(k) * 2 + c)

    sp_peers = [(dp, lax.rem(sp + k, S)) for k in range(1, S)]
    dp_peers = [(lax.rem(dp + k, D), sp) for k in range(1, D)]
    has_prev, has_next = sp > 0, sp < S - 1
    prev_dev, next_dev = (dp, sp - 1), (dp, sp + 1)

    counters = {"r": 0, "l": 0}
    sends = []

    def bundle(whole):
        i = counters["r"]
        counters["r"] += 1

        def start(src, dst, dev):
            pltpu.make_async_remote_copy(
                src_ref=src, dst_ref=dst, send_sem=ssem.at[i], recv_sem=rsem.at[i],
                device_id=dev, device_id_type=MESH_ID,
            ).start()

        def wait():
            pltpu.make_async_copy(whole, whole, rsem.at[i]).wait()

        def finish():
            pltpu.make_async_copy(whole, whole, ssem.at[i]).wait()

        sends.append(finish)
        return start, wait

    def remote(src, dst, dev):
        start, wait = bundle(dst)
        start(src, dst, dev)
        return wait

    def to_peers(src, dst_of, peers, whole):
        start, wait = bundle(whole)
        for k, peer in enumerate(peers):
            start(src, dst_of(k), peer)
        return wait

    def local(src, dst):
        i = counters["l"]
        counters["l"] += 1
        copy = pltpu.make_async_copy(src, dst, lsem.at[i])
        copy.start()
        return copy

    @pl.when(sp == 0)
    def _():
        uprev[...] = jnp.zeros_like(uprev)
        vgr[0] = jnp.zeros(vgr.shape[1:], F32)
        chr_[0] = jnp.zeros(chr_.shape[1:], BF16)
        gr[0] = jnp.zeros(gr.shape[1:], BF16)
        cgr[0] = jnp.zeros(cgr.shape[1:], BF16)

    @pl.when(sp == S - 1)
    def _():
        unext[...] = jnp.zeros_like(unext)
        vgr[1] = jnp.zeros(vgr.shape[1:], F32)
        chr_[1] = jnp.zeros(chr_.shape[1:], BF16)
        gr[1] = jnp.zeros(gr.shape[1:], BF16)
        cgr[1] = jnp.zeros(cgr.shape[1:], BF16)

    barrier = pltpu.get_barrier_semaphore()
    for peer in sp_peers + dp_peers:
        pl.semaphore_signal(barrier, inc=1, device_id=peer, device_id_type=MESH_ID)
    per = D * LANES // 512
    rows_last = 2048 // D // LANES
    small[...] = jnp.zeros_like(small)
    for ch in range(9):
        small[0:8, ch * 9 : ch * 9 + 9] = (rgb[ch] if ch < 3 else stemd[ch - 3]).astype(F32)
    place = lax.broadcasted_iota(jnp.int32, (1, LANES), 1) // (LANES // per)
    for j, ref in enumerate((g1, b1, g2, b2)):
        row = jnp.concatenate([ref[...].astype(F32)] * per, axis=1)
        small[8 + j : 9 + j, :] = jnp.where(place == lax.rem(dp, per), row, 0.0)
    for j, ref in enumerate((g3, b3)):
        small[12 + j * rows_last : 12 + (j + 1) * rows_last, :] = ref[...].astype(F32)
    own_small = local(small, sm.at[dp])
    own = [
        local(wf_in, wf.at[dp]), local(wd0_in, wd.at[0, :, dp]), local(wd1_in, wd.at[1, :, dp]),
        local(wr_in, wr.at[dp]), local(we_in, we.at[dp]), local(wm_in, wm.at[:, dp]), local(wl_in, wl.at[dp]),
    ]

    def load_cot(part):
        lo = part * PART
        return local(sc_hbm.at[pl.ds(lo, PART)], sc.at[pl.ds(lo % (2 * PART), PART)])

    load_sc = [load_cot(0), load_cot(1)]
    load_x = [local(x_hbm.at[:, r], x3.at[pl.ds(r * NF, NF)]) for r in range(2)]
    load_ct = [local(ct_hbm.at[:, r], ct3.at[pl.ds(r * NF, NF)]) for r in range(2)]
    pl.semaphore_wait(barrier, S - 1 + D - 1)

    halo_waits = []

    def halo(to_prev, to_next, from_prev, from_next, land_prev, land_next):
        i = counters["r"]
        counters["r"] += 2

        def up():
            return pltpu.make_async_remote_copy(
                src_ref=to_prev, dst_ref=land_next, send_sem=ssem.at[i], recv_sem=rsem.at[i],
                device_id=prev_dev, device_id_type=MESH_ID)

        def down():
            return pltpu.make_async_remote_copy(
                src_ref=to_next, dst_ref=land_prev, send_sem=ssem.at[i + 1], recv_sem=rsem.at[i + 1],
                device_id=next_dev, device_id_type=MESH_ID)

        @pl.when(has_prev)
        def _():
            up().start()

        @pl.when(has_next)
        def _():
            down().start()

        def wait():
            @pl.when(has_prev)
            def _():
                down().wait_recv()

            @pl.when(has_next)
            def _():
                up().wait_recv()

        def finish():
            @pl.when(has_prev)
            def _():
                up().wait_send()

            @pl.when(has_next)
            def _():
                down().wait_send()

        halo_waits.append(finish)
        return wait, finish

    wait_small = to_peers(small, lambda k: sm.at[dp], dp_peers, sm.at[pl.ds(0, D - 1)])
    wait_edges, _ = halo(clip, clip, None, None, uprev, unext)

    def gather(mode, dst, eager=True):
        wide = {"A": 1, "B": SX, "D": S}[mode]
        first_q = {"A": q_own, "B": c * SX, "D": 0}[mode]
        only = pl.ds(dp, 1)
        z_links = {bit: bundle(dst(pl.ds(0, DZ // (2 * bit)), first_q, wide)) for bit in z_bits}
        y_start, y_wait = bundle(dst(pl.ds(0, DZ), first_q, wide))
        if mode == "A":
            x_start, x_wait = bundle(dst(pl.ds(0, (D - 1) * (SX - 1)), first_q, 1))
        if mode != "D":
            c_start, c_wait = bundle(dst(pl.ds(0, D - 1), c * SX, SX))
        mine = dst(pl.ds(dp, 1), first_q, wide)
        for bit in reversed(z_bits):
            z_links[bit][0](mine, mine, at_zy(z_pair(bit), y))
        y_start(mine, mine, y_peer)
        yield

        def to_x(part):
            for k in range(1, SX):
                x_start(part, part, x_peer(k))

        def fan(part):
            if eager and mode == "A":
                to_x(part)
            if mode != "D":
                c_start(part, part, c_peer)

        for bit in reversed(z_bits):
            z_links[bit][1]()
            for zz in z_class(z_pair(bit), bit):
                part = dst(pl.ds(zz * 2 + y, 1), first_q, wide)
                for lower in z_bits:
                    if lower < bit:
                        z_links[lower][0](part, part, at_zy(z_pair(lower), y))
                y_start(part, part, y_peer)
                fan(part)
            yield
        y_wait()
        for zz in range(DZ):
            fan(dst(pl.ds(zz * 2 + oy, 1), first_q, wide))
        if mode == "A" and not eager:
            yield "x"
            for n in range(1, D):
                to_x(dst(pl.ds(lax.rem(dp + n, D), 1), first_q, wide))
        yield
        if mode == "A":
            x_wait()
            for k in range(1, SX):
                for n in range(1, D):
                    part = dst(pl.ds(lax.rem(dp + n, D), 1), c * SX + x_from(k), 1)
                    c_start(part, part, c_peer)
            yield
        if mode != "D":
            c_wait()

    def lane_block(index, width, count):
        return pl.ds(pl.multiple_of(index * width, width), width * count)

    fr, fw = wf_in.shape[0], wf_in.shape[1] // S
    mw = wm_in.shape[2] // S
    lr, lw = wl_in.shape[0], wl_in.shape[1] // S

    def first_part(mode, lo, n):
        rows = pl.ds(lo, n)
        return gather(mode, lambda d, q, w: wf.at[d, rows, lane_block(q, fw, w)], True)

    def mid_part(mode, lo, n):
        rows = pl.ds(lo, n)
        return gather(mode, lambda d, q, w: wm.at[rows, d, :, lane_block(q, mw, w)])

    def last_part(mode, lo, n):
        rows = pl.ds(lo, n)
        return gather(mode, lambda d, q, w: wl.at[d, rows, lane_block(q, lw, w)])

    for copy in own:
        copy.wait()
    part_b = fr * 3 // 8
    part_a = (fr - part_b) // 2
    chunks = [
        (0, first_part("A", 0, part_a)),
        (0, first_part("B", 2 * part_a, part_b)),
        (0, first_part("A", part_a, part_a)),
        (1, gather("D", lambda d, q, w: wr.at[d])),
        (1, gather("B", lambda d, q, w: wd.at[c, :, d])),
        (1, gather("D", lambda d, q, w: we.at[d])),
        (1, mid_part("A", 0, 2)), (2, mid_part("B", 2, 3)), (2, mid_part("A", 5, 2)), (3, mid_part("A", 7, 2)),
        (4, last_part("B", 0, lr // 2)), (4, last_part("A", lr // 2, lr // 2)),
    ]
    slot = [0]
    arrived = set()

    held = set()

    def pump(free=0, low=0, high=99):
        for n, (start, chunk) in enumerate(chunks):
            if start > slot[0] or n in arrived or not low <= n < high:
                continue
            if n in held:
                if free == 0:
                    continue
                free -= 1
                held.remove(n)
            try:
                if next(chunk) == "x":
                    held.add(n)
            except StopIteration:
                arrived.add(n)
        slot[0] += 1

    def need(low, high):
        while not arrived.issuperset(range(low, high)):
            pump(len(chunks), low, high)

    pump()

    own_small.wait()
    wait_small()
    wt = sm[:, 0:8, :].reshape(D * 8, LANES)[:, 0:96].astype(BF16)
    for i in range(8):
        rows = dot_nn(wt, band[i])
        for n in range(3):
            tff[n, pl.ds(i, D * 8, stride=8), :] = rows[:, n * LANES : (n + 1) * LANES]
    for n in range(3):
        columns = min(288 - n * LANES, LANES)
        tf[:, n * LANES : n * LANES + columns] = tff[n, :, 0:columns].astype(BF16)
        tb[n * LANES : n * LANES + columns, :] = tff[n].T[0:columns].astype(BF16)

    def mid_vec(j):
        parts = []
        for m in range(D // per):
            row = sm[m * per, 8 + j : 9 + j, :]
            for n in range(1, per):
                row = row + sm[m * per + n, 8 + j : 9 + j, :]
            parts.append(row)
        return jnp.concatenate(parts, axis=1)

    def last_vec(j):
        return jnp.concatenate(
            [sm[d, 8 + j + n : 9 + j + n, :] for d in range(D) for n in range(rows_last)], axis=1)

    gain_1, bias_1, gain_2, bias_2 = [mid_vec(j) for j in range(4)]
    gain_3, bias_3 = last_vec(4), last_vec(4 + rows_last)

    wait_edges()
    row8 = lax.broadcasted_iota(jnp.int32, (8, LANES), 0)

    def load_frame(f, carry):
        ust[f, 0:24, :] = clip[f].astype(F32)
        above, below = uprev[f].astype(F32), unext[f].astype(F32)
        halo_rows = jnp.zeros((8, LANES), F32)
        for ch in range(3):
            halo_rows = jnp.where(row8 == 2 * ch, above[ch * 8 + 7 : ch * 8 + 8], halo_rows)
            halo_rows = jnp.where(row8 == 2 * ch + 1, below[ch * 8 : ch * 8 + 1], halo_rows)
        ust[f, 24:32, :] = halo_rows
        return carry

    lax.fori_loop(0, NF, load_frame, 0)
    zt = tff
    zt[...] = jnp.zeros_like(zt)

    def stem_frame(f, carry):
        before_at, after_at = lax.rem(f + NF - 1, NF), lax.rem(f + 1, NF)
        k_here, k_next = keep[f].astype(F32), keep[after_at].astype(F32)
        frame = ust[f]
        stacked = jnp.concatenate(
            [frame, k_here * (frame - ust[before_at]), k_next * (ust[after_at] - frame)], axis=0)
        stacked = stacked.astype(BF16).astype(F32)
        lane = lax.broadcasted_iota(jnp.int32, stacked.shape, 1)
        left = jnp.where(lane == 0, 0.0, pltpu.roll(stacked, 1, 1))
        right = jnp.where(lane == LANES - 1, 0.0, pltpu.roll(stacked, LANES - 1, 1))
        taps = jnp.concatenate([left, stacked, right], axis=0).astype(BF16)
        place = lax.rem(f, 2 * PART)
        cot = sc[place]
        so[place] = dot_nn(tf[...], taps).astype(BF16)
        back = dot_nn(tb[...], cot)
        dg[f] = (
            jnp.where(lane == LANES - 1, 0.0, pltpu.roll(back[0:96], LANES - 1, 1))
            + back[96:192]
            + jnp.where(lane == 0, 0.0, pltpu.roll(back[192:288], 1, 1)))
        cross = dot_nt(cot, taps)
        for n in range(3):
            columns = min(288 - n * LANES, LANES)
            zt[n, :, 0:columns] += cross[:, n * LANES : n * LANES + columns]
        return carry

    store_so = []
    for part in range(NF // PART):
        lo = part * PART
        load_sc[part].wait()
        if part >= 2:
            store_so[part - 2].wait()
        lax.fori_loop(lo, lo + PART, stem_frame, 0)
        store_so.append(local(so.at[pl.ds(lo % (2 * PART), PART)], so_hbm.at[pl.ds(lo, PART)]))
        if part + 2 < NF // PART:
            load_sc.append(load_cot(part + 2))
        if part % 2:
            pump()
    for copy in store_so[-2:]:
        copy.wait()

    def video_frame(f, carry):
        before_at, after_at = lax.rem(f + NF - 1, NF), lax.rem(f + 1, NF)
        k_here, k_next = keep[f].astype(F32), keep[after_at].astype(F32)
        total = (
            dg[f, 0:32] + k_here * dg[f, 32:64] - k_next * dg[after_at, 32:64]
            + k_here * dg[before_at, 64:96] - k_next * dg[f, 64:96])
        vg_out[f] = total[0:24]
        vgh[f] = total[24:32]
        return carry

    lax.fori_loop(0, NF, video_frame, 0)
    wait_video, _ = halo(vgh, vgh, None, None, vgr.at[0], vgr.at[1])

    stem_grad = jnp.zeros((D * 8, 96), F32)
    for i in range(8):
        for n in range(3):
            part = zt[n, pl.ds(i, D * 8, stride=8), :]
            high = part.astype(BF16)
            low = (part - high.astype(F32)).astype(BF16)
            table = band[i, :, n * LANES : (n + 1) * LANES]
            stem_grad = stem_grad + dot_nt(high, table) + dot_nt(low, table)
    stg[...] = jnp.concatenate([stem_grad, jnp.zeros((D * 8, LANES - 96), F32)], axis=1)
    wait_stem = to_peers(stg, lambda k: stgr.at[k], sp_peers, stgr)

    def rows_loop(group, fn, init):
        def body(i, carry):
            start = (i // (GW // STEP)) * NW + group * GW + (i % (GW // STEP)) * STEP
            return fn(pl.multiple_of(start, STEP), carry)
        return lax.fori_loop(0, 2 * (GW // STEP), body, init)

    def fold(values):
        return values.reshape(STEP // 8, 8, values.shape[1]).sum(axis=0)

    def sp_send(i, parts):
        width = parts[0].shape[1]
        fill = [jnp.zeros((8 - len(parts), width), F32)] if len(parts) < 8 else []
        stat_s[i] = jnp.concatenate(parts + fill, axis=0)
        return to_peers(stat_s.at[i], lambda k: stat_r.at[i, k], sp_peers, stat_r.at[i])

    def sp_total(i, wait):
        wait()
        total = stat_s[i]
        for k in range(S - 1):
            total = total + stat_r[i, k]
        return total

    pixels = jnp.float32(GROUP * 2 * S * 16)
    inv_pixels = 1.0 / (GROUP * 2 * S * 16)

    def two_sums(ref):
        parts = []
        for group in range(NG):
            def add(start, carry):
                value = ref[pl.ds(start, STEP), :]
                return carry[0] + fold(value), carry[1] + fold(value * value)
            zero = jnp.zeros((8, ref.shape[1]), F32)
            one, two = rows_loop(group, add, (zero, zero))
            parts += [jnp.sum(one, axis=0, keepdims=True), jnp.sum(two, axis=0, keepdims=True)]
        return parts

    def moments(total, row):
        mean = total[row : row + 1] * inv_pixels
        variance = total[row + 1 : row + 2] * inv_pixels - mean * mean
        return mean, lax.rsqrt(variance + EPS)

    for copy in load_x:
        copy.wait()
    need(0, 3)
    xs = x3[...].reshape(2 * NW, x3.shape[2])
    for n in range(2):
        z1[:, n * 256 : (n + 1) * 256] = dot_nn(xs, wf[:, :, n * 256 : (n + 1) * 256].reshape(x3.shape[2], 256))
    copies = sp_send(0, two_sums(z1))
    pump(2)
    need(3, 6)
    total = sp_total(0, copies)
    inv_1 = []
    for group in range(NG):
        mean, inv = moments(total, 2 * group)
        inv_1.append(inv)

        def apply_1(start, carry):
            normed = (z1[pl.ds(start, STEP), :] - mean) * inv
            act = jax.nn.silu(gain_1 * normed + bias_1)
            z1[pl.ds(start, STEP), :] = normed
            z3[pl.ds(start, STEP), 0:512] = act
            fab[pl.ds(start, STEP), :] = act.astype(BF16)
            return carry
        rows_loop(group, apply_1, 0)

    rd[...] = dot_nn(fab[...], wr[...].reshape(512, LANES))
    for r in range(2):
        for f in range(NF):
            here = r * NW + f * 16
            past = r * NW + ((f - 1) % NF) * 16
            diff = keep[f].astype(F32) * (rd[here : here + 16, :] - rd[past : past + 16, :])
            chb[r, f * 16 : f * 16 + 16, :] = diff.astype(BF16)
    wait_change, free_change = halo(chb, chb, None, None, chr_.at[0], chr_.at[1])

    def put_shifts(ref, at, values, count, flip):
        width = values.shape[1]
        down, up = shift_down(values, count), shift_up(values, count)
        low, high = (up, down) if flip else (down, up)
        ref[at, :, 0:width] = low.astype(BF16)
        ref[at, :, width : 2 * width] = values.astype(BF16)
        ref[at, :, 2 * width : 3 * width] = high.astype(BF16)

    change = [chb[r].astype(F32) for r in range(2)]
    for r in range(2):
        put_shifts(cs, 1 + r, change[r], 1, False)

    def pool(upper, lower):
        return (pair_sum(upper + lower) * 0.25).astype(BF16).astype(F32)

    put_shifts(ps, 1, pool(change[0], change[1]), 2, False)
    pump(2)
    wait_change()
    above = [chr_[0, r].astype(F32) for r in range(2)]
    below = [chr_[1, r].astype(F32) for r in range(2)]
    put_shifts(cs, 0, above[1], 1, False)
    put_shifts(cs, 3, below[0], 1, False)
    put_shifts(ps, 0, pool(above[0], above[1]), 2, False)
    put_shifts(ps, 2, pool(below[0], below[1]), 2, False)
    full = jnp.zeros((2 * NW, LANES), F32)
    half = jnp.zeros((NW, LANES), F32)
    for a in range(3):
        full = full + dot_nn(cs[a : a + 2].reshape(2 * NW, 384), wd[0, 3 * a : 3 * a + 3].reshape(384, LANES))
        half = half + dot_nn(ps[a], wd[1, 3 * a : 3 * a + 3].reshape(384, LANES))
    comb[...] = (full + jnp.concatenate([half, half], axis=0)).astype(BF16)
    gt[...] = dot_nn(comb[...], we[...].reshape(LANES, 512))

    def apply_gate(i, carry):
        start = pl.multiple_of(i * STEP, STEP)
        gate = jax.nn.sigmoid(gt[pl.ds(start, STEP), :])
        gt[pl.ds(start, STEP), :] = gate
        gated = (z3[pl.ds(start, STEP), 0:512] * (1.0 + gate)).astype(BF16)
        gb[pl.ds(start, STEP), :] = gated
        return carry

    lax.fori_loop(0, 2 * NW // STEP, apply_gate, 0)
    wait_gated, free_gated = halo(gb.at[pl.ds(0, NW)], gb.at[pl.ds(NW, NW)], None, None, gr.at[0], gr.at[1])

    def spread(dst, at, src_fn, flip):
        def body(i, carry):
            start = pl.multiple_of(i * STEP, STEP)
            values = src_fn(start).astype(F32)
            down, up = shift_down(values, 1), shift_up(values, 1)
            low, high = (up, down) if flip else (down, up)
            dst[at, pl.ds(start, STEP), 0:512] = low.astype(BF16)
            dst[at, pl.ds(start, STEP), 512:1024] = values.astype(BF16)
            dst[at, pl.ds(start, STEP), 1024:1536] = high.astype(BF16)
            return carry
        lax.fori_loop(0, NW // STEP, body, 0)

    for r in range(2):
        spread(gs, 1 + r, lambda start, r=r: gb[pl.ds(r * NW + start, STEP), :], False)

    def taps_of(a):
        return wm[3 * a : 3 * a + 3].reshape(1536, 512)

    need(6, 10)
    z2[...] = dot_nn(gs[1:3].reshape(2 * NW, 1536), taps_of(1))
    z2[0:NW, :] += dot_nn(gs[2], taps_of(2))
    z2[NW : 2 * NW, :] += dot_nn(gs[1], taps_of(0))
    wait_gated()
    spread(gs, 0, lambda start: gr[0, pl.ds(start, STEP), :], False)
    spread(gs, 3, lambda start: gr[1, pl.ds(start, STEP), :], False)
    z2[0:NW, :] += dot_nn(gs[0], taps_of(0))
    z2[NW : 2 * NW, :] += dot_nn(gs[3], taps_of(2))
    copies = sp_send(1, two_sums(z2))
    need(10, 12)
    for copy in load_ct:
        copy.wait()
    total = sp_total(1, copies)
    inv_2 = []
    for group in range(NG):
        mean, inv = moments(total, 2 * group)
        inv_2.append(inv)

        def apply_2(start, carry):
            normed = (z2[pl.ds(start, STEP), :] - mean) * inv
            z2[pl.ds(start, STEP), :] = normed
            sab[pl.ds(start, STEP), :] = jax.nn.silu(gain_2 * normed + bias_2).astype(BF16)
            return carry
        rows_loop(group, apply_2, 0)

    def ct_rows(start, lo, width):
        return ct3[pl.ds(start // 16, STEP // 16), :, lo : lo + width].reshape(STEP, width).astype(F32)

    def x_rows(start, lo, width):
        return x3[pl.ds(start // 16, STEP // 16), :, lo : lo + width].reshape(STEP, width).astype(F32)

    last_copies = []
    for n in range(4):
        lo = n * 512
        z3[:, lo : lo + 512] = dot_nn(sab[...], wl[:, :, lo : lo + 512].reshape(512, 512))
        parts = []
        for group in range(NG):
            def add_3(start, carry):
                value = z3[pl.ds(start, STEP), lo : lo + 512]
                cot = ct_rows(start, lo, 512)
                return (carry[0] + fold(value), carry[1] + fold(value * value),
                        carry[2] + fold(cot), carry[3] + fold(cot * value))
            zero = jnp.zeros((8, 512), F32)
            sums = rows_loop(group, add_3, (zero, zero, zero, zero))
            parts += [jnp.sum(item, axis=0, keepdims=True) for item in sums]
        st3_s[n] = jnp.concatenate(parts, axis=0)
        last_copies.append(to_peers(st3_s.at[n], lambda k, n=n: st3_r.at[n, k], sp_peers, st3_r.at[n]))
    gain_3_grad, bias_3_grad = [], []
    stores = []

    def free_part():
        if len(stores) >= 2:
            for copy in stores[-2]:
                copy.wait()

    def store_part(n, target):
        stores.append([local(ost.at[n % 2, pl.ds(r * NF, NF)], target.at[:, r, :, pl.ds(n * 512, 512)]) for r in range(2)])

    for n in range(4):
        lo = n * 512
        free_part()
        last_copies[n]()
        total = st3_s[n]
        for k in range(S - 1):
            total = total + st3_r[n, k]
        gain, bias = gain_3[:, lo : lo + 512], bias_3[:, lo : lo + 512]
        gain_sum = bias_sum = jnp.zeros((1, 512), F32)
        for group in range(NG):
            row = 4 * group
            mean, inv = moments(total, row)
            cot_sum = total[row + 2 : row + 3]
            cot_normed = inv * (total[row + 3 : row + 4] - mean * cot_sum)
            gain_sum, bias_sum = gain_sum + cot_normed, bias_sum + cot_sum
            cot_mean, slope_mean = cot_sum * inv_pixels, cot_normed * inv_pixels
            scale = gain * inv

            def apply_3(start, carry):
                normed = (z3[pl.ds(start, STEP), lo : lo + 512] - mean) * inv
                cot = ct_rows(start, lo, 512)
                out = x_rows(start, lo, 512) + gain * normed + bias
                ost[n % 2, pl.ds(start // 16, STEP // 16)] = out.astype(BF16).reshape(STEP // 16, 16, 512)
                lgb[pl.ds(start, STEP), lo : lo + 512] = (
                    scale * (cot - cot_mean - normed * slope_mean)).astype(BF16)
                return carry
            rows_loop(group, apply_3, 0)
        store_part(n, out_hbm)
        gain_3_grad.append(gain_sum)
        bias_3_grad.append(bias_sum)

    def each(count, fn):
        def body(i, carry):
            fn(i)
            return carry
        lax.fori_loop(0, count, body, 0)

    def share(block, several):
        x_start, x_wait = bundle(several.at[pl.ds(0, SX - 1)])
        c_start, c_wait = bundle(several)
        for k in range(1, SX):
            x_start(block(q_own), block(q_own), x_peer(k))
        c_start(block(q_own), block(q_own), c_peer)
        yield
        x_wait()
        for k in range(1, SX):
            part = block(c * SX + x_from(k))
            c_start(part, part, c_peer)
        yield
        c_wait()

    def z_steps(part, rz, add):
        at = 0
        for bit in z_bits:
            keep_z, give_z = z_class(z, bit), z_class(z_pair(bit), bit)
            start, wait = bundle(rz.at[pl.ds(at, len(keep_z))])
            for j, zz in enumerate(give_z):
                start(part(zz), rz.at[at + j], at_zy(z_pair(bit), y))
            yield
            wait()
            for j, zz in enumerate(keep_z):
                add(part(zz), rz.at[at + j])
            at += len(keep_z)

    def wide_first(grad, lo, n, order, rc, rx, ry, rz, fb):
        rows = pl.ds(lo, n)
        half = pl.ds(c * SX, SX)
        mine = q_own

        def add(dst, *others):
            value = dst[...].astype(F32)
            for other in others:
                value = value + other[...].astype(F32)
            dst[...] = value.astype(BF16)

        wait = remote(grad.at[pl.ds(oc * SX, SX), :, :, rows], rc, c_peer)
        yield
        wait()

        def add_c(i):
            for xx in range(SX):
                for yy in range(2):
                    add(grad.at[c * SX + xx, i, yy, rows], rc.at[xx, i, yy])
        each(DZ, add_c)
        if order == "xyz":
            start, wait = bundle(rx)
            for k in range(1, SX):
                start(grad.at[c * SX + x_to(k), :, :, rows], rx.at[k - 1], x_peer(k))
            yield
            wait()

            def add_x(i):
                for yy in range(2):
                    add(grad.at[mine, i, yy, rows], *[rx.at[k, i, yy] for k in range(SX - 1)])
            each(DZ, add_x)
            wait = remote(grad.at[mine, :, oy, rows], ry, y_peer)
            yield
            wait()
            each(DZ, lambda i: add(grad.at[mine, i, y, rows], ry.at[i]))
            yield from z_steps(lambda zz: grad.at[mine, zz, y, rows], rz, add)
            parts = []
        else:
            wait = remote(grad.at[half, :, oy, rows], ry, y_peer)
            yield
            wait()

            def add_y(i):
                for xx in range(SX):
                    add(grad.at[c * SX + xx, i, y, rows], ry.at[xx, i])
            each(DZ, add_y)
            def add_half(dst, src):
                for xx in range(SX):
                    add(dst.at[xx], src.at[xx])
            yield from z_steps(lambda zz: grad.at[half, zz, y, rows], rz, add_half)
            start, wait = bundle(rx)
            for k in range(1, SX):
                start(grad.at[c * SX + x_to(k), z, y, rows], rx.at[k - 1], x_peer(k))
            yield
            wait()
            parts = [rx.at[k] for k in range(SX - 1)]
        value = grad[mine, z, y, rows].astype(F32)
        for part in parts:
            value = value + part[...].astype(F32)
        fb[mine, rows] = value.astype(BF16)
        yield from share(lambda q: fb.at[q, rows], fb.at[pl.ds(0, SX), rows])

    def wide_mid(grad, lo, n, order, rc, rx, ry, rz, fb):
        taps = pl.ds(lo, n)
        half = pl.ds(c * SX, SX)
        mine = q_own

        def add(dst, *others):
            value = dst[...].astype(F32)
            for other in others:
                value = value + other[...].astype(F32)
            dst[...] = value.astype(BF16)

        wait = remote(grad.at[pl.ds(oc * SX, SX), taps], rc, c_peer)
        yield
        wait()

        def add_c(i):
            t, zz = i // DZ, i % DZ
            for xx in range(SX):
                add(grad.at[c * SX + xx, lo + t, zz], rc.at[xx, t, zz])
        each(n * DZ, add_c)
        if order == "xyz":
            start, wait = bundle(rx)
            for k in range(1, SX):
                start(grad.at[c * SX + x_to(k), taps], rx.at[k - 1], x_peer(k))
            yield
            wait()

            def add_x(i):
                t, zz = i // DZ, i % DZ
                add(grad.at[mine, lo + t, zz], *[rx.at[k, t, zz] for k in range(SX - 1)])
            each(n * DZ, add_x)
            wait = remote(grad.at[mine, taps, :, oy], ry, y_peer)
            yield
            wait()

            def add_y(i):
                t, zz = i // DZ, i % DZ
                add(grad.at[mine, lo + t, zz, y], ry.at[t, zz])
            each(n * DZ, add_y)
            def add_taps(dst, src):
                each(n, lambda t: add(dst.at[t], src.at[t]))
            yield from z_steps(lambda zz: grad.at[mine, taps, zz, y], rz, add_taps)
            parts = []
        else:
            wait = remote(grad.at[half, taps, :, oy], ry, y_peer)
            yield
            wait()

            def add_y(i):
                t, zz = i // DZ, i % DZ
                for xx in range(SX):
                    add(grad.at[c * SX + xx, lo + t, zz, y], ry.at[xx, t, zz])
            each(n * DZ, add_y)
            def add_half(dst, src):
                for xx in range(SX):
                    each(n, lambda t, xx=xx: add(dst.at[xx, t], src.at[xx, t]))
            yield from z_steps(lambda zz: grad.at[half, taps, zz, y], rz, add_half)
            start, wait = bundle(rx)
            for k in range(1, SX):
                start(grad.at[c * SX + x_to(k), taps, z, y], rx.at[k - 1], x_peer(k))
            yield
            wait()
            parts = [rx.at[k] for k in range(SX - 1)]

        def finish(t):
            value = grad[mine, lo + t, z, y].astype(F32)
            for part in parts:
                value = value + part[t].astype(F32)
            fb[mine, lo + t] = value.astype(BF16)
        each(n, finish)
        yield from share(lambda q: fb.at[q, taps], fb.at[pl.ds(0, SX), taps])

    def reduce_diff():
        wait = remote(g_diff.at[oc], rcd, c_peer)
        yield
        wait()

        def add_c(i):
            t, zz = i // DZ, i % DZ
            for yy in range(2):
                value = g_diff[c, t, zz, yy].astype(F32) + rcd[t, zz, yy].astype(F32)
                g_diff[c, t, zz, yy] = value.astype(BF16)
        each(9 * DZ, add_c)
        wait = remote(g_diff.at[c, :, :, oy], ryd, y_peer)
        yield
        wait()

        def add_y(i):
            t, zz = i // DZ, i % DZ
            value = g_diff[c, t, zz, y].astype(F32) + ryd[t, zz].astype(F32)
            g_diff[c, t, zz, y] = value.astype(BF16)
        each(9 * DZ, add_y)
        def add_taps(dst, src):
            def one(t):
                dst[t] = (dst[t].astype(F32) + src[t].astype(F32)).astype(BF16)
            each(9, one)
        yield from z_steps(lambda zz: g_diff.at[c, :, zz, y], rzd, add_taps)

        def widen(t):
            fdx[t] = g_diff[c, t, z, y].astype(F32)
        each(9, widen)
        start, wait = bundle(rxd)
        for k in range(1, SX):
            start(fdx, rxd.at[k - 1], x_peer(k))
        yield
        wait()

        def add_x(t):
            value = fdx[t]
            for k in range(1, SX):
                value = value + rxd[k - 1, t]
            fdo[c, t] = value
        each(9, add_x)
        wait = remote(fdo.at[c], fdo.at[c], c_peer)
        yield
        wait()
        od_out[...] = fdo[...]

    def reduce_rest():
        wait = remote(g_re, rcr, c_peer)
        yield
        wait()

        def add_c(zz):
            for yy in range(2):
                value = g_re[zz, yy].astype(F32) + rcr[zz, yy].astype(F32)
                rcr[zz, yy] = value.astype(BF16)
        each(DZ, add_c)
        wait = remote(rcr.at[:, oy], ryr, y_peer)
        yield
        wait()

        def add_y(zz):
            value = rcr[zz, y].astype(F32) + ryr[zz].astype(F32)
            rcr[zz, y] = value.astype(BF16)
        each(DZ, add_y)
        def add_z(dst, src):
            dst[...] = (dst[...].astype(F32) + src[...].astype(F32)).astype(BF16)
        yield from z_steps(lambda zz: rcr.at[zz, y], rzr, add_z)
        frx[...] = rcr[z, y].astype(F32)
        start, wait = bundle(rxr)
        for k in range(1, SX):
            start(frx, rxr.at[k - 1], x_peer(k))
        yield
        wait()
        value = frx[...]
        for k in range(1, SX):
            value = value + rxr[k - 1]
        n_red, n_exp = or_out.shape[0], oe_out.shape[0]
        or_out[...] = value[0:n_red]
        for b in range(4):
            oe_out[:, b * LANES : (b + 1) * LANES] = value[n_red + b * n_exp : n_red + (b + 1) * n_exp]

    bufs = [bufs[n : n + 4] for n in range(0, len(bufs), 4)]
    spans_f, spans_m, spans_l = portions(fr, 9, lr)
    red_first = [wide_first(g_first, lo, n, order, *bufs.pop(0), fbf) for order, lo, n in spans_f]
    red_mid = [wide_mid(g_mid, lo, n, order, *bufs.pop(0), fbm) for order, lo, n in spans_m]
    red_last = [wide_first(g_last, lo, n, order, *bufs.pop(0), fbl) for order, lo, n in spans_l]
    chains = {"d": reduce_diff(), "r": reduce_rest()}
    for name, parts in (("f", red_first), ("m", red_mid), ("l", red_last)):
        chains.update({name + str(n): part for n, part in enumerate(parts)})

    def at(point):
        for name in ORDER[point]:
            next(chains[name], None)

    for finish in (free_gated, free_change):
        finish()
        halo_waits.remove(finish)
    mgb, mgr = gb, gr
    sg2, gg = z3.at[:, 0:512], z3.at[:, 512:1024]
    sg2[...] = dot_nt(lgb[...], wl[...].reshape(512, 2048))
    parts = []
    for group in range(NG):
        def slope_2(start, carry):
            normed = z2[pl.ds(start, STEP), :]
            _, slope = silu_parts(gain_2 * normed + bias_2)
            value = sg2[pl.ds(start, STEP), :] * slope
            sg2[pl.ds(start, STEP), :] = value
            return carry[0] + fold(value), carry[1] + fold(value * normed)
        zero = jnp.zeros((8, 512), F32)
        sums = rows_loop(group, slope_2, (zero, zero))
        parts += [jnp.sum(item, axis=0, keepdims=True) for item in sums]
    copies = sp_send(2, parts)
    for n in range(4):
        g_last[n] = dot_tn(sab[...], lgb[:, n * 512 : (n + 1) * 512]).astype(BF16).reshape(DZ, 2, lr, 512)
    at("dwl")
    at("bn2")
    total = sp_total(2, copies)
    gain_2_grad = bias_2_grad = jnp.zeros((1, 512), F32)
    for group in range(NG):
        row = 2 * group
        bias_sum, gain_sum = total[row : row + 1], total[row + 1 : row + 2]
        gain_2_grad, bias_2_grad = gain_2_grad + gain_sum, bias_2_grad + bias_sum
        scale = gain_2 * inv_2[group]

        def apply_2b(start, carry):
            value = sg2[pl.ds(start, STEP), :] - bias_sum * inv_pixels
            value = scale * (value - z2[pl.ds(start, STEP), :] * (gain_sum * inv_pixels))
            mgb[pl.ds(start, STEP), :] = value.astype(BF16)
            return carry
        rows_loop(group, apply_2b, 0)
    wait_mid, _ = halo(mgb.at[pl.ds(0, NW)], mgb.at[pl.ds(NW, NW)], None, None, mgr.at[0], mgr.at[1])
    at("mid")
    for a in range(3):
        for b in range(3):
            grad = dot_tn(gs[a : a + 2, :, b * 512 : (b + 1) * 512].reshape(2 * NW, 512), mgb[...]).astype(BF16)
            for qq in range(S):
                g_mid[qq, 3 * a + b] = grad[:, qq * mw : (qq + 1) * mw].reshape(DZ, 2, wm_in.shape[1], mw)
        next(red_mid[a])
    mgs = gs
    for r in range(2):
        spread(mgs, 1 + r, lambda start, r=r: mgb[pl.ds(r * NW + start, STEP), :], True)

    def back_taps(lhs, a):
        total = dot_nt(lhs[:, 0:512], wm[3 * a].reshape(512, 512))
        for b in range(1, 3):
            total = total + dot_nt(lhs[:, b * 512 : (b + 1) * 512], wm[3 * a + b].reshape(512, 512))
        return total

    gg[...] = back_taps(mgs[1:3].reshape(2 * NW, 1536), 1)
    gg[0:NW, :] += back_taps(mgs[2], 0)
    gg[NW : 2 * NW, :] += back_taps(mgs[1], 2)
    at("own")
    wait_mid()
    spread(mgs, 0, lambda start: mgr[0, pl.ds(start, STEP), :], True)
    spread(mgs, 3, lambda start: mgr[1, pl.ds(start, STEP), :], True)
    gg[0:NW, :] += back_taps(mgs[0], 2)
    gg[NW : 2 * NW, :] += back_taps(mgs[3], 0)

    def gate_back(i, carry):
        start = pl.multiple_of(i * STEP, STEP)
        gate = gt[pl.ds(start, STEP), :]
        act = jax.nn.silu(gain_1 * z1[pl.ds(start, STEP), :] + bias_1)
        value = gg[pl.ds(start, STEP), :] * act * gate * (1.0 - gate)
        fgb[pl.ds(start, STEP), :] = value.astype(BF16)
        return carry

    lax.fori_loop(0, 2 * NW // STEP, gate_back, 0)
    cg = dot_nt(fgb[...], we[...].reshape(LANES, 512)).astype(BF16)
    cg_rows = [cg[r * NW : (r + 1) * NW].astype(F32) for r in range(2)]
    hg = pair_sum(cg_rows[0] + cg_rows[1]).astype(BF16)
    for r in range(2):
        cgx[r, 0] = cg_rows[r].astype(BF16)
        cgx[r, 1] = hg
    wait_cg, _ = halo(cgx.at[0], cgx.at[1], None, None, cgr.at[0], cgr.at[1])
    at("gate")
    n_exp = we_in.shape[0]
    grad = dot_tn(comb[...], fgb[...]).astype(BF16)
    n_red = wr_in.shape[0]
    for b in range(4):
        g_re[:, :, n_red + b * n_exp : n_red + (b + 1) * n_exp, :] = grad[
            :, b * LANES : (b + 1) * LANES].reshape(DZ, 2, n_exp, LANES)
    for r in range(2):
        put_shifts(cgs, 1 + r, cg_rows[r], 1, True)
    put_shifts(hgs, 1, hg.astype(F32), 2, True)
    for a in range(3):
        grad = dot_tn(cs[a : a + 2].reshape(2 * NW, 384), cg).astype(BF16)
        g_diff[0, 3 * a : 3 * a + 3] = grad.reshape(3, DZ, 2, wd0_in.shape[1], LANES)
        grad = (0.5 * dot_tn(ps[a], hg)).astype(BF16)
        g_diff[1, 3 * a : 3 * a + 3] = grad.reshape(3, DZ, 2, wd0_in.shape[1], LANES)
    at("diff")
    wait_cg()
    put_shifts(cgs, 0, cgr[0, 0].astype(F32), 1, True)
    put_shifts(cgs, 3, cgr[1, 0].astype(F32), 1, True)
    put_shifts(hgs, 0, cgr[0, 1].astype(F32), 2, True)
    put_shifts(hgs, 2, cgr[1, 1].astype(F32), 2, True)
    full = jnp.zeros((2 * NW, LANES), F32)
    half = jnp.zeros((NW, LANES), F32)
    for a in range(3):
        for b in range(3):
            lanes = slice(b * LANES, (b + 1) * LANES)
            full = full + dot_nt(
                cgs[2 - a : 4 - a, :, lanes].reshape(2 * NW, LANES), wd[0, 3 * a + b].reshape(LANES, LANES))
            half = half + dot_nt(hgs[2 - a, :, lanes], wd[1, 3 * a + b].reshape(LANES, LANES))
    rd[...] = full + 0.25 * jnp.concatenate([half, half], axis=0)
    for r in range(2):
        for f in range(NF):
            here = r * NW + f * 16
            after = r * NW + ((f + 1) % NF) * 16
            diff = (keep[f].astype(F32) * rd[here : here + 16, :]
                    - keep[(f + 1) % NF].astype(F32) * rd[after : after + 16, :])
            chb[r, f * 16 : f * 16 + 16, :] = diff.astype(BF16)
    rgb = chb[...].reshape(2 * NW, LANES)
    sg2[...] = dot_nt(rgb, wr[...].reshape(512, LANES))

    parts = []
    for group in range(NG):
        def slope_1(start, carry):
            normed = z1[pl.ds(start, STEP), :]
            _, slope = silu_parts(gain_1 * normed + bias_1)
            value = gg[pl.ds(start, STEP), :] * (1.0 + gt[pl.ds(start, STEP), :]) + sg2[pl.ds(start, STEP), :]
            value = value * slope
            sg2[pl.ds(start, STEP), :] = value
            return carry[0] + fold(value), carry[1] + fold(value * normed)
        zero = jnp.zeros((8, 512), F32)
        sums = rows_loop(group, slope_1, (zero, zero))
        parts += [jnp.sum(item, axis=0, keepdims=True) for item in sums]
    copies = sp_send(3, parts)
    g_re[:, :, 0:n_red, :] = dot_tn(fab[...], rgb).astype(BF16).reshape(DZ, 2, n_red, LANES)
    at("bn1")
    total = sp_total(3, copies)
    gain_1_grad = bias_1_grad = jnp.zeros((1, 512), F32)
    for group in range(NG):
        row = 2 * group
        bias_sum, gain_sum = total[row : row + 1], total[row + 1 : row + 2]
        gain_1_grad, bias_1_grad = gain_1_grad + gain_sum, bias_1_grad + bias_sum
        scale = gain_1 * inv_1[group]

        def apply_1b(start, carry):
            value = sg2[pl.ds(start, STEP), :] - bias_sum * inv_pixels
            value = scale * (value - z1[pl.ds(start, STEP), :] * (gain_sum * inv_pixels))
            fgb[pl.ds(start, STEP), :] = value.astype(BF16)
            return carry
        rows_loop(group, apply_1b, 0)

    wait_stem()
    stem_total = stg[...]
    for k in range(S - 1):
        stem_total = stem_total + stgr[k]
    gain_3_all = jnp.concatenate(gain_3_grad, axis=1)
    bias_3_all = jnp.concatenate(bias_3_grad, axis=1)
    for d in range(D):
        mid_at, last_at = (d // per) * LANES, d * rows_last * LANES
        rows = [v[:, mid_at : mid_at + LANES] for v in (gain_1_grad, bias_1_grad, gain_2_grad, bias_2_grad)]
        for v in (gain_3_all, bias_3_all):
            rows += [v[:, last_at + n * LANES : last_at + (n + 1) * LANES] for n in range(rows_last)]
        sms[d, 0:8, :] = stem_total[d * 8 : d * 8 + 8]
        sms[d, 8:16, :] = jnp.concatenate(rows, axis=0)
    small_start, wait_small_back = bundle(smr)
    for k in range(1, D):
        small_start(sms.at[lax.rem(dp + k, D)], smr.at[k - 1], dp_peers[k - 1])

    at("fg")
    for n in range(4):
        grad = dot_tn(x3[:, :, n * 512 : (n + 1) * 512].reshape(2 * NW, 512), fgb[...]).astype(BF16)
        per_chunk = 512 // (2 * fr)
        for qq in range(S):
            g_first[qq, n * per_chunk : (n + 1) * per_chunk] = grad[:, qq * fw : (qq + 1) * fw].reshape(
                per_chunk, 2, fr, fw)
    at("dwf")
    at("add")
    weights_first = wf[...].reshape(2048, 512)
    for n in range(4):
        lo = n * 512
        free_part()
        z3[:, lo : lo + 512] = dot_nt(fgb[...], weights_first[lo : lo + 512])

        def apply_in(i, carry):
            start = pl.multiple_of(i * STEP, STEP)
            value = z3[pl.ds(start, STEP), lo : lo + 512] + ct_rows(start, lo, 512)
            ost[n % 2, pl.ds(start // 16, STEP // 16)] = value.astype(BF16).reshape(STEP // 16, 16, 512)
            return carry
        lax.fori_loop(0, 2 * NW // STEP, apply_in, 0)
        store_part(n, ig_hbm)
        at("in" + str(n))
    for point in sorted(ORDER):
        if point[0] == "t":
            at(point)
    for chain in chains.values():
        for _ in chain:
            pass
    grad_stores = [local(fbf, fbf_hbm), local(fbm, fbm_hbm), local(fbl, fbl_hbm)]

    assert counters["r"] <= ssem.shape[0] and counters["l"] <= lsem.shape[0], counters
    wait_video()

    def video_edges(f, carry):
        for ch in range(3):
            rows = slice(ch * 8, ch * 8 + 8)
            from_prev = vgr[0, f, ch * 2 + 1 : ch * 2 + 2, :]
            from_next = vgr[1, f, ch * 2 : ch * 2 + 1, :]
            vg_out[f, rows] += jnp.where(row8 == 0, from_prev, jnp.where(row8 == 7, from_next, 0.0))
        return carry

    lax.fori_loop(0, NF, video_edges, 0)
    value = sms[dp]
    wait_small_back()
    for k in range(D - 1):
        value = value + smr[k]
    osm_out[...] = value
    for finish in sends + halo_waits:
        finish()
    for copy in grad_stores:
        copy.wait()
    for part in stores[-2:]:
        for copy in part:
            copy.wait()


def final_kernel(
    sizes, so, vg, out, ig, fbf, fbm, fbl, gr, gd, ge, gsm,
    so_o, vg_o, out_o, ig_o, rgb_o, stemd_o, first_o, mid_o, last_o, red_o, dfull_o, dhalf_o, exp_o,
    g1_o, b1_o, g2_o, b2_o, g3_o, b3_o, sems, so_v, out_v, ig_v, vg_v,
):
    D, S = sizes
    loads, copies = [], []
    for src, through, dst in ((so, so_v, so_o), (out, out_v, out_o), (ig, ig_v, ig_o), (vg, vg_v, vg_o)):
        half = src.shape[0] // 2
        for rows in (pl.ds(0, half), pl.ds(half, half)):
            n = len(loads)
            loads.append(pltpu.make_async_copy(src.at[rows], through.at[rows], sems.at[0, n]))
            copies.append(pltpu.make_async_copy(through.at[rows], dst.at[rows], sems.at[1, n]))
    for copy in loads:
        copy.start()
    for load, copy in zip(loads, copies):
        load.wait()
        copy.start()
    fw, lw = fbf.shape[2], fbl.shape[2]
    for q in range(S):
        first_o[:, q * fw : (q + 1) * fw] = fbf[q].astype(F32)
        last_o[:, q * lw : (q + 1) * lw] = fbl[q].astype(F32)
        for t in range(9):
            mid_o[t, :, q * fw : (q + 1) * fw] = fbm[q, t].astype(F32)
    red_o[...] = gr[...]
    dfull_o[...] = gd[0]
    dhalf_o[...] = gd[1]
    exp_o[...] = ge[...]
    for ch in range(9):
        value = gsm[0:8, ch * 9 : ch * 9 + 9]
        if ch < 3:
            rgb_o[ch] = value
        else:
            stemd_o[ch - 3] = value
    width = g1_o.shape[0]
    per = LANES // width
    here = lax.rem(lax.axis_index("dp"), per)
    for j, ref in enumerate((g1_o, b1_o, g2_o, b2_o)):
        row = gsm[8 + j]
        value = row[0:width]
        for n in range(1, per):
            value = jnp.where(here == n, row[n * width : (n + 1) * width], value)
        ref[...] = value
    count = g3_o.shape[0] // LANES
    for j, ref in enumerate((g3_o, b3_o)):
        for n in range(count):
            ref[n * LANES : (n + 1) * LANES] = gsm[12 + j * count + n]
    for copy in copies:
        copy.wait()


def on_device_kernel(
    clip_video, section_input, keep_mask, w_rgb, w_stem_diff, w_first, w_middle, w_last, w_reduce,
    w_diff_full, w_diff_half, w_expand, gain_first, bias_first, gain_middle, bias_middle, gain_last,
    bias_last, stem_cot, section_cot,
):
    D, S = lax.axis_size("dp"), lax.axis_size("sp")
    DZ, SX = D // 2, S // 2
    NF = clip_video.shape[0]
    NW = NF * 16
    width = 512 // D
    band = jnp.asarray(band_table(8), BF16)
    fr, fw = w_first.shape[0], 512 // S
    mr, lr, rr = w_middle.shape[1], w_last.shape[0], w_reduce.shape[0]
    dr, er = w_diff_full.shape[1], w_expand.shape[0]
    lw = 2048 // S
    shape = jax.ShapeDtypeStruct
    vm = pltpu.VMEM
    any_spec = pl.BlockSpec(memory_space=pl.ANY)
    vmem_spec = pl.BlockSpec(memory_space=pltpu.VMEM)
    n_rem, n_loc = 146, 48
    re_rows = rr + 4 * er
    scratch = [
        pltpu.SemaphoreType.DMA((n_rem,)), pltpu.SemaphoreType.DMA((n_rem,)), pltpu.SemaphoreType.DMA((n_loc,)),
        vm((D, fr, 512), BF16), vm((9, D, mr, 512), BF16), vm((D, lr, 2048), BF16),
        vm((D, rr, LANES), BF16), vm((2, 9, D, dr, LANES), BF16), vm((D, er, 512), BF16),
        vm((2 * NF, 16, 2048), BF16), vm((2 * NF, 16, 2048), BF16),
        vm((2 * PART, 512, LANES), BF16), vm((2 * PART, 512, LANES), BF16),
        vm((NF, 32, LANES), F32), vm((NF, 24, LANES), BF16), vm((NF, 24, LANES), BF16),
        vm((16, LANES), F32), vm((D, 16, LANES), F32), vm((512, 288), BF16), vm((3, 512, LANES), F32), vm((288, 512), BF16),
        vm((NF, 96, LANES), F32),
        vm((NF, 8, LANES), F32), vm((2, NF, 8, LANES), F32), vm((D * 8, LANES), F32), vm((S - 1, D * 8, LANES), F32),
        vm((4, 8, 512), F32), vm((4, S - 1, 8, 512), F32), vm((4, 8, 512), F32), vm((4, S - 1, 8, 512), F32),
        vm((2 * NW, 512), F32), vm((2 * NW, 512), BF16), vm((2 * NW, 512), F32),
        vm((2 * NW, LANES), F32), vm((2, NW, LANES), BF16), vm((2, 2, NW, LANES), BF16),
        vm((4, NW, 384), BF16), vm((3, NW, 384), BF16), vm((2 * NW, LANES), BF16),
        vm((2 * NW, 512), BF16), vm((2, NW, 512), BF16), vm((4, NW, 1536), BF16),
        vm((2 * NW, 512), F32), vm((2 * NW, 512), BF16), vm((2 * NW, 2048), F32), vm((2 * NW, 2048), BF16),
        vm((2, 2, NW, LANES), BF16), vm((2, 2, NW, LANES), BF16),
        vm((4, NW, 384), BF16), vm((3, NW, 384), BF16), vm((2 * NW, 512), BF16), vm((2, 2 * NF, 16, 512), BF16),
        vm((S, DZ, 2, fr, fw), BF16), vm((S, 9, DZ, 2, mr, fw), BF16), vm((S, DZ, 2, lr, lw), BF16),
        vm((2, 9, DZ, 2, dr, LANES), BF16), vm((DZ, 2, re_rows, LANES), BF16),
        vm((9, DZ, 2, dr, LANES), BF16), vm((9, DZ, dr, LANES), BF16), vm((DZ - 1, 9, dr, LANES), BF16),
        vm((9, dr, LANES), F32), vm((SX - 1, 9, dr, LANES), F32), vm((2, 9, dr, LANES), F32),
        vm((DZ, 2, re_rows, LANES), BF16), vm((DZ, re_rows, LANES), BF16), vm((DZ - 1, re_rows, LANES), BF16),
        vm((re_rows, LANES), F32), vm((SX - 1, re_rows, LANES), F32),
        vm((S, fr, fw), BF16), vm((S, 9, mr, fw), BF16), vm((S, lr, lw), BF16),
        vm((D, 16, LANES), F32), vm((D - 1, 16, LANES), F32),
    ]

    def landing(spans, shape_of):
        for order, _, n in spans:
            extra = (SX,) if order == "yzx" else ()
            scratch.append(vm((SX,) + shape_of(n, (DZ, 2)), BF16))
            scratch.append(vm((SX - 1,) + shape_of(n, (DZ, 2) if order == "xyz" else ()), BF16))
            scratch.append(vm(extra + shape_of(n, (DZ,)), BF16))
            scratch.append(vm((DZ - 1,) + extra + shape_of(n, ()), BF16))

    spans_f, spans_m, spans_l = portions(fr, 9, lr)
    landing(spans_f, lambda n, lead: lead + (n, fw))
    landing(spans_m, lambda n, lead: (n,) + lead + (mr, fw))
    landing(spans_l, lambda n, lead: lead + (n, lw))
    outs = pl.pallas_call(
        functools.partial(whole_kernel, (D, S, NF)),
        out_shape=(
            shape((NF, 512, LANES), BF16), shape((NF, 24, LANES), F32),
            shape(section_input.shape, BF16), shape(section_input.shape, BF16),
            shape((S, fr, fw), BF16), shape((S, 9, mr, fw), BF16), shape((S, lr, lw), BF16), shape((rr, LANES), F32),
            shape((2, 9, dr, LANES), F32), shape((er, 512), F32), shape((16, LANES), F32),
        ),
        in_specs=[pl.BlockSpec(memory_space=pltpu.SMEM)] + [vmem_spec] * 10 + [any_spec] * 10,
        out_specs=(any_spec, vmem_spec) + (any_spec,) * 5 + (vmem_spec,) * 4,
        scratch_shapes=scratch,
        compiler_params=pltpu.CompilerParams(
            collective_id=0, has_side_effects=True, vmem_limit_bytes=VMEM_BYTES),
        name="tdn_blocks",
    )(
        keep_mask, clip_video.reshape(NF, 24, LANES), w_rgb.transpose(1, 2, 0), w_stem_diff.transpose(1, 2, 0),
        gain_first.reshape(1, -1), bias_first.reshape(1, -1), gain_middle.reshape(1, -1), bias_middle.reshape(1, -1),
        gain_last.reshape(-1, LANES), bias_last.reshape(-1, LANES), band, section_input, section_cot, stem_cot.reshape(NF, 512, LANES),
        w_first, w_middle, w_last, w_reduce, w_diff_full, w_diff_half, w_expand,
    )
    results = (
        shape(stem_cot.shape, BF16), shape(clip_video.shape, F32), shape(section_input.shape, BF16),
        shape(section_input.shape, BF16), shape((3, 8, 9), F32), shape((6, 8, 9), F32),
        shape(w_first.shape, F32), shape(w_middle.shape, F32), shape(w_last.shape, F32), shape(w_reduce.shape, F32),
        shape(w_diff_full.shape, F32), shape(w_diff_half.shape, F32), shape(w_expand.shape, F32),
    ) + (shape((width,), F32),) * 4 + (shape((2048 // D,), F32),) * 2
    so, vg, section_output, input_grad, *grads = outs
    finals = pl.pallas_call(
        functools.partial(final_kernel, (D, S)),
        out_shape=results,
        in_specs=[any_spec] * 4 + [vmem_spec] * 7,
        out_specs=(any_spec,) * 4 + (vmem_spec,) * 15,
        scratch_shapes=[
            pltpu.SemaphoreType.DMA((2, 8)), vm(stem_cot.shape, BF16), vm(section_input.shape, BF16),
            vm(section_input.shape, BF16), vm(clip_video.shape, F32)],
        compiler_params=pltpu.CompilerParams(vmem_limit_bytes=VMEM_BYTES),
        name="final_outputs",
    )(so.reshape(stem_cot.shape), vg.reshape(clip_video.shape), section_output, input_grad, *grads)
    return finals[0:4] + (finals[4].transpose(2, 0, 1), finals[5].transpose(2, 0, 1)) + finals[6:]


def fits_kernel(mesh):
    dp_count, sp_count = mesh.shape["dp"], mesh.shape["sp"]
    return (
        dp_count % 2 == 0 and dp_count & (dp_count - 1) == 0 and sp_count % 2 == 0 and H5 == 2 * sp_count and HS == 8 * sp_count
        and TDM_C % (16 * dp_count) == 0 and STEM_C == 8 * dp_count and MID // sp_count % LANES == 0
        and C5 // dp_count % LANES == 0 and (dp_count - 1) * (sp_count // 2 - 1) <= dp_count
    )


def solution(mesh):
    placed = (
        P("dp", None, "sp", None),
        P("dp", "sp", None, None),
        P("dp"),
        P(None, None, "dp"),
        P(None, None, "dp"),
        P("dp", None),
        P(None, "dp", None),
        P("dp", None),
        P("dp", None),
        P(None, "dp", None),
        P(None, "dp", None),
        P("dp", None),
        P("dp"),
        P("dp"),
        P("dp"),
        P("dp"),
        P("dp"),
        P("dp"),
        P("dp", None, "sp", None),
        P("dp", "sp", None, None),
    )
    return jax.shard_map(
        on_device_kernel if fits_kernel(mesh) else on_device,
        mesh=mesh,
        in_specs=placed,
        out_specs=(
            P("dp", None, "sp", None),
            P("dp", None, "sp", None),
            P("dp", "sp", None, None),
            P("dp", "sp", None, None),
            P(None, None, "dp"),
            P(None, None, "dp"),
            P("dp", None),
            P(None, "dp", None),
            P("dp", None),
            P("dp", None),
            P(None, "dp", None),
            P(None, "dp", None),
            P("dp", None),
            P("dp"),
            P("dp"),
            P("dp"),
            P("dp"),
            P("dp"),
            P("dp"),
        ),
        check_vma=False,
    )
```

```python
import functools

import jax
import jax.numpy as jnp
import numpy as np
from jax import lax
from jax.experimental import pallas as pl
from jax.experimental.pallas import tpu as pltpu
from jax.sharding import PartitionSpec as P

H5, HS, MID, TDM_C, C5, STEM_C = 8, 32, 512, 128, 2048, 64
VMEM_BYTES = 63 * 2**20

MICRO = 2


EPS = 1e-05


def with_halo(block, sides, width):
    for axis, dim in sides:
        count = lax.axis_size(axis)
        forward = [(i, i + 1) for i in range(count - 1)]
        backward = [(target, source) for source, target in forward]
        low = lax.ppermute(
            lax.slice_in_dim(block, block.shape[dim] - width, None, axis=dim), axis, forward
        )
        high = lax.ppermute(lax.slice_in_dim(block, 0, width, axis=dim), axis, backward)
        block = jnp.concatenate([low, block, high], axis=dim)
    return block


def silu_slope(values):
    sig_value = jax.nn.sigmoid(values)
    return sig_value * (1.0 + values * (1.0 - sig_value))


def tap_window(padded, row_off, col_off, row_count, col_count, row_axis):
    part_rows = lax.slice_in_dim(padded, row_off, row_off + row_count, axis=row_axis)
    return lax.slice_in_dim(part_rows, col_off, col_off + col_count, axis=row_axis + 1)


def pad_columns(haloed, row_axis):
    widths = [(0, 0)] * haloed.ndim
    widths[row_axis + 1] = (1, 1)
    return jnp.pad(haloed, widths)


def tap_conv(haloed, kernel, channels_last):
    row_axis = 1 if channels_last else 2
    row_count = haloed.shape[row_axis] - 2
    col_count = haloed.shape[row_axis + 1]
    padded = pad_columns(haloed, row_axis)
    einsum_form = "fhwc,cd->fhwd" if channels_last else "fchw,cd->fdhw"
    result = None
    for tap_index in range(9):
        window = tap_window(padded, tap_index // 3, tap_index % 3, row_count, col_count, row_axis)
        tap_term = jnp.einsum(
            einsum_form, window, kernel[tap_index], preferred_element_type=jnp.float32
        )
        result = tap_term if result is None else result + tap_term
    return result


def tap_conv_back(grad_halo, kernel, channels_last):
    row_axis = 1 if channels_last else 2
    row_count = grad_halo.shape[row_axis] - 2
    col_count = grad_halo.shape[row_axis + 1]
    padded = pad_columns(grad_halo, row_axis)
    einsum_form = "fhwd,cd->fhwc" if channels_last else "fdhw,cd->fchw"
    result = None
    for tap_index in range(9):
        window = tap_window(
            padded, 2 - tap_index // 3, 2 - tap_index % 3, row_count, col_count, row_axis
        )
        tap_term = jnp.einsum(
            einsum_form, window, kernel[tap_index], preferred_element_type=jnp.float32
        )
        result = tap_term if result is None else result + tap_term
    return result


def tap_kernel_grad(haloed, out_grad, channels_last):
    row_axis = 1 if channels_last else 2
    row_count = out_grad.shape[row_axis]
    col_count = out_grad.shape[row_axis + 1]
    padded = pad_columns(haloed, row_axis)
    einsum_form = "fhwc,fhwd->cd" if channels_last else "fchw,fdhw->cd"
    tap_list = []
    for tap_index in range(9):
        window = tap_window(padded, tap_index // 3, tap_index % 3, row_count, col_count, row_axis)
        tap_list.append(
            jnp.einsum(einsum_form, window, out_grad, preferred_element_type=jnp.float32)
        )
    return jnp.stack(tap_list, axis=0)


def pair_mean(values):
    return values.reshape(
        values.shape[0], values.shape[1] // 2, 2, values.shape[2] // 2, 2, values.shape[3]
    ).mean(axis=(2, 4))


def pair_total(values):
    return values.reshape(
        values.shape[0], values.shape[1] // 2, 2, values.shape[2] // 2, 2, values.shape[3]
    ).sum(axis=(2, 4))


def pair_grow(values):
    return jnp.repeat(jnp.repeat(values, 2, axis=1), 2, axis=2)


def norm_forward(pre_norm, gain, bias, pixel_count):
    local_sums = (jnp.sum(pre_norm, axis=(0, 1, 2)), jnp.sum(pre_norm * pre_norm, axis=(0, 1, 2)))
    total_sum, total_square = lax.psum((local_sums[0], local_sums[1]), "sp")
    mean_value = total_sum / pixel_count
    variance = total_square / pixel_count - mean_value * mean_value
    inverse = lax.rsqrt(variance + EPS)
    normed = (pre_norm - mean_value) * inverse
    return (normed, inverse, gain * normed + bias)


def norm_backward(out_grad, normed, inverse, gain, pixel_count):
    local_bias = jnp.sum(out_grad, axis=(0, 1, 2))
    local_gain = jnp.sum(out_grad * normed, axis=(0, 1, 2))
    total_bias, total_gain = lax.psum((local_bias, local_gain), "sp")
    pre_grad = (
        gain * inverse * (out_grad - total_bias / pixel_count - normed * total_gain / pixel_count)
    )
    return (pre_grad, local_gain, local_bias)


def reduce_grads(grads):
    summed = (
        lax.psum_scatter(grads[0], "dp", scatter_dimension=2, tiled=True),
        lax.psum_scatter(grads[1], "dp", scatter_dimension=2, tiled=True),
        lax.psum_scatter(grads[2], "dp", scatter_dimension=0, tiled=True),
        lax.psum_scatter(grads[3], "dp", scatter_dimension=1, tiled=True),
        lax.psum_scatter(grads[4], "dp", scatter_dimension=0, tiled=True),
        lax.psum_scatter(grads[5], "dp", scatter_dimension=0, tiled=True),
        lax.psum_scatter(grads[6], "dp", scatter_dimension=1, tiled=True),
        lax.psum_scatter(grads[7], "dp", scatter_dimension=1, tiled=True),
        lax.psum_scatter(grads[8], "dp", scatter_dimension=0, tiled=True),
        lax.psum_scatter(grads[9], "dp", scatter_dimension=0, tiled=True),
        lax.psum_scatter(grads[10], "dp", scatter_dimension=0, tiled=True),
        lax.psum_scatter(grads[11], "dp", scatter_dimension=0, tiled=True),
        lax.psum_scatter(grads[12], "dp", scatter_dimension=0, tiled=True),
        lax.psum_scatter(grads[13], "dp", scatter_dimension=0, tiled=True),
        lax.psum_scatter(grads[14], "dp", scatter_dimension=0, tiled=True),
    )
    return (
        lax.psum(summed[0].astype(jnp.bfloat16), "sp").astype(jnp.float32),
        lax.psum(summed[1].astype(jnp.bfloat16), "sp").astype(jnp.float32),
        lax.psum(summed[2].astype(jnp.bfloat16), "sp").astype(jnp.float32),
        lax.psum(summed[3].astype(jnp.bfloat16), "sp").astype(jnp.float32),
        lax.psum(summed[4].astype(jnp.bfloat16), "sp").astype(jnp.float32),
        lax.psum(summed[5].astype(jnp.bfloat16), "sp").astype(jnp.float32),
        lax.psum(summed[6].astype(jnp.bfloat16), "sp").astype(jnp.float32),
        lax.psum(summed[7].astype(jnp.bfloat16), "sp").astype(jnp.float32),
        lax.psum(summed[8].astype(jnp.bfloat16), "sp").astype(jnp.float32),
        lax.psum(summed[9].astype(jnp.bfloat16), "sp").astype(jnp.float32),
        lax.psum(summed[10].astype(jnp.bfloat16), "sp").astype(jnp.float32),
        lax.psum(summed[11].astype(jnp.bfloat16), "sp").astype(jnp.float32),
        lax.psum(summed[12].astype(jnp.bfloat16), "sp").astype(jnp.float32),
        lax.psum(summed[13].astype(jnp.bfloat16), "sp").astype(jnp.float32),
        lax.psum(summed[14].astype(jnp.bfloat16), "sp").astype(jnp.float32),
    )


def run_micro(
    video_part, feat_part, keep_part, stem_grad_in, section_grad_in, weights, pixel_count
):
    (
        rgb_k,
        stemd_k,
        first_k,
        middle_k,
        last_k,
        reduce_k,
        dfull_k,
        dhalf_k,
        expand_k,
        gain_one,
        bias_one,
        gain_two,
        bias_two,
        gain_three,
        bias_three,
    ) = weights
    keep_float = keep_part.astype(jnp.float32)
    keep_col = keep_float[:, None, None, None]
    next_col = jnp.roll(keep_float, -1)[:, None, None, None]
    frames_halo = with_halo(video_part, (("sp", 2),), 1)
    frames_wide = frames_halo.astype(jnp.float32)
    before = keep_col * (frames_wide - jnp.roll(frames_wide, 1, axis=0))
    after = next_col * (jnp.roll(frames_wide, -1, axis=0) - frames_wide)
    diff_stack = jnp.concatenate([before, after], axis=1).astype(jnp.bfloat16)
    stem_out = (tap_conv(frames_halo, rgb_k, False) + tap_conv(diff_stack, stemd_k, False)).astype(
        jnp.bfloat16
    )
    cot_halo = with_halo(stem_grad_in, (("sp", 2),), 1)
    direct_grad = tap_conv_back(cot_halo, rgb_k, False)
    diff_grad = tap_conv_back(cot_halo, stemd_k, False)
    before_grad = keep_col * diff_grad[:, :3]
    after_grad = next_col * diff_grad[:, 3:]
    video_grad = (
        direct_grad
        + before_grad
        - jnp.roll(before_grad, -1, axis=0)
        + jnp.roll(after_grad, 1, axis=0)
        - after_grad
    )
    rgb_grad = tap_kernel_grad(frames_halo, stem_grad_in, False)
    stemd_grad = tap_kernel_grad(diff_stack, stem_grad_in, False)
    row_count = feat_part.shape[1]
    col_count = feat_part.shape[2]
    first_pre = jnp.einsum("fhwc,cd->fhwd", feat_part, first_k, preferred_element_type=jnp.float32)
    normed_one, inverse_one, norm_one = norm_forward(
        first_pre, gain_one.astype(jnp.float32), bias_one.astype(jnp.float32), pixel_count
    )
    first_act = jax.nn.silu(norm_one)
    first_low = first_act.astype(jnp.bfloat16)
    reduced = jnp.einsum("fhwc,cd->fhwd", first_low, reduce_k, preferred_element_type=jnp.float32)
    change_low = (keep_col * (reduced - jnp.roll(reduced, 1, axis=0))).astype(jnp.bfloat16)
    change_halo = with_halo(change_low, (("sp", 1),), 2)
    near_rows = change_halo[:, 1 : row_count + 3]
    full_out = tap_conv(near_rows, dfull_k, True)
    pooled = pair_mean(change_halo.astype(jnp.float32)).astype(jnp.bfloat16)
    half_out = tap_conv(pooled, dhalf_k, True)
    combined_low = (full_out + pair_grow(half_out)).astype(jnp.bfloat16)
    gate_value = jax.nn.sigmoid(
        jnp.einsum("fhwc,cd->fhwd", combined_low, expand_k, preferred_element_type=jnp.float32)
    )
    gated_low = (first_act * (1.0 + gate_value)).astype(jnp.bfloat16)
    gated_halo = with_halo(gated_low, (("sp", 1),), 1)
    middle_pre = tap_conv(gated_halo, middle_k, True)
    normed_two, inverse_two, norm_two = norm_forward(
        middle_pre, gain_two.astype(jnp.float32), bias_two.astype(jnp.float32), pixel_count
    )
    second_low = jax.nn.silu(norm_two).astype(jnp.bfloat16)
    last_pre = jnp.einsum("fhwc,cd->fhwd", second_low, last_k, preferred_element_type=jnp.float32)
    normed_three, inverse_three, norm_three = norm_forward(
        last_pre, gain_three.astype(jnp.float32), bias_three.astype(jnp.float32), pixel_count
    )
    section_out = (feat_part.astype(jnp.float32) + norm_three).astype(jnp.bfloat16)
    out_grad = section_grad_in.astype(jnp.float32)
    last_grad, gain_three_grad, bias_three_grad = norm_backward(
        out_grad, normed_three, inverse_three, gain_three.astype(jnp.float32), pixel_count
    )
    last_grad_low = last_grad.astype(jnp.bfloat16)
    last_k_grad = jnp.einsum(
        "fhwc,fhwd->cd", second_low, last_grad_low, preferred_element_type=jnp.float32
    )
    second_grad = jnp.einsum(
        "fhwd,cd->fhwc", last_grad_low, last_k, preferred_element_type=jnp.float32
    ) * silu_slope(norm_two)
    middle_grad, gain_two_grad, bias_two_grad = norm_backward(
        second_grad, normed_two, inverse_two, gain_two.astype(jnp.float32), pixel_count
    )
    middle_low = middle_grad.astype(jnp.bfloat16)
    middle_halo = with_halo(middle_low, (("sp", 1),), 1)
    gated_grad = tap_conv_back(middle_halo, middle_k, True)
    middle_k_grad = tap_kernel_grad(gated_halo, middle_low, True)
    gate_grad = (gated_grad * first_act * gate_value * (1.0 - gate_value)).astype(jnp.bfloat16)
    expand_grad = jnp.einsum(
        "fhwc,fhwd->cd", combined_low, gate_grad, preferred_element_type=jnp.float32
    )
    combined_grad = jnp.einsum(
        "fhwd,cd->fhwc", gate_grad, expand_k, preferred_element_type=jnp.float32
    ).astype(jnp.bfloat16)
    half_grad = pair_total(combined_grad.astype(jnp.float32)).astype(jnp.bfloat16)
    stacked = jnp.concatenate([combined_grad, jnp.repeat(half_grad, 2, axis=1)], axis=2)
    stacked_halo = with_halo(stacked, (("sp", 1),), 2)
    full_grad_halo = stacked_halo[:, 1 : row_count + 3, :col_count]
    half_grad_halo = stacked_halo[:, 0::2, col_count:]
    change_grad = tap_conv_back(full_grad_halo, dfull_k, True) + 0.25 * pair_grow(
        tap_conv_back(half_grad_halo, dhalf_k, True)
    )
    dfull_grad = tap_kernel_grad(near_rows, combined_grad, True)
    dhalf_grad = tap_kernel_grad(pooled, half_grad, True)
    weighted = keep_col * change_grad
    reduced_grad = (weighted - jnp.roll(weighted, -1, axis=0)).astype(jnp.bfloat16)
    reduce_grad = jnp.einsum(
        "fhwc,fhwd->cd", first_low, reduced_grad, preferred_element_type=jnp.float32
    )
    first_sum = gated_grad * (1.0 + gate_value) + jnp.einsum(
        "fhwd,cd->fhwc", reduced_grad, reduce_k, preferred_element_type=jnp.float32
    )
    first_grad, gain_one_grad, bias_one_grad = norm_backward(
        first_sum * silu_slope(norm_one),
        normed_one,
        inverse_one,
        gain_one.astype(jnp.float32),
        pixel_count,
    )
    first_grad_low = first_grad.astype(jnp.bfloat16)
    first_k_grad = jnp.einsum(
        "fhwc,fhwd->cd", feat_part, first_grad_low, preferred_element_type=jnp.float32
    )
    input_grad = (
        out_grad
        + jnp.einsum("fhwd,cd->fhwc", first_grad_low, first_k, preferred_element_type=jnp.float32)
    ).astype(jnp.bfloat16)
    grads = (
        rgb_grad,
        stemd_grad,
        first_k_grad,
        middle_k_grad,
        last_k_grad,
        reduce_grad,
        dfull_grad,
        dhalf_grad,
        expand_grad,
        gain_one_grad,
        bias_one_grad,
        gain_two_grad,
        bias_two_grad,
        gain_three_grad,
        bias_three_grad,
    )
    return ((stem_out, video_grad, section_out, input_grad), grads)


def add_trees(first_tree, second_tree):
    if first_tree is None:
        return second_tree
    return jax.tree.map(
        lambda left_part, right_part: left_part + right_part, first_tree, second_tree
    )


def on_device(
    clip_video,
    section_input,
    keep_mask,
    w_rgb,
    w_stem_diff,
    w_first,
    w_middle,
    w_last,
    w_reduce,
    w_diff_full,
    w_diff_half,
    w_expand,
    gain_first,
    bias_first,
    gain_middle,
    bias_middle,
    gain_last,
    bias_last,
    stem_cot,
    section_cot,
):
    micro_frames = clip_video.shape[0] // MICRO
    pixel_count = (
        micro_frames * section_input.shape[1] * lax.axis_size("sp") * section_input.shape[2]
    )
    results = []
    grad_totals = None
    for micro_index in range(MICRO):
        weights = (
            lax.all_gather(w_rgb, "dp", axis=2, tiled=True),
            lax.all_gather(w_stem_diff, "dp", axis=2, tiled=True),
            lax.all_gather(w_first, "dp", axis=0, tiled=True),
            lax.all_gather(w_middle, "dp", axis=1, tiled=True),
            lax.all_gather(w_last, "dp", axis=0, tiled=True),
            lax.all_gather(w_reduce, "dp", axis=0, tiled=True),
            lax.all_gather(w_diff_full, "dp", axis=1, tiled=True),
            lax.all_gather(w_diff_half, "dp", axis=1, tiled=True),
            lax.all_gather(w_expand, "dp", axis=0, tiled=True),
            lax.all_gather(gain_first, "dp", axis=0, tiled=True),
            lax.all_gather(bias_first, "dp", axis=0, tiled=True),
            lax.all_gather(gain_middle, "dp", axis=0, tiled=True),
            lax.all_gather(bias_middle, "dp", axis=0, tiled=True),
            lax.all_gather(gain_last, "dp", axis=0, tiled=True),
            lax.all_gather(bias_last, "dp", axis=0, tiled=True),
        )
        low_end = micro_index * micro_frames
        high_end = low_end + micro_frames
        outputs, grads = run_micro(
            clip_video[low_end:high_end],
            section_input[low_end:high_end],
            keep_mask[low_end:high_end],
            stem_cot[low_end:high_end],
            section_cot[low_end:high_end],
            weights,
            pixel_count,
        )
        results.append(outputs)
        grad_totals = add_trees(grad_totals, reduce_grads(grads))
    stem_features = jnp.concatenate([item[0] for item in results], axis=0)
    video_grad = jnp.concatenate([item[1] for item in results], axis=0)
    section_output = jnp.concatenate([item[2] for item in results], axis=0)
    section_input_grad = jnp.concatenate([item[3] for item in results], axis=0)
    return (
        stem_features,
        video_grad,
        section_output,
        section_input_grad,
        grad_totals[0],
        grad_totals[1],
        grad_totals[2],
        grad_totals[3],
        grad_totals[4],
        grad_totals[5],
        grad_totals[6],
        grad_totals[7],
        grad_totals[8],
        grad_totals[9],
        grad_totals[10],
        grad_totals[11],
        grad_totals[12],
        grad_totals[13],
        grad_totals[14],
    )


F32 = jnp.float32
BF16 = jnp.bfloat16
MESH_ID = pl.DeviceIdType.MESH
GROUP = 8
LANES = 128
STEP = 32
PART = 2


def dot_nn(left, right):
    return lax.dot_general(left, right, (((1,), (0,)), ((), ())), preferred_element_type=F32)


def dot_nt(left, right):
    return lax.dot_general(left, right, (((1,), (1,)), ((), ())), preferred_element_type=F32)


def dot_tn(left, right):
    return lax.dot_general(left, right, (((0,), (0,)), ((), ())), preferred_element_type=F32)


def shift_down(values, count):
    size = values.shape[0]
    column = lax.broadcasted_iota(jnp.int32, values.shape, 0) & 15
    return jnp.where(column < count, 0.0, pltpu.roll(values, count, 0))


def shift_up(values, count):
    size = values.shape[0]
    column = lax.broadcasted_iota(jnp.int32, values.shape, 0) & 15
    return jnp.where(column >= 16 - count, 0.0, pltpu.roll(values, size - count, 0))


def pair_sum(values):
    size = values.shape[0]
    parity = lax.broadcasted_iota(jnp.int32, values.shape, 0) & 1
    return values + jnp.where(parity == 0, pltpu.roll(values, size - 1, 0), pltpu.roll(values, 1, 0))


def band_table(rows):
    table = np.zeros((rows, 96, 3 * LANES), np.float32)
    for i in range(rows):
        for a in range(3):
            for b in range(3):
                for ch in range(9):
                    base = (b * 3 + ch // 3) * 32
                    row = i + a - 1
                    if row < 0:
                        n = base + 24 + (ch % 3) * 2
                    elif row >= rows:
                        n = base + 24 + (ch % 3) * 2 + 1
                    else:
                        n = base + (ch % 3) * 8 + row
                    table[i, ch * 9 + 3 * a + b, n] = 1.0
    return table


def portions(first_rows, taps, last_rows):
    cut = first_rows // 2
    return (
        (("xyz", 0, cut), ("yzx", cut, first_rows - cut)),
        (("xyz", 0, 2), ("yzx", 2, 4), ("xyz", 6, taps - 6)),
        (("xyz", 0, last_rows // 2), ("yzx", last_rows // 2, last_rows // 2)),
    )


ORDER = {
    "dwl": ("l0", "l1"),
    "bn2": ("l1",),
    "mid": ("l0",),
    "own": ("m1",),
    "gate": ("m0", "l1"),
    "diff": ("d", "l0", "l1"),
    "bn1": ("r", "d", "l1", "l0",),
    "fg": ("m2",),
    "dwf": ("f0", "f1", "m0", "m1", "r", "d", "l0",),
    "add": ("f0", "f1"),
    "in0": ("m1", "m0", "l0",),
    "in1": ("l1", "r", "d"),
    "in2": ("m2",),
    "in3": ("m1", "m0", "l0", "r", "d"),
    "t0": ("f0", "f1", "m2", "l1", "m1"),
    "t1": ("f0", "f1", "m2", "m0", "m1", "r", "d", "l0", "l1"),
    "t2": ("f0", "f1", "m2", "m0", "m1", "r", "d", "l0", "l1"),
    "t4": ("f0", "f1", "m2", "m1", "m0", "r", "d", "l0", "l1",),
    "t5": ("f0", "f1", "m2", "m1", "m0", "r", "d", "l0", "l1",),
    "t3": ("f0", "f1", "m2", "m0", "m1", "r", "d", "l0", "l1"),
}


def silu_parts(values):
    sig = jax.nn.sigmoid(values)
    return values * sig, sig * (1.0 + values * (1.0 - sig))


def whole_kernel(
    sizes, keep, clip, rgb, stemd, g1, b1, g2, b2, g3, b3, band, x_hbm, ct_hbm, sc_hbm, wf_in, wm_in, wl_in, wr_in, wd0_in, wd1_in, we_in,
    so_hbm, vg_out, out_hbm, ig_hbm, fbf_hbm, fbm_hbm, fbl_hbm, or_out, od_out, oe_out, osm_out,
    ssem, rsem, lsem, wf, wm, wl, wr, wd, we, x3, ct3, sc, so, ust, uprev, unext, small, sm, tf, tff, tb, dg,
    vgh, vgr, stg, stgr, stat_s, stat_r, st3_s, st3_r, z1, fab, gt, rd, chb, chr_, cs, ps, comb,
    gb, gr, gs, z2, sab, z3, lgb, cgx, cgr, cgs, hgs, fgb, ost,
    g_first, g_mid, g_last, g_diff, g_re, rcd, ryd, rzd, fdx, rxd, fdo, rcr, ryr, rzr, frx, rxr, fbf, fbm, fbl, sms, smr, *bufs,
):
    D, S, NF = sizes
    DZ, SX = D // 2, S // 2
    NG = NF // GROUP
    NW = NF * 16
    GW = GROUP * 16
    dp, sp = lax.axis_index("dp"), lax.axis_index("sp")
    z, y = dp // 2, dp % 2
    x, c = sp // 2, sp % 2
    oy, oc = 1 - y, 1 - c
    q_own = c * SX + x

    def at_zy(zz, yy):
        return (zz * 2 + yy, sp)

    y_peer = at_zy(z, oy)
    c_peer = (dp, x * 2 + oc)

    z_bits = [1 << n for n in range(DZ.bit_length() - 1)]

    def z_pair(bit):
        return z + bit - 2 * bit * ((z // bit) % 2)

    def z_class(zz, bit):
        return [zz % (2 * bit) + 2 * bit * j for j in range(DZ // (2 * bit))]

    def x_to(k):
        return lax.rem(x + k, SX)

    def x_from(k):
        return lax.rem(x + SX - k, SX)

    def x_peer(k):
        return (dp, x_to(k) * 2 + c)

    sp_peers = [(dp, lax.rem(sp + k, S)) for k in range(1, S)]
    dp_peers = [(lax.rem(dp + k, D), sp) for k in range(1, D)]
    has_prev, has_next = sp > 0, sp < S - 1
    prev_dev, next_dev = (dp, sp - 1), (dp, sp + 1)

    counters = {"r": 0, "l": 0}
    sends = []

    def bundle(whole):
        i = counters["r"]
        counters["r"] += 1

        def start(src, dst, dev):
            pltpu.make_async_remote_copy(
                src_ref=src, dst_ref=dst, send_sem=ssem.at[i], recv_sem=rsem.at[i],
                device_id=dev, device_id_type=MESH_ID,
            ).start()

        def wait():
            pltpu.make_async_copy(whole, whole, rsem.at[i]).wait()

        def finish():
            pltpu.make_async_copy(whole, whole, ssem.at[i]).wait()

        sends.append(finish)
        return start, wait

    def remote(src, dst, dev):
        start, wait = bundle(dst)
        start(src, dst, dev)
        return wait

    def to_peers(src, dst_of, peers, whole):
        start, wait = bundle(whole)
        for k, peer in enumerate(peers):
            start(src, dst_of(k), peer)
        return wait

    def local(src, dst):
        i = counters["l"]
        counters["l"] += 1
        copy = pltpu.make_async_copy(src, dst, lsem.at[i])
        copy.start()
        return copy

    @pl.when(sp == 0)
    def _():
        uprev[...] = jnp.zeros_like(uprev)
        vgr[0] = jnp.zeros(vgr.shape[1:], F32)
        chr_[0] = jnp.zeros(chr_.shape[1:], BF16)
        gr[0] = jnp.zeros(gr.shape[1:], BF16)
        cgr[0] = jnp.zeros(cgr.shape[1:], BF16)

    @pl.when(sp == S - 1)
    def _():
        unext[...] = jnp.zeros_like(unext)
        vgr[1] = jnp.zeros(vgr.shape[1:], F32)
        chr_[1] = jnp.zeros(chr_.shape[1:], BF16)
        gr[1] = jnp.zeros(gr.shape[1:], BF16)
        cgr[1] = jnp.zeros(cgr.shape[1:], BF16)

    barrier = pltpu.get_barrier_semaphore()
    for peer in sp_peers + dp_peers:
        pl.semaphore_signal(barrier, inc=1, device_id=peer, device_id_type=MESH_ID)
    per = D * LANES // 512
    rows_last = 2048 // D // LANES
    small[...] = jnp.zeros_like(small)
    for ch in range(9):
        small[0:8, ch * 9 : ch * 9 + 9] = (rgb[ch] if ch < 3 else stemd[ch - 3]).astype(F32)
    place = lax.broadcasted_iota(jnp.int32, (1, LANES), 1) // (LANES // per)
    for j, ref in enumerate((g1, b1, g2, b2)):
        row = jnp.concatenate([ref[...].astype(F32)] * per, axis=1)
        small[8 + j : 9 + j, :] = jnp.where(place == lax.rem(dp, per), row, 0.0)
    for j, ref in enumerate((g3, b3)):
        small[12 + j * rows_last : 12 + (j + 1) * rows_last, :] = ref[...].astype(F32)
    own_small = local(small, sm.at[dp])
    own = [
        local(wf_in, wf.at[dp]), local(wd0_in, wd.at[0, :, dp]), local(wd1_in, wd.at[1, :, dp]),
        local(wr_in, wr.at[dp]), local(we_in, we.at[dp]), local(wm_in, wm.at[:, dp]), local(wl_in, wl.at[dp]),
    ]

    def load_cot(part):
        lo = part * PART
        return local(sc_hbm.at[pl.ds(lo, PART)], sc.at[pl.ds(lo % (2 * PART), PART)])

    load_sc = [load_cot(0), load_cot(1)]
    load_x = [local(x_hbm.at[:, r], x3.at[pl.ds(r * NF, NF)]) for r in range(2)]
    load_ct = [local(ct_hbm.at[:, r], ct3.at[pl.ds(r * NF, NF)]) for r in range(2)]
    pl.semaphore_wait(barrier, S - 1 + D - 1)

    halo_waits = []

    def halo(to_prev, to_next, from_prev, from_next, land_prev, land_next):
        i = counters["r"]
        counters["r"] += 2

        def up():
            return pltpu.make_async_remote_copy(
                src_ref=to_prev, dst_ref=land_next, send_sem=ssem.at[i], recv_sem=rsem.at[i],
                device_id=prev_dev, device_id_type=MESH_ID)

        def down():
            return pltpu.make_async_remote_copy(
                src_ref=to_next, dst_ref=land_prev, send_sem=ssem.at[i + 1], recv_sem=rsem.at[i + 1],
                device_id=next_dev, device_id_type=MESH_ID)

        @pl.when(has_prev)
        def _():
            up().start()

        @pl.when(has_next)
        def _():
            down().start()

        def wait():
            @pl.when(has_prev)
            def _():
                down().wait_recv()

            @pl.when(has_next)
            def _():
                up().wait_recv()

        def finish():
            @pl.when(has_prev)
            def _():
                up().wait_send()

            @pl.when(has_next)
            def _():
                down().wait_send()

        halo_waits.append(finish)
        return wait, finish

    wait_small = to_peers(small, lambda k: sm.at[dp], dp_peers, sm.at[pl.ds(0, D - 1)])
    wait_edges, _ = halo(clip, clip, None, None, uprev, unext)

    def gather(mode, dst, eager=True):
        wide = {"A": 1, "B": SX, "D": S}[mode]
        first_q = {"A": q_own, "B": c * SX, "D": 0}[mode]
        only = pl.ds(dp, 1)
        z_links = {bit: bundle(dst(pl.ds(0, DZ // (2 * bit)), first_q, wide)) for bit in z_bits}
        y_start, y_wait = bundle(dst(pl.ds(0, DZ), first_q, wide))
        if mode == "A":
            x_start, x_wait = bundle(dst(pl.ds(0, (D - 1) * (SX - 1)), first_q, 1))
        if mode != "D":
            c_start, c_wait = bundle(dst(pl.ds(0, D - 1), c * SX, SX))
        mine = dst(pl.ds(dp, 1), first_q, wide)
        for bit in reversed(z_bits):
            z_links[bit][0](mine, mine, at_zy(z_pair(bit), y))
        y_start(mine, mine, y_peer)
        yield

        def to_x(part):
            for k in range(1, SX):
                x_start(part, part, x_peer(k))

        def fan(part):
            if eager and mode == "A":
                to_x(part)
            if mode != "D":
                c_start(part, part, c_peer)

        for bit in reversed(z_bits):
            z_links[bit][1]()
            for zz in z_class(z_pair(bit), bit):
                part = dst(pl.ds(zz * 2 + y, 1), first_q, wide)
                for lower in z_bits:
                    if lower < bit:
                        z_links[lower][0](part, part, at_zy(z_pair(lower), y))
                y_start(part, part, y_peer)
                fan(part)
            yield
        y_wait()
        for zz in range(DZ):
            fan(dst(pl.ds(zz * 2 + oy, 1), first_q, wide))
        if mode == "A" and not eager:
            yield "x"
            for n in range(1, D):
                to_x(dst(pl.ds(lax.rem(dp + n, D), 1), first_q, wide))
        yield
        if mode == "A":
            x_wait()
            for k in range(1, SX):
                for n in range(1, D):
                    part = dst(pl.ds(lax.rem(dp + n, D), 1), c * SX + x_from(k), 1)
                    c_start(part, part, c_peer)
            yield
        if mode != "D":
            c_wait()

    def lane_block(index, width, count):
        return pl.ds(pl.multiple_of(index * width, width), width * count)

    fr, fw = wf_in.shape[0], wf_in.shape[1] // S
    mw = wm_in.shape[2] // S
    lr, lw = wl_in.shape[0], wl_in.shape[1] // S

    def first_part(mode, lo, n):
        rows = pl.ds(lo, n)
        return gather(mode, lambda d, q, w: wf.at[d, rows, lane_block(q, fw, w)], True)

    def mid_part(mode, lo, n):
        rows = pl.ds(lo, n)
        return gather(mode, lambda d, q, w: wm.at[rows, d, :, lane_block(q, mw, w)])

    def last_part(mode, lo, n):
        rows = pl.ds(lo, n)
        return gather(mode, lambda d, q, w: wl.at[d, rows, lane_block(q, lw, w)])

    for copy in own:
        copy.wait()
    part_b = fr * 3 // 8
    part_a = (fr - part_b) // 2
    chunks = [
        (0, first_part("A", 0, part_a)),
        (0, first_part("B", 2 * part_a, part_b)),
        (0, first_part("A", part_a, part_a)),
        (1, gather("D", lambda d, q, w: wr.at[d])),
        (1, gather("B", lambda d, q, w: wd.at[c, :, d])),
        (1, gather("D", lambda d, q, w: we.at[d])),
        (1, mid_part("A", 0, 2)), (2, mid_part("B", 2, 3)), (2, mid_part("A", 5, 2)), (3, mid_part("A", 7, 2)),
        (4, last_part("B", 0, lr // 2)), (4, last_part("A", lr // 2, lr // 2)),
    ]
    slot = [0]
    arrived = set()

    held = set()

    def pump(free=0, low=0, high=99):
        for n, (start, chunk) in enumerate(chunks):
            if start > slot[0] or n in arrived or not low <= n < high:
                continue
            if n in held:
                if free == 0:
                    continue
                free -= 1
                held.remove(n)
            try:
                if next(chunk) == "x":
                    held.add(n)
            except StopIteration:
                arrived.add(n)
        slot[0] += 1

    def need(low, high):
        while not arrived.issuperset(range(low, high)):
            pump(len(chunks), low, high)

    pump()

    own_small.wait()
    wait_small()
    wt = sm[:, 0:8, :].reshape(D * 8, LANES)[:, 0:96].astype(BF16)
    for i in range(8):
        rows = dot_nn(wt, band[i])
        for n in range(3):
            tff[n, pl.ds(i, D * 8, stride=8), :] = rows[:, n * LANES : (n + 1) * LANES]
    for n in range(3):
        columns = min(288 - n * LANES, LANES)
        tf[:, n * LANES : n * LANES + columns] = tff[n, :, 0:columns].astype(BF16)
        tb[n * LANES : n * LANES + columns, :] = tff[n].T[0:columns].astype(BF16)

    def mid_vec(j):
        parts = []
        for m in range(D // per):
            row = sm[m * per, 8 + j : 9 + j, :]
            for n in range(1, per):
                row = row + sm[m * per + n, 8 + j : 9 + j, :]
            parts.append(row)
        return jnp.concatenate(parts, axis=1)

    def last_vec(j):
        return jnp.concatenate(
            [sm[d, 8 + j + n : 9 + j + n, :] for d in range(D) for n in range(rows_last)], axis=1)

    gain_1, bias_1, gain_2, bias_2 = [mid_vec(j) for j in range(4)]
    gain_3, bias_3 = last_vec(4), last_vec(4 + rows_last)

    wait_edges()
    row8 = lax.broadcasted_iota(jnp.int32, (8, LANES), 0)

    def load_frame(f, carry):
        ust[f, 0:24, :] = clip[f].astype(F32)
        above, below = uprev[f].astype(F32), unext[f].astype(F32)
        halo_rows = jnp.zeros((8, LANES), F32)
        for ch in range(3):
            halo_rows = jnp.where(row8 == 2 * ch, above[ch * 8 + 7 : ch * 8 + 8], halo_rows)
            halo_rows = jnp.where(row8 == 2 * ch + 1, below[ch * 8 : ch * 8 + 1], halo_rows)
        ust[f, 24:32, :] = halo_rows
        return carry

    lax.fori_loop(0, NF, load_frame, 0)
    zt = tff
    zt[...] = jnp.zeros_like(zt)

    def stem_frame(f, carry):
        before_at, after_at = lax.rem(f + NF - 1, NF), lax.rem(f + 1, NF)
        k_here, k_next = keep[f].astype(F32), keep[after_at].astype(F32)
        frame = ust[f]
        stacked = jnp.concatenate(
            [frame, k_here * (frame - ust[before_at]), k_next * (ust[after_at] - frame)], axis=0)
        stacked = stacked.astype(BF16).astype(F32)
        lane = lax.broadcasted_iota(jnp.int32, stacked.shape, 1)
        left = jnp.where(lane == 0, 0.0, pltpu.roll(stacked, 1, 1))
        right = jnp.where(lane == LANES - 1, 0.0, pltpu.roll(stacked, LANES - 1, 1))
        taps = jnp.concatenate([left, stacked, right], axis=0).astype(BF16)
        place = lax.rem(f, 2 * PART)
        cot = sc[place]
        so[place] = dot_nn(tf[...], taps).astype(BF16)
        back = dot_nn(tb[...], cot)
        dg[f] = (
            jnp.where(lane == LANES - 1, 0.0, pltpu.roll(back[0:96], LANES - 1, 1))
            + back[96:192]
            + jnp.where(lane == 0, 0.0, pltpu.roll(back[192:288], 1, 1)))
        cross = dot_nt(cot, taps)
        for n in range(3):
            columns = min(288 - n * LANES, LANES)
            zt[n, :, 0:columns] += cross[:, n * LANES : n * LANES + columns]
        return carry

    store_so = []
    for part in range(NF // PART):
        lo = part * PART
        load_sc[part].wait()
        if part >= 2:
            store_so[part - 2].wait()
        lax.fori_loop(lo, lo + PART, stem_frame, 0)
        store_so.append(local(so.at[pl.ds(lo % (2 * PART), PART)], so_hbm.at[pl.ds(lo, PART)]))
        if part + 2 < NF // PART:
            load_sc.append(load_cot(part + 2))
        if part % 2:
            pump()
    for copy in store_so[-2:]:
        copy.wait()

    def video_frame(f, carry):
        before_at, after_at = lax.rem(f + NF - 1, NF), lax.rem(f + 1, NF)
        k_here, k_next = keep[f].astype(F32), keep[after_at].astype(F32)
        total = (
            dg[f, 0:32] + k_here * dg[f, 32:64] - k_next * dg[after_at, 32:64]
            + k_here * dg[before_at, 64:96] - k_next * dg[f, 64:96])
        vg_out[f] = total[0:24]
        vgh[f] = total[24:32]
        return carry

    lax.fori_loop(0, NF, video_frame, 0)
    wait_video, _ = halo(vgh, vgh, None, None, vgr.at[0], vgr.at[1])

    stem_grad = jnp.zeros((D * 8, 96), F32)
    for i in range(8):
        for n in range(3):
            part = zt[n, pl.ds(i, D * 8, stride=8), :]
            high = part.astype(BF16)
            low = (part - high.astype(F32)).astype(BF16)
            table = band[i, :, n * LANES : (n + 1) * LANES]
            stem_grad = stem_grad + dot_nt(high, table) + dot_nt(low, table)
    stg[...] = jnp.concatenate([stem_grad, jnp.zeros((D * 8, LANES - 96), F32)], axis=1)
    wait_stem = to_peers(stg, lambda k: stgr.at[k], sp_peers, stgr)

    def rows_loop(group, fn, init):
        def body(i, carry):
            start = (i // (GW // STEP)) * NW + group * GW + (i % (GW // STEP)) * STEP
            return fn(pl.multiple_of(start, STEP), carry)
        return lax.fori_loop(0, 2 * (GW // STEP), body, init)

    def fold(values):
        return values.reshape(STEP // 8, 8, values.shape[1]).sum(axis=0)

    def sp_send(i, parts):
        width = parts[0].shape[1]
        fill = [jnp.zeros((8 - len(parts), width), F32)] if len(parts) < 8 else []
        stat_s[i] = jnp.concatenate(parts + fill, axis=0)
        return to_peers(stat_s.at[i], lambda k: stat_r.at[i, k], sp_peers, stat_r.at[i])

    def sp_total(i, wait):
        wait()
        total = stat_s[i]
        for k in range(S - 1):
            total = total + stat_r[i, k]
        return total

    pixels = jnp.float32(GROUP * 2 * S * 16)
    inv_pixels = 1.0 / (GROUP * 2 * S * 16)

    def two_sums(ref):
        parts = []
        for group in range(NG):
            def add(start, carry):
                value = ref[pl.ds(start, STEP), :]
                return carry[0] + fold(value), carry[1] + fold(value * value)
            zero = jnp.zeros((8, ref.shape[1]), F32)
            one, two = rows_loop(group, add, (zero, zero))
            parts += [jnp.sum(one, axis=0, keepdims=True), jnp.sum(two, axis=0, keepdims=True)]
        return parts

    def moments(total, row):
        mean = total[row : row + 1] * inv_pixels
        variance = total[row + 1 : row + 2] * inv_pixels - mean * mean
        return mean, lax.rsqrt(variance + EPS)

    for copy in load_x:
        copy.wait()
    need(0, 3)
    xs = x3[...].reshape(2 * NW, x3.shape[2])
    for n in range(2):
        z1[:, n * 256 : (n + 1) * 256] = dot_nn(xs, wf[:, :, n * 256 : (n + 1) * 256].reshape(x3.shape[2], 256))
    copies = sp_send(0, two_sums(z1))
    pump(2)
    need(3, 6)
    total = sp_total(0, copies)
    inv_1 = []
    for group in range(NG):
        mean, inv = moments(total, 2 * group)
        inv_1.append(inv)

        def apply_1(start, carry):
            normed = (z1[pl.ds(start, STEP), :] - mean) * inv
            act = jax.nn.silu(gain_1 * normed + bias_1)
            z1[pl.ds(start, STEP), :] = normed
            z3[pl.ds(start, STEP), 0:512] = act
            fab[pl.ds(start, STEP), :] = act.astype(BF16)
            return carry
        rows_loop(group, apply_1, 0)

    rd[...] = dot_nn(fab[...], wr[...].reshape(512, LANES))
    for r in range(2):
        for f in range(NF):
            here = r * NW + f * 16
            past = r * NW + ((f - 1) % NF) * 16
            diff = keep[f].astype(F32) * (rd[here : here + 16, :] - rd[past : past + 16, :])
            chb[r, f * 16 : f * 16 + 16, :] = diff.astype(BF16)
    wait_change, free_change = halo(chb, chb, None, None, chr_.at[0], chr_.at[1])

    def put_shifts(ref, at, values, count, flip):
        width = values.shape[1]
        down, up = shift_down(values, count), shift_up(values, count)
        low, high = (up, down) if flip else (down, up)
        ref[at, :, 0:width] = low.astype(BF16)
        ref[at, :, width : 2 * width] = values.astype(BF16)
        ref[at, :, 2 * width : 3 * width] = high.astype(BF16)

    change = [chb[r].astype(F32) for r in range(2)]
    for r in range(2):
        put_shifts(cs, 1 + r, change[r], 1, False)

    def pool(upper, lower):
        return (pair_sum(upper + lower) * 0.25).astype(BF16).astype(F32)

    put_shifts(ps, 1, pool(change[0], change[1]), 2, False)
    pump(2)
    wait_change()
    above = [chr_[0, r].astype(F32) for r in range(2)]
    below = [chr_[1, r].astype(F32) for r in range(2)]
    put_shifts(cs, 0, above[1], 1, False)
    put_shifts(cs, 3, below[0], 1, False)
    put_shifts(ps, 0, pool(above[0], above[1]), 2, False)
    put_shifts(ps, 2, pool(below[0], below[1]), 2, False)
    full = jnp.zeros((2 * NW, LANES), F32)
    half = jnp.zeros((NW, LANES), F32)
    for a in range(3):
        full = full + dot_nn(cs[a : a + 2].reshape(2 * NW, 384), wd[0, 3 * a : 3 * a + 3].reshape(384, LANES))
        half = half + dot_nn(ps[a], wd[1, 3 * a : 3 * a + 3].reshape(384, LANES))
    comb[...] = (full + jnp.concatenate([half, half], axis=0)).astype(BF16)
    gt[...] = dot_nn(comb[...], we[...].reshape(LANES, 512))

    def apply_gate(i, carry):
        start = pl.multiple_of(i * STEP, STEP)
        gate = jax.nn.sigmoid(gt[pl.ds(start, STEP), :])
        gt[pl.ds(start, STEP), :] = gate
        gated = (z3[pl.ds(start, STEP), 0:512] * (1.0 + gate)).astype(BF16)
        gb[pl.ds(start, STEP), :] = gated
        return carry

    lax.fori_loop(0, 2 * NW // STEP, apply_gate, 0)
    wait_gated, free_gated = halo(gb.at[pl.ds(0, NW)], gb.at[pl.ds(NW, NW)], None, None, gr.at[0], gr.at[1])

    def spread(dst, at, src_fn, flip):
        def body(i, carry):
            start = pl.multiple_of(i * STEP, STEP)
            values = src_fn(start).astype(F32)
            down, up = shift_down(values, 1), shift_up(values, 1)
            low, high = (up, down) if flip else (down, up)
            dst[at, pl.ds(start, STEP), 0:512] = low.astype(BF16)
            dst[at, pl.ds(start, STEP), 512:1024] = values.astype(BF16)
            dst[at, pl.ds(start, STEP), 1024:1536] = high.astype(BF16)
            return carry
        lax.fori_loop(0, NW // STEP, body, 0)

    for r in range(2):
        spread(gs, 1 + r, lambda start, r=r: gb[pl.ds(r * NW + start, STEP), :], False)

    def taps_of(a):
        return wm[3 * a : 3 * a + 3].reshape(1536, 512)

    need(6, 10)
    z2[...] = dot_nn(gs[1:3].reshape(2 * NW, 1536), taps_of(1))
    z2[0:NW, :] += dot_nn(gs[2], taps_of(2))
    z2[NW : 2 * NW, :] += dot_nn(gs[1], taps_of(0))
    wait_gated()
    spread(gs, 0, lambda start: gr[0, pl.ds(start, STEP), :], False)
    spread(gs, 3, lambda start: gr[1, pl.ds(start, STEP), :], False)
    z2[0:NW, :] += dot_nn(gs[0], taps_of(0))
    z2[NW : 2 * NW, :] += dot_nn(gs[3], taps_of(2))
    copies = sp_send(1, two_sums(z2))
    need(10, 12)
    for copy in load_ct:
        copy.wait()
    total = sp_total(1, copies)
    inv_2 = []
    for group in range(NG):
        mean, inv = moments(total, 2 * group)
        inv_2.append(inv)

        def apply_2(start, carry):
            normed = (z2[pl.ds(start, STEP), :] - mean) * inv
            z2[pl.ds(start, STEP), :] = normed
            sab[pl.ds(start, STEP), :] = jax.nn.silu(gain_2 * normed + bias_2).astype(BF16)
            return carry
        rows_loop(group, apply_2, 0)

    def ct_rows(start, lo, width):
        return ct3[pl.ds(start // 16, STEP // 16), :, lo : lo + width].reshape(STEP, width).astype(F32)

    def x_rows(start, lo, width):
        return x3[pl.ds(start // 16, STEP // 16), :, lo : lo + width].reshape(STEP, width).astype(F32)

    last_copies = []
    for n in range(4):
        lo = n * 512
        z3[:, lo : lo + 512] = dot_nn(sab[...], wl[:, :, lo : lo + 512].reshape(512, 512))
        parts = []
        for group in range(NG):
            def add_3(start, carry):
                value = z3[pl.ds(start, STEP), lo : lo + 512]
                cot = ct_rows(start, lo, 512)
                return (carry[0] + fold(value), carry[1] + fold(value * value),
                        carry[2] + fold(cot), carry[3] + fold(cot * value))
            zero = jnp.zeros((8, 512), F32)
            sums = rows_loop(group, add_3, (zero, zero, zero, zero))
            parts += [jnp.sum(item, axis=0, keepdims=True) for item in sums]
        st3_s[n] = jnp.concatenate(parts, axis=0)
        last_copies.append(to_peers(st3_s.at[n], lambda k, n=n: st3_r.at[n, k], sp_peers, st3_r.at[n]))
    gain_3_grad, bias_3_grad = [], []
    stores = []

    def free_part():
        if len(stores) >= 2:
            for copy in stores[-2]:
                copy.wait()

    def store_part(n, target):
        stores.append([local(ost.at[n % 2, pl.ds(r * NF, NF)], target.at[:, r, :, pl.ds(n * 512, 512)]) for r in range(2)])

    for n in range(4):
        lo = n * 512
        free_part()
        last_copies[n]()
        total = st3_s[n]
        for k in range(S - 1):
            total = total + st3_r[n, k]
        gain, bias = gain_3[:, lo : lo + 512], bias_3[:, lo : lo + 512]
        gain_sum = bias_sum = jnp.zeros((1, 512), F32)
        for group in range(NG):
            row = 4 * group
            mean, inv = moments(total, row)
            cot_sum = total[row + 2 : row + 3]
            cot_normed = inv * (total[row + 3 : row + 4] - mean * cot_sum)
            gain_sum, bias_sum = gain_sum + cot_normed, bias_sum + cot_sum
            cot_mean, slope_mean = cot_sum * inv_pixels, cot_normed * inv_pixels
            scale = gain * inv

            def apply_3(start, carry):
                normed = (z3[pl.ds(start, STEP), lo : lo + 512] - mean) * inv
                cot = ct_rows(start, lo, 512)
                out = x_rows(start, lo, 512) + gain * normed + bias
                ost[n % 2, pl.ds(start // 16, STEP // 16)] = out.astype(BF16).reshape(STEP // 16, 16, 512)
                lgb[pl.ds(start, STEP), lo : lo + 512] = (
                    scale * (cot - cot_mean - normed * slope_mean)).astype(BF16)
                return carry
            rows_loop(group, apply_3, 0)
        store_part(n, out_hbm)
        gain_3_grad.append(gain_sum)
        bias_3_grad.append(bias_sum)

    def each(count, fn):
        def body(i, carry):
            fn(i)
            return carry
        lax.fori_loop(0, count, body, 0)

    def share(block, several):
        x_start, x_wait = bundle(several.at[pl.ds(0, SX - 1)])
        c_start, c_wait = bundle(several)
        for k in range(1, SX):
            x_start(block(q_own), block(q_own), x_peer(k))
        c_start(block(q_own), block(q_own), c_peer)
        yield
        x_wait()
        for k in range(1, SX):
            part = block(c * SX + x_from(k))
            c_start(part, part, c_peer)
        yield
        c_wait()

    def z_steps(part, rz, add):
        at = 0
        for bit in z_bits:
            keep_z, give_z = z_class(z, bit), z_class(z_pair(bit), bit)
            start, wait = bundle(rz.at[pl.ds(at, len(keep_z))])
            for j, zz in enumerate(give_z):
                start(part(zz), rz.at[at + j], at_zy(z_pair(bit), y))
            yield
            wait()
            for j, zz in enumerate(keep_z):
                add(part(zz), rz.at[at + j])
            at += len(keep_z)

    def wide_first(grad, lo, n, order, rc, rx, ry, rz, fb):
        rows = pl.ds(lo, n)
        half = pl.ds(c * SX, SX)
        mine = q_own

        def add(dst, *others):
            value = dst[...].astype(F32)
            for other in others:
                value = value + other[...].astype(F32)
            dst[...] = value.astype(BF16)

        wait = remote(grad.at[pl.ds(oc * SX, SX), :, :, rows], rc, c_peer)
        yield
        wait()

        def add_c(i):
            for xx in range(SX):
                for yy in range(2):
                    add(grad.at[c * SX + xx, i, yy, rows], rc.at[xx, i, yy])
        each(DZ, add_c)
        if order == "xyz":
            start, wait = bundle(rx)
            for k in range(1, SX):
                start(grad.at[c * SX + x_to(k), :, :, rows], rx.at[k - 1], x_peer(k))
            yield
            wait()

            def add_x(i):
                for yy in range(2):
                    add(grad.at[mine, i, yy, rows], *[rx.at[k, i, yy] for k in range(SX - 1)])
            each(DZ, add_x)
            wait = remote(grad.at[mine, :, oy, rows], ry, y_peer)
            yield
            wait()
            each(DZ, lambda i: add(grad.at[mine, i, y, rows], ry.at[i]))
            yield from z_steps(lambda zz: grad.at[mine, zz, y, rows], rz, add)
            parts = []
        else:
            wait = remote(grad.at[half, :, oy, rows], ry, y_peer)
            yield
            wait()

            def add_y(i):
                for xx in range(SX):
                    add(grad.at[c * SX + xx, i, y, rows], ry.at[xx, i])
            each(DZ, add_y)
            def add_half(dst, src):
                for xx in range(SX):
                    add(dst.at[xx], src.at[xx])
            yield from z_steps(lambda zz: grad.at[half, zz, y, rows], rz, add_half)
            start, wait = bundle(rx)
            for k in range(1, SX):
                start(grad.at[c * SX + x_to(k), z, y, rows], rx.at[k - 1], x_peer(k))
            yield
            wait()
            parts = [rx.at[k] for k in range(SX - 1)]
        value = grad[mine, z, y, rows].astype(F32)
        for part in parts:
            value = value + part[...].astype(F32)
        fb[mine, rows] = value.astype(BF16)
        yield from share(lambda q: fb.at[q, rows], fb.at[pl.ds(0, SX), rows])

    def wide_mid(grad, lo, n, order, rc, rx, ry, rz, fb):
        taps = pl.ds(lo, n)
        half = pl.ds(c * SX, SX)
        mine = q_own

        def add(dst, *others):
            value = dst[...].astype(F32)
            for other in others:
                value = value + other[...].astype(F32)
            dst[...] = value.astype(BF16)

        wait = remote(grad.at[pl.ds(oc * SX, SX), taps], rc, c_peer)
        yield
        wait()

        def add_c(i):
            t, zz = i // DZ, i % DZ
            for xx in range(SX):
                add(grad.at[c * SX + xx, lo + t, zz], rc.at[xx, t, zz])
        each(n * DZ, add_c)
        if order == "xyz":
            start, wait = bundle(rx)
            for k in range(1, SX):
                start(grad.at[c * SX + x_to(k), taps], rx.at[k - 1], x_peer(k))
            yield
            wait()

            def add_x(i):
                t, zz = i // DZ, i % DZ
                add(grad.at[mine, lo + t, zz], *[rx.at[k, t, zz] for k in range(SX - 1)])
            each(n * DZ, add_x)
            wait = remote(grad.at[mine, taps, :, oy], ry, y_peer)
            yield
            wait()

            def add_y(i):
                t, zz = i // DZ, i % DZ
                add(grad.at[mine, lo + t, zz, y], ry.at[t, zz])
            each(n * DZ, add_y)
            def add_taps(dst, src):
                each(n, lambda t: add(dst.at[t], src.at[t]))
            yield from z_steps(lambda zz: grad.at[mine, taps, zz, y], rz, add_taps)
            parts = []
        else:
            wait = remote(grad.at[half, taps, :, oy], ry, y_peer)
            yield
            wait()

            def add_y(i):
                t, zz = i // DZ, i % DZ
                for xx in range(SX):
                    add(grad.at[c * SX + xx, lo + t, zz, y], ry.at[xx, t, zz])
            each(n * DZ, add_y)
            def add_half(dst, src):
                for xx in range(SX):
                    each(n, lambda t, xx=xx: add(dst.at[xx, t], src.at[xx, t]))
            yield from z_steps(lambda zz: grad.at[half, taps, zz, y], rz, add_half)
            start, wait = bundle(rx)
            for k in range(1, SX):
                start(grad.at[c * SX + x_to(k), taps, z, y], rx.at[k - 1], x_peer(k))
            yield
            wait()
            parts = [rx.at[k] for k in range(SX - 1)]

        def finish(t):
            value = grad[mine, lo + t, z, y].astype(F32)
            for part in parts:
                value = value + part[t].astype(F32)
            fb[mine, lo + t] = value.astype(BF16)
        each(n, finish)
        yield from share(lambda q: fb.at[q, taps], fb.at[pl.ds(0, SX), taps])

    def reduce_diff():
        wait = remote(g_diff.at[oc], rcd, c_peer)
        yield
        wait()

        def add_c(i):
            t, zz = i // DZ, i % DZ
            for yy in range(2):
                value = g_diff[c, t, zz, yy].astype(F32) + rcd[t, zz, yy].astype(F32)
                g_diff[c, t, zz, yy] = value.astype(BF16)
        each(9 * DZ, add_c)
        wait = remote(g_diff.at[c, :, :, oy], ryd, y_peer)
        yield
        wait()

        def add_y(i):
            t, zz = i // DZ, i % DZ
            value = g_diff[c, t, zz, y].astype(F32) + ryd[t, zz].astype(F32)
            g_diff[c, t, zz, y] = value.astype(BF16)
        each(9 * DZ, add_y)
        def add_taps(dst, src):
            def one(t):
                dst[t] = (dst[t].astype(F32) + src[t].astype(F32)).astype(BF16)
            each(9, one)
        yield from z_steps(lambda zz: g_diff.at[c, :, zz, y], rzd, add_taps)

        def widen(t):
            fdx[t] = g_diff[c, t, z, y].astype(F32)
        each(9, widen)
        start, wait = bundle(rxd)
        for k in range(1, SX):
            start(fdx, rxd.at[k - 1], x_peer(k))
        yield
        wait()

        def add_x(t):
            value = fdx[t]
            for k in range(1, SX):
                value = value + rxd[k - 1, t]
            fdo[c, t] = value
        each(9, add_x)
        wait = remote(fdo.at[c], fdo.at[c], c_peer)
        yield
        wait()
        od_out[...] = fdo[...]

    def reduce_rest():
        wait = remote(g_re, rcr, c_peer)
        yield
        wait()

        def add_c(zz):
            for yy in range(2):
                value = g_re[zz, yy].astype(F32) + rcr[zz, yy].astype(F32)
                rcr[zz, yy] = value.astype(BF16)
        each(DZ, add_c)
        wait = remote(rcr.at[:, oy], ryr, y_peer)
        yield
        wait()

        def add_y(zz):
            value = rcr[zz, y].astype(F32) + ryr[zz].astype(F32)
            rcr[zz, y] = value.astype(BF16)
        each(DZ, add_y)
        def add_z(dst, src):
            dst[...] = (dst[...].astype(F32) + src[...].astype(F32)).astype(BF16)
        yield from z_steps(lambda zz: rcr.at[zz, y], rzr, add_z)
        frx[...] = rcr[z, y].astype(F32)
        start, wait = bundle(rxr)
        for k in range(1, SX):
            start(frx, rxr.at[k - 1], x_peer(k))
        yield
        wait()
        value = frx[...]
        for k in range(1, SX):
            value = value + rxr[k - 1]
        n_red, n_exp = or_out.shape[0], oe_out.shape[0]
        or_out[...] = value[0:n_red]
        for b in range(4):
            oe_out[:, b * LANES : (b + 1) * LANES] = value[n_red + b * n_exp : n_red + (b + 1) * n_exp]

    bufs = [bufs[n : n + 4] for n in range(0, len(bufs), 4)]
    spans_f, spans_m, spans_l = portions(fr, 9, lr)
    red_first = [wide_first(g_first, lo, n, order, *bufs.pop(0), fbf) for order, lo, n in spans_f]
    red_mid = [wide_mid(g_mid, lo, n, order, *bufs.pop(0), fbm) for order, lo, n in spans_m]
    red_last = [wide_first(g_last, lo, n, order, *bufs.pop(0), fbl) for order, lo, n in spans_l]
    chains = {"d": reduce_diff(), "r": reduce_rest()}
    for name, parts in (("f", red_first), ("m", red_mid), ("l", red_last)):
        chains.update({name + str(n): part for n, part in enumerate(parts)})

    def at(point):
        for name in ORDER[point]:
            next(chains[name], None)

    for finish in (free_gated, free_change):
        finish()
        halo_waits.remove(finish)
    mgb, mgr = gb, gr
    sg2, gg = z3.at[:, 0:512], z3.at[:, 512:1024]
    sg2[...] = dot_nt(lgb[...], wl[...].reshape(512, 2048))
    parts = []
    for group in range(NG):
        def slope_2(start, carry):
            normed = z2[pl.ds(start, STEP), :]
            _, slope = silu_parts(gain_2 * normed + bias_2)
            value = sg2[pl.ds(start, STEP), :] * slope
            sg2[pl.ds(start, STEP), :] = value
            return carry[0] + fold(value), carry[1] + fold(value * normed)
        zero = jnp.zeros((8, 512), F32)
        sums = rows_loop(group, slope_2, (zero, zero))
        parts += [jnp.sum(item, axis=0, keepdims=True) for item in sums]
    copies = sp_send(2, parts)
    for n in range(4):
        g_last[n] = dot_tn(sab[...], lgb[:, n * 512 : (n + 1) * 512]).astype(BF16).reshape(DZ, 2, lr, 512)
    at("dwl")
    at("bn2")
    total = sp_total(2, copies)
    gain_2_grad = bias_2_grad = jnp.zeros((1, 512), F32)
    for group in range(NG):
        row = 2 * group
        bias_sum, gain_sum = total[row : row + 1], total[row + 1 : row + 2]
        gain_2_grad, bias_2_grad = gain_2_grad + gain_sum, bias_2_grad + bias_sum
        scale = gain_2 * inv_2[group]

        def apply_2b(start, carry):
            value = sg2[pl.ds(start, STEP), :] - bias_sum * inv_pixels
            value = scale * (value - z2[pl.ds(start, STEP), :] * (gain_sum * inv_pixels))
            mgb[pl.ds(start, STEP), :] = value.astype(BF16)
            return carry
        rows_loop(group, apply_2b, 0)
    wait_mid, _ = halo(mgb.at[pl.ds(0, NW)], mgb.at[pl.ds(NW, NW)], None, None, mgr.at[0], mgr.at[1])
    at("mid")
    for a in range(3):
        for b in range(3):
            grad = dot_tn(gs[a : a + 2, :, b * 512 : (b + 1) * 512].reshape(2 * NW, 512), mgb[...]).astype(BF16)
            for qq in range(S):
                g_mid[qq, 3 * a + b] = grad[:, qq * mw : (qq + 1) * mw].reshape(DZ, 2, wm_in.shape[1], mw)
        next(red_mid[a])
    mgs = gs
    for r in range(2):
        spread(mgs, 1 + r, lambda start, r=r: mgb[pl.ds(r * NW + start, STEP), :], True)

    def back_taps(lhs, a):
        total = dot_nt(lhs[:, 0:512], wm[3 * a].reshape(512, 512))
        for b in range(1, 3):
            total = total + dot_nt(lhs[:, b * 512 : (b + 1) * 512], wm[3 * a + b].reshape(512, 512))
        return total

    gg[...] = back_taps(mgs[1:3].reshape(2 * NW, 1536), 1)
    gg[0:NW, :] += back_taps(mgs[2], 0)
    gg[NW : 2 * NW, :] += back_taps(mgs[1], 2)
    at("own")
    wait_mid()
    spread(mgs, 0, lambda start: mgr[0, pl.ds(start, STEP), :], True)
    spread(mgs, 3, lambda start: mgr[1, pl.ds(start, STEP), :], True)
    gg[0:NW, :] += back_taps(mgs[0], 2)
    gg[NW : 2 * NW, :] += back_taps(mgs[3], 0)

    def gate_back(i, carry):
        start = pl.multiple_of(i * STEP, STEP)
        gate = gt[pl.ds(start, STEP), :]
        act = jax.nn.silu(gain_1 * z1[pl.ds(start, STEP), :] + bias_1)
        value = gg[pl.ds(start, STEP), :] * act * gate * (1.0 - gate)
        fgb[pl.ds(start, STEP), :] = value.astype(BF16)
        return carry

    lax.fori_loop(0, 2 * NW // STEP, gate_back, 0)
    cg = dot_nt(fgb[...], we[...].reshape(LANES, 512)).astype(BF16)
    cg_rows = [cg[r * NW : (r + 1) * NW].astype(F32) for r in range(2)]
    hg = pair_sum(cg_rows[0] + cg_rows[1]).astype(BF16)
    for r in range(2):
        cgx[r, 0] = cg_rows[r].astype(BF16)
        cgx[r, 1] = hg
    wait_cg, _ = halo(cgx.at[0], cgx.at[1], None, None, cgr.at[0], cgr.at[1])
    at("gate")
    n_exp = we_in.shape[0]
    grad = dot_tn(comb[...], fgb[...]).astype(BF16)
    n_red = wr_in.shape[0]
    for b in range(4):
        g_re[:, :, n_red + b * n_exp : n_red + (b + 1) * n_exp, :] = grad[
            :, b * LANES : (b + 1) * LANES].reshape(DZ, 2, n_exp, LANES)
    for r in range(2):
        put_shifts(cgs, 1 + r, cg_rows[r], 1, True)
    put_shifts(hgs, 1, hg.astype(F32), 2, True)
    for a in range(3):
        grad = dot_tn(cs[a : a + 2].reshape(2 * NW, 384), cg).astype(BF16)
        g_diff[0, 3 * a : 3 * a + 3] = grad.reshape(3, DZ, 2, wd0_in.shape[1], LANES)
        grad = (0.5 * dot_tn(ps[a], hg)).astype(BF16)
        g_diff[1, 3 * a : 3 * a + 3] = grad.reshape(3, DZ, 2, wd0_in.shape[1], LANES)
    at("diff")
    wait_cg()
    put_shifts(cgs, 0, cgr[0, 0].astype(F32), 1, True)
    put_shifts(cgs, 3, cgr[1, 0].astype(F32), 1, True)
    put_shifts(hgs, 0, cgr[0, 1].astype(F32), 2, True)
    put_shifts(hgs, 2, cgr[1, 1].astype(F32), 2, True)
    full = jnp.zeros((2 * NW, LANES), F32)
    half = jnp.zeros((NW, LANES), F32)
    for a in range(3):
        for b in range(3):
            lanes = slice(b * LANES, (b + 1) * LANES)
            full = full + dot_nt(
                cgs[2 - a : 4 - a, :, lanes].reshape(2 * NW, LANES), wd[0, 3 * a + b].reshape(LANES, LANES))
            half = half + dot_nt(hgs[2 - a, :, lanes], wd[1, 3 * a + b].reshape(LANES, LANES))
    rd[...] = full + 0.25 * jnp.concatenate([half, half], axis=0)
    for r in range(2):
        for f in range(NF):
            here = r * NW + f * 16
            after = r * NW + ((f + 1) % NF) * 16
            diff = (keep[f].astype(F32) * rd[here : here + 16, :]
                    - keep[(f + 1) % NF].astype(F32) * rd[after : after + 16, :])
            chb[r, f * 16 : f * 16 + 16, :] = diff.astype(BF16)
    rgb = chb[...].reshape(2 * NW, LANES)
    sg2[...] = dot_nt(rgb, wr[...].reshape(512, LANES))

    parts = []
    for group in range(NG):
        def slope_1(start, carry):
            normed = z1[pl.ds(start, STEP), :]
            _, slope = silu_parts(gain_1 * normed + bias_1)
            value = gg[pl.ds(start, STEP), :] * (1.0 + gt[pl.ds(start, STEP), :]) + sg2[pl.ds(start, STEP), :]
            value = value * slope
            sg2[pl.ds(start, STEP), :] = value
            return carry[0] + fold(value), carry[1] + fold(value * normed)
        zero = jnp.zeros((8, 512), F32)
        sums = rows_loop(group, slope_1, (zero, zero))
        parts += [jnp.sum(item, axis=0, keepdims=True) for item in sums]
    copies = sp_send(3, parts)
    g_re[:, :, 0:n_red, :] = dot_tn(fab[...], rgb).astype(BF16).reshape(DZ, 2, n_red, LANES)
    at("bn1")
    total = sp_total(3, copies)
    gain_1_grad = bias_1_grad = jnp.zeros((1, 512), F32)
    for group in range(NG):
        row = 2 * group
        bias_sum, gain_sum = total[row : row + 1], total[row + 1 : row + 2]
        gain_1_grad, bias_1_grad = gain_1_grad + gain_sum, bias_1_grad + bias_sum
        scale = gain_1 * inv_1[group]

        def apply_1b(start, carry):
            value = sg2[pl.ds(start, STEP), :] - bias_sum * inv_pixels
            value = scale * (value - z1[pl.ds(start, STEP), :] * (gain_sum * inv_pixels))
            fgb[pl.ds(start, STEP), :] = value.astype(BF16)
            return carry
        rows_loop(group, apply_1b, 0)

    wait_stem()
    stem_total = stg[...]
    for k in range(S - 1):
        stem_total = stem_total + stgr[k]
    gain_3_all = jnp.concatenate(gain_3_grad, axis=1)
    bias_3_all = jnp.concatenate(bias_3_grad, axis=1)
    for d in range(D):
        mid_at, last_at = (d // per) * LANES, d * rows_last * LANES
        rows = [v[:, mid_at : mid_at + LANES] for v in (gain_1_grad, bias_1_grad, gain_2_grad, bias_2_grad)]
        for v in (gain_3_all, bias_3_all):
            rows += [v[:, last_at + n * LANES : last_at + (n + 1) * LANES] for n in range(rows_last)]
        sms[d, 0:8, :] = stem_total[d * 8 : d * 8 + 8]
        sms[d, 8:16, :] = jnp.concatenate(rows, axis=0)
    small_start, wait_small_back = bundle(smr)
    for k in range(1, D):
        small_start(sms.at[lax.rem(dp + k, D)], smr.at[k - 1], dp_peers[k - 1])

    at("fg")
    for n in range(4):
        grad = dot_tn(x3[:, :, n * 512 : (n + 1) * 512].reshape(2 * NW, 512), fgb[...]).astype(BF16)
        per_chunk = 512 // (2 * fr)
        for qq in range(S):
            g_first[qq, n * per_chunk : (n + 1) * per_chunk] = grad[:, qq * fw : (qq + 1) * fw].reshape(
                per_chunk, 2, fr, fw)
    at("dwf")
    at("add")
    weights_first = wf[...].reshape(2048, 512)
    for n in range(4):
        lo = n * 512
        free_part()
        z3[:, lo : lo + 512] = dot_nt(fgb[...], weights_first[lo : lo + 512])

        def apply_in(i, carry):
            start = pl.multiple_of(i * STEP, STEP)
            value = z3[pl.ds(start, STEP), lo : lo + 512] + ct_rows(start, lo, 512)
            ost[n % 2, pl.ds(start // 16, STEP // 16)] = value.astype(BF16).reshape(STEP // 16, 16, 512)
            return carry
        lax.fori_loop(0, 2 * NW // STEP, apply_in, 0)
        store_part(n, ig_hbm)
        at("in" + str(n))
    for point in sorted(ORDER):
        if point[0] == "t":
            at(point)
    for chain in chains.values():
        for _ in chain:
            pass
    grad_stores = [local(fbf, fbf_hbm), local(fbm, fbm_hbm), local(fbl, fbl_hbm)]

    assert counters["r"] <= ssem.shape[0] and counters["l"] <= lsem.shape[0], counters
    wait_video()

    def video_edges(f, carry):
        for ch in range(3):
            rows = slice(ch * 8, ch * 8 + 8)
            from_prev = vgr[0, f, ch * 2 + 1 : ch * 2 + 2, :]
            from_next = vgr[1, f, ch * 2 : ch * 2 + 1, :]
            vg_out[f, rows] += jnp.where(row8 == 0, from_prev, jnp.where(row8 == 7, from_next, 0.0))
        return carry

    lax.fori_loop(0, NF, video_edges, 0)
    value = sms[dp]
    wait_small_back()
    for k in range(D - 1):
        value = value + smr[k]
    osm_out[...] = value
    for finish in sends + halo_waits:
        finish()
    for copy in grad_stores:
        copy.wait()
    for part in stores[-2:]:
        for copy in part:
            copy.wait()


def final_kernel(
    sizes, so, vg, out, ig, fbf, fbm, fbl, gr, gd, ge, gsm,
    so_o, vg_o, out_o, ig_o, rgb_o, stemd_o, first_o, mid_o, last_o, red_o, dfull_o, dhalf_o, exp_o,
    g1_o, b1_o, g2_o, b2_o, g3_o, b3_o, sems, so_v, out_v, ig_v, vg_v,
):
    D, S = sizes
    loads, copies = [], []
    for src, through, dst in ((so, so_v, so_o), (out, out_v, out_o), (ig, ig_v, ig_o), (vg, vg_v, vg_o)):
        half = src.shape[0] // 2
        for rows in (pl.ds(0, half), pl.ds(half, half)):
            n = len(loads)
            loads.append(pltpu.make_async_copy(src.at[rows], through.at[rows], sems.at[0, n]))
            copies.append(pltpu.make_async_copy(through.at[rows], dst.at[rows], sems.at[1, n]))
    for copy in loads:
        copy.start()
    for load, copy in zip(loads, copies):
        load.wait()
        copy.start()
    fw, lw = fbf.shape[2], fbl.shape[2]
    for q in range(S):
        first_o[:, q * fw : (q + 1) * fw] = fbf[q].astype(F32)
        last_o[:, q * lw : (q + 1) * lw] = fbl[q].astype(F32)
        for t in range(9):
            mid_o[t, :, q * fw : (q + 1) * fw] = fbm[q, t].astype(F32)
    red_o[...] = gr[...]
    dfull_o[...] = gd[0]
    dhalf_o[...] = gd[1]
    exp_o[...] = ge[...]
    for ch in range(9):
        value = gsm[0:8, ch * 9 : ch * 9 + 9]
        if ch < 3:
            rgb_o[ch] = value
        else:
            stemd_o[ch - 3] = value
    width = g1_o.shape[0]
    per = LANES // width
    here = lax.rem(lax.axis_index("dp"), per)
    for j, ref in enumerate((g1_o, b1_o, g2_o, b2_o)):
        row = gsm[8 + j]
        value = row[0:width]
        for n in range(1, per):
            value = jnp.where(here == n, row[n * width : (n + 1) * width], value)
        ref[...] = value
    count = g3_o.shape[0] // LANES
    for j, ref in enumerate((g3_o, b3_o)):
        for n in range(count):
            ref[n * LANES : (n + 1) * LANES] = gsm[12 + j * count + n]
    for copy in copies:
        copy.wait()


def on_device_kernel(
    clip_video, section_input, keep_mask, w_rgb, w_stem_diff, w_first, w_middle, w_last, w_reduce,
    w_diff_full, w_diff_half, w_expand, gain_first, bias_first, gain_middle, bias_middle, gain_last,
    bias_last, stem_cot, section_cot,
):
    D, S = lax.axis_size("dp"), lax.axis_size("sp")
    DZ, SX = D // 2, S // 2
    NF = clip_video.shape[0]
    NW = NF * 16
    width = 512 // D
    band = jnp.asarray(band_table(8), BF16)
    fr, fw = w_first.shape[0], 512 // S
    mr, lr, rr = w_middle.shape[1], w_last.shape[0], w_reduce.shape[0]
    dr, er = w_diff_full.shape[1], w_expand.shape[0]
    lw = 2048 // S
    shape = jax.ShapeDtypeStruct
    vm = pltpu.VMEM
    any_spec = pl.BlockSpec(memory_space=pl.ANY)
    vmem_spec = pl.BlockSpec(memory_space=pltpu.VMEM)
    n_rem, n_loc = 146, 48
    re_rows = rr + 4 * er
    scratch = [
        pltpu.SemaphoreType.DMA((n_rem,)), pltpu.SemaphoreType.DMA((n_rem,)), pltpu.SemaphoreType.DMA((n_loc,)),
        vm((D, fr, 512), BF16), vm((9, D, mr, 512), BF16), vm((D, lr, 2048), BF16),
        vm((D, rr, LANES), BF16), vm((2, 9, D, dr, LANES), BF16), vm((D, er, 512), BF16),
        vm((2 * NF, 16, 2048), BF16), vm((2 * NF, 16, 2048), BF16),
        vm((2 * PART, 512, LANES), BF16), vm((2 * PART, 512, LANES), BF16),
        vm((NF, 32, LANES), F32), vm((NF, 24, LANES), BF16), vm((NF, 24, LANES), BF16),
        vm((16, LANES), F32), vm((D, 16, LANES), F32), vm((512, 288), BF16), vm((3, 512, LANES), F32), vm((288, 512), BF16),
        vm((NF, 96, LANES), F32),
        vm((NF, 8, LANES), F32), vm((2, NF, 8, LANES), F32), vm((D * 8, LANES), F32), vm((S - 1, D * 8, LANES), F32),
        vm((4, 8, 512), F32), vm((4, S - 1, 8, 512), F32), vm((4, 8, 512), F32), vm((4, S - 1, 8, 512), F32),
        vm((2 * NW, 512), F32), vm((2 * NW, 512), BF16), vm((2 * NW, 512), F32),
        vm((2 * NW, LANES), F32), vm((2, NW, LANES), BF16), vm((2, 2, NW, LANES), BF16),
        vm((4, NW, 384), BF16), vm((3, NW, 384), BF16), vm((2 * NW, LANES), BF16),
        vm((2 * NW, 512), BF16), vm((2, NW, 512), BF16), vm((4, NW, 1536), BF16),
        vm((2 * NW, 512), F32), vm((2 * NW, 512), BF16), vm((2 * NW, 2048), F32), vm((2 * NW, 2048), BF16),
        vm((2, 2, NW, LANES), BF16), vm((2, 2, NW, LANES), BF16),
        vm((4, NW, 384), BF16), vm((3, NW, 384), BF16), vm((2 * NW, 512), BF16), vm((2, 2 * NF, 16, 512), BF16),
        vm((S, DZ, 2, fr, fw), BF16), vm((S, 9, DZ, 2, mr, fw), BF16), vm((S, DZ, 2, lr, lw), BF16),
        vm((2, 9, DZ, 2, dr, LANES), BF16), vm((DZ, 2, re_rows, LANES), BF16),
        vm((9, DZ, 2, dr, LANES), BF16), vm((9, DZ, dr, LANES), BF16), vm((DZ - 1, 9, dr, LANES), BF16),
        vm((9, dr, LANES), F32), vm((SX - 1, 9, dr, LANES), F32), vm((2, 9, dr, LANES), F32),
        vm((DZ, 2, re_rows, LANES), BF16), vm((DZ, re_rows, LANES), BF16), vm((DZ - 1, re_rows, LANES), BF16),
        vm((re_rows, LANES), F32), vm((SX - 1, re_rows, LANES), F32),
        vm((S, fr, fw), BF16), vm((S, 9, mr, fw), BF16), vm((S, lr, lw), BF16),
        vm((D, 16, LANES), F32), vm((D - 1, 16, LANES), F32),
    ]

    def landing(spans, shape_of):
        for order, _, n in spans:
            extra = (SX,) if order == "yzx" else ()
            scratch.append(vm((SX,) + shape_of(n, (DZ, 2)), BF16))
            scratch.append(vm((SX - 1,) + shape_of(n, (DZ, 2) if order == "xyz" else ()), BF16))
            scratch.append(vm(extra + shape_of(n, (DZ,)), BF16))
            scratch.append(vm((DZ - 1,) + extra + shape_of(n, ()), BF16))

    spans_f, spans_m, spans_l = portions(fr, 9, lr)
    landing(spans_f, lambda n, lead: lead + (n, fw))
    landing(spans_m, lambda n, lead: (n,) + lead + (mr, fw))
    landing(spans_l, lambda n, lead: lead + (n, lw))
    outs = pl.pallas_call(
        functools.partial(whole_kernel, (D, S, NF)),
        out_shape=(
            shape((NF, 512, LANES), BF16), shape((NF, 24, LANES), F32),
            shape(section_input.shape, BF16), shape(section_input.shape, BF16),
            shape((S, fr, fw), BF16), shape((S, 9, mr, fw), BF16), shape((S, lr, lw), BF16), shape((rr, LANES), F32),
            shape((2, 9, dr, LANES), F32), shape((er, 512), F32), shape((16, LANES), F32),
        ),
        in_specs=[pl.BlockSpec(memory_space=pltpu.SMEM)] + [vmem_spec] * 10 + [any_spec] * 10,
        out_specs=(any_spec, vmem_spec) + (any_spec,) * 5 + (vmem_spec,) * 4,
        scratch_shapes=scratch,
        compiler_params=pltpu.CompilerParams(
            collective_id=0, has_side_effects=True, vmem_limit_bytes=VMEM_BYTES),
        name="tdn_blocks",
    )(
        keep_mask, clip_video.reshape(NF, 24, LANES), w_rgb.transpose(1, 2, 0), w_stem_diff.transpose(1, 2, 0),
        gain_first.reshape(1, -1), bias_first.reshape(1, -1), gain_middle.reshape(1, -1), bias_middle.reshape(1, -1),
        gain_last.reshape(-1, LANES), bias_last.reshape(-1, LANES), band, section_input, section_cot, stem_cot.reshape(NF, 512, LANES),
        w_first, w_middle, w_last, w_reduce, w_diff_full, w_diff_half, w_expand,
    )
    results = (
        shape(stem_cot.shape, BF16), shape(clip_video.shape, F32), shape(section_input.shape, BF16),
        shape(section_input.shape, BF16), shape((3, 8, 9), F32), shape((6, 8, 9), F32),
        shape(w_first.shape, F32), shape(w_middle.shape, F32), shape(w_last.shape, F32), shape(w_reduce.shape, F32),
        shape(w_diff_full.shape, F32), shape(w_diff_half.shape, F32), shape(w_expand.shape, F32),
    ) + (shape((width,), F32),) * 4 + (shape((2048 // D,), F32),) * 2
    so, vg, section_output, input_grad, *grads = outs
    finals = pl.pallas_call(
        functools.partial(final_kernel, (D, S)),
        out_shape=results,
        in_specs=[any_spec] * 4 + [vmem_spec] * 7,
        out_specs=(any_spec,) * 4 + (vmem_spec,) * 15,
        scratch_shapes=[
            pltpu.SemaphoreType.DMA((2, 8)), vm(stem_cot.shape, BF16), vm(section_input.shape, BF16),
            vm(section_input.shape, BF16), vm(clip_video.shape, F32)],
        compiler_params=pltpu.CompilerParams(vmem_limit_bytes=VMEM_BYTES),
        name="final_outputs",
    )(so.reshape(stem_cot.shape), vg.reshape(clip_video.shape), section_output, input_grad, *grads)
    return finals[0:4] + (finals[4].transpose(2, 0, 1), finals[5].transpose(2, 0, 1)) + finals[6:]


def fits_kernel(mesh):
    dp_count, sp_count = mesh.shape["dp"], mesh.shape["sp"]
    return (
        dp_count % 2 == 0 and dp_count & (dp_count - 1) == 0 and sp_count % 2 == 0 and H5 == 2 * sp_count and HS == 8 * sp_count
        and TDM_C % (16 * dp_count) == 0 and STEM_C == 8 * dp_count and MID // sp_count % LANES == 0
        and C5 // dp_count % LANES == 0 and (dp_count - 1) * (sp_count // 2 - 1) <= dp_count
    )


def solution(mesh):
    placed = (
        P("dp", None, "sp", None),
        P("dp", "sp", None, None),
        P("dp"),
        P(None, None, "dp"),
        P(None, None, "dp"),
        P("dp", None),
        P(None, "dp", None),
        P("dp", None),
        P("dp", None),
        P(None, "dp", None),
        P(None, "dp", None),
        P("dp", None),
        P("dp"),
        P("dp"),
        P("dp"),
        P("dp"),
        P("dp"),
        P("dp"),
        P("dp", None, "sp", None),
        P("dp", "sp", None, None),
    )
    return jax.shard_map(
        on_device_kernel if fits_kernel(mesh) else on_device,
        mesh=mesh,
        in_specs=placed,
        out_specs=(
            P("dp", None, "sp", None),
            P("dp", None, "sp", None),
            P("dp", "sp", None, None),
            P("dp", "sp", None, None),
            P(None, None, "dp"),
            P(None, None, "dp"),
            P("dp", None),
            P(None, "dp", None),
            P("dp", None),
            P("dp", None),
            P(None, "dp", None),
            P(None, "dp", None),
            P("dp", None),
            P("dp"),
            P("dp"),
            P("dp"),
            P("dp"),
            P("dp"),
            P("dp"),
        ),
        check_vma=False,
    )
```
